32 devices in a mesh: tm: 8 (over z, x), batch: 4 (over y, core).
Axes of the slice: x: 2, y: 2, z: 4, core: 2. Of those that a mesh axis runs over, the one named last changes fastest.
Arguments:
- clip_input: bfloat16 [32, 64, 8, 256], P('batch', 'tm'), may hold values from -6 to 6
- frame_counts: int32 [32], replicated, may hold values from 8 to 64, as said below
- clip_order: int32 [4, 8], replicated, may hold values from 0 to 7, each once within a row
- cotangent: float32 [32, 512], P('batch'), may hold values from -6 to 6
- kernel_one: float32 [9, 256, 512], P(None, 'batch', 'tm'), may hold values from -0.125 to 0.125
- kernel_one_mean: float32 [9, 256, 512], P(None, 'batch', 'tm'), may hold values from -0.00018310547 to 0.00018310547
- kernel_one_square: float32 [9, 256, 512], P(None, 'batch', 'tm'), may hold values from 3.5300842e-11 to 5.648135e-10
- kernel_two: float32 [9, 512, 512], P(None, 'batch', 'tm'), may hold values from -0.09375 to 0.09375
- kernel_two_mean: float32 [9, 512, 512], P(None, 'batch', 'tm'), may hold values from -0.00018310547 to 0.00018310547
- kernel_two_square: float32 [9, 512, 512], P(None, 'batch', 'tm'), may hold values from 3.5300842e-11 to 5.648135e-10
- norm_params: float32 [4, 512], P(None, 'tm')
- norm_mean: float32 [4, 512], P(None, 'tm'), may hold values from -0.0007324219 to 0.0007324219
- norm_square: float32 [4, 512], P(None, 'tm'), may hold values from 5.648135e-10 to 9.037016e-09
Outputs:
- pooled: float32 [32, 512], P('batch')
- input_grad: bfloat16 [32, 64, 8, 256], P('batch', 'tm')
- grad_norm: float32 [], replicated
- kernel_one_grad: float32 [9, 256, 512], P(None, 'batch', 'tm')
- kernel_one_mean_new: float32 [9, 256, 512], P(None, 'batch', 'tm')
- kernel_one_square_new: float32 [9, 256, 512], P(None, 'batch', 'tm')
- kernel_one_new: float32 [9, 256, 512], P(None, 'batch', 'tm')
- kernel_one_copy: bfloat16 [9, 256, 512], P(None, 'batch', 'tm')
- kernel_two_grad: float32 [9, 512, 512], P(None, 'batch', 'tm')
- kernel_two_mean_new: float32 [9, 512, 512], P(None, 'batch', 'tm')
- kernel_two_square_new: float32 [9, 512, 512], P(None, 'batch', 'tm')
- kernel_two_new: float32 [9, 512, 512], P(None, 'batch', 'tm')
- kernel_two_copy: bfloat16 [9, 512, 512], P(None, 'batch', 'tm')
- norm_grad: float32 [4, 512], P(None, 'tm')
- norm_mean_new: float32 [4, 512], P(None, 'tm')
- norm_square_new: float32 [4, 512], P(None, 'tm')
- norm_new: float32 [4, 512], P(None, 'tm')
- norm_copy: bfloat16 [4, 512], P(None, 'tm')
The draws below stay inside these ranges and needn't reach their ends.
Inputs may be any that keep to these rules, and one draw needn't show every extreme that they name: `frame_counts`: in every group of 8 consecutive clips one clip, drawn from the seed, has all 64 frames valid. `clip_order`: each row holds every number below 8 once.
All inputs are finite; a program needn't handle non-finite values.
Results may differ from the reference program's by a relative error of at most 0.012.
Values may be sent and summed in bfloat16 or wider, within the bound.
No kernel may reach another device: no remote copies, remote signals or barrier semaphores. Data moves between devices by JAX's collectives and lax.ppermute only.
A program may use at most 128 MiB of HBM per device.

```python
import math
import jax
import jax.numpy as jnp
from jax import lax

C1 = 256
C2 = 512
MEL = 8
CL_MB = 2
MB = 4
STEP = 10
FRAMES = 64
CL_DEV = 8
CLIPS = 32
N_BATCH = 4


def draw_frame_counts(key, part):
    key = jax.random.fold_in(key, 3)
    count_key, pick_key = jax.random.split(key)
    group_total = CLIPS // CL_DEV
    lowest = max(2, FRAMES // 8)
    drawn = jax.random.randint(count_key, (group_total, CL_DEV), lowest, FRAMES + 1)
    chosen = jax.random.randint(pick_key, (group_total, 1), 0, CL_DEV)
    full_mask = jnp.arange(CL_DEV)[None, :] == chosen
    return jnp.where(full_mask, FRAMES, drawn).reshape(CLIPS).astype(jnp.int32)


def draw_norm_params(key, part):
    key = jax.random.fold_in(key, 7)
    gain_key, shift_key = jax.random.split(key)
    channel_ramp = jnp.arange(C2, dtype=jnp.float32) / max(C2 - 1, 1)
    gain_rows = (1.0 + 2.0 * channel_ramp) * jax.random.uniform(gain_key, (2, C2), jnp.float32, 0.8, 1.2)
    shift_rows = 0.3 * jax.random.normal(shift_key, (2, C2), jnp.float32)
    return jnp.stack([gain_rows[0], shift_rows[0], gain_rows[1], shift_rows[1]]).astype(jnp.float32)


def level_of(own_key, shape, shards, least, largest):
    level, own = 1.0, jax.random.fold_in(own_key, 6)
    for axis_at, blocks in shards:
        steps = jnp.exp(jax.random.uniform(jax.random.fold_in(own, axis_at), (blocks,), jnp.float32, least / len(shards), largest / len(shards)))
        level = level * jnp.repeat(steps, shape[axis_at] // blocks).reshape([-1 if axis == axis_at else 1 for axis in range(len(shape))])
    return level


def gaussian(own_key, extent, deviation, reach, cuts=(), kind=jnp.bfloat16):
    factor_of = level_of(own_key, extent, cuts, -0.22, 0.18) if cuts else 1.0
    result = jax.random.normal(own_key, extent, jnp.float32) * deviation * factor_of
    return jnp.minimum(jnp.maximum(result, -reach), reach).astype(kind)


def setup_inputs(seed: int = 0) -> dict:
    key_list = jax.random.split(jax.random.key(seed), 14)
    return {
        "clip_input": gaussian(key_list[0], (CLIPS, FRAMES, MEL, C1), 1.0, 6.0, ((0, 4), (1, 8))),
        "frame_counts": draw_frame_counts(jax.random.fold_in(key_list[13], 71), 0),
        "clip_order": jax.vmap(lambda own: jax.random.permutation(own, CL_DEV))(jax.random.split(key_list[2], N_BATCH)).reshape((N_BATCH, CL_DEV)).astype(jnp.int32),
        "cotangent": gaussian(key_list[3], (CLIPS, C2), 1.0, 6.0, ((0, 4),), jnp.float32),
        "kernel_one": gaussian(key_list[4], (9, C1, C2), (9 * C1) ** -0.5, 0.125, ((1, 4), (2, 8)), jnp.float32),
        "kernel_one_mean": gaussian(key_list[5], (9, C1, C2), (0.055 / (9 * C1 * C2 + 9 * C2 * C2 + 4 * C2) ** 0.5), 0.00018310547, ((1, 4), (2, 8)), jnp.float32),
        "kernel_one_square": jnp.clip(jnp.exp(math.log(5.648134737690214e-10) - 2.7725887 * jax.random.uniform(key_list[6], (9, C1, C2), jnp.float32) ** level_of(key_list[6], (9, C1, C2), ((1, 4), (2, 8)), -0.2, 0.2)), 3.5300842110563835e-11, 5.648134737690214e-10),
        "kernel_two": gaussian(key_list[7], (9, C2, C2), (9 * C2) ** -0.5, 0.09375, ((1, 4), (2, 8)), jnp.float32),
        "kernel_two_mean": gaussian(key_list[8], (9, C2, C2), (0.055 / (9 * C1 * C2 + 9 * C2 * C2 + 4 * C2) ** 0.5), 0.00018310547, ((1, 4), (2, 8)), jnp.float32),
        "kernel_two_square": jnp.clip(jnp.exp(math.log(5.648134737690214e-10) - 2.7725887 * jax.random.uniform(key_list[9], (9, C2, C2), jnp.float32) ** level_of(key_list[9], (9, C2, C2), ((1, 4), (2, 8)), -0.2, 0.2)), 3.5300842110563835e-11, 5.648134737690214e-10),
        "norm_params": draw_norm_params(jax.random.fold_in(key_list[13], 71), 0),
        "norm_mean": gaussian(key_list[11], (4, C2), (0.22 / (9 * C1 * C2 + 9 * C2 * C2 + 4 * C2) ** 0.5), 0.0007324219, ((1, 8),), jnp.float32),
        "norm_square": jnp.clip(jnp.exp(math.log(9.037015580304342e-09) - 2.7725887 * jax.random.uniform(key_list[12], (4, C2), jnp.float32) ** level_of(key_list[12], (4, C2), ((1, 8),), -0.2, 0.2)), 5.648134737690214e-10, 9.037015580304342e-09),
    }


BETA_ONE = 0.9
BETA_TWO = 0.999
ADAM_EPS = 1e-08
NORM_EPS = 1e-05
WEIGHT_DECAY = 0.01
CLIP_NORM = 0.5
GAIN_RATE = 1.0

@jax.custom_vjp
def low(v):
    return lax.optimization_barrier(v.astype(jnp.bfloat16)).astype(jnp.float32)

@jax.custom_vjp
def low_back(v):
    return v

def low_keep(v):
    return (low(v), None)

def low_pass(kept, grad):
    return (grad,)

def back_keep(v):
    return (v, None)

def back_low(kept, grad):
    return (low(grad),)
low.defvjp(low_keep, low_pass)
low_back.defvjp(back_keep, back_low)

def conv_same(field_data, kernel):
    return lax.conv_general_dilated(field_data, kernel, (1, 1), 'SAME', dimension_numbers=('NHWC', 'HWIO', 'NHWC'), precision=lax.Precision.HIGHEST)

def norm_apply(pre_norm, frame_mask, pixels, gain_row, shift_row):
    masked = pre_norm * frame_mask
    channel_mean = lax.optimization_barrier(jnp.sum(masked, axis=(0, 1, 2))) / pixels
    variance = lax.optimization_barrier(jnp.sum(masked * pre_norm, axis=(0, 1, 2))) / pixels - channel_mean * channel_mean
    return gain_row * ((pre_norm - channel_mean) * lax.rsqrt(variance + NORM_EPS)) + shift_row

def adam_step(weight, moment, square, summed, factor, step_rate, decay_rate):
    clipped = summed * factor
    moment_new = BETA_ONE * moment + (1.0 - BETA_ONE) * clipped
    square_new = BETA_TWO * square + (1.0 - BETA_TWO) * clipped * clipped
    corrected = moment_new / (1.0 - BETA_ONE ** STEP)
    scaled = jnp.sqrt(square_new / (1.0 - BETA_TWO ** STEP)) + ADAM_EPS
    weight_new = weight - step_rate * (corrected / scaled + decay_rate * weight)
    return (clipped, moment_new, square_new, weight_new, weight_new.astype(jnp.bfloat16))

def reference(clip_input, frame_counts, clip_order, cotangent, kernel_one, kernel_one_mean, kernel_one_square, kernel_two, kernel_two_mean, kernel_two_square, norm_params, norm_mean, norm_square):
    slot_table = jnp.arange(N_BATCH, dtype=jnp.int32)[:, None] * CL_DEV + clip_order
    groups = jnp.transpose(slot_table.reshape(N_BATCH, MB, CL_MB), (1, 0, 2)).reshape(MB, N_BATCH * CL_MB)
    frame_place = jnp.arange(FRAMES, dtype=jnp.int32)
    pooled_place = 2 * jnp.arange(FRAMES // 2, dtype=jnp.int32) + 1

    def forward(inputs, weight_one, weight_two, gain_params):
        first_kernel = low(weight_one).reshape(3, 3, C1, C2)
        second_kernel = low(weight_two).reshape(3, 3, C2, C2)
        gain_table = low(gain_params)
        pooled = jnp.zeros((CLIPS, C2), jnp.float32)
        for micro_step in range(MB):
            slot_ids = groups[micro_step]
            clip_counts = frame_counts[slot_ids]
            frame_mask = (frame_place[None, :] < clip_counts[:, None]).astype(jnp.float32)[:, :, None, None]
            pixels = (MEL * jnp.sum(clip_counts)).astype(jnp.float32)
            masked_input = inputs[slot_ids] * frame_mask
            pre_one = low_back(conv_same(masked_input, first_kernel))
            hidden = low(jax.nn.silu(norm_apply(pre_one, frame_mask, pixels, gain_table[0], gain_table[1])) * frame_mask)
            pre_two = low_back(conv_same(hidden, second_kernel))
            activation = jax.nn.silu(norm_apply(pre_two, frame_mask, pixels, gain_table[2], gain_table[3])) * frame_mask
            pooled_cells = activation.reshape(N_BATCH * CL_MB, FRAMES // 2, 2, MEL // 2, 2, C2).mean(axis=(2, 4))
            summary = pooled_cells.mean(axis=2)
            pool_mask = (pooled_place[None, :] < clip_counts[:, None]).astype(jnp.float32)[:, :, None]
            halves = (clip_counts // 2).astype(jnp.float32)[:, None]
            clip_rows = lax.optimization_barrier(jnp.sum(summary * pool_mask, axis=1)) / halves + jnp.log(lax.optimization_barrier(jnp.sum(jnp.exp(summary) * pool_mask, axis=1)) / halves)
            pooled = pooled.at[slot_ids].set(clip_rows)
        return pooled
    pooled, pullback = jax.vjp(forward, clip_input.astype(jnp.float32), kernel_one, kernel_two, norm_params)
    input_grad, sum_one, sum_two, norm_sum = pullback(cotangent)
    grad_norm = jnp.sqrt(jnp.sum(sum_one * sum_one) + jnp.sum(sum_two * sum_two) + jnp.sum(norm_sum * norm_sum))
    factor = jnp.minimum(1.0, CLIP_NORM / (grad_norm + 1e-06))
    one_grad, one_moment, one_square, one_new, one_copy = adam_step(kernel_one, kernel_one_mean, kernel_one_square, sum_one, factor, (9 * C1) ** (-0.5), WEIGHT_DECAY)
    two_grad, two_moment, two_square, two_new, two_copy = adam_step(kernel_two, kernel_two_mean, kernel_two_square, sum_two, factor, (9 * C2) ** (-0.5), WEIGHT_DECAY)
    gain_grad, gain_moment, gain_square, gain_new, gain_copy = adam_step(norm_params, norm_mean, norm_square, norm_sum, factor, GAIN_RATE, 0.0)
    return (pooled, input_grad.astype(jnp.bfloat16), grad_norm, one_grad, one_moment, one_square, one_new, one_copy, two_grad, two_moment, two_square, two_new, two_copy, gain_grad, gain_moment, gain_square, gain_new, gain_copy)
```

```python
import functools

import jax
import jax.numpy as jnp
from jax import lax
from jax.experimental import pallas as pl
from jax.experimental.pallas import tpu as pltpu
from jax.sharding import Mesh, PartitionSpec as P

C1 = 256
C2 = 512
MEL = 8
FR_DEV = 8
CL_MB = 2
MB = 4
STEP = 10


BETA_ONE = 0.9
BETA_TWO = 0.999
ADAM_EPS = 1e-08
NORM_EPS = 1e-05
WEIGHT_DECAY = 0.01
CLIP_NORM = 0.5
GAIN_RATE = 1.0


def extended(block, sides, width):
    for axis, dim in sides:
        count = lax.axis_size(axis)
        forward = [(i, i + 1) for i in range(count - 1)]
        backward = [(target, source) for source, target in forward]
        low = lax.ppermute(
            lax.slice_in_dim(block, block.shape[dim] - width, None, axis=dim), axis, forward
        )
        high = lax.ppermute(lax.slice_in_dim(block, 0, width, axis=dim), axis, backward)
        block = jnp.concatenate([low, block, high], axis=dim)
    return block


def silu_slope(shaped):
    sigmoid_value = jax.nn.sigmoid(shaped)
    return sigmoid_value * (1.0 + shaped * (1.0 - sigmoid_value))


def pad_mel(field_data):
    return jnp.pad(field_data, ((0, 0), (0, 0), (1, 1), (0, 0)))


def frame_rim(field_data):
    return pad_mel(extended(field_data, (("tm", 1),), 1))


def grad_rim(field_data):
    return pad_mel(extended(field_data, (("tm", 1),), 1))


def patches(padded, frame_count, mel_count):
    pieces = [
        padded[:, step_time : step_time + frame_count, step_mel : step_mel + mel_count, :]
        for step_time in range(3)
        for step_mel in range(3)
    ]
    columns = jnp.concatenate(pieces, axis=-1)
    return columns.reshape(-1, columns.shape[-1])


def norm_forward(pre_norm, frame_mask, pixels, gain_row, shift_row):
    masked = pre_norm * frame_mask
    total_sum, square_sum = lax.psum(
        (jnp.sum(masked, axis=(0, 1, 2)), jnp.sum(masked * pre_norm, axis=(0, 1, 2))),
        ("tm", "batch"),
    )
    channel_mean = total_sum / pixels
    variance = square_sum / pixels - channel_mean * channel_mean
    inv_scale = lax.rsqrt(variance + NORM_EPS)
    normed = (pre_norm - channel_mean) * inv_scale
    return (normed, inv_scale, gain_row * normed + shift_row)


def norm_backward(outer_grad, frame_mask, shaped, normed, inv_scale, gain_row, pixels):
    slope_grad = outer_grad * frame_mask * silu_slope(shaped)
    shift_grad, gain_grad = lax.psum(
        (jnp.sum(slope_grad, axis=(0, 1, 2)), jnp.sum(slope_grad * normed, axis=(0, 1, 2))),
        ("tm", "batch"),
    )
    pre_grad = (
        frame_mask
        * inv_scale
        * gain_row
        * (slope_grad - shift_grad / pixels - normed * gain_grad / pixels)
    )
    return (pre_grad.astype(jnp.bfloat16), gain_grad, shift_grad)


def adam_step(weight, moment, square, summed, factor, step_rate, decay_rate):
    clipped = summed * factor
    moment_new = BETA_ONE * moment + (1.0 - BETA_ONE) * clipped
    square_new = BETA_TWO * square + (1.0 - BETA_TWO) * clipped * clipped
    corrected = moment_new / (1.0 - BETA_ONE**STEP)
    scaled = jnp.sqrt(square_new / (1.0 - BETA_TWO**STEP)) + ADAM_EPS
    weight_new = weight - step_rate * (corrected / scaled + decay_rate * weight)
    return (clipped, moment_new, square_new, weight_new, weight_new.astype(jnp.bfloat16))


def contract_rows(columns, grads):
    return lax.dot_general(
        columns, grads, (((0,), (0,)), ((), ())), preferred_element_type=jnp.float32
    )


def general_body(
    clip_input,
    frame_counts,
    clip_order,
    cotangent,
    kernel_one,
    kernel_one_mean,
    kernel_one_square,
    kernel_two,
    kernel_two_mean,
    kernel_two_square,
    norm_params,
    norm_mean,
    norm_square,
):
    batch_count = lax.axis_size("batch")
    tm_count = lax.axis_size("tm")
    tm_index = lax.axis_index("tm")
    batch_index = lax.axis_index("batch")
    half_frames = FR_DEV // 2
    counts_table = jnp.take_along_axis(frame_counts.reshape(batch_count, -1), clip_order, axis=1)
    valid_pixels = (
        MEL * jnp.sum(counts_table.reshape(batch_count, MB, CL_MB), axis=(0, 2))
    ).astype(jnp.float32)
    local_order = lax.dynamic_index_in_dim(clip_order, batch_index, 0, keepdims=False)
    local_counts = lax.dynamic_index_in_dim(counts_table, batch_index, 0, keepdims=False)
    frame_place = tm_index * FR_DEV + jnp.arange(FR_DEV, dtype=jnp.int32)
    pooled_place = 2 * (tm_index * half_frames + jnp.arange(half_frames, dtype=jnp.int32)) + 1
    low_one = kernel_one.astype(jnp.bfloat16)
    low_two = kernel_two.astype(jnp.bfloat16)
    low_gains = norm_params.astype(jnp.bfloat16)
    shape_out = (CL_MB, FR_DEV, MEL, C2)
    pooled = jnp.zeros((MB * CL_MB, C2), jnp.float32)
    input_grad = jnp.zeros(clip_input.shape, jnp.bfloat16)
    sum_one = jnp.zeros((9 * C1, C2), jnp.float32)
    sum_two = jnp.zeros((9 * C2, C2), jnp.float32)
    norm_sum = jnp.zeros((4, C2), jnp.float32)
    for micro_step in range(MB):
        tm_parts = (
            lax.all_gather(low_one, "tm", axis=2, tiled=True),
            lax.all_gather(low_two, "tm", axis=2, tiled=True),
            lax.all_gather(low_gains, "tm", axis=1, tiled=True),
        )
        full_one, full_two = (
            lax.all_gather(tm_parts[0], "batch", axis=1, tiled=True),
            lax.all_gather(tm_parts[1], "batch", axis=1, tiled=True),
        )
        weights = (full_one, full_two, tm_parts[2])
        gain_table = weights[2].astype(jnp.float32)
        flat_one = weights[0].reshape(9 * C1, C2)
        flat_two = weights[1].reshape(9 * C2, C2)
        slot_ids = local_order[micro_step * CL_MB : (micro_step + 1) * CL_MB]
        clip_counts = local_counts[micro_step * CL_MB : (micro_step + 1) * CL_MB]
        frame_mask = (frame_place[None, :] < clip_counts[:, None]).astype(jnp.float32)[
            :, :, None, None
        ]
        pool_mask = (pooled_place[None, :] < clip_counts[:, None]).astype(jnp.float32)[:, :, None]
        halves = (clip_counts // 2).astype(jnp.float32)[:, None]
        pixels = valid_pixels[micro_step]
        masked_input = jnp.take(clip_input, slot_ids, axis=0) * frame_mask.astype(jnp.bfloat16)
        input_columns = patches(frame_rim(masked_input), FR_DEV, MEL)
        pre_one = jnp.dot(input_columns, flat_one, preferred_element_type=jnp.float32).reshape(
            shape_out
        )
        normed_one, scale_one, shaped_one = norm_forward(
            pre_one, frame_mask, pixels, gain_table[0], gain_table[1]
        )
        hidden = (jax.nn.silu(shaped_one) * frame_mask).astype(jnp.bfloat16)
        hidden_columns = patches(frame_rim(hidden), FR_DEV, MEL)
        pre_two = jnp.dot(hidden_columns, flat_two, preferred_element_type=jnp.float32).reshape(
            shape_out
        )
        normed_two, scale_two, shaped_two = norm_forward(
            pre_two, frame_mask, pixels, gain_table[2], gain_table[3]
        )
        activation = jax.nn.silu(shaped_two) * frame_mask
        summary = jnp.mean(activation.reshape(CL_MB, half_frames, 2, MEL, C2), axis=(2, 3))
        exp_summary = jnp.exp(summary)
        mean_part, exp_part = lax.psum(
            (jnp.sum(summary * pool_mask, axis=1), jnp.sum(exp_summary * pool_mask, axis=1)), "tm"
        )
        pooled = pooled.at[slot_ids].set(mean_part / halves + jnp.log(exp_part / halves))
        cot_rows = jnp.take(cotangent, slot_ids, axis=0)[:, None, :]
        summary_grad = pool_mask * (
            cot_rows / halves[:, :, None] + cot_rows * exp_summary / exp_part[:, None, :]
        )
        activation_grad = jnp.broadcast_to(
            (summary_grad / (2 * MEL))[:, :, None, None, :], (CL_MB, half_frames, 2, MEL, C2)
        ).reshape(shape_out)
        grad_two, gain_two_grad, shift_two_grad = norm_backward(
            activation_grad, frame_mask, shaped_two, normed_two, scale_two, gain_table[2], pixels
        )
        sum_two = sum_two + contract_rows(hidden_columns, grad_two.reshape(-1, C2))
        flip_two = weights[1][::-1].transpose(0, 2, 1).reshape(9 * C2, C2)
        hidden_grad = jnp.dot(
            patches(grad_rim(grad_two), FR_DEV, MEL), flip_two, preferred_element_type=jnp.float32
        ).reshape(shape_out)
        grad_one, gain_one_grad, shift_one_grad = norm_backward(
            hidden_grad, frame_mask, shaped_one, normed_one, scale_one, gain_table[0], pixels
        )
        sum_one = sum_one + contract_rows(input_columns, grad_one.reshape(-1, C2))
        flip_one = weights[0][::-1].transpose(0, 2, 1).reshape(9 * C2, C1)
        rows_grad = jnp.dot(
            patches(grad_rim(grad_one), FR_DEV, MEL), flip_one, preferred_element_type=jnp.float32
        ).reshape(CL_MB, FR_DEV, MEL, C1)
        input_grad = input_grad.at[slot_ids].set((rows_grad * frame_mask).astype(jnp.bfloat16))
        norm_sum = norm_sum + jnp.stack(
            [gain_one_grad, shift_one_grad, gain_two_grad, shift_two_grad]
        )
    batch_parts = (
        lax.psum_scatter(sum_one.reshape(9, C1, C2), "batch", scatter_dimension=1, tiled=True),
        lax.psum_scatter(sum_two.reshape(9, C2, C2), "batch", scatter_dimension=1, tiled=True),
    )
    grad_one_shard, grad_two_shard = (
        lax.psum_scatter(batch_parts[0], "tm", scatter_dimension=2, tiled=True),
        lax.psum_scatter(batch_parts[1], "tm", scatter_dimension=2, tiled=True),
    )
    shard_width = C2 // tm_count
    norm_shard = lax.dynamic_slice_in_dim(norm_sum, tm_index * shard_width, shard_width, 1)
    norm_term = jnp.where(batch_index == 0, jnp.sum(norm_shard * norm_shard), 0.0)
    own_squares = (
        jnp.sum(grad_one_shard * grad_one_shard)
        + jnp.sum(grad_two_shard * grad_two_shard)
        + norm_term
    )
    grad_norm = jnp.sqrt(lax.psum(own_squares, ("tm", "batch")))
    factor = jnp.minimum(1.0, CLIP_NORM / (grad_norm + 1e-06))
    first_update = adam_step(
        kernel_one,
        kernel_one_mean,
        kernel_one_square,
        grad_one_shard,
        factor,
        (9 * C1) ** (-0.5),
        WEIGHT_DECAY,
    )
    second_update = adam_step(
        kernel_two,
        kernel_two_mean,
        kernel_two_square,
        grad_two_shard,
        factor,
        (9 * C2) ** (-0.5),
        WEIGHT_DECAY,
    )
    norm_update = adam_step(norm_params, norm_mean, norm_square, norm_shard, factor, GAIN_RATE, 0.0)
    return (pooled, input_grad, grad_norm) + first_update + second_update + norm_update


AXES = ("z", "x", "y", "core")
BF = jnp.bfloat16
F32 = jnp.float32
ROWS = 512
CLIPS_CORE = 4
LANES = 128
TAPS = 9
ANY = pl.BlockSpec(memory_space=pl.ANY)
VM = pl.BlockSpec(memory_space=pltpu.VMEM)
SM = pl.BlockSpec(memory_space=pltpu.SMEM)
VMEM_LIMIT = 56 * 1024 * 1024


def shape_of(shape, dtype):
    return jax.ShapeDtypeStruct(shape, dtype)


def call(kernel, out, in_specs, out_specs, scratch=(), flops=0, moved=0):
    return pl.pallas_call(
        kernel,
        out_shape=out,
        in_specs=in_specs,
        out_specs=out_specs,
        scratch_shapes=list(scratch),
        compiler_params=pltpu.CompilerParams(vmem_limit_bytes=VMEM_LIMIT),
        cost_estimate=pl.CostEstimate(flops=flops, bytes_accessed=moved, transcendentals=0),
    )


def swap(value, axis, step=1):
    size = lax.axis_size(axis)
    return lax.ppermute(value, axis, [(i, i ^ step) for i in range(size)])


def run_copies(copies, sems):
    started = []
    for at, (source, target) in enumerate(copies):
        copy = pltpu.make_async_copy(source, target, sems.at[at])
        copy.start()
        started.append(copy)
    for copy in started:
        copy.wait()


def time_shift(rows, step):
    zero = jnp.zeros((MEL, rows.shape[1]), rows.dtype)
    if step == 1:
        return jnp.concatenate([rows[MEL:], zero], axis=0)
    if step == -1:
        return jnp.concatenate([zero, rows[:-MEL]], axis=0)
    return rows


def mel_shift(rows, step):
    if step == 0:
        return rows
    cube = rows.reshape(rows.shape[0] // MEL, MEL, rows.shape[1])
    turned = pltpu.roll(cube, (-step) % MEL, 1)
    place = lax.broadcasted_iota(jnp.int32, cube.shape, 1) + step
    keep = (place >= 0) & (place < MEL)
    return jnp.where(keep, turned, 0.0).reshape(rows.shape)


def valid_rows(count, width):
    frame = lax.broadcasted_iota(jnp.int32, (ROWS, width), 0) // MEL
    return (frame < count).astype(F32)


def dot_nt(left, right):
    return lax.dot_general(left, right, (((1,), (1,)), ((), ())), preferred_element_type=F32)


def dot_nn(left, right):
    return lax.dot_general(left, right, (((1,), (0,)), ((), ())), preferred_element_type=F32)


def dot_tn(left, right):
    return lax.dot_general(left, right, (((0,), (0,)), ((), ())), preferred_element_type=F32)


def lanes_of(tap):
    return slice(tap * LANES, (tap + 1) * LANES)


def gather_taps(product):
    total = None
    for mel in range(3):
        column = None
        for time in range(3):
            term = time_shift(product[:, lanes_of(3 * time + mel)], time - 1)
            column = term if column is None else column + term
        column = mel_shift(column, mel - 1)
        total = column if total is None else total + column
    return total


def scatter_taps(grad, target, base):
    for mel in range(3):
        moved = mel_shift(grad, 1 - mel)
        for time in range(3):
            target[base : base + ROWS, lanes_of(3 * time + mel)] = time_shift(moved, 1 - time).astype(
                BF
            )


def channel_sums(first, second):
    return (jnp.sum(first, axis=0, keepdims=True), jnp.sum(second, axis=0, keepdims=True))


def norm_rows(own_ref, other_ref, pixels):
    mean = (own_ref[0:1, :] + other_ref[0:1, :]) / pixels
    square = (own_ref[1:2, :] + other_ref[1:2, :]) / pixels
    return mean, lax.rsqrt(square - mean * mean + NORM_EPS)


def put_pair(ref, first, second):
    ref[...] = jnp.zeros(ref.shape, F32)
    ref[0:1, :] = first
    ref[1:2, :] = second


def take_kernel(ids_ref, clip_ref, *rest):
    outs, sems = rest[:MB], rest[MB]
    z = lax.axis_index("z")
    copies = []
    for step in range(MB):
        plane = jnp.bitwise_xor(z, step)
        for j in range(CL_MB):
            copies.append((clip_ref.at[ids_ref[plane * CL_MB + j]], outs[step].at[j]))
    run_copies(copies, sems)


def weights_kernel(one_ref, two_ref, one_keep, one_send, two_keep, two_send, turned):
    y = lax.axis_index("y")
    for tap in range(TAPS):
        for source, width, keep, send in (
            (one_ref, 64, one_keep, one_send),
            (two_ref, 128, two_keep, two_send),
        ):
            turned[:, 0:width] = jnp.swapaxes(source[tap], 0, 1)
            keep[tap] = turned[pl.ds(y * 32, 32), 0:width].astype(BF)
            send[tap] = turned[pl.ds((1 - y) * 32, 32), 0:width].astype(BF)


def first_conv_kernel(
    counts_ref, a0, a1, a23, b0, b1, b23, w_own, w_other, pre_ref, x_ref, weight_ref, stat_ref, low, sems
):
    z, x, y, core = (lax.axis_index(axis) for axis in AXES)
    copies = []
    for step in range(MB):
        z_of = jnp.bitwise_xor(z, step)
        for j, pieces in (
            (0, ((a0, 0, x, y), (a1, 0, 1 - x, y), (a23, 0, x, 1 - y), (a23, MB, 1 - x, 1 - y))),
            (1, ((b0, 0, x, y), (b1, 0, x, 1 - y), (b23, 0, 1 - x, y), (b23, MB, 1 - x, 1 - y))),
        ):
            for source, base, x_of, y_of in pieces:
                row = pl.multiple_of((y_of * CL_MB + j) * ROWS + (z_of * 2 + x_of) * 64, 64)
                copies.append((source.at[base + step], x_ref.at[pl.ds(row, 64), :]))
    run = []
    for at, (source, target) in enumerate(copies):
        copy = pltpu.make_async_copy(source, target, sems.at[at])
        copy.start()
        run.append(copy)
    place_in = lax.broadcasted_iota(jnp.int32, (256, 256), 0)
    place_out = lax.broadcasted_iota(jnp.int32, (256, 256), 1)
    source_in = ((place_out // 64) % 2) * 128 + (place_out // 128) * 64 + place_out % 64
    spread = (place_in == source_in).astype(BF)
    for step in range(MB):
        z_of = jnp.bitwise_xor(z, step)
        own, other = w_own[step, 0:288, :], w_other[step, 0:288, :]
        zero, one = jnp.where(core == 0, own, other), jnp.where(core == 0, other, own)
        both = dot_nn(jnp.concatenate([zero, one], axis=1), spread).astype(BF)
        for tap in range(TAPS):
            weight_ref[tap, z_of] = both[tap * 32 : (tap + 1) * 32]
    for copy in run:
        copy.wait()
    weight = weight_ref[...].reshape(TAPS * LANES, C1)
    first = jnp.zeros((1, LANES), F32)
    second = jnp.zeros((1, LANES), F32)
    for clip in range(CLIPS_CORE):
        span = slice(clip * ROWS, (clip + 1) * ROWS)
        mask = valid_rows(counts_ref[clip], C1)
        masked = x_ref[span, :] * mask.astype(BF)
        x_ref[span, :] = masked
        pre = gather_taps(dot_nt(masked, weight))
        pre_ref[span, :] = pre
        kept = pre * mask[:, 0:LANES]
        plus = channel_sums(kept, kept * pre)
        first, second = first + plus[0], second + plus[1]
    put_pair(stat_ref, first, second)


def hidden_kernel(counts_ref, pixels_ref, pre_ref, own_ref, other_ref, gain_ref, a_ref, b_ref):
    mean, scale = norm_rows(own_ref, other_ref, pixels_ref[0])
    for clip in range(CLIPS_CORE):
        pre = pre_ref[clip * ROWS : (clip + 1) * ROWS, :]
        shaped = gain_ref[0:1, :] * ((pre - mean) * scale) + gain_ref[1:2, :]
        value = shaped * jax.nn.sigmoid(shaped) * valid_rows(counts_ref[clip], LANES)
        target = a_ref if clip < 2 else b_ref
        target[(clip % 2) * ROWS : (clip % 2 + 1) * ROWS, :] = value.astype(BF)


def second_weight_kernel(own_ref, other_ref, weight_ref, pieces, sems):
    z, y, core = (lax.axis_index(axis) for axis in ("z", "y", "core"))
    copies = []
    for source, core_of in ((own_ref, core), (other_ref, 1 - core)):
        for step in range(MB):
            for turn in range(2):
                y_of = jnp.bitwise_xor(y, turn)
                copies.append(
                    (source.at[step, turn], pieces.at[jnp.bitwise_xor(z, step), y_of * 2 + core_of])
                )
    run_copies(copies, sems)
    place_in = lax.broadcasted_iota(jnp.int32, (C2, C2), 0)
    place_out = lax.broadcasted_iota(jnp.int32, (C2, C2), 1)
    source_in = ((place_out // 32) % 4) * 128 + (place_out // 128) * 32 + place_out % 32
    spread = (place_in == source_in).astype(BF)
    for step in range(MB):
        natural = jnp.concatenate([pieces[step, part] for part in range(4)], axis=1)
        both = dot_nn(natural, spread).astype(BF)
        for tap in range(TAPS):
            weight_ref[tap, step] = both[tap * 32 : (tap + 1) * 32]


def hidden_copies(a0, a1, a23, b0, b1, b23, target):
    x, y = lax.axis_index("x"), lax.axis_index("y")
    copies = []
    for source, base, half, x_of, y_of in (
        (a0, None, 0, x, y),
        (a1, None, 0, 1 - x, y),
        (a23, 0, 0, x, 1 - y),
        (a23, 1, 0, 1 - x, 1 - y),
        (b0, None, 1, x, y),
        (b1, None, 1, x, 1 - y),
        (b23, 0, 1, 1 - x, y),
        (b23, 1, 1, 1 - x, 1 - y),
    ):
        lane = pl.multiple_of((x_of * 2 + y_of) * LANES, LANES)
        piece = source if base is None else source.at[base]
        copies.append((piece, target.at[pl.ds(half * 2 * ROWS, 2 * ROWS), pl.ds(lane, LANES)]))
    return copies


def second_conv_kernel(
    counts_ref, a0, a1, a23, b0, b1, b23, weight_ref, pre_ref, stat_ref, hidden, sems
):
    run_copies(hidden_copies(a0, a1, a23, b0, b1, b23, hidden), sems)
    weight = weight_ref[...].reshape(TAPS * LANES, C2)
    first = jnp.zeros((1, LANES), F32)
    second = jnp.zeros((1, LANES), F32)
    for clip in range(CLIPS_CORE):
        span = slice(clip * ROWS, (clip + 1) * ROWS)
        pre = gather_taps(dot_nt(hidden[span, :], weight))
        pre_ref[span, :] = pre
        kept = pre * valid_rows(counts_ref[clip], LANES)
        plus = channel_sums(kept, kept * pre)
        first, second = first + plus[0], second + plus[1]
    put_pair(stat_ref, first, second)


def pool_kernel(
    counts_ref, pixels_ref, pre_ref, own_ref, other_ref, gain_ref, cot_ref, slope_ref, sum_ref, pooled_ref
):
    mean, scale = norm_rows(own_ref, other_ref, pixels_ref[0])
    first = jnp.zeros((1, LANES), F32)
    second = jnp.zeros((1, LANES), F32)
    pooled_ref[...] = jnp.zeros(pooled_ref.shape, F32)
    slots = ROWS // (2 * MEL)
    for clip in range(CLIPS_CORE):
        span = slice(clip * ROWS, (clip + 1) * ROWS)
        count = counts_ref[clip]
        mask = valid_rows(count, LANES)
        normed = (pre_ref[span, :] - mean) * scale
        shaped = gain_ref[2:3, :] * normed + gain_ref[3:4, :]
        gate = jax.nn.sigmoid(shaped)
        active = (shaped * gate * mask).reshape(slots, 2 * MEL, LANES)
        summary = jnp.sum(active, axis=1) / (2 * MEL)
        slot = lax.broadcasted_iota(jnp.int32, (slots, LANES), 0)
        keep = (2 * slot + 1 < count).astype(F32)
        raised = jnp.exp(summary)
        exp_total = jnp.sum(raised * keep, axis=0, keepdims=True)
        halves = (count // 2).astype(F32)
        pooled_ref[clip : clip + 1, :] = jnp.sum(
            summary * keep, axis=0, keepdims=True
        ) / halves + jnp.log(exp_total / halves)
        cot = cot_ref[clip : clip + 1, :]
        summary_grad = keep * (cot / halves + cot * raised / exp_total) / (2 * MEL)
        spread = jnp.broadcast_to(summary_grad[:, None, :], (slots, 2 * MEL, LANES))
        slope = spread.reshape(ROWS, LANES) * mask * (gate * (1.0 + shaped * (1.0 - gate)))
        slope_ref[span, :] = slope
        plus = channel_sums(slope, slope * normed)
        first, second = first + plus[0], second + plus[1]
    put_pair(sum_ref, first, second)


def pre_grad(slope, pre, mask, mean, scale, gain, sums, pixels):
    normed = (pre - mean) * scale
    return mask * (scale * gain) * (slope - sums[0] / pixels - normed * (sums[1] / pixels))


def pair_sums(own_ref, other_ref):
    return (own_ref[0:1, :] + other_ref[0:1, :], own_ref[1:2, :] + other_ref[1:2, :])


def hidden_grad_kernel(
    counts_ref,
    pixels_ref,
    slope_ref,
    pre_ref,
    own_ref,
    other_ref,
    sum_own,
    sum_other,
    gain_ref,
    weight_ref,
    grad_ref,
    a_keep,
    a_send,
    b_keep,
    b_send,
    columns,
    partial,
):
    x, y = lax.axis_index("x"), lax.axis_index("y")
    pixels = pixels_ref[0]
    mean, scale = norm_rows(own_ref, other_ref, pixels)
    sums = pair_sums(sum_own, sum_other)
    weight = weight_ref[...].reshape(TAPS * LANES, C2)
    for clip in range(CLIPS_CORE):
        span = slice(clip * ROWS, (clip + 1) * ROWS)
        mask = valid_rows(counts_ref[clip], LANES)
        grad = pre_grad(
            slope_ref[span, :], pre_ref[span, :], mask, mean, scale, gain_ref[2:3, :], sums, pixels
        )
        grad_ref[span, :] = grad.astype(BF)
        scatter_taps(grad, columns, 0)
        partial[...] = dot_nn(columns[...], weight)
        rows = slice((clip % 2) * ROWS, (clip % 2 + 1) * ROWS)
        for other in range(2):
            if clip < 2:
                keep_lane, send_lane = x * 2 + other, (1 - x) * 2 + other
                keep, send = a_keep, a_send
            else:
                keep_lane, send_lane = other * 2 + y, other * 2 + 1 - y
                keep, send = b_keep, b_send
            keep[other, rows, :] = partial[:, pl.ds(pl.multiple_of(keep_lane * LANES, LANES), LANES)]
            send[other, rows, :] = partial[
                :, pl.ds(pl.multiple_of(send_lane * LANES, LANES), LANES)
            ].astype(BF)


def second_weight_grad_kernel(
    a0, a1, a23, b0, b1, b23, grad_ref, keep_ref, send_ref, hidden, columns, natural, sems
):
    core = lax.axis_index("core")
    run = []
    for at, (source, target) in enumerate(hidden_copies(a0, a1, a23, b0, b1, b23, hidden)):
        copy = pltpu.make_async_copy(source, target, sems.at[at])
        copy.start()
        run.append(copy)
    for clip in range(CLIPS_CORE):
        grad = grad_ref[clip * ROWS : (clip + 1) * ROWS, :].astype(F32)
        scatter_taps(grad, columns, clip * ROWS)
    for copy in run:
        copy.wait()
    place_in = lax.broadcasted_iota(jnp.int32, (C2, C2), 0)
    place_out = lax.broadcasted_iota(jnp.int32, (C2, C2), 1)
    source_in = ((place_out // 32) % 4) * 128 + (place_out // 128) * 32 + place_out % 32
    spread = (place_in == source_in).astype(BF)
    for tap in range(TAPS):
        chip = dot_tn(columns[:, lanes_of(tap)], hidden[...]).astype(BF)
        natural[...] = dot_nn(chip, spread)
        for y_of in range(2):
            keep = natural[:, pl.ds(pl.multiple_of((y_of * 2 + core) * LANES, LANES), LANES)]
            send = natural[:, pl.ds(pl.multiple_of((y_of * 2 + 1 - core) * LANES, LANES), LANES)]
            for z_of in range(MB):
                rows = slice(z_of * 32, (z_of + 1) * 32)
                keep_ref[z_of, y_of, tap] = keep[rows].astype(BF)
                send_ref[z_of, y_of, tap] = send[rows].astype(BF)


def first_slope_kernel(
    counts_ref,
    pixels_ref,
    a_keep,
    a_got,
    b_keep,
    b_got,
    pre_ref,
    own_ref,
    other_ref,
    gain_ref,
    slope_ref,
    sum_ref,
):
    mean, scale = norm_rows(own_ref, other_ref, pixels_ref[0])
    first = jnp.zeros((1, LANES), F32)
    second = jnp.zeros((1, LANES), F32)
    for clip in range(CLIPS_CORE):
        span = slice(clip * ROWS, (clip + 1) * ROWS)
        rows = slice((clip % 2) * ROWS, (clip % 2 + 1) * ROWS)
        keep, got = (a_keep, a_got) if clip < 2 else (b_keep, b_got)
        outer = keep[rows, :] + got[rows, :].astype(F32)
        normed = (pre_ref[span, :] - mean) * scale
        shaped = gain_ref[0:1, :] * normed + gain_ref[1:2, :]
        gate = jax.nn.sigmoid(shaped)
        slope = outer * valid_rows(counts_ref[clip], LANES) * (gate * (1.0 + shaped * (1.0 - gate)))
        slope_ref[span, :] = slope
        plus = channel_sums(slope, slope * normed)
        first, second = first + plus[0], second + plus[1]
    put_pair(sum_ref, first, second)


def first_weight_grad_kernel(
    counts_ref,
    pixels_ref,
    slope_ref,
    pre_ref,
    own_ref,
    other_ref,
    sum_own,
    sum_other,
    gain_ref,
    x_ref,
    keep_ref,
    send_ref,
    columns_ref,
):
    core = lax.axis_index("core")
    pixels = pixels_ref[0]
    mean, scale = norm_rows(own_ref, other_ref, pixels)
    sums = pair_sums(sum_own, sum_other)
    for clip in range(CLIPS_CORE):
        span = slice(clip * ROWS, (clip + 1) * ROWS)
        mask = valid_rows(counts_ref[clip], LANES)
        grad = pre_grad(
            slope_ref[span, :], pre_ref[span, :], mask, mean, scale, gain_ref[0:1, :], sums, pixels
        )
        scatter_taps(grad, columns_ref, clip * ROWS)
    place_in = lax.broadcasted_iota(jnp.int32, (C1, C1), 0)
    place_out = lax.broadcasted_iota(jnp.int32, (C1, C1), 1)
    core_of = jnp.where(place_out < 128, core, 1 - core)
    source_in = ((place_out // 64) % 2) * 128 + core_of * 64 + place_out % 64
    spread = (place_in == source_in).astype(BF)
    for tap in range(TAPS):
        part = dot_tn(columns_ref[:, lanes_of(tap)], x_ref[...]).astype(BF)
        both = dot_nn(part, spread)
        for z_of in range(MB):
            rows = slice(z_of * 32, (z_of + 1) * 32)
            keep_ref[z_of, tap] = both[rows, 0:LANES].astype(BF)
            send_ref[z_of, tap] = both[rows, LANES : 2 * LANES].astype(BF)


def input_grad_kernel(columns_ref, weight_ref, a_keep, a_send, b_keep, b_send, partial):
    x, y = lax.axis_index("x"), lax.axis_index("y")
    weight = weight_ref[...].reshape(TAPS * LANES, C1)
    for clip in range(CLIPS_CORE):
        partial[clip] = dot_nn(columns_ref[clip * ROWS : (clip + 1) * ROWS, :], weight)
    for z_of in range(MB):
        for other in range(2):
            keep_row = pl.multiple_of((z_of * 2 + x) * 64, 64)
            send_row = pl.multiple_of((z_of * 2 + 1 - x) * 64, 64)
            a_keep[other, z_of] = partial[other * CL_MB, pl.ds(keep_row, 64), :]
            a_send[other, z_of] = partial[other * CL_MB, pl.ds(send_row, 64), :].astype(BF)
            row = (z_of * 2 + other) * 64
            b_keep[other, z_of] = partial[y * CL_MB + 1, row : row + 64, :]
            b_send[other, z_of] = partial[(1 - y) * CL_MB + 1, row : row + 64, :].astype(BF)


def pick(table, index):
    return lax.dynamic_index_in_dim(table, index, 0, keepdims=False)


def fast_body(
    clip_input,
    frame_counts,
    clip_order,
    cotangent,
    kernel_one,
    kernel_one_mean,
    kernel_one_square,
    kernel_two,
    kernel_two_mean,
    kernel_two_square,
    norm_params,
    norm_mean,
    norm_square,
):
    z, x, y, core = (lax.axis_index(axis) for axis in AXES)
    group = y * 2 + core
    own_order = pick(clip_order, group)
    pieces = call(
        take_kernel,
        [shape_of((CL_MB, 64, C1), BF)] * MB,
        [SM, ANY],
        [ANY] * MB,
        [pltpu.SemaphoreType.DMA((MB * CL_MB,))],
    )(own_order, clip_input.reshape(MB * CL_MB, 64, C1))
    arrived = [pieces[0]] + [swap(pieces[step], "z", step) for step in range(1, MB)]

    one_keep, one_send, two_keep, two_send = call(
        weights_kernel,
        [shape_of((TAPS, 32, 64), BF)] * 2 + [shape_of((TAPS, 32, 128), BF)] * 2,
        [VM, VM],
        [VM] * 4,
        [pltpu.VMEM((64, 128), F32)],
    )(kernel_one, kernel_two)
    one_got, two_got = swap(one_send, "y"), swap(two_send, "y")
    one_flat = jnp.where(
        y == 0,
        jnp.concatenate([one_keep, one_got], axis=2),
        jnp.concatenate([one_got, one_keep], axis=2),
    ).reshape(288, LANES)
    low_gains = lax.dynamic_slice_in_dim(norm_params.astype(BF), y * 32, 32, 1).reshape(1, LANES)
    one_flat = jnp.concatenate([one_flat, jnp.pad(low_gains, ((0, 15), (0, 0)))], axis=0)
    one_all = jnp.stack([one_flat] + [swap(one_flat, "z", step) for step in range(1, MB)])
    one_other = swap(one_all, "core")

    hit = clip_order[:, :, None] == jnp.arange(MB * CL_MB, dtype=jnp.int32)
    table = jnp.sum(hit * frame_counts.reshape(-1, 1, MB * CL_MB), axis=2)
    plane = lax.dynamic_slice_in_dim(table.reshape(-1, MB, CL_MB), z, 1, 1)[:, 0]
    pixels = (MEL * jnp.sum(plane)).astype(F32).reshape(1)
    counts = lax.dynamic_slice_in_dim(plane.reshape(2, 2, CL_MB), core, 1, 1).reshape(CLIPS_CORE)

    a0 = jnp.stack([piece[0] for piece in arrived])
    b0 = jnp.stack([piece[1] for piece in arrived])
    a1, b1 = swap(a0, "x"), swap(b0, "y")
    a23, b23 = swap(jnp.concatenate([a0, a1]), "y"), swap(jnp.concatenate([b0, b1]), "x")

    pre_one, masked, weight_one, stat_one = call(
        first_conv_kernel,
        [
            shape_of((CLIPS_CORE * ROWS, LANES), F32),
            shape_of((CLIPS_CORE * ROWS, C1), BF),
            shape_of((TAPS, MB, 32, C1), BF),
            shape_of((8, LANES), F32),
        ],
        [SM] + [ANY] * 6 + [VM, VM],
        [VM] * 4,
        [pltpu.VMEM((8, 128), F32), pltpu.SemaphoreType.DMA((8 * MB,))],
    )(counts, a0, a1, a23, b0, b1, b23, one_all, one_other)
    stat_one_other = swap(stat_one, "core")

    gain_parts = one_all[:, 288, :].reshape(MB, 4, 32)
    gain_rows = jnp.stack([pick(gain_parts, jnp.bitwise_xor(z, at)) for at in range(MB)], axis=1)
    gains = gain_rows.reshape(4, LANES).astype(F32)

    two_flat = jnp.stack([two_keep.reshape(288, LANES), two_got.reshape(288, LANES)])
    two_all = jnp.stack([two_flat] + [swap(two_flat, "z", step) for step in range(1, MB)])
    two_other = swap(two_all, "core")
    weight_two = call(
        second_weight_kernel,
        shape_of((TAPS, MB, 32, C2), BF),
        [ANY, ANY],
        VM,
        [pltpu.VMEM((MB, 4, 288, LANES), BF), pltpu.SemaphoreType.DMA((16,))],
    )(two_all, two_other)

    ha0, hb0 = call(
        hidden_kernel,
        [shape_of((2 * ROWS, LANES), BF)] * 2,
        [SM, SM] + [VM] * 4,
        [VM] * 2,
    )(counts, pixels, pre_one, stat_one, stat_one_other, gains)
    ha1, hb1 = swap(ha0, "x"), swap(hb0, "y")
    ha23, hb23 = swap(jnp.stack([ha0, ha1]), "y"), swap(jnp.stack([hb0, hb1]), "x")
    hidden_parts = (ha0, ha1, ha23, hb0, hb1, hb23)

    cot_rows = jnp.take(cotangent, lax.dynamic_slice_in_dim(own_order, z * CL_MB, CL_MB, 0), axis=0)
    cot_chips = cot_rows.reshape(CL_MB, MB, 2, 2, 32)
    cot_x = lax.dynamic_index_in_dim(cot_chips, x, 2, keepdims=False)
    cot_own = lax.dynamic_index_in_dim(cot_x, y, 2, keepdims=False).reshape(CL_MB, LANES)
    cot_send = lax.dynamic_index_in_dim(cot_x, 1 - y, 2, keepdims=False).reshape(CL_MB, LANES)
    cot_got = swap(cot_send, "y")
    cots = jnp.where(
        y == 0, jnp.concatenate([cot_own, cot_got]), jnp.concatenate([cot_got, cot_own])
    )

    pre_two, stat_two = call(
        second_conv_kernel,
        [shape_of((CLIPS_CORE * ROWS, LANES), F32), shape_of((8, LANES), F32)],
        [SM] + [ANY] * 6 + [VM],
        [VM] * 2,
        [pltpu.VMEM((CLIPS_CORE * ROWS, C2), BF), pltpu.SemaphoreType.DMA((8,))],
    )(counts, *hidden_parts, weight_two)
    stat_two_other = swap(stat_two, "core")
    slope_two, sum_two, pooled_own = call(
        pool_kernel,
        [
            shape_of((CLIPS_CORE * ROWS, LANES), F32),
            shape_of((8, LANES), F32),
            shape_of((8, LANES), F32),
        ],
        [SM, SM] + [VM] * 5,
        [VM] * 3,
    )(counts, pixels, pre_two, stat_two, stat_two_other, gains, cots)
    sum_two_other = swap(sum_two, "core")
    grad_two, a_keep, a_send, b_keep, b_send = call(
        hidden_grad_kernel,
        [shape_of((CLIPS_CORE * ROWS, LANES), BF)]
        + [shape_of((2, 2 * ROWS, LANES), F32), shape_of((2, 2 * ROWS, LANES), BF)] * 2,
        [SM, SM] + [VM] * 8,
        [VM] * 5,
        [pltpu.VMEM((ROWS, TAPS * LANES), BF), pltpu.VMEM((ROWS, C2), F32)],
    )(
        counts,
        pixels,
        slope_two,
        pre_two,
        stat_two,
        stat_two_other,
        sum_two,
        sum_two_other,
        gains,
        weight_two,
    )
    a_got, b_got = swap(a_send, "x"), swap(b_send, "y")
    two_part, two_part_send = call(
        second_weight_grad_kernel,
        [shape_of((MB, 2, TAPS, 32, LANES), BF)] * 2,
        [ANY] * 6 + [VM],
        [VM] * 2,
        [
            pltpu.VMEM((CLIPS_CORE * ROWS, C2), BF),
            pltpu.VMEM((CLIPS_CORE * ROWS, TAPS * LANES), BF),
            pltpu.VMEM((LANES, C2), F32),
            pltpu.SemaphoreType.DMA((8,)),
        ],
    )(*hidden_parts, grad_two)
    a_mid, b_mid = a_keep + a_got.astype(F32), b_keep + b_got.astype(F32)
    a_last = swap(pick(a_mid, 1 - y).astype(BF), "y")
    b_last = swap(pick(b_mid, 1 - x).astype(BF), "x")
    slope_one, sum_one = call(
        first_slope_kernel,
        [shape_of((CLIPS_CORE * ROWS, LANES), F32), shape_of((8, LANES), F32)],
        [SM, SM] + [VM] * 8,
        [VM] * 2,
    )(
        counts,
        pixels,
        pick(a_mid, y),
        a_last,
        pick(b_mid, x),
        b_last,
        pre_one,
        stat_one,
        stat_one_other,
        gains,
    )
    sum_one_other = swap(sum_one, "core")
    one_part, one_part_send, columns = call(
        first_weight_grad_kernel,
        [shape_of((MB, TAPS, 32, LANES), BF)] * 2
        + [shape_of((CLIPS_CORE * ROWS, TAPS * LANES), BF)],
        [SM, SM] + [VM] * 8,
        [VM] * 3,
    )(
        counts,
        pixels,
        slope_one,
        pre_one,
        stat_one,
        stat_one_other,
        sum_one,
        sum_one_other,
        gains,
        masked,
    )

    two_core = two_part.astype(F32) + swap(two_part_send, "core").astype(F32)
    two_sum = pick(two_core, z)
    for step in range(1, MB):
        two_sum = two_sum + swap(
            pick(two_core, jnp.bitwise_xor(z, step)).astype(BF), "z", step
        ).astype(F32)

    one_core = one_part.astype(F32) + swap(one_part_send, "core").astype(F32)
    norm_rows_own = jnp.concatenate(
        [
            (sum_one + sum_one_other)[1:2],
            (sum_one + sum_one_other)[0:1],
            (sum_two + sum_two_other)[1:2],
            (sum_two + sum_two_other)[0:1],
        ]
    )
    norm_z = norm_rows_own.reshape(4, MB, 32).transpose(1, 0, 2).reshape(MB, 1, LANES)
    norm_high = norm_z.astype(BF)
    norm_low = (norm_z - norm_high.astype(F32)).astype(BF)
    one_rows = jnp.concatenate(
        [
            one_core.reshape(MB, 288, LANES).astype(BF),
            norm_high,
            norm_low,
            jnp.zeros((MB, 14, LANES), BF),
        ],
        axis=1,
    )
    one_sum = pick(one_core, z).reshape(288, LANES)
    norm_sum = pick(norm_z, z)
    for step in range(1, MB):
        got = swap(pick(one_rows, jnp.bitwise_xor(z, step)), "z", step).astype(F32)
        one_sum = one_sum + got[0:288]
        norm_sum = norm_sum + got[288:289] + got[289:290]
    own_squares = (
        jnp.sum(one_sum * one_sum)
        + jnp.sum(two_sum * two_sum)
        + jnp.where(core == 0, jnp.sum(norm_sum * norm_sum), 0.0)
    )
    told = lax.all_to_all(
        jnp.broadcast_to(own_squares, (32, LANES)), AXES, 0, 0, tiled=True
    )
    grad_norm = jnp.sqrt(jnp.sum(told[:, 0]))
    factor = jnp.minimum(1.0, CLIP_NORM / (grad_norm + 1e-06))

    two_shard_send = pick(two_sum, 1 - y)
    two_shard_keep = pick(two_sum, y)
    two_shard_got = swap(two_shard_send, "y")
    one_cut = one_sum.reshape(TAPS, 32, LANES)
    one_keep_sum = lax.dynamic_slice_in_dim(one_cut, y * 64, 64, 2)
    one_send_sum = lax.dynamic_slice_in_dim(one_cut, (1 - y) * 64, 64, 2)
    norm_keep = norm_sum.reshape(4, 32)
    norm_got = swap(norm_keep, "y")
    one_got_sum = swap(one_send_sum, "y")

    def in_order(keep, got, axis):
        return jnp.where(
            y == 0, jnp.concatenate([keep, got], axis), jnp.concatenate([got, keep], axis)
        )

    grad_one_shard = jnp.swapaxes(in_order(one_keep_sum, one_got_sum, 1), 1, 2)
    grad_two_shard = jnp.swapaxes(in_order(two_shard_keep, two_shard_got, 1), 1, 2)
    norm_shard = in_order(norm_keep, norm_got, 1)

    first_update = adam_step(
        kernel_one, kernel_one_mean, kernel_one_square, grad_one_shard, factor, (9 * C1) ** (-0.5), WEIGHT_DECAY
    )
    second_update = adam_step(
        kernel_two, kernel_two_mean, kernel_two_square, grad_two_shard, factor, (9 * C2) ** (-0.5), WEIGHT_DECAY
    )
    norm_update = adam_step(norm_params, norm_mean, norm_square, norm_shard, factor, GAIN_RATE, 0.0)

    ia_keep, ia_send, ib_keep, ib_send = call(
        input_grad_kernel,
        [shape_of((2, MB, 64, C1), F32), shape_of((2, MB, 64, C1), BF)] * 2,
        [VM, VM],
        [VM] * 4,
        [pltpu.VMEM((CLIPS_CORE, ROWS, C1), F32)],
    )(columns, weight_one)
    ia_mid = ia_keep + swap(ia_send, "x").astype(F32)
    ib_mid = ib_keep + swap(ib_send, "y").astype(F32)
    ia = pick(ia_mid, y) + swap(pick(ia_mid, 1 - y).astype(BF), "y").astype(F32)
    ib = pick(ib_mid, x) + swap(pick(ib_mid, 1 - x).astype(BF), "x").astype(F32)
    own_counts = pick(counts.reshape(2, CL_MB), y)
    frame = (jnp.arange(MB) * 2 + x)[:, None] * 8 + jnp.arange(64)[None, :] // MEL
    both = jnp.stack([ia, ib], axis=1)
    masked_grad = jnp.where(
        frame[:, None, :, None] < own_counts[None, :, None, None], both, 0.0
    ).astype(BF)
    final = [pick(masked_grad, z)] + [
        swap(pick(masked_grad, jnp.bitwise_xor(z, step)), "z", step) for step in range(1, MB)
    ]
    stacked = jnp.stack(final)
    ranks = jnp.argmax(own_order[None, :] == jnp.arange(MB * CL_MB)[:, None], axis=1)
    source = jnp.bitwise_xor(ranks // CL_MB, z) * CL_MB + ranks % CL_MB
    input_grad = jnp.take(stacked.reshape(MB * CL_MB, 8, MEL, C1), source, axis=0)

    pooled_four = pooled_own[0:CLIPS_CORE].reshape(2, CL_MB, MB, 32)
    pooled_got = swap(pick(pooled_four, 1 - y), "y")
    pooled_y = jnp.stack(
        [
            jnp.where(y == 0, pick(pooled_four, y), pooled_got),
            jnp.where(y == 0, pooled_got, pick(pooled_four, y)),
        ],
        axis=2,
    )
    pooled_x_got = swap(pooled_y, "x")
    pooled_x = jnp.where(
        x == 0,
        jnp.stack([pooled_y, pooled_x_got], axis=2),
        jnp.stack([pooled_x_got, pooled_y], axis=2),
    ).reshape(CL_MB, C2)
    pooled_all = jnp.stack([pooled_x] + [swap(pooled_x, "z", step) for step in range(1, MB)])
    pooled = jnp.take(pooled_all.reshape(MB * CL_MB, C2), source, axis=0)
    return (pooled, input_grad, grad_norm) + first_update + second_update + norm_update


def solution(mesh):
    if mesh.shape["tm"] == 2 * MB and mesh.shape["batch"] == 4:
        grid = Mesh(mesh.devices.reshape(MB, 2, 2, 2), AXES)
        tm, batch, chosen = ("z", "x"), ("y", "core"), fast_body
    else:
        grid, tm, batch, chosen = mesh, "tm", "batch", general_body
    kernels = (P(None, batch, tm),) * 3
    norms = (P(None, tm),) * 3
    in_specs = (P(batch, tm, None, None), P(), P(), P(batch, None)) + 2 * kernels + norms
    out_specs = (P(batch, None), P(batch, tm, None, None), P())
    out_specs = out_specs + (P(None, batch, tm),) * 10 + (P(None, tm),) * 5
    return jax.shard_map(chosen, mesh=grid, in_specs=in_specs, out_specs=out_specs, check_vma=False)
```

```python
import functools

import jax
import jax.numpy as jnp
from jax import lax
from jax.experimental import pallas as pl
from jax.experimental.pallas import tpu as pltpu
from jax.sharding import Mesh, PartitionSpec as P

C1 = 256
C2 = 512
MEL = 8
FR_DEV = 8
CL_MB = 2
MB = 4
STEP = 10


BETA_ONE = 0.9
BETA_TWO = 0.999
ADAM_EPS = 1e-08
NORM_EPS = 1e-05
WEIGHT_DECAY = 0.01
CLIP_NORM = 0.5
GAIN_RATE = 1.0


def extended(block, sides, width):
    for axis, dim in sides:
        count = lax.axis_size(axis)
        forward = [(i, i + 1) for i in range(count - 1)]
        backward = [(target, source) for source, target in forward]
        low = lax.ppermute(
            lax.slice_in_dim(block, block.shape[dim] - width, None, axis=dim), axis, forward
        )
        high = lax.ppermute(lax.slice_in_dim(block, 0, width, axis=dim), axis, backward)
        block = jnp.concatenate([low, block, high], axis=dim)
    return block


def silu_slope(shaped):
    sigmoid_value = jax.nn.sigmoid(shaped)
    return sigmoid_value * (1.0 + shaped * (1.0 - sigmoid_value))


def pad_mel(field_data):
    return jnp.pad(field_data, ((0, 0), (0, 0), (1, 1), (0, 0)))


def frame_rim(field_data):
    return pad_mel(extended(field_data, (("tm", 1),), 1))


def grad_rim(field_data):
    return pad_mel(extended(field_data, (("tm", 1),), 1))


def patches(padded, frame_count, mel_count):
    pieces = [
        padded[:, step_time : step_time + frame_count, step_mel : step_mel + mel_count, :]
        for step_time in range(3)
        for step_mel in range(3)
    ]
    columns = jnp.concatenate(pieces, axis=-1)
    return columns.reshape(-1, columns.shape[-1])


def norm_forward(pre_norm, frame_mask, pixels, gain_row, shift_row):
    masked = pre_norm * frame_mask
    total_sum, square_sum = lax.psum(
        (jnp.sum(masked, axis=(0, 1, 2)), jnp.sum(masked * pre_norm, axis=(0, 1, 2))),
        ("tm", "batch"),
    )
    channel_mean = total_sum / pixels
    variance = square_sum / pixels - channel_mean * channel_mean
    inv_scale = lax.rsqrt(variance + NORM_EPS)
    normed = (pre_norm - channel_mean) * inv_scale
    return (normed, inv_scale, gain_row * normed + shift_row)


def norm_backward(outer_grad, frame_mask, shaped, normed, inv_scale, gain_row, pixels):
    slope_grad = outer_grad * frame_mask * silu_slope(shaped)
    shift_grad, gain_grad = lax.psum(
        (jnp.sum(slope_grad, axis=(0, 1, 2)), jnp.sum(slope_grad * normed, axis=(0, 1, 2))),
        ("tm", "batch"),
    )
    pre_grad = (
        frame_mask
        * inv_scale
        * gain_row
        * (slope_grad - shift_grad / pixels - normed * gain_grad / pixels)
    )
    return (pre_grad.astype(jnp.bfloat16), gain_grad, shift_grad)


def adam_step(weight, moment, square, summed, factor, step_rate, decay_rate):
    clipped = summed * factor
    moment_new = BETA_ONE * moment + (1.0 - BETA_ONE) * clipped
    square_new = BETA_TWO * square + (1.0 - BETA_TWO) * clipped * clipped
    corrected = moment_new / (1.0 - BETA_ONE**STEP)
    scaled = jnp.sqrt(square_new / (1.0 - BETA_TWO**STEP)) + ADAM_EPS
    weight_new = weight - step_rate * (corrected / scaled + decay_rate * weight)
    return (clipped, moment_new, square_new, weight_new, weight_new.astype(jnp.bfloat16))


def contract_rows(columns, grads):
    return lax.dot_general(
        columns, grads, (((0,), (0,)), ((), ())), preferred_element_type=jnp.float32
    )


def general_body(
    clip_input,
    frame_counts,
    clip_order,
    cotangent,
    kernel_one,
    kernel_one_mean,
    kernel_one_square,
    kernel_two,
    kernel_two_mean,
    kernel_two_square,
    norm_params,
    norm_mean,
    norm_square,
):
    batch_count = lax.axis_size("batch")
    tm_count = lax.axis_size("tm")
    tm_index = lax.axis_index("tm")
    batch_index = lax.axis_index("batch")
    half_frames = FR_DEV // 2
    counts_table = jnp.take_along_axis(frame_counts.reshape(batch_count, -1), clip_order, axis=1)
    valid_pixels = (
        MEL * jnp.sum(counts_table.reshape(batch_count, MB, CL_MB), axis=(0, 2))
    ).astype(jnp.float32)
    local_order = lax.dynamic_index_in_dim(clip_order, batch_index, 0, keepdims=False)
    local_counts = lax.dynamic_index_in_dim(counts_table, batch_index, 0, keepdims=False)
    frame_place = tm_index * FR_DEV + jnp.arange(FR_DEV, dtype=jnp.int32)
    pooled_place = 2 * (tm_index * half_frames + jnp.arange(half_frames, dtype=jnp.int32)) + 1
    low_one = kernel_one.astype(jnp.bfloat16)
    low_two = kernel_two.astype(jnp.bfloat16)
    low_gains = norm_params.astype(jnp.bfloat16)
    shape_out = (CL_MB, FR_DEV, MEL, C2)
    pooled = jnp.zeros((MB * CL_MB, C2), jnp.float32)
    input_grad = jnp.zeros(clip_input.shape, jnp.bfloat16)
    sum_one = jnp.zeros((9 * C1, C2), jnp.float32)
    sum_two = jnp.zeros((9 * C2, C2), jnp.float32)
    norm_sum = jnp.zeros((4, C2), jnp.float32)
    for micro_step in range(MB):
        tm_parts = (
            lax.all_gather(low_one, "tm", axis=2, tiled=True),
            lax.all_gather(low_two, "tm", axis=2, tiled=True),
            lax.all_gather(low_gains, "tm", axis=1, tiled=True),
        )
        full_one, full_two = (
            lax.all_gather(tm_parts[0], "batch", axis=1, tiled=True),
            lax.all_gather(tm_parts[1], "batch", axis=1, tiled=True),
        )
        weights = (full_one, full_two, tm_parts[2])
        gain_table = weights[2].astype(jnp.float32)
        flat_one = weights[0].reshape(9 * C1, C2)
        flat_two = weights[1].reshape(9 * C2, C2)
        slot_ids = local_order[micro_step * CL_MB : (micro_step + 1) * CL_MB]
        clip_counts = local_counts[micro_step * CL_MB : (micro_step + 1) * CL_MB]
        frame_mask = (frame_place[None, :] < clip_counts[:, None]).astype(jnp.float32)[
            :, :, None, None
        ]
        pool_mask = (pooled_place[None, :] < clip_counts[:, None]).astype(jnp.float32)[:, :, None]
        halves = (clip_counts // 2).astype(jnp.float32)[:, None]
        pixels = valid_pixels[micro_step]
        masked_input = jnp.take(clip_input, slot_ids, axis=0) * frame_mask.astype(jnp.bfloat16)
        input_columns = patches(frame_rim(masked_input), FR_DEV, MEL)
        pre_one = jnp.dot(input_columns, flat_one, preferred_element_type=jnp.float32).reshape(
            shape_out
        )
        normed_one, scale_one, shaped_one = norm_forward(
            pre_one, frame_mask, pixels, gain_table[0], gain_table[1]
        )
        hidden = (jax.nn.silu(shaped_one) * frame_mask).astype(jnp.bfloat16)
        hidden_columns = patches(frame_rim(hidden), FR_DEV, MEL)
        pre_two = jnp.dot(hidden_columns, flat_two, preferred_element_type=jnp.float32).reshape(
            shape_out
        )
        normed_two, scale_two, shaped_two = norm_forward(
            pre_two, frame_mask, pixels, gain_table[2], gain_table[3]
        )
        activation = jax.nn.silu(shaped_two) * frame_mask
        summary = jnp.mean(activation.reshape(CL_MB, half_frames, 2, MEL, C2), axis=(2, 3))
        exp_summary = jnp.exp(summary)
        mean_part, exp_part = lax.psum(
            (jnp.sum(summary * pool_mask, axis=1), jnp.sum(exp_summary * pool_mask, axis=1)), "tm"
        )
        pooled = pooled.at[slot_ids].set(mean_part / halves + jnp.log(exp_part / halves))
        cot_rows = jnp.take(cotangent, slot_ids, axis=0)[:, None, :]
        summary_grad = pool_mask * (
            cot_rows / halves[:, :, None] + cot_rows * exp_summary / exp_part[:, None, :]
        )
        activation_grad = jnp.broadcast_to(
            (summary_grad / (2 * MEL))[:, :, None, None, :], (CL_MB, half_frames, 2, MEL, C2)
        ).reshape(shape_out)
        grad_two, gain_two_grad, shift_two_grad = norm_backward(
            activation_grad, frame_mask, shaped_two, normed_two, scale_two, gain_table[2], pixels
        )
        sum_two = sum_two + contract_rows(hidden_columns, grad_two.reshape(-1, C2))
        flip_two = weights[1][::-1].transpose(0, 2, 1).reshape(9 * C2, C2)
        hidden_grad = jnp.dot(
            patches(grad_rim(grad_two), FR_DEV, MEL), flip_two, preferred_element_type=jnp.float32
        ).reshape(shape_out)
        grad_one, gain_one_grad, shift_one_grad = norm_backward(
            hidden_grad, frame_mask, shaped_one, normed_one, scale_one, gain_table[0], pixels
        )
        sum_one = sum_one + contract_rows(input_columns, grad_one.reshape(-1, C2))
        flip_one = weights[0][::-1].transpose(0, 2, 1).reshape(9 * C2, C1)
        rows_grad = jnp.dot(
            patches(grad_rim(grad_one), FR_DEV, MEL), flip_one, preferred_element_type=jnp.float32
        ).reshape(CL_MB, FR_DEV, MEL, C1)
        input_grad = input_grad.at[slot_ids].set((rows_grad * frame_mask).astype(jnp.bfloat16))
        norm_sum = norm_sum + jnp.stack(
            [gain_one_grad, shift_one_grad, gain_two_grad, shift_two_grad]
        )
    batch_parts = (
        lax.psum_scatter(sum_one.reshape(9, C1, C2), "batch", scatter_dimension=1, tiled=True),
        lax.psum_scatter(sum_two.reshape(9, C2, C2), "batch", scatter_dimension=1, tiled=True),
    )
    grad_one_shard, grad_two_shard = (
        lax.psum_scatter(batch_parts[0], "tm", scatter_dimension=2, tiled=True),
        lax.psum_scatter(batch_parts[1], "tm", scatter_dimension=2, tiled=True),
    )
    shard_width = C2 // tm_count
    norm_shard = lax.dynamic_slice_in_dim(norm_sum, tm_index * shard_width, shard_width, 1)
    norm_term = jnp.where(batch_index == 0, jnp.sum(norm_shard * norm_shard), 0.0)
    own_squares = (
        jnp.sum(grad_one_shard * grad_one_shard)
        + jnp.sum(grad_two_shard * grad_two_shard)
        + norm_term
    )
    grad_norm = jnp.sqrt(lax.psum(own_squares, ("tm", "batch")))
    factor = jnp.minimum(1.0, CLIP_NORM / (grad_norm + 1e-06))
    first_update = adam_step(
        kernel_one,
        kernel_one_mean,
        kernel_one_square,
        grad_one_shard,
        factor,
        (9 * C1) ** (-0.5),
        WEIGHT_DECAY,
    )
    second_update = adam_step(
        kernel_two,
        kernel_two_mean,
        kernel_two_square,
        grad_two_shard,
        factor,
        (9 * C2) ** (-0.5),
        WEIGHT_DECAY,
    )
    norm_update = adam_step(norm_params, norm_mean, norm_square, norm_shard, factor, GAIN_RATE, 0.0)
    return (pooled, input_grad, grad_norm) + first_update + second_update + norm_update


AXES = ("z", "x", "y", "core")
BF = jnp.bfloat16
F32 = jnp.float32
ROWS = 512
CLIPS_CORE = 4
PIXELS = ROWS * CLIPS_CORE
HALF = PIXELS // 2
LANES = 128
TAPS = 9
CHUNK = TAPS * 32
ANY = pl.BlockSpec(memory_space=pl.ANY)
VM = pl.BlockSpec(memory_space=pltpu.VMEM)
SM = pl.BlockSpec(memory_space=pltpu.SMEM)
VMEM_LIMIT = 28 * 1024 * 1024


def shape_of(shape, dtype=BF):
    return jax.ShapeDtypeStruct(shape, dtype)


def call(kernel, out, in_specs, out_specs, scratch=(), flops=0, moved=0):
    return pl.pallas_call(
        kernel,
        out_shape=out,
        in_specs=in_specs,
        out_specs=out_specs,
        scratch_shapes=list(scratch),
        compiler_params=pltpu.CompilerParams(vmem_limit_bytes=VMEM_LIMIT),
        cost_estimate=pl.CostEstimate(flops=flops, bytes_accessed=moved, transcendentals=0),
    )


def swap(value, axis, step=1):
    size = lax.axis_size(axis)
    return lax.ppermute(value, axis, [(i, i ^ step) for i in range(size)])


def start_copies(copies, sems):
    started = []
    for at, (source, target) in enumerate(copies):
        copy = pltpu.make_async_copy(source, target, sems.at[at])
        copy.start()
        started.append(copy)
    return started


def wait_all(copies):
    for copy in copies:
        copy.wait()


def place(*axes):
    found = tuple(lax.axis_index(axis) for axis in axes)
    return found if len(found) > 1 else found[0]


def clip_counts(order_ref, counts_ref):
    z, core = place("z", "core")
    counts = []
    for group in range(2):
        for j in range(CL_MB):
            row = group * 2 + core
            counts.append(counts_ref[row * 8 + order_ref[row, z * CL_MB + j]])
    return counts


def pixel_count(order_ref, counts_ref):
    z = place("z")
    total = 0
    for row in range(4):
        for j in range(CL_MB):
            total = total + counts_ref[row * 8 + order_ref[row, z * CL_MB + j]]
    return (MEL * total).astype(F32)


def time_shift(rows, step):
    zero = jnp.zeros((MEL, rows.shape[1]), rows.dtype)
    if step == 1:
        return jnp.concatenate([rows[MEL:], zero], axis=0)
    if step == -1:
        return jnp.concatenate([zero, rows[:-MEL]], axis=0)
    return rows


def mel_shift(rows, step):
    if step == 0:
        return rows
    cube = rows.reshape(rows.shape[0] // MEL, MEL, rows.shape[1])
    turned = pltpu.roll(cube, (-step) % MEL, 1)
    bin_at = lax.broadcasted_iota(jnp.int32, cube.shape, 1) + step
    keep = (bin_at >= 0) & (bin_at < MEL)
    return jnp.where(keep, turned, 0.0).reshape(rows.shape)


def valid_rows(count, width):
    frame = lax.broadcasted_iota(jnp.int32, (ROWS, width), 0) // MEL
    return (frame < count).astype(F32)


def dot_nt(left, right):
    return lax.dot_general(left, right, (((1,), (1,)), ((), ())), preferred_element_type=F32)


def dot_nn(left, right):
    return lax.dot_general(left, right, (((1,), (0,)), ((), ())), preferred_element_type=F32)


def dot_tn(left, right):
    return lax.dot_general(left, right, (((0,), (0,)), ((), ())), preferred_element_type=F32)


def lanes_of(tap):
    return slice(tap * LANES, (tap + 1) * LANES)


def gather_taps(product):
    total = None
    for mel in range(3):
        column = None
        for time in range(3):
            term = time_shift(product[:, lanes_of(3 * time + mel)], time - 1)
            column = term if column is None else column + term
        column = mel_shift(column, mel - 1)
        total = column if total is None else total + column
    return total


def scatter_taps(grad, target, base):
    for mel in range(3):
        moved = mel_shift(grad, 1 - mel)
        for time in range(3):
            target[base : base + ROWS, lanes_of(3 * time + mel)] = time_shift(moved, 1 - time).astype(
                BF
            )


def channel_sums(first, second):
    return (jnp.sum(first, axis=0, keepdims=True), jnp.sum(second, axis=0, keepdims=True))


def pair_sums(own_ref, other_ref):
    return (own_ref[0:1, :] + other_ref[0:1, :], own_ref[1:2, :] + other_ref[1:2, :])


def norm_rows(own_ref, other_ref, pixels):
    total, squares = pair_sums(own_ref, other_ref)
    mean = total / pixels
    return mean, lax.rsqrt(squares / pixels - mean * mean + NORM_EPS)


def put_pair(ref, first, second):
    ref[...] = jnp.zeros(ref.shape, F32)
    ref[0:1, :] = first
    ref[1:2, :] = second


def exchange_matrix(rows, columns, source_of):
    row = lax.broadcasted_iota(jnp.int32, (rows, columns), 0)
    column = lax.broadcasted_iota(jnp.int32, (rows, columns), 1)
    return (row == source_of(column)).astype(BF)


def block_exchange(column):
    return ((column // 32) % 4) * 128 + (column // 128) * 32 + column % 32


def lane_index(rows):
    return lax.broadcasted_iota(jnp.int32, (rows, LANES), 1)


def prepare_kernel(
    order_ref, clip_ref, one_ref, two_ref, norm_ref, cot_ref, p0, p1, p2, p3, one_keep, one_send,
    two_keep, two_send, gain_ref, cot_own, sems
):
    z, x, y, core = place(*AXES)
    group = y * 2 + core
    copies = []
    for step, piece in enumerate((p0, p1, p2, p3)):
        plane = jnp.bitwise_xor(z, step)
        for j in range(CL_MB):
            clip = order_ref[group, plane * CL_MB + j]
            copies.append((clip_ref.at[clip], piece.at[j]))
    started = start_copies(copies, sems)
    for tap in range(TAPS):
        turned = jnp.swapaxes(one_ref[tap], 0, 1)
        rows = [turned[at * 16 : (at + 1) * 16] for at in range(4)]
        low = jnp.concatenate([rows[0], rows[1]], axis=1).astype(BF)
        high = jnp.concatenate([rows[2], rows[3]], axis=1).astype(BF)
        span = slice(tap * 16, (tap + 1) * 16)
        one_keep[span, :] = jnp.where(y == 0, low, high)
        one_send[span, :] = jnp.where(y == 0, high, low)
        low, high = two_ref[tap, 0:32, :].astype(BF), two_ref[tap, 32:64, :].astype(BF)
        span = slice(tap * 32, (tap + 1) * 32)
        two_keep[span, :] = jnp.where(y == 0, low, high)
        two_send[span, :] = jnp.where(y == 0, high, low)
    wide = jnp.concatenate([norm_ref[...], norm_ref[...]], axis=1)
    wide = jnp.concatenate([wide, jnp.zeros((4, LANES), F32)], axis=0)
    turned = pltpu.roll(wide, (z * 32 - y * 32) % LANES, 1)
    gain_rows = jnp.where(lane_index(8) // 32 == z, turned, 0.0)
    gain_ref[...] = jnp.concatenate([gain_rows, jnp.zeros((8, LANES), F32)], axis=0).astype(BF)

    def cot_rows(y_of):
        rows = []
        for j in range(CL_MB):
            row = cot_ref[pl.ds(order_ref[group, z * CL_MB + j], 1), :]
            picked = jnp.zeros((1, LANES), F32)
            for block in range(MB):
                moved = pltpu.roll(
                    jnp.broadcast_to(row[:, lanes_of(block)], (8, LANES)),
                    (block * 32 - x * 64 - y_of * 32) % LANES,
                    1,
                )[0:1]
                picked = jnp.where(lane_index(1) // 32 == block, moved, picked)
            rows.append(picked)
        return rows

    own, send = cot_rows(y), cot_rows(1 - y)
    cot_own[...] = jnp.concatenate(own + [jnp.zeros((6, LANES), F32)], axis=0)
    high = [row.astype(BF).astype(F32) for row in send]
    rest = [row - top for row, top in zip(send, high)]
    middle = [row.astype(BF).astype(F32) for row in rest]
    low = [row - top for row, top in zip(rest, middle)]
    packed = jnp.concatenate(high + middle + low + [jnp.zeros((10, LANES), F32)], axis=0)
    two_send[CHUNK : CHUNK + 16, :] = packed.astype(BF)
    wait_all(started)


def first_conv_kernel(
    order_ref, counts_ref, a0, a1, a2, a3, b0, b1, b2, b3, o0, o1, o2, o3, s0, s1, s2, s3,
    pre_ref, x_ref, weight_ref, stat_ref, gain_ref, sems
):
    z, x, y, core = place(*AXES)
    copies = []
    for j, pieces in (
        (0, ((a0, x, y), (a1, 1 - x, y), (a2, x, 1 - y), (a3, 1 - x, 1 - y))),
        (1, ((b0, x, y), (b1, x, 1 - y), (b2, 1 - x, y), (b3, 1 - x, 1 - y))),
    ):
        for source, x_of, y_of in pieces:
            for step in range(MB):
                frames = (jnp.bitwise_xor(z, step) * 2 + x_of) * 64
                row = pl.multiple_of((y_of * CL_MB + j) * ROWS + frames, 64)
                copies.append((source.at[step], x_ref.at[pl.ds(row, 64), :]))
    started = start_copies(copies, sems)
    gains = jnp.zeros((8, LANES), F32)
    for half in range(2):

        def source_of(column, half=half):
            from_core = jnp.bitwise_xor((column // 64) % 2, core)
            from_y = jnp.bitwise_xor(column // 128, y)
            return from_core * 256 + from_y * 128 + half * 64 + column % 64

        spread = exchange_matrix(512, C1, source_of)
        for step, (own, other) in enumerate(((o0, s0), (o1, s1), (o2, s2), (o3, s3))):
            z_of = jnp.bitwise_xor(z, step)
            four = jnp.concatenate([own[0:144], own[144:288], other[0:144], other[144:288]], axis=1)
            both = dot_nn(four, spread).astype(BF)
            for tap in range(TAPS):
                weight_ref[tap, z_of, half * 16 : half * 16 + 16] = both[tap * 16 : (tap + 1) * 16]
            if half == 0:
                gains = gains + own[CHUNK : CHUNK + 16].astype(F32)[0:8]
    gain_ref[...] = gains
    counts = clip_counts(order_ref, counts_ref)
    wait_all(started)
    weight = weight_ref[...].reshape(TAPS * LANES, C1)
    first = jnp.zeros((1, LANES), F32)
    second = jnp.zeros((1, LANES), F32)
    for clip in range(CLIPS_CORE):
        span = slice(clip * ROWS, (clip + 1) * ROWS)
        mask = valid_rows(counts[clip], C1)
        masked = x_ref[span, :] * mask.astype(BF)
        x_ref[span, :] = masked
        pre = gather_taps(dot_nt(masked, weight))
        pre_ref[span, :] = pre
        kept = pre * mask[:, 0:LANES]
        plus = channel_sums(kept, kept * pre)
        first, second = first + plus[0], second + plus[1]
    put_pair(stat_ref, first, second)


def hidden_kernel(order_ref, counts_ref, pre_ref, own_ref, other_ref, gain_ref, a_ref, b_ref):
    mean, scale = norm_rows(own_ref, other_ref, pixel_count(order_ref, counts_ref))
    counts = clip_counts(order_ref, counts_ref)
    for clip in range(CLIPS_CORE):
        pre = pre_ref[clip * ROWS : (clip + 1) * ROWS, :]
        shaped = gain_ref[0:1, :] * ((pre - mean) * scale) + gain_ref[1:2, :]
        value = shaped * jax.nn.sigmoid(shaped) * valid_rows(counts[clip], LANES)
        target = a_ref if clip < 2 else b_ref
        target[(clip % 2) * ROWS : (clip % 2 + 1) * ROWS, :] = value.astype(BF)


def second_weight_kernel(o0, o1, o2, o3, s0, s1, s2, s3, weight_ref, pieces, sems):
    z, y, core = place("z", "y", "core")
    copies = []
    for step, (own, other) in enumerate(((o0, s0), (o1, s1), (o2, s2), (o3, s3))):
        for source, core_of in ((own, core), (other, 1 - core)):
            for turn in range(2):
                part = jnp.bitwise_xor(y, turn) * 2 + core_of
                copies.append(
                    (
                        source.at[pl.ds(turn * CHUNK, CHUNK), :],
                        pieces.at[jnp.bitwise_xor(z, step), part],
                    )
                )
    started = start_copies(copies, sems)
    spread = exchange_matrix(C2, C2, block_exchange)
    wait_all(started)
    for z_of in range(MB):
        natural = jnp.concatenate([pieces[z_of, part] for part in range(4)], axis=1)
        both = dot_nn(natural, spread).astype(BF)
        for tap in range(TAPS):
            weight_ref[tap, z_of] = both[tap * 32 : (tap + 1) * 32]


def hidden_copies(parts, target):
    x, y = place("x", "y")
    chips = ((x, y), (1 - x, y), (x, 1 - y), (1 - x, 1 - y), (x, y), (x, 1 - y), (1 - x, y), (1 - x, 1 - y))
    copies = []
    for at, (source, (x_of, y_of)) in enumerate(zip(parts, chips)):
        lane = pl.multiple_of((x_of * 2 + y_of) * LANES, LANES)
        copies.append((source, target.at[pl.ds((at // 4) * HALF, HALF), pl.ds(lane, LANES)]))
    return copies


def second_conv_kernel(order_ref, counts_ref, *rest):
    parts, (weight_ref, pre_ref, stat_ref, hidden, sems) = rest[:8], rest[8:]
    started = start_copies(hidden_copies(parts, hidden), sems)
    counts = clip_counts(order_ref, counts_ref)
    weight = weight_ref[...].reshape(TAPS * LANES, C2)
    wait_all(started)
    first = jnp.zeros((1, LANES), F32)
    second = jnp.zeros((1, LANES), F32)
    for clip in range(CLIPS_CORE):
        span = slice(clip * ROWS, (clip + 1) * ROWS)
        pre = gather_taps(dot_nt(hidden[span, :], weight))
        pre_ref[span, :] = pre
        kept = pre * valid_rows(counts[clip], LANES)
        plus = channel_sums(kept, kept * pre)
        first, second = first + plus[0], second + plus[1]
    put_pair(stat_ref, first, second)


def pool_kernel(
    order_ref, counts_ref, pre_ref, own_ref, other_ref, gain_ref, cot_own, cot_got,
    slope_ref, sum_ref, pooled_ref
):
    y = place("y")
    counts = clip_counts(order_ref, counts_ref)
    mean, scale = norm_rows(own_ref, other_ref, pixel_count(order_ref, counts_ref))
    first = jnp.zeros((1, LANES), F32)
    second = jnp.zeros((1, LANES), F32)
    slots = ROWS // (2 * MEL)
    got = cot_got[CHUNK : CHUNK + 16, :].astype(F32)
    pooled = []
    for clip in range(CLIPS_CORE):
        span = slice(clip * ROWS, (clip + 1) * ROWS)
        count = counts[clip]
        j = clip % CL_MB
        told = got[j : j + 1] + got[2 + j : 3 + j] + got[4 + j : 5 + j]
        cot = jnp.where(y == clip // CL_MB, cot_own[j : j + 1, :], told)
        mask = valid_rows(count, LANES)
        normed = (pre_ref[span, :] - mean) * scale
        shaped = gain_ref[2:3, :] * normed + gain_ref[3:4, :]
        gate = jax.nn.sigmoid(shaped)
        active = (shaped * gate * mask).reshape(slots, 2 * MEL, LANES)
        summary = jnp.sum(active, axis=1) / (2 * MEL)
        slot = lax.broadcasted_iota(jnp.int32, (slots, LANES), 0)
        keep = (2 * slot + 1 < count).astype(F32)
        raised = jnp.exp(summary)
        exp_total = jnp.sum(raised * keep, axis=0, keepdims=True)
        halves = (count // 2).astype(F32)
        pooled.append(
            jnp.sum(summary * keep, axis=0, keepdims=True) / halves + jnp.log(exp_total / halves)
        )
        summary_grad = keep * (cot / halves + cot * raised / exp_total) / (2 * MEL)
        spread = jnp.broadcast_to(summary_grad[:, None, :], (slots, 2 * MEL, LANES))
        slope = spread.reshape(ROWS, LANES) * mask * (gate * (1.0 + shaped * (1.0 - gate)))
        slope_ref[span, :] = slope
        plus = channel_sums(slope, slope * normed)
        first, second = first + plus[0], second + plus[1]
    put_pair(sum_ref, first, second)
    high = [row.astype(BF).astype(F32) for row in pooled]
    low = [row - top for row, top in zip(pooled, high)]
    rows = jnp.concatenate(high + low + [jnp.zeros((8, LANES), F32)], axis=0)
    pooled_ref[...] = rows.astype(BF)


def pre_grad(slope, pre, mask, mean, scale, gain, sums, pixels):
    normed = (pre - mean) * scale
    return mask * (scale * gain) * (slope - sums[0] / pixels - normed * (sums[1] / pixels))


def hidden_grad_kernel(
    order_ref, counts_ref, slope_ref, pre_ref, own_ref, other_ref, sum_own, sum_other, gain_ref,
    weight_ref, pooled_ref, grad_ref, a_own, a_mid, a_far, a_near, b_own, b_mid, b_far, b_near,
    columns, partial
):
    x, y = place("x", "y")
    counts = clip_counts(order_ref, counts_ref)
    pixels = pixel_count(order_ref, counts_ref)
    mean, scale = norm_rows(own_ref, other_ref, pixels)
    sums = pair_sums(sum_own, sum_other)
    weight = weight_ref[...].reshape(TAPS * LANES, C2)
    a_near[HALF : HALF + 16, :] = pooled_ref[...]

    def lane(x_of, y_of):
        return pl.ds(pl.multiple_of((x_of * 2 + y_of) * LANES, LANES), LANES)

    for clip in range(CLIPS_CORE):
        span = slice(clip * ROWS, (clip + 1) * ROWS)
        mask = valid_rows(counts[clip], LANES)
        grad = pre_grad(
            slope_ref[span, :], pre_ref[span, :], mask, mean, scale, gain_ref[2:3, :], sums, pixels
        )
        grad_ref[span, :] = grad.astype(BF)
        scatter_taps(grad, columns, 0)
        partial[...] = dot_nn(columns[...], weight)
        rows = slice((clip % 2) * ROWS, (clip % 2 + 1) * ROWS)
        far = partial[:, lane(1 - x, 1 - y)].astype(BF)
        if clip < 2:
            a_own[rows, :] = partial[:, lane(x, y)]
            a_mid[rows, :] = partial[:, lane(x, 1 - y)]
            a_near[rows, :] = partial[:, lane(1 - x, y)].astype(BF)
            a_far[rows, :] = far
        else:
            b_own[rows, :] = partial[:, lane(x, y)]
            b_mid[rows, :] = partial[:, lane(1 - x, y)]
            b_near[rows, :] = partial[:, lane(x, 1 - y)].astype(BF)
            b_far[rows, :] = far


def pass_on_kernel(a_mid, a_got, b_mid, b_got, a_next, b_next):
    a_next[...] = (a_mid[...] + a_got[...].astype(F32)).astype(BF)
    b_next[...] = (b_mid[...] + b_got[...].astype(F32)).astype(BF)


def second_weight_grad_kernel(*rest):
    parts, (grad_ref, keep_ref, send_ref, hidden, columns, natural, sems) = rest[:8], rest[8:]
    core = place("core")
    started = start_copies(hidden_copies(parts, hidden), sems)
    for clip in range(CLIPS_CORE):
        grad = grad_ref[clip * ROWS : (clip + 1) * ROWS, :].astype(F32)
        scatter_taps(grad, columns, clip * ROWS)
    spread = exchange_matrix(C2, C2, block_exchange)
    wait_all(started)
    for tap in range(TAPS):
        chip = dot_tn(columns[:, lanes_of(tap)], hidden[...]).astype(BF)
        natural[...] = dot_nn(chip, spread)
        for y_of in range(2):
            keep = natural[:, pl.ds(pl.multiple_of((y_of * 2 + core) * LANES, LANES), LANES)]
            send = natural[:, pl.ds(pl.multiple_of((y_of * 2 + 1 - core) * LANES, LANES), LANES)]
            for z_of in range(MB):
                rows = slice(z_of * 32, (z_of + 1) * 32)
                target = slice(tap * 32, (tap + 1) * 32)
                keep_ref[z_of, y_of, target] = keep[rows].astype(BF)
                send_ref[z_of, y_of, target] = send[rows].astype(BF)


def second_core_kernel(keep_ref, got_ref, own_ref, n1, n2, n3):
    z = place("z")
    own_ref[...] = keep_ref[z].astype(F32) + got_ref[z].astype(F32)
    for step, target in ((1, n1), (2, n2), (3, n3)):
        at = jnp.bitwise_xor(z, step)
        target[...] = (keep_ref[at].astype(F32) + got_ref[at].astype(F32)).astype(BF)


def second_sum_kernel(own_ref, g1, g2, g3, keep_ref, send_ref, square_ref):
    y = place("y")
    total = own_ref[...] + g1[...].astype(F32) + g2[...].astype(F32) + g3[...].astype(F32)
    keep_ref[...] = jnp.where(y == 0, total[0], total[1])
    send_ref[...] = jnp.where(y == 0, total[1], total[0])
    square_ref[...] = jnp.sum(total * total, axis=(0, 1), keepdims=False)[None, :] * jnp.ones((8, 1), F32)


def first_slope_kernel(
    order_ref, counts_ref, a_own, a_near, a_last, b_own, b_near, b_last, pre_ref, own_ref, other_ref,
    gain_ref, slope_ref, sum_ref
):
    counts = clip_counts(order_ref, counts_ref)
    mean, scale = norm_rows(own_ref, other_ref, pixel_count(order_ref, counts_ref))
    first = jnp.zeros((1, LANES), F32)
    second = jnp.zeros((1, LANES), F32)
    for clip in range(CLIPS_CORE):
        span = slice(clip * ROWS, (clip + 1) * ROWS)
        rows = slice((clip % 2) * ROWS, (clip % 2 + 1) * ROWS)
        own, near, last = (a_own, a_near, a_last) if clip < 2 else (b_own, b_near, b_last)
        outer = own[rows, :] + near[rows, :].astype(F32) + last[rows, :].astype(F32)
        normed = (pre_ref[span, :] - mean) * scale
        shaped = gain_ref[0:1, :] * normed + gain_ref[1:2, :]
        gate = jax.nn.sigmoid(shaped)
        slope = outer * valid_rows(counts[clip], LANES) * (gate * (1.0 + shaped * (1.0 - gate)))
        slope_ref[span, :] = slope
        plus = channel_sums(slope, slope * normed)
        first, second = first + plus[0], second + plus[1]
    put_pair(sum_ref, first, second)


def first_weight_grad_kernel(
    order_ref, counts_ref, slope_ref, pre_ref, own_ref, other_ref, sum_own, sum_other, gain_ref, x_ref,
    keep_ref, send_ref, grad_ref, columns
):
    core = place("core")
    counts = clip_counts(order_ref, counts_ref)
    pixels = pixel_count(order_ref, counts_ref)
    mean, scale = norm_rows(own_ref, other_ref, pixels)
    sums = pair_sums(sum_own, sum_other)
    for clip in range(CLIPS_CORE):
        span = slice(clip * ROWS, (clip + 1) * ROWS)
        mask = valid_rows(counts[clip], LANES)
        grad = pre_grad(
            slope_ref[span, :], pre_ref[span, :], mask, mean, scale, gain_ref[0:1, :], sums, pixels
        )
        grad_ref[span, :] = grad.astype(BF)
        scatter_taps(grad, columns, clip * ROWS)

    def source_of(column):
        core_of = jnp.where(column < 128, core, 1 - core)
        return ((column // 64) % 2) * 128 + core_of * 64 + column % 64

    spread = exchange_matrix(C1, C1, source_of)
    for tap in range(TAPS):
        part = dot_tn(columns[:, lanes_of(tap)], x_ref[...]).astype(BF)
        both = dot_nn(part, spread).astype(BF)
        for z_of in range(MB):
            rows = slice(z_of * 32, (z_of + 1) * 32)
            target = slice(tap * 32, (tap + 1) * 32)
            keep_ref[z_of, target] = both[rows, 0:LANES]
            send_ref[z_of, target] = both[rows, LANES : 2 * LANES]


def first_core_kernel(
    keep_ref, got_ref, one_own, one_other, two_own, two_other, pooled_own, pooled_near, pooled_last,
    own_ref, n0, n1, n2, n3, scratch
):
    z, x, y = place("z", "x", "y")
    own_ref[...] = keep_ref[z].astype(F32) + got_ref[z].astype(F32)
    one, two = pair_sums(one_own, one_other), pair_sums(two_own, two_other)
    sums = jnp.concatenate([one[1], one[0], two[1], two[0]], axis=0)
    high = sums.astype(BF).astype(F32)
    norm_tile = jnp.concatenate([high, sums - high, jnp.zeros((8, LANES), F32)], axis=0).astype(BF)
    last = pooled_last[HALF : HALF + 32, :].astype(F32)
    near = pooled_near[HALF : HALF + 16, :].astype(F32)
    own = pooled_own[...].astype(F32)
    for rows, x_of, y_of in (
        (own, x, y),
        (near, 1 - x, y),
        (last[0:16], x, 1 - y),
        (last[16:32], 1 - x, 1 - y),
    ):
        for part in range(2):
            for j in range(CL_MB):
                row = jnp.where(
                    y == 0, rows[part * 4 + j : part * 4 + j + 1], rows[part * 4 + 2 + j : part * 4 + 3 + j]
                )
                scratch[pl.ds((x_of * 2 + y_of) * 4 + part * 2 + j, 1), :] = row
    pooled_tile = scratch[...].astype(BF)
    for step, target in ((0, n0), (1, n1), (2, n2), (3, n3)):
        at = jnp.bitwise_xor(z, step)
        target[0:CHUNK, :] = (keep_ref[at].astype(F32) + got_ref[at].astype(F32)).astype(BF)
        target[CHUNK : CHUNK + 16, :] = norm_tile
        target[CHUNK + 16 : CHUNK + 32, :] = pooled_tile


def first_sum_kernel(own_ref, n0, g1, g2, g3, square_two, told_ref, keep_ref, send_ref, norm_ref):
    z, y, core = place("z", "y", "core")
    total = own_ref[...]
    norm = n0[CHUNK : CHUNK + 16, :].astype(F32)
    for got in (g1, g2, g3):
        total = total + got[0:CHUNK, :].astype(F32)
        norm = norm + got[CHUNK : CHUNK + 16, :].astype(F32)
    norm = norm[0:4] + norm[4:8]
    mine = (lane_index(4) // 32 == z) & (core == 0)
    squares = jnp.sum(total * total, axis=0, keepdims=True) + jnp.sum(
        jnp.where(mine, norm * norm, 0.0), axis=0, keepdims=True
    )
    told_ref[...] = jnp.broadcast_to(squares + square_two[0:1, :], told_ref.shape)
    turned = pltpu.roll(total, 64, 1)
    low = jnp.where(y == 0, total, turned)
    high = jnp.where(y == 0, turned, total)
    left = lane_index(144) < 64
    keep_ref[...] = jnp.where(left, low[0:144], pltpu.roll(low[144:288], 64, 1))
    send_ref[0:144, :] = jnp.where(left, high[0:144], pltpu.roll(high[144:288], 64, 1))
    rows = jnp.concatenate([norm, jnp.zeros((4, LANES), F32)], axis=0)
    send_ref[144:152, :] = rows
    norm_ref[...] = rows


def shard_kernel(keep_ref, got_ref, norm_ref, one_ref, norm_out):
    z, y = place("z", "y")
    keep, got = keep_ref[...], got_ref[0:144, :]
    first, second = jnp.where(y == 0, keep, got), jnp.where(y == 0, got, keep)
    spans = []
    for half in (first, second):
        spans.append(jnp.concatenate([half[:, 0:64], half[:, 64:128]], axis=0))
    for tap in range(TAPS):
        rows = [span[tap * 32 : (tap + 1) * 32] for span in spans]
        one_ref[tap] = jnp.swapaxes(jnp.concatenate(rows, axis=0), 0, 1)
    keep, got = norm_ref[...], got_ref[144:152, :]
    first, second = jnp.where(y == 0, keep, got), jnp.where(y == 0, got, keep)
    low = pltpu.roll(first, (0 - z * 32) % LANES, 1)
    high = pltpu.roll(second, (32 - z * 32) % LANES, 1)
    norm_out[...] = jnp.where(lane_index(8) < 32, low, high)[0:4, 0:64]


def input_grad_kernel(
    grad_ref, weight_ref, a_own, a_mid, a_far, a_near, b_own, b_mid, b_far, b_near, columns, partial
):
    x, y = place("x", "y")
    weight = weight_ref[...].reshape(TAPS * LANES, C1)
    for clip in range(CLIPS_CORE):
        grad = grad_ref[clip * ROWS : (clip + 1) * ROWS, :].astype(F32)
        scatter_taps(grad, columns, 0)
        partial[clip] = dot_nn(columns[...], weight)

    def part(x_of, y_of, j, z_of):
        return partial[y_of * CL_MB + j, pl.ds(pl.multiple_of((z_of * 2 + x_of) * 64, 64), 64), :]

    for z_of in range(MB):
        a_own[z_of] = part(x, y, 0, z_of)
        a_mid[z_of] = part(x, 1 - y, 0, z_of)
        a_near[z_of] = part(1 - x, y, 0, z_of).astype(BF)
        a_far[z_of] = part(1 - x, 1 - y, 0, z_of).astype(BF)
        b_own[z_of] = part(x, y, 1, z_of)
        b_mid[z_of] = part(1 - x, y, 1, z_of)
        b_near[z_of] = part(x, 1 - y, 1, z_of).astype(BF)
        b_far[z_of] = part(1 - x, 1 - y, 1, z_of).astype(BF)


def input_sum_kernel(order_ref, counts_ref, a_own, a_near, a_last, b_own, b_near, b_last, f0, f1, f2, f3):
    z, x, y, core = place(*AXES)
    row = y * 2 + core
    for j, (own, near, last) in enumerate(((a_own, a_near, a_last), (b_own, b_near, b_last))):
        count = counts_ref[row * 8 + order_ref[row, z * CL_MB + j]]
        for step, target in enumerate((f0, f1, f2, f3)):
            at = jnp.bitwise_xor(z, step)
            total = own[at] + near[at].astype(F32) + last[at].astype(F32)
            frame = (at * 2 + x) * 8 + lax.broadcasted_iota(jnp.int32, (64, C1), 0) // MEL
            target[j] = jnp.where(frame < count, total, 0.0).astype(BF)


def finish_kernel(order_ref, f0, g1, g2, g3, n0, n1, n2, n3, grad_ref, pooled_ref, scratch):
    z, y, core = place("z", "y", "core")
    row = y * 2 + core
    for step, (piece, told) in enumerate(((f0, n0), (g1, n1), (g2, n2), (g3, n3))):
        at = jnp.bitwise_xor(z, step)
        rows = told[CHUNK + 16 : CHUNK + 32, :].astype(F32)
        for j in range(CL_MB):
            clip = order_ref[row, at * CL_MB + j]
            grad_ref[clip] = piece[j]
            for part in range(2):
                chips = [rows[chip * 4 + part * 2 + j : chip * 4 + part * 2 + j + 1] for chip in range(4)]
                scratch[part, pl.ds(clip, 1), :] = jnp.concatenate(chips, axis=1)
    spread = exchange_matrix(C2, C2, block_exchange)
    pooled_ref[...] = dot_nn(scratch[0].astype(BF), spread) + dot_nn(scratch[1].astype(BF), spread)


def spread_plane(a0, b0):
    a1, b1 = swap(a0, "x"), swap(b0, "y")
    a2, b2 = swap(a0, "y"), swap(b0, "x")
    a3, b3 = swap(a1, "y"), swap(b1, "x")
    return (a0, a1, a2, a3, b0, b1, b2, b3)


def fast_body(
    clip_input,
    frame_counts,
    clip_order,
    cotangent,
    kernel_one,
    kernel_one_mean,
    kernel_one_square,
    kernel_two,
    kernel_two_mean,
    kernel_two_square,
    norm_params,
    norm_mean,
    norm_square,
):
    table = (clip_order, frame_counts)
    p0, p1, p2, p3, one_keep, one_send, two_keep, two_send, gain_rows, cot_own = call(
        prepare_kernel,
        [shape_of((CL_MB, 64, C1))] * MB
        + [shape_of((144, LANES))] * 2
        + [shape_of((CHUNK, LANES)), shape_of((CHUNK + 16, LANES)), shape_of((16, LANES))]
        + [shape_of((8, LANES), F32)],
        [SM, ANY, VM, VM, VM, VM],
        [VM] * 10,
        [pltpu.SemaphoreType.DMA((MB * CL_MB,))],
    )(
        clip_order,
        clip_input.reshape(MB * CL_MB, 64, C1),
        kernel_one,
        jnp.swapaxes(kernel_two, 1, 2),
        norm_params,
        cotangent,
    )
    arrived = [p0] + [swap(piece, "z", step) for step, piece in ((1, p1), (2, p2), (3, p3))]
    one_got = swap(one_send, "y")
    two_got = swap(two_send, "y")
    a0 = jnp.stack([piece[0] for piece in arrived])
    b0 = jnp.stack([piece[1] for piece in arrived])
    inputs = spread_plane(a0, b0)

    one_flat = jnp.concatenate([one_keep, one_got, gain_rows])
    one_parts = [one_flat] + [swap(one_flat, "z", step) for step in range(1, MB)]
    one_others = [swap(part, "core") for part in one_parts]
    pre_one, masked, weight_one, stat_one, gains = call(
        first_conv_kernel,
        [
            shape_of((PIXELS, LANES), F32),
            shape_of((PIXELS, C1)),
            shape_of((TAPS, MB, 32, C1)),
            shape_of((8, LANES), F32),
            shape_of((8, LANES), F32),
        ],
        [SM, SM] + [ANY] * 8 + [VM] * 8,
        [VM] * 5,
        [pltpu.SemaphoreType.DMA((8 * MB,))],
        flops=2 * PIXELS * C1 * TAPS * LANES,
    )(*table, *inputs, *one_parts, *one_others)
    stat_one_other = swap(stat_one, "core")

    two_flat = jnp.concatenate([two_keep, two_got[0:CHUNK]])
    two_parts = [two_flat] + [swap(two_flat, "z", step) for step in range(1, MB)]
    two_others = [swap(part, "core") for part in two_parts]
    weight_two = call(
        second_weight_kernel,
        shape_of((TAPS, MB, 32, C2)),
        [ANY] * 8,
        VM,
        [pltpu.VMEM((MB, 4, CHUNK, LANES), BF), pltpu.SemaphoreType.DMA((16,))],
        flops=2 * TAPS * LANES * C2 * C2,
    )(*two_parts, *two_others)

    ha0, hb0 = call(
        hidden_kernel, [shape_of((HALF, LANES))] * 2, [SM, SM] + [VM] * 4, [VM] * 2
    )(*table, pre_one, stat_one, stat_one_other, gains)
    hidden_parts = spread_plane(ha0, hb0)

    pre_two, stat_two = call(
        second_conv_kernel,
        [shape_of((PIXELS, LANES), F32), shape_of((8, LANES), F32)],
        [SM, SM] + [ANY] * 8 + [VM],
        [VM] * 2,
        [pltpu.VMEM((PIXELS, C2), BF), pltpu.SemaphoreType.DMA((8,))],
        flops=2 * PIXELS * C2 * TAPS * LANES,
    )(*table, *hidden_parts, weight_two)
    stat_two_other = swap(stat_two, "core")
    slope_two, sum_two, pooled_own = call(
        pool_kernel,
        [shape_of((PIXELS, LANES), F32), shape_of((8, LANES), F32), shape_of((16, LANES))],
        [SM, SM] + [VM] * 6,
        [VM] * 3,
    )(*table, pre_two, stat_two, stat_two_other, gains, cot_own, two_got)
    sum_two_other = swap(sum_two, "core")
    grad_two, a_own, a_mid, a_far, a_near, b_own, b_mid, b_far, b_near = call(
        hidden_grad_kernel,
        [shape_of((PIXELS, LANES))]
        + [shape_of((HALF, LANES), F32)] * 2
        + [shape_of((HALF, LANES)), shape_of((HALF + 16, LANES))]
        + [shape_of((HALF, LANES), F32)] * 2
        + [shape_of((HALF, LANES))] * 2,
        [SM, SM] + [VM] * 9,
        [VM] * 9,
        [pltpu.VMEM((ROWS, TAPS * LANES), BF), pltpu.VMEM((ROWS, C2), F32)],
        flops=2 * PIXELS * C2 * TAPS * LANES,
    )(
        *table, slope_two, pre_two, stat_two, stat_two_other, sum_two, sum_two_other, gains,
        weight_two, pooled_own,
    )
    a_got, b_got = swap(a_far, "x"), swap(b_far, "y")
    a_near, b_near = swap(a_near, "x"), swap(b_near, "y")
    two_part, two_part_send = call(
        second_weight_grad_kernel,
        [shape_of((MB, 2, CHUNK, LANES))] * 2,
        [ANY] * 8 + [VM],
        [VM] * 2,
        [
            pltpu.VMEM((PIXELS, C2), BF),
            pltpu.VMEM((PIXELS, TAPS * LANES), BF),
            pltpu.VMEM((LANES, C2), F32),
            pltpu.SemaphoreType.DMA((8,)),
        ],
        flops=2 * PIXELS * C2 * TAPS * LANES,
    )(*hidden_parts, grad_two)
    a_next, b_next = call(
        pass_on_kernel, [shape_of((HALF, LANES))] * 2, [VM] * 4, [VM] * 2
    )(a_mid, a_got, b_mid, b_got)
    a_next = jnp.concatenate([a_next, pooled_own, a_near[HALF:]])
    a_last, b_last = swap(a_next, "y"), swap(b_next, "x")
    slope_one, sum_one = call(
        first_slope_kernel,
        [shape_of((PIXELS, LANES), F32), shape_of((8, LANES), F32)],
        [SM, SM] + [VM] * 10,
        [VM] * 2,
    )(*table, a_own, a_near, a_last, b_own, b_near, b_last, pre_one, stat_one, stat_one_other, gains)
    sum_one_other = swap(sum_one, "core")
    one_part, one_part_send, grad_one = call(
        first_weight_grad_kernel,
        [shape_of((MB, CHUNK, LANES))] * 2 + [shape_of((PIXELS, LANES))],
        [SM, SM] + [VM] * 8,
        [VM] * 3,
        [pltpu.VMEM((PIXELS, TAPS * LANES), BF)],
        flops=2 * PIXELS * C1 * TAPS * LANES,
    )(
        *table, slope_one, pre_one, stat_one, stat_one_other, sum_one, sum_one_other, gains, masked
    )

    two_own, t1, t2, t3 = call(
        second_core_kernel,
        [shape_of((2, CHUNK, LANES), F32)] + [shape_of((2, CHUNK, LANES))] * 3,
        [VM] * 2,
        [VM] * 4,
    )(two_part, swap(two_part_send, "core"))
    two_keep_sum, two_send_sum, square_two = call(
        second_sum_kernel,
        [shape_of((CHUNK, LANES), F32)] * 2 + [shape_of((8, LANES), F32)],
        [VM] * 4,
        [VM] * 3,
    )(two_own, swap(t1, "z", 1), swap(t2, "z", 2), swap(t3, "z", 3))
    two_got_sum = swap(two_send_sum, "y")

    one_own, n0, n1, n2, n3 = call(
        first_core_kernel,
        [shape_of((CHUNK, LANES), F32)] + [shape_of((CHUNK + 32, LANES))] * MB,
        [VM] * 9,
        [VM] * 5,
        [pltpu.VMEM((16, LANES), F32)],
    )(
        one_part, swap(one_part_send, "core"), sum_one, sum_one_other, sum_two, sum_two_other,
        pooled_own, a_near, a_last,
    )
    g1, g2, g3 = swap(n1, "z", 1), swap(n2, "z", 2), swap(n3, "z", 3)
    told, one_keep_sum, one_send_sum, norm_sum = call(
        first_sum_kernel,
        [
            shape_of((32, LANES), F32),
            shape_of((144, LANES), F32),
            shape_of((152, LANES), F32),
            shape_of((8, LANES), F32),
        ],
        [VM] * 6,
        [VM] * 4,
    )(one_own, n0, g1, g2, g3, square_two)
    told = lax.all_to_all(told, AXES, 0, 0, tiled=True)
    grad_norm = jnp.sqrt(jnp.sum(told))
    factor = jnp.minimum(1.0, CLIP_NORM / (grad_norm + 1e-06))
    one_got_sum = swap(one_send_sum, "y")
    grad_one_shard, norm_shard = call(
        shard_kernel,
        [shape_of((TAPS, 64, 64), F32), shape_of((4, 64), F32)],
        [VM] * 3,
        [VM] * 2,
    )(one_keep_sum, one_got_sum, norm_sum)
    y = lax.axis_index("y")
    cut = (TAPS, 32, LANES)
    keep, got = two_keep_sum.reshape(cut), two_got_sum.reshape(cut)
    grad_two_shard = jnp.where(
        y == 0, jnp.concatenate([keep, got], axis=1), jnp.concatenate([got, keep], axis=1)
    )
    grad_two_shard = jnp.swapaxes(grad_two_shard, 1, 2)

    first_update = adam_step(
        kernel_one, kernel_one_mean, kernel_one_square, grad_one_shard, factor, (9 * C1) ** (-0.5), WEIGHT_DECAY
    )
    second_update = adam_step(
        kernel_two, kernel_two_mean, kernel_two_square, grad_two_shard, factor, (9 * C2) ** (-0.5), WEIGHT_DECAY
    )
    norm_update = adam_step(norm_params, norm_mean, norm_square, norm_shard, factor, GAIN_RATE, 0.0)

    block = (MB, 64, C1)
    ia_own, ia_mid, ia_far, ia_near, ib_own, ib_mid, ib_far, ib_near = call(
        input_grad_kernel,
        ([shape_of(block, F32)] * 2 + [shape_of(block)] * 2) * 2,
        [VM, VM],
        [VM] * 8,
        [pltpu.VMEM((ROWS, TAPS * LANES), BF), pltpu.VMEM((CLIPS_CORE, ROWS, C1), F32)],
        flops=2 * PIXELS * C1 * TAPS * LANES,
    )(grad_one, weight_one)
    ia_got, ib_got = swap(ia_far, "x"), swap(ib_far, "y")
    ia_near, ib_near = swap(ia_near, "x"), swap(ib_near, "y")
    ia_next, ib_next = call(pass_on_kernel, [shape_of(block)] * 2, [VM] * 4, [VM] * 2)(
        ia_mid, ia_got, ib_mid, ib_got
    )
    ia_last, ib_last = swap(ia_next, "y"), swap(ib_next, "x")
    f0, f1, f2, f3 = call(
        input_sum_kernel, [shape_of((CL_MB, 64, C1))] * MB, [SM, SM] + [VM] * 6, [VM] * 4
    )(*table, ia_own, ia_near, ia_last, ib_own, ib_near, ib_last)
    input_grad, pooled = call(
        finish_kernel,
        [shape_of((MB * CL_MB, 64, C1)), shape_of((MB * CL_MB, C2), F32)],
        [SM] + [VM] * 8,
        [VM] * 2,
        [pltpu.VMEM((2, MB * CL_MB, C2), F32)],
    )(clip_order, f0, swap(f1, "z", 1), swap(f2, "z", 2), swap(f3, "z", 3), n0, g1, g2, g3)
    input_grad = input_grad.reshape(clip_input.shape)
    return (pooled, input_grad, grad_norm) + first_update + second_update + norm_update


def solution(mesh):
    if mesh.shape["tm"] == 2 * MB and mesh.shape["batch"] == 4:
        grid = Mesh(mesh.devices.reshape(MB, 2, 2, 2), AXES)
        tm, batch, chosen = ("z", "x"), ("y", "core"), fast_body
    else:
        grid, tm, batch, chosen = mesh, "tm", "batch", general_body
    kernels = (P(None, batch, tm),) * 3
    norms = (P(None, tm),) * 3
    in_specs = (P(batch, tm, None, None), P(), P(), P(batch, None)) + 2 * kernels + norms
    out_specs = (P(batch, None), P(batch, tm, None, None), P())
    out_specs = out_specs + (P(None, batch, tm),) * 10 + (P(None, tm),) * 5
    return jax.shard_map(chosen, mesh=grid, in_specs=in_specs, out_specs=out_specs, check_vma=False)
```

```python
import functools

import jax
import jax.numpy as jnp
from jax import lax
from jax.experimental import pallas as pl
from jax.experimental.pallas import tpu as pltpu
from jax.sharding import Mesh, PartitionSpec as P

OPT = {'flop': 200000000.0, 'zorder': [2, 3, 1], 'merge_w': False, 'w1_after_in': False, 'core_w1': 1, 'core_w1_after_xy': False, 'fwd_after_core_w1': False, 'w2_after': 0, 'w2_before': 1, 'core_w2_after': 1, 'kw2_after': False, 'rs': 'two', 'pass_after_g2': True, 'pass_after_near': False, 'core_g2_after': True, 'k5_after': True, 'core1_after_g2': False, 'core_g1_after_g2': True, 'a2a_after_core1': False, 'sum_after_f': False, 'sum_after_y': True, 'f_after_sum': False, 'told_after_f': True, 'core_w1_after': 0, 'y2_after': 1}
C1 = 256
C2 = 512
MEL = 8
FR_DEV = 8
CL_MB = 2
MB = 4
STEP = 10


BETA_ONE = 0.9
BETA_TWO = 0.999
ADAM_EPS = 1e-08
NORM_EPS = 1e-05
WEIGHT_DECAY = 0.01
CLIP_NORM = 0.5
GAIN_RATE = 1.0


def extended(block, sides, width):
    for axis, dim in sides:
        count = lax.axis_size(axis)
        forward = [(i, i + 1) for i in range(count - 1)]
        backward = [(target, source) for source, target in forward]
        low = lax.ppermute(
            lax.slice_in_dim(block, block.shape[dim] - width, None, axis=dim), axis, forward
        )
        high = lax.ppermute(lax.slice_in_dim(block, 0, width, axis=dim), axis, backward)
        block = jnp.concatenate([low, block, high], axis=dim)
    return block


def silu_slope(shaped):
    sigmoid_value = jax.nn.sigmoid(shaped)
    return sigmoid_value * (1.0 + shaped * (1.0 - sigmoid_value))


def pad_mel(field_data):
    return jnp.pad(field_data, ((0, 0), (0, 0), (1, 1), (0, 0)))


def frame_rim(field_data):
    return pad_mel(extended(field_data, (("tm", 1),), 1))


def grad_rim(field_data):
    return pad_mel(extended(field_data, (("tm", 1),), 1))


def patches(padded, frame_count, mel_count):
    pieces = [
        padded[:, step_time : step_time + frame_count, step_mel : step_mel + mel_count, :]
        for step_time in range(3)
        for step_mel in range(3)
    ]
    columns = jnp.concatenate(pieces, axis=-1)
    return columns.reshape(-1, columns.shape[-1])


def norm_forward(pre_norm, frame_mask, pixels, gain_row, shift_row):
    masked = pre_norm * frame_mask
    total_sum, square_sum = lax.psum(
        (jnp.sum(masked, axis=(0, 1, 2)), jnp.sum(masked * pre_norm, axis=(0, 1, 2))),
        ("tm", "batch"),
    )
    channel_mean = total_sum / pixels
    variance = square_sum / pixels - channel_mean * channel_mean
    inv_scale = lax.rsqrt(variance + NORM_EPS)
    normed = (pre_norm - channel_mean) * inv_scale
    return (normed, inv_scale, gain_row * normed + shift_row)


def norm_backward(outer_grad, frame_mask, shaped, normed, inv_scale, gain_row, pixels):
    slope_grad = outer_grad * frame_mask * silu_slope(shaped)
    shift_grad, gain_grad = lax.psum(
        (jnp.sum(slope_grad, axis=(0, 1, 2)), jnp.sum(slope_grad * normed, axis=(0, 1, 2))),
        ("tm", "batch"),
    )
    pre_grad = (
        frame_mask
        * inv_scale
        * gain_row
        * (slope_grad - shift_grad / pixels - normed * gain_grad / pixels)
    )
    return (pre_grad.astype(jnp.bfloat16), gain_grad, shift_grad)


def adam_step(weight, moment, square, summed, factor, step_rate, decay_rate):
    clipped = summed * factor
    moment_new = BETA_ONE * moment + (1.0 - BETA_ONE) * clipped
    square_new = BETA_TWO * square + (1.0 - BETA_TWO) * clipped * clipped
    corrected = moment_new / (1.0 - BETA_ONE**STEP)
    scaled = jnp.sqrt(square_new / (1.0 - BETA_TWO**STEP)) + ADAM_EPS
    weight_new = weight - step_rate * (corrected / scaled + decay_rate * weight)
    return (clipped, moment_new, square_new, weight_new, weight_new.astype(jnp.bfloat16))


def contract_rows(columns, grads):
    return lax.dot_general(
        columns, grads, (((0,), (0,)), ((), ())), preferred_element_type=jnp.float32
    )


def general_body(
    clip_input,
    frame_counts,
    clip_order,
    cotangent,
    kernel_one,
    kernel_one_mean,
    kernel_one_square,
    kernel_two,
    kernel_two_mean,
    kernel_two_square,
    norm_params,
    norm_mean,
    norm_square,
):
    batch_count = lax.axis_size("batch")
    tm_count = lax.axis_size("tm")
    tm_index = lax.axis_index("tm")
    batch_index = lax.axis_index("batch")
    half_frames = FR_DEV // 2
    counts_table = jnp.take_along_axis(frame_counts.reshape(batch_count, -1), clip_order, axis=1)
    valid_pixels = (
        MEL * jnp.sum(counts_table.reshape(batch_count, MB, CL_MB), axis=(0, 2))
    ).astype(jnp.float32)
    local_order = lax.dynamic_index_in_dim(clip_order, batch_index, 0, keepdims=False)
    local_counts = lax.dynamic_index_in_dim(counts_table, batch_index, 0, keepdims=False)
    frame_place = tm_index * FR_DEV + jnp.arange(FR_DEV, dtype=jnp.int32)
    pooled_place = 2 * (tm_index * half_frames + jnp.arange(half_frames, dtype=jnp.int32)) + 1
    low_one = kernel_one.astype(jnp.bfloat16)
    low_two = kernel_two.astype(jnp.bfloat16)
    low_gains = norm_params.astype(jnp.bfloat16)
    shape_out = (CL_MB, FR_DEV, MEL, C2)
    pooled = jnp.zeros((MB * CL_MB, C2), jnp.float32)
    input_grad = jnp.zeros(clip_input.shape, jnp.bfloat16)
    sum_one = jnp.zeros((9 * C1, C2), jnp.float32)
    sum_two = jnp.zeros((9 * C2, C2), jnp.float32)
    norm_sum = jnp.zeros((4, C2), jnp.float32)
    for micro_step in range(MB):
        tm_parts = (
            lax.all_gather(low_one, "tm", axis=2, tiled=True),
            lax.all_gather(low_two, "tm", axis=2, tiled=True),
            lax.all_gather(low_gains, "tm", axis=1, tiled=True),
        )
        full_one, full_two = (
            lax.all_gather(tm_parts[0], "batch", axis=1, tiled=True),
            lax.all_gather(tm_parts[1], "batch", axis=1, tiled=True),
        )
        weights = (full_one, full_two, tm_parts[2])
        gain_table = weights[2].astype(jnp.float32)
        flat_one = weights[0].reshape(9 * C1, C2)
        flat_two = weights[1].reshape(9 * C2, C2)
        slot_ids = local_order[micro_step * CL_MB : (micro_step + 1) * CL_MB]
        clip_counts = local_counts[micro_step * CL_MB : (micro_step + 1) * CL_MB]
        frame_mask = (frame_place[None, :] < clip_counts[:, None]).astype(jnp.float32)[
            :, :, None, None
        ]
        pool_mask = (pooled_place[None, :] < clip_counts[:, None]).astype(jnp.float32)[:, :, None]
        halves = (clip_counts // 2).astype(jnp.float32)[:, None]
        pixels = valid_pixels[micro_step]
        masked_input = jnp.take(clip_input, slot_ids, axis=0) * frame_mask.astype(jnp.bfloat16)
        input_columns = patches(frame_rim(masked_input), FR_DEV, MEL)
        pre_one = jnp.dot(input_columns, flat_one, preferred_element_type=jnp.float32).reshape(
            shape_out
        )
        normed_one, scale_one, shaped_one = norm_forward(
            pre_one, frame_mask, pixels, gain_table[0], gain_table[1]
        )
        hidden = (jax.nn.silu(shaped_one) * frame_mask).astype(jnp.bfloat16)
        hidden_columns = patches(frame_rim(hidden), FR_DEV, MEL)
        pre_two = jnp.dot(hidden_columns, flat_two, preferred_element_type=jnp.float32).reshape(
            shape_out
        )
        normed_two, scale_two, shaped_two = norm_forward(
            pre_two, frame_mask, pixels, gain_table[2], gain_table[3]
        )
        activation = jax.nn.silu(shaped_two) * frame_mask
        summary = jnp.mean(activation.reshape(CL_MB, half_frames, 2, MEL, C2), axis=(2, 3))
        exp_summary = jnp.exp(summary)
        mean_part, exp_part = lax.psum(
            (jnp.sum(summary * pool_mask, axis=1), jnp.sum(exp_summary * pool_mask, axis=1)), "tm"
        )
        pooled = pooled.at[slot_ids].set(mean_part / halves + jnp.log(exp_part / halves))
        cot_rows = jnp.take(cotangent, slot_ids, axis=0)[:, None, :]
        summary_grad = pool_mask * (
            cot_rows / halves[:, :, None] + cot_rows * exp_summary / exp_part[:, None, :]
        )
        activation_grad = jnp.broadcast_to(
            (summary_grad / (2 * MEL))[:, :, None, None, :], (CL_MB, half_frames, 2, MEL, C2)
        ).reshape(shape_out)
        grad_two, gain_two_grad, shift_two_grad = norm_backward(
            activation_grad, frame_mask, shaped_two, normed_two, scale_two, gain_table[2], pixels
        )
        sum_two = sum_two + contract_rows(hidden_columns, grad_two.reshape(-1, C2))
        flip_two = weights[1][::-1].transpose(0, 2, 1).reshape(9 * C2, C2)
        hidden_grad = jnp.dot(
            patches(grad_rim(grad_two), FR_DEV, MEL), flip_two, preferred_element_type=jnp.float32
        ).reshape(shape_out)
        grad_one, gain_one_grad, shift_one_grad = norm_backward(
            hidden_grad, frame_mask, shaped_one, normed_one, scale_one, gain_table[0], pixels
        )
        sum_one = sum_one + contract_rows(input_columns, grad_one.reshape(-1, C2))
        flip_one = weights[0][::-1].transpose(0, 2, 1).reshape(9 * C2, C1)
        rows_grad = jnp.dot(
            patches(grad_rim(grad_one), FR_DEV, MEL), flip_one, preferred_element_type=jnp.float32
        ).reshape(CL_MB, FR_DEV, MEL, C1)
        input_grad = input_grad.at[slot_ids].set((rows_grad * frame_mask).astype(jnp.bfloat16))
        norm_sum = norm_sum + jnp.stack(
            [gain_one_grad, shift_one_grad, gain_two_grad, shift_two_grad]
        )
    batch_parts = (
        lax.psum_scatter(sum_one.reshape(9, C1, C2), "batch", scatter_dimension=1, tiled=True),
        lax.psum_scatter(sum_two.reshape(9, C2, C2), "batch", scatter_dimension=1, tiled=True),
    )
    grad_one_shard, grad_two_shard = (
        lax.psum_scatter(batch_parts[0], "tm", scatter_dimension=2, tiled=True),
        lax.psum_scatter(batch_parts[1], "tm", scatter_dimension=2, tiled=True),
    )
    shard_width = C2 // tm_count
    norm_shard = lax.dynamic_slice_in_dim(norm_sum, tm_index * shard_width, shard_width, 1)
    norm_term = jnp.where(batch_index == 0, jnp.sum(norm_shard * norm_shard), 0.0)
    own_squares = (
        jnp.sum(grad_one_shard * grad_one_shard)
        + jnp.sum(grad_two_shard * grad_two_shard)
        + norm_term
    )
    grad_norm = jnp.sqrt(lax.psum(own_squares, ("tm", "batch")))
    factor = jnp.minimum(1.0, CLIP_NORM / (grad_norm + 1e-06))
    first_update = adam_step(
        kernel_one,
        kernel_one_mean,
        kernel_one_square,
        grad_one_shard,
        factor,
        (9 * C1) ** (-0.5),
        WEIGHT_DECAY,
    )
    second_update = adam_step(
        kernel_two,
        kernel_two_mean,
        kernel_two_square,
        grad_two_shard,
        factor,
        (9 * C2) ** (-0.5),
        WEIGHT_DECAY,
    )
    norm_update = adam_step(norm_params, norm_mean, norm_square, norm_shard, factor, GAIN_RATE, 0.0)
    return (pooled, input_grad, grad_norm) + first_update + second_update + norm_update


AXES = ("z", "x", "y", "core")
BF = jnp.bfloat16
F32 = jnp.float32
ROWS = 512
CLIPS_CORE = 4
PIXELS = ROWS * CLIPS_CORE
HALF = PIXELS // 2
LANES = 128
TAPS = 9
CHUNK = TAPS * 32
ANY = pl.BlockSpec(memory_space=pl.ANY)
VM = pl.BlockSpec(memory_space=pltpu.VMEM)
SM = pl.BlockSpec(memory_space=pltpu.SMEM)
HB = pl.BlockSpec(memory_space=pltpu.HBM)
VMEM_LIMIT = 16 * 1024 * 1024


def shape_of(shape, dtype=BF):
    return jax.ShapeDtypeStruct(shape, dtype)


def call(kernel, out, in_specs, out_specs, scratch=(), limit=VMEM_LIMIT):
    cost = COSTS[kernel]
    return pl.pallas_call(
        kernel,
        out_shape=out,
        in_specs=in_specs,
        out_specs=out_specs,
        scratch_shapes=list(scratch),
        compiler_params=pltpu.CompilerParams(vmem_limit_bytes=limit),
        cost_estimate=pl.CostEstimate(
            flops=int(cost * FLOP_SCALE), bytes_accessed=int(cost * BYTE_SCALE), transcendentals=0
        ),
    )


def swap(value, axis, step=1):
    size = lax.axis_size(axis)
    return lax.ppermute(value, axis, [(i, i ^ step) for i in range(size)])


def start_copies(copies, sems, base=0):
    started = []
    for at, (source, target) in enumerate(copies):
        copy = pltpu.make_async_copy(source, target, sems.at[base + at])
        copy.start()
        started.append(copy)
    return started


def wait_all(copies):
    for copy in copies:
        copy.wait()


def place(*axes):
    found = tuple(lax.axis_index(axis) for axis in axes)
    return found if len(found) > 1 else found[0]


def after(value, *others):
    return lax.optimization_barrier((value,) + others)[0]


def pin(name, value, *others):
    return after(value, *others) if OPT[name] else value


def steps_of():
    return OPT["zorder"]


def write_facts(order_ref, counts_ref, facts_ref):
    z, core = place("z", "core")
    row_of = lax.broadcasted_iota(jnp.int32, (8, LANES), 0)
    facts = jnp.zeros((8, LANES), jnp.int32)
    total = 0
    for row in range(4):
        for j in range(CL_MB):
            total = total + counts_ref[row * 8 + order_ref[row, z * CL_MB + j]]
    facts = jnp.where(row_of == 4, MEL * total, facts)
    for group in range(2):
        for j in range(CL_MB):
            row = group * 2 + core
            count = counts_ref[row * 8 + order_ref[row, z * CL_MB + j]]
            facts = jnp.where(row_of == group * CL_MB + j, count, facts)
    facts_ref[...] = facts


def count_row(facts_ref, clip):
    return facts_ref[clip : clip + 1, :]


def pixel_row(facts_ref):
    return facts_ref[4:5, :].astype(F32)


def time_shift(rows, step):
    zero = jnp.zeros((MEL, rows.shape[1]), rows.dtype)
    if step == 1:
        return jnp.concatenate([rows[MEL:], zero], axis=0)
    if step == -1:
        return jnp.concatenate([zero, rows[:-MEL]], axis=0)
    return rows


def mel_shift(rows, step):
    if step == 0:
        return rows
    cube = rows.reshape(rows.shape[0] // MEL, MEL, rows.shape[1])
    turned = pltpu.roll(cube, (-step) % MEL, 1)
    bin_at = lax.broadcasted_iota(jnp.int32, cube.shape, 1) + step
    keep = (bin_at >= 0) & (bin_at < MEL)
    return jnp.where(keep, turned, 0.0).reshape(rows.shape)


def valid_rows(facts_ref, clip):
    frame = lax.broadcasted_iota(jnp.int32, (ROWS, LANES), 0) // MEL
    return (frame < count_row(facts_ref, clip)).astype(F32)


def dot_nt(left, right):
    return lax.dot_general(left, right, (((1,), (1,)), ((), ())), preferred_element_type=F32)


def dot_nn(left, right):
    return lax.dot_general(left, right, (((1,), (0,)), ((), ())), preferred_element_type=F32)


def dot_tn(left, right):
    return lax.dot_general(left, right, (((0,), (0,)), ((), ())), preferred_element_type=F32)


def lanes_of(tap):
    return slice(tap * LANES, (tap + 1) * LANES)


def gather_taps(product):
    total = None
    for mel in range(3):
        column = None
        for time in range(3):
            term = time_shift(product[:, lanes_of(3 * time + mel)], time - 1)
            column = term if column is None else column + term
        column = mel_shift(column, mel - 1)
        total = column if total is None else total + column
    return total


def scatter_taps(grad, target, base):
    for mel in range(3):
        moved = mel_shift(grad, 1 - mel)
        for time in range(3):
            target[base : base + ROWS, lanes_of(3 * time + mel)] = time_shift(moved, 1 - time).astype(
                BF
            )


def channel_sums(first, second):
    return (jnp.sum(first, axis=0, keepdims=True), jnp.sum(second, axis=0, keepdims=True))


def pair_sums(own_ref, other_ref):
    return (own_ref[0:1, :] + other_ref[0:1, :], own_ref[1:2, :] + other_ref[1:2, :])


def norm_rows(own_ref, other_ref, pixels):
    total, squares = pair_sums(own_ref, other_ref)
    mean = total / pixels
    return mean, lax.rsqrt(squares / pixels - mean * mean + NORM_EPS)


def put_pair(ref, first, second):
    ref[...] = jnp.zeros(ref.shape, F32)
    ref[0:1, :] = first
    ref[1:2, :] = second


def exchange_matrix(rows, columns, source_of):
    row = lax.broadcasted_iota(jnp.int32, (rows, columns), 0)
    column = lax.broadcasted_iota(jnp.int32, (rows, columns), 1)
    return (row == source_of(column)).astype(BF)


def block_exchange(column):
    return ((column // 32) % 4) * 128 + (column // 128) * 32 + column % 32


def lane_index(rows):
    return lax.broadcasted_iota(jnp.int32, (rows, LANES), 1)


def prepare_kernel(
    order_ref, counts_ref, clip_ref, one_in, two_in, norm_in, cot_in, p0, p1, p2, p3, one_keep,
    two_keep, send_ref, gain_ref, cot_own, facts_ref, one_ref, two_ref, norm_ref, cot_ref, sems
):
    z, x, y, core = place(*AXES)
    group = y * 2 + core
    loads = start_copies(
        [(one_in, one_ref), (two_in, two_ref), (norm_in, norm_ref), (cot_in, cot_ref)], sems
    )
    copies = []
    for step, piece in enumerate((p0, p1, p2, p3)):
        plane = jnp.bitwise_xor(z, step)
        for j in range(CL_MB):
            clip = order_ref[group, plane * CL_MB + j]
            copies.append((clip_ref.at[clip], piece.at[j]))
    started = start_copies(copies, sems, 4)
    write_facts(order_ref, counts_ref, facts_ref)
    wait_all(loads)
    for tap in range(TAPS):
        turned = jnp.swapaxes(one_ref[tap], 0, 1)
        rows = [turned[at * 16 : (at + 1) * 16] for at in range(4)]
        low = jnp.concatenate([rows[0], rows[1]], axis=1).astype(BF)
        high = jnp.concatenate([rows[2], rows[3]], axis=1).astype(BF)
        span = slice(tap * 16, (tap + 1) * 16)
        one_keep[span, :] = jnp.where(y == 0, low, high)
        send_ref[span, :] = jnp.where(y == 0, high, low)
        low, high = two_ref[tap, 0:32, :].astype(BF), two_ref[tap, 32:64, :].astype(BF)
        span = slice(tap * 32, (tap + 1) * 32)
        two_keep[span, :] = jnp.where(y == 0, low, high)
        span = slice(144 + tap * 32, 144 + (tap + 1) * 32)
        send_ref[span, :] = jnp.where(y == 0, high, low)
    wide = jnp.concatenate([norm_ref[...], norm_ref[...]], axis=1)
    wide = jnp.concatenate([wide, jnp.zeros((4, LANES), F32)], axis=0)
    turned = pltpu.roll(wide, (z * 32 - y * 32) % LANES, 1)
    gain_rows = jnp.where(lane_index(8) // 32 == z, turned, 0.0)
    gain_ref[...] = jnp.concatenate([gain_rows, jnp.zeros((8, LANES), F32)], axis=0).astype(BF)

    def cot_rows(y_of):
        rows = []
        for j in range(CL_MB):
            row = cot_ref[pl.ds(order_ref[group, z * CL_MB + j], 1), :]
            picked = jnp.zeros((1, LANES), F32)
            for block in range(MB):
                moved = pltpu.roll(
                    jnp.broadcast_to(row[:, lanes_of(block)], (8, LANES)),
                    (block * 32 - x * 64 - y_of * 32) % LANES,
                    1,
                )[0:1]
                picked = jnp.where(lane_index(1) // 32 == block, moved, picked)
            rows.append(picked)
        return rows

    own, send = cot_rows(y), cot_rows(1 - y)
    cot_own[...] = jnp.concatenate(own + [jnp.zeros((6, LANES), F32)], axis=0)
    high = [row.astype(BF).astype(F32) for row in send]
    rest = [row - top for row, top in zip(send, high)]
    middle = [row.astype(BF).astype(F32) for row in rest]
    low = [row - top for row, top in zip(rest, middle)]
    packed = jnp.concatenate(high + middle + low + [jnp.zeros((10, LANES), F32)], axis=0)
    send_ref[144 + CHUNK : 160 + CHUNK, :] = packed.astype(BF)
    wait_all(started)


def first_conv_kernel(
    facts_ref, a0, a1, a23, b0, b1, b23, o0, o1, o2, o3, others,
    pre_ref, x_ref, weight_ref, stat_ref, gain_ref, sems
):
    z, x, y, core = place(*AXES)
    copies = []
    for j, pieces in (
        (0, ((a0, 0, x, y), (a1, 0, 1 - x, y), (a23, 0, x, 1 - y), (a23, MB, 1 - x, 1 - y))),
        (1, ((b0, 0, x, y), (b1, 0, x, 1 - y), (b23, 0, 1 - x, y), (b23, MB, 1 - x, 1 - y))),
    ):
        for source, base, x_of, y_of in pieces:
            for step in range(MB):
                frames = (jnp.bitwise_xor(z, step) * 2 + x_of) * 64
                row = pl.multiple_of((y_of * CL_MB + j) * ROWS + frames, 64)
                copies.append((source.at[base + step], x_ref.at[pl.ds(row, 64), :]))
    started = start_copies(copies, sems)
    gains = jnp.zeros((8, LANES), F32)
    for half in range(2):

        def source_of(column, half=half):
            from_core = jnp.bitwise_xor((column // 64) % 2, core)
            from_y = jnp.bitwise_xor(column // 128, y)
            return from_core * 256 + from_y * 128 + half * 64 + column % 64

        spread = exchange_matrix(512, C1, source_of)
        for step, own in enumerate((o0, o1, o2, o3)):
            z_of = jnp.bitwise_xor(z, step)
            other = others[step * 304 : step * 304 + 288]
            four = jnp.concatenate([own[0:144], own[144:288], other[0:144], other[144:288]], axis=1)
            both = dot_nn(four, spread).astype(BF)
            for tap in range(TAPS):
                weight_ref[tap, z_of, half * 16 : half * 16 + 16] = both[tap * 16 : (tap + 1) * 16]
            if half == 0:
                gains = gains + own[CHUNK : CHUNK + 16].astype(F32)[0:8]
    gain_ref[...] = gains
    wait_all(started)
    weight = weight_ref[...].reshape(TAPS * LANES, C1)
    first = jnp.zeros((1, LANES), F32)
    second = jnp.zeros((1, LANES), F32)
    for clip in range(CLIPS_CORE):
        span = slice(clip * ROWS, (clip + 1) * ROWS)
        mask = valid_rows(facts_ref, clip)
        masked = x_ref[span, :] * jnp.concatenate([mask, mask], axis=1).astype(BF)
        x_ref[span, :] = masked
        pre = gather_taps(dot_nt(masked, weight))
        pre_ref[span, :] = pre
        kept = pre * mask
        plus = channel_sums(kept, kept * pre)
        first, second = first + plus[0], second + plus[1]
    put_pair(stat_ref, first, second)


def hidden_kernel(facts_ref, pre_ref, own_ref, other_ref, gain_ref, a_ref, b_ref):
    mean, scale = norm_rows(own_ref, other_ref, pixel_row(facts_ref))
    for clip in range(CLIPS_CORE):
        pre = pre_ref[clip * ROWS : (clip + 1) * ROWS, :]
        shaped = gain_ref[0:1, :] * ((pre - mean) * scale) + gain_ref[1:2, :]
        value = shaped * jax.nn.sigmoid(shaped) * valid_rows(facts_ref, clip)
        target = a_ref if clip < 2 else b_ref
        target[(clip % 2) * ROWS : (clip % 2 + 1) * ROWS, :] = value.astype(BF)


def second_weight_kernel(own_ref, other_ref, weight_ref, pieces, sems):
    z, y, core = place("z", "y", "core")
    copies = []
    for step in range(MB):
        for source, core_of in ((own_ref, core), (other_ref, 1 - core)):
            for turn in range(2):
                part = jnp.bitwise_xor(y, turn) * 2 + core_of
                copies.append(
                    (
                        source.at[pl.ds((step * 2 + turn) * CHUNK, CHUNK), :],
                        pieces.at[jnp.bitwise_xor(z, step), part],
                    )
                )
    started = start_copies(copies, sems)
    spread = exchange_matrix(C2, C2, block_exchange)
    wait_all(started)
    for z_of in range(MB):
        natural = jnp.concatenate([pieces[z_of, part] for part in range(4)], axis=1)
        both = dot_nn(natural, spread).astype(BF)
        for tap in range(TAPS):
            weight_ref[tap, z_of] = both[tap * 32 : (tap + 1) * 32]


def hidden_copies(parts, target):
    x, y = place("x", "y")
    chips = ((x, y), (1 - x, y), (x, 1 - y), (1 - x, 1 - y), (x, y), (x, 1 - y), (1 - x, y), (1 - x, 1 - y))
    copies = []
    for at, (source, (x_of, y_of)) in enumerate(zip(parts, chips)):
        lane = pl.multiple_of((x_of * 2 + y_of) * LANES, LANES)
        copies.append((source, target.at[pl.ds((at // 4) * HALF, HALF), pl.ds(lane, LANES)]))
    return copies


def second_conv_kernel(facts_ref, *rest):
    parts, (weight_ref, pre_ref, stat_ref, hidden, sems) = rest[:8], rest[8:]
    started = start_copies(hidden_copies(parts, hidden), sems)
    weight = weight_ref[...].reshape(TAPS * LANES, C2)
    wait_all(started)
    first = jnp.zeros((1, LANES), F32)
    second = jnp.zeros((1, LANES), F32)
    for clip in range(CLIPS_CORE):
        span = slice(clip * ROWS, (clip + 1) * ROWS)
        pre = gather_taps(dot_nt(hidden[span, :], weight))
        pre_ref[span, :] = pre
        kept = pre * valid_rows(facts_ref, clip)
        plus = channel_sums(kept, kept * pre)
        first, second = first + plus[0], second + plus[1]
    put_pair(stat_ref, first, second)


def pool_kernel(
    facts_ref, pre_ref, own_ref, other_ref, gain_ref, cot_own, cot_got,
    slope_ref, sum_ref, pooled_ref
):
    y = place("y")
    mean, scale = norm_rows(own_ref, other_ref, pixel_row(facts_ref))
    first = jnp.zeros((1, LANES), F32)
    second = jnp.zeros((1, LANES), F32)
    slots = ROWS // (2 * MEL)
    got = cot_got[144 + CHUNK : 160 + CHUNK, :].astype(F32)
    pooled = []
    for clip in range(CLIPS_CORE):
        span = slice(clip * ROWS, (clip + 1) * ROWS)
        count = count_row(facts_ref, clip)
        j = clip % CL_MB
        told = got[j : j + 1] + got[2 + j : 3 + j] + got[4 + j : 5 + j]
        cot = jnp.where(y == clip // CL_MB, cot_own[j : j + 1, :], told)
        mask = valid_rows(facts_ref, clip)
        normed = (pre_ref[span, :] - mean) * scale
        shaped = gain_ref[2:3, :] * normed + gain_ref[3:4, :]
        gate = jax.nn.sigmoid(shaped)
        active = (shaped * gate * mask).reshape(slots, 2 * MEL, LANES)
        summary = jnp.sum(active, axis=1) / (2 * MEL)
        slot = lax.broadcasted_iota(jnp.int32, (slots, LANES), 0)
        keep = (2 * slot + 1 < count).astype(F32)
        raised = jnp.exp(summary)
        exp_total = jnp.sum(raised * keep, axis=0, keepdims=True)
        halves = (count // 2).astype(F32)
        pooled.append(
            jnp.sum(summary * keep, axis=0, keepdims=True) / halves + jnp.log(exp_total / halves)
        )
        summary_grad = keep * (cot / halves + cot * raised / exp_total) / (2 * MEL)
        spread = jnp.broadcast_to(summary_grad[:, None, :], (slots, 2 * MEL, LANES))
        slope = spread.reshape(ROWS, LANES) * mask * (gate * (1.0 + shaped * (1.0 - gate)))
        slope_ref[span, :] = slope
        plus = channel_sums(slope, slope * normed)
        first, second = first + plus[0], second + plus[1]
    put_pair(sum_ref, first, second)
    high = [row.astype(BF).astype(F32) for row in pooled]
    low = [row - top for row, top in zip(pooled, high)]
    rows = jnp.concatenate(high + low + [jnp.zeros((8, LANES), F32)], axis=0)
    pooled_ref[...] = rows.astype(BF)


def pre_grad(slope, pre, mask, mean, scale, gain, sums, pixels):
    normed = (pre - mean) * scale
    return mask * (scale * gain) * (slope - sums[0] / pixels - normed * (sums[1] / pixels))


def grad_columns_kernel(
    facts_ref, slope_ref, pre_ref, own_ref, other_ref, sum_own, sum_other, gain_ref, weight_ref,
    columns, a_far, b_far
):
    x, y = place("x", "y")
    pixels = pixel_row(facts_ref)
    mean, scale = norm_rows(own_ref, other_ref, pixels)
    sums = pair_sums(sum_own, sum_other)
    lane = pl.multiple_of(((1 - x) * 2 + 1 - y) * LANES, LANES)
    weight = weight_ref[:, :, :, pl.ds(lane, LANES)].reshape(TAPS * LANES, LANES)
    for clip in range(CLIPS_CORE):
        span = slice(clip * ROWS, (clip + 1) * ROWS)
        mask = valid_rows(facts_ref, clip)
        grad = pre_grad(
            slope_ref[span, :], pre_ref[span, :], mask, mean, scale, gain_ref[2:3, :], sums, pixels
        )
        scatter_taps(grad, columns, clip * ROWS)
        rows = slice((clip % 2) * ROWS, (clip % 2 + 1) * ROWS)
        target = a_far if clip < 2 else b_far
        target[rows, :] = dot_nn(columns[span, :], weight).astype(BF)


def hidden_grad_kernel(
    columns, weight_ref, pooled_ref, a_own, a_mid, a_near, b_own, b_mid, b_near, partial
):
    x, y = place("x", "y")
    weight = weight_ref[...].reshape(TAPS * LANES, C2)
    a_near[HALF : HALF + 16, :] = pooled_ref[...]

    def lane(x_of, y_of):
        return pl.ds(pl.multiple_of((x_of * 2 + y_of) * LANES, LANES), LANES)

    for clip in range(CLIPS_CORE):
        span = slice(clip * ROWS, (clip + 1) * ROWS)
        partial[...] = dot_nn(columns[span, :], weight)
        rows = slice((clip % 2) * ROWS, (clip % 2 + 1) * ROWS)
        if clip < 2:
            a_own[rows, :] = partial[:, lane(x, y)]
            a_mid[rows, :] = partial[:, lane(x, 1 - y)]
            a_near[rows, :] = partial[:, lane(1 - x, y)].astype(BF)
        else:
            b_own[rows, :] = partial[:, lane(x, y)]
            b_mid[rows, :] = partial[:, lane(1 - x, y)]
            b_near[rows, :] = partial[:, lane(x, 1 - y)].astype(BF)


def both_grad_kernel(
    facts_ref, slope_ref, pre_ref, own_ref, other_ref, sum_own, sum_other, gain_ref, weight_ref,
    pooled_ref, columns, a_own, a_mid, a_send, b_own, b_mid, b_send, partial
):
    x, y = place("x", "y")
    pixels = pixel_row(facts_ref)
    mean, scale = norm_rows(own_ref, other_ref, pixels)
    sums = pair_sums(sum_own, sum_other)
    weight = weight_ref[...].reshape(TAPS * LANES, C2)
    a_send[2 * HALF : 2 * HALF + 16, :] = pooled_ref[...]

    def lane(x_of, y_of):
        return pl.ds(pl.multiple_of((x_of * 2 + y_of) * LANES, LANES), LANES)

    for clip in range(CLIPS_CORE):
        span = slice(clip * ROWS, (clip + 1) * ROWS)
        mask = valid_rows(facts_ref, clip)
        grad = pre_grad(
            slope_ref[span, :], pre_ref[span, :], mask, mean, scale, gain_ref[2:3, :], sums, pixels
        )
        scatter_taps(grad, columns, clip * ROWS)
        partial[...] = dot_nn(columns[span, :], weight)
        rows = slice((clip % 2) * ROWS, (clip % 2 + 1) * ROWS)
        near_rows = slice(HALF + (clip % 2) * ROWS, HALF + (clip % 2 + 1) * ROWS)
        far = partial[:, lane(1 - x, 1 - y)].astype(BF)
        if clip < 2:
            a_own[rows, :] = partial[:, lane(x, y)]
            a_mid[rows, :] = partial[:, lane(x, 1 - y)]
            a_send[rows, :] = far
            a_send[near_rows, :] = partial[:, lane(1 - x, y)].astype(BF)
        else:
            b_own[rows, :] = partial[:, lane(x, y)]
            b_mid[rows, :] = partial[:, lane(1 - x, y)]
            b_send[rows, :] = far
            b_send[near_rows, :] = partial[:, lane(x, 1 - y)].astype(BF)


def pass_on_kernel(a_mid, a_got, b_mid, b_got, a_next, b_next):
    a_next[...] = (a_mid[...] + a_got[0:HALF].astype(F32)).astype(BF)
    b_next[...] = (b_mid[...] + b_got[0:HALF].astype(F32)).astype(BF)


def second_weight_grad_kernel(*rest):
    parts, (columns, keep_ref, send_ref, hidden, natural, sems) = rest[:8], rest[8:]
    core = place("core")
    started = start_copies(hidden_copies(parts, hidden), sems)
    spread = exchange_matrix(C2, C2, block_exchange)
    wait_all(started)
    for clip in range(CLIPS_CORE):
        span = slice(clip * ROWS, (clip + 1) * ROWS)
        hidden[span, :] = dot_nn(hidden[span, :], spread).astype(BF)
    for tap in range(TAPS):
        natural[...] = dot_tn(columns[:, lanes_of(tap)], hidden[...])
        for y_of in range(2):
            keep = natural[:, pl.ds(pl.multiple_of((y_of * 2 + core) * LANES, LANES), LANES)]
            send = natural[:, pl.ds(pl.multiple_of((y_of * 2 + 1 - core) * LANES, LANES), LANES)]
            for z_of in range(MB):
                rows = slice(z_of * 32, (z_of + 1) * 32)
                target = slice(tap * 32, (tap + 1) * 32)
                keep_ref[z_of, y_of, target] = keep[rows]
                send_ref[z_of, y_of, target] = send[rows]


def second_core_kernel(keep_ref, got_ref, own_ref, n1, n2, n3):
    z = place("z")
    own_ref[...] = keep_ref[z] + got_ref[z]
    for step, target in ((1, n1), (2, n2), (3, n3)):
        at = jnp.bitwise_xor(z, step)
        target[...] = (keep_ref[at] + got_ref[at]).astype(BF)


def second_sum_kernel(own_ref, g1, g2, g3, keep_ref, send_ref, square_ref):
    y = place("y")
    total = own_ref[...] + g1[...].astype(F32) + g2[...].astype(F32) + g3[...].astype(F32)
    keep_ref[...] = jnp.where(y == 0, total[0], total[1])
    send_ref[...] = jnp.where(y == 0, total[1], total[0])
    square_ref[...] = jnp.sum(total * total, axis=(0, 1), keepdims=False)[None, :] * jnp.ones((8, 1), F32)


def first_slope_kernel(
    facts_ref, a_own, a_near, a_last, b_own, b_near, b_last, pre_ref, own_ref, other_ref,
    gain_ref, slope_ref, sum_ref
):
    mean, scale = norm_rows(own_ref, other_ref, pixel_row(facts_ref))
    first = jnp.zeros((1, LANES), F32)
    second = jnp.zeros((1, LANES), F32)
    for clip in range(CLIPS_CORE):
        span = slice(clip * ROWS, (clip + 1) * ROWS)
        rows = slice((clip % 2) * ROWS, (clip % 2 + 1) * ROWS)
        own, near, last = (a_own, a_near, a_last) if clip < 2 else (b_own, b_near, b_last)
        base = near.shape[0] // HALF * HALF - HALF
        near_rows = slice(base + (clip % 2) * ROWS, base + (clip % 2 + 1) * ROWS)
        outer = own[rows, :] + near[near_rows, :].astype(F32) + last[rows, :].astype(F32)
        normed = (pre_ref[span, :] - mean) * scale
        shaped = gain_ref[0:1, :] * normed + gain_ref[1:2, :]
        gate = jax.nn.sigmoid(shaped)
        slope = outer * valid_rows(facts_ref, clip) * (gate * (1.0 + shaped * (1.0 - gate)))
        slope_ref[span, :] = slope
        plus = channel_sums(slope, slope * normed)
        first, second = first + plus[0], second + plus[1]
    put_pair(sum_ref, first, second)


def first_grads_kernel(
    facts_ref, slope_ref, pre_ref, own_ref, other_ref, sum_own, sum_other, gain_ref, weight_ref, x_ref,
    part_ref, keep_ref, send_ref, columns, turned
):
    core = place("core")
    pixels = pixel_row(facts_ref)
    mean, scale = norm_rows(own_ref, other_ref, pixels)
    sums = pair_sums(sum_own, sum_other)
    weight = weight_ref[...].reshape(TAPS * LANES, C1)

    def source_of(column):
        core_of = jnp.where(column < 128, core, 1 - core)
        return ((column // 64) % 2) * 128 + core_of * 64 + column % 64

    spread = exchange_matrix(C1, C1, source_of)
    for clip in range(CLIPS_CORE):
        span = slice(clip * ROWS, (clip + 1) * ROWS)
        mask = valid_rows(facts_ref, clip)
        grad = pre_grad(
            slope_ref[span, :], pre_ref[span, :], mask, mean, scale, gain_ref[0:1, :], sums, pixels
        )
        scatter_taps(grad, columns, clip * ROWS)
        partial = dot_nn(columns[span, :], weight).astype(BF)
        turned[span, :] = dot_nn(x_ref[span, :], spread).astype(BF)
        for z_of in range(MB):
            for x_of in range(2):
                target = slice(((clip % 2) * MB + z_of) * 64, ((clip % 2) * MB + z_of + 1) * 64)
                rows = slice((z_of * 2 + x_of) * 64, (z_of * 2 + x_of + 1) * 64)
                part_ref[x_of * 2 + clip // 2, target, :] = partial[rows]
    for tap in range(TAPS):
        both = dot_tn(columns[:, lanes_of(tap)], turned[...])
        for z_of in range(MB):
            rows = slice(z_of * 32, (z_of + 1) * 32)
            target = slice(tap * 32, (tap + 1) * 32)
            keep_ref[z_of, target] = both[rows, 0:LANES]
            send_ref[z_of, target] = both[rows, LANES : 2 * LANES]


def first_core_kernel(
    keep_ref, got_ref, one_own, one_other, two_own, two_other, pooled_own, pooled_near, pooled_last,
    own_ref, n0, n1, n2, n3, scratch
):
    z, x, y = place("z", "x", "y")
    own_ref[...] = keep_ref[z] + got_ref[z]
    one, two = pair_sums(one_own, one_other), pair_sums(two_own, two_other)
    sums = jnp.concatenate([one[1], one[0], two[1], two[0]], axis=0)
    high = sums.astype(BF).astype(F32)
    norm_tile = jnp.concatenate([high, sums - high, jnp.zeros((8, LANES), F32)], axis=0).astype(BF)
    last = pooled_last[HALF : HALF + 32, :].astype(F32)
    near = pooled_near[...].astype(F32)
    own = pooled_own[...].astype(F32)
    for rows, x_of, y_of in (
        (own, x, y),
        (near, 1 - x, y),
        (last[0:16], x, 1 - y),
        (last[16:32], 1 - x, 1 - y),
    ):
        for part in range(2):
            for j in range(CL_MB):
                row = jnp.where(
                    y == 0, rows[part * 4 + j : part * 4 + j + 1], rows[part * 4 + 2 + j : part * 4 + 3 + j]
                )
                scratch[pl.ds((x_of * 2 + y_of) * 4 + part * 2 + j, 1), :] = row
    pooled_tile = scratch[...].astype(BF)
    for step, target in ((0, n0), (1, n1), (2, n2), (3, n3)):
        at = jnp.bitwise_xor(z, step)
        target[0:CHUNK, :] = (keep_ref[at] + got_ref[at]).astype(BF)
        target[CHUNK : CHUNK + 16, :] = norm_tile
        target[CHUNK + 16 : CHUNK + 32, :] = pooled_tile


def first_sum_kernel(own_ref, n0, g1, g2, g3, square_two, told_ref, keep_ref, send_ref, norm_ref):
    z, y, core = place("z", "y", "core")
    total = own_ref[...]
    norm = n0[CHUNK : CHUNK + 16, :].astype(F32)
    for got in (g1, g2, g3):
        total = total + got[0:CHUNK, :].astype(F32)
        norm = norm + got[CHUNK : CHUNK + 16, :].astype(F32)
    norm = norm[0:4] + norm[4:8]
    mine = (lane_index(4) // 32 == z) & (core == 0)
    squares = jnp.sum(total * total, axis=0, keepdims=True) + jnp.sum(
        jnp.where(mine, norm * norm, 0.0), axis=0, keepdims=True
    )
    first_rows = lax.broadcasted_iota(jnp.int32, told_ref.shape, 0) % 8 == 0
    told_ref[...] = jnp.where(first_rows, squares + square_two[0:1, :], 0.0)
    turned = pltpu.roll(total, 64, 1)
    low = jnp.where(y == 0, total, turned)
    high = jnp.where(y == 0, turned, total)
    left = lane_index(144) < 64
    keep_ref[...] = jnp.where(left, low[0:144], pltpu.roll(low[144:288], 64, 1))
    send_ref[0:144, :] = jnp.where(left, high[0:144], pltpu.roll(high[144:288], 64, 1))
    rows = jnp.concatenate([norm, jnp.zeros((4, LANES), F32)], axis=0)
    send_ref[144:152, :] = rows
    norm_ref[...] = rows


def shard_kernel(keep_ref, got_ref, norm_ref, one_ref, norm_out):
    z, y = place("z", "y")
    keep, got = keep_ref[...], got_ref[0:144, :]
    first, second = jnp.where(y == 0, keep, got), jnp.where(y == 0, got, keep)
    spans = []
    for half in (first, second):
        spans.append(jnp.concatenate([half[:, 0:64], half[:, 64:128]], axis=0))
    for tap in range(TAPS):
        rows = [span[tap * 32 : (tap + 1) * 32] for span in spans]
        one_ref[tap] = jnp.swapaxes(jnp.concatenate(rows, axis=0), 0, 1)
    keep, got = norm_ref[...], got_ref[144:152, :]
    first, second = jnp.where(y == 0, keep, got), jnp.where(y == 0, got, keep)
    low = pltpu.roll(first, (0 - z * 32) % LANES, 1)
    high = pltpu.roll(second, (32 - z * 32) % LANES, 1)
    norm_out[...] = jnp.where(lane_index(8) < 32, low, high)[0:4, 0:64]


def input_sum_kernel(facts_ref, got_ref, f0, f1, f2, f3):
    z, x, y = place("z", "x", "y")
    for j in range(CL_MB):
        count = jnp.where(y == 0, count_row(facts_ref, j), count_row(facts_ref, CL_MB + j))
        count = jnp.concatenate([count, count], axis=1)
        for step, target in enumerate((f0, f1, f2, f3)):
            at = jnp.bitwise_xor(z, step)
            rows = pl.ds(pl.multiple_of((j * MB + at) * 64, 64), 64)
            total = got_ref[0, rows, :].astype(F32)
            for chip in range(1, 4):
                total = total + got_ref[chip, rows, :].astype(F32)
            frame = (at * 2 + x) * 8 + lax.broadcasted_iota(jnp.int32, (64, C1), 0) // MEL
            target[j] = jnp.where(frame < count, total, 0.0).astype(BF)


def finish_kernel(order_ref, f0, g1, g2, g3, n0, n1, n2, n3, grad_ref, pooled_ref, scratch):
    z, y, core = place("z", "y", "core")
    row = y * 2 + core
    for step, (piece, told) in enumerate(((f0, n0), (g1, n1), (g2, n2), (g3, n3))):
        at = jnp.bitwise_xor(z, step)
        rows = told[CHUNK + 16 : CHUNK + 32, :].astype(F32)
        for j in range(CL_MB):
            clip = order_ref[row, at * CL_MB + j]
            grad_ref[clip] = piece[j]
            for part in range(2):
                chips = [rows[chip * 4 + part * 2 + j : chip * 4 + part * 2 + j + 1] for chip in range(4)]
                scratch[part, pl.ds(clip, 1), :] = jnp.concatenate(chips, axis=1)
    spread = exchange_matrix(C2, C2, block_exchange)
    pooled_ref[...] = dot_nn(scratch[0].astype(BF), spread) + dot_nn(scratch[1].astype(BF), spread)


FLOP_SCALE = OPT['flop']
BYTE_SCALE = 0
COSTS = {
    prepare_kernel: 3,
    first_conv_kernel: 4,
    hidden_kernel: 0.4,
    second_weight_kernel: 2.8,
    second_conv_kernel: 3.5,
    pool_kernel: 1.1,
    grad_columns_kernel: 1.7,
    hidden_grad_kernel: 3.4,
    both_grad_kernel: 4,
    second_weight_grad_kernel: 5,
    pass_on_kernel: 0.2,
    second_core_kernel: 0.2,
    second_sum_kernel: 0.2,
    first_slope_kernel: 0.8,
    first_grads_kernel: 4,
    first_core_kernel: 0.2,
    first_sum_kernel: 0.8,
    shard_kernel: 0.3,
    input_sum_kernel: 0.3,
    finish_kernel: 1.5,
}


def spread_plane(a0, b0):
    a1, b1 = swap(a0, "x"), swap(b0, "y")
    a2, b2 = swap(a0, "y"), swap(b0, "x")
    a3, b3 = swap(a1, "y"), swap(b1, "x")
    return (a0, a1, a2, a3, b0, b1, b2, b3)


def fast_body(
    clip_input,
    frame_counts,
    clip_order,
    cotangent,
    kernel_one,
    kernel_one_mean,
    kernel_one_square,
    kernel_two,
    kernel_two_mean,
    kernel_two_square,
    norm_params,
    norm_mean,
    norm_square,
):
    one_view, two_view = kernel_one, jnp.swapaxes(kernel_two, 1, 2)
    p0, p1, p2, p3, one_keep, two_keep, send, gain_rows, cot_own, facts = call(
        prepare_kernel,
        [shape_of((CL_MB, 64, C1))] * MB
        + [shape_of((144, LANES)), shape_of((CHUNK, LANES)), shape_of((160 + CHUNK, LANES))]
        + [shape_of((16, LANES)), shape_of((8, LANES), F32), shape_of((8, LANES), jnp.int32)],
        [SM, SM] + [HB] * 5,
        [VM] * 10,
        [
            pltpu.VMEM(one_view.shape, F32),
            pltpu.VMEM(two_view.shape, F32),
            pltpu.VMEM(norm_params.shape, F32),
            pltpu.VMEM(cotangent.shape, F32),
            pltpu.SemaphoreType.DMA((4 + MB * CL_MB,)),
        ],
        limit=62 * 1024 * 1024,
    )(
        clip_order,
        frame_counts,
        clip_input.reshape(MB * CL_MB, 64, C1),
        one_view,
        two_view,
        norm_params,
        cotangent,
    )
    def spread_z(values):
        got = {step: swap(values[step], "z", step) for step in steps_of()}
        return [values[0]] + [got[step] for step in (1, 2, 3)]

    arrived = spread_z([p0, p1, p2, p3])
    got = swap(send, "y")
    a0 = jnp.stack([piece[0] for piece in arrived])
    b0 = jnp.stack([piece[1] for piece in arrived])
    one_flat = pin("w1_after_in", jnp.concatenate([one_keep, got[0:144], gain_rows]), a0, b0)
    a1, b1 = swap(a0, "x"), swap(b0, "y")
    if OPT["merge_w"]:
        flat = jnp.concatenate([one_flat, two_keep, got[144 : 144 + CHUNK]])
        one_parts = spread_z([flat] * 4)
    else:
        one_parts = spread_z([one_flat] * 4)
    a01, b01 = jnp.concatenate([a0, a1]), jnp.concatenate([b0, b1])
    if OPT["core_w1_after"] < 2:
        deps = (a1, b1) if OPT["core_w1_after"] else ()
        if OPT["core_w1"] == 4:
            one_others = jnp.concatenate([swap(after(part[0:304], *deps), "core") for part in one_parts])
        else:
            one_others = swap(after(jnp.concatenate([part[0:304] for part in one_parts]), *deps), "core")
        a01, b01 = pin("fwd_after_core_w1", a01, one_others), pin("fwd_after_core_w1", b01, one_others)
        a23, b23 = swap(a01, "y"), swap(b01, "x")
    else:
        a23, b23 = swap(a01, "y"), swap(b01, "x")
        deps = (a23, b23)
        if OPT["core_w1"] == 4:
            one_others = jnp.concatenate([swap(after(part[0:304], *deps), "core") for part in one_parts])
        else:
            one_others = swap(after(jnp.concatenate([part[0:304] for part in one_parts]), *deps), "core")
    inputs = (a0, a1, a23, b0, b1, b23)
    if OPT["merge_w"]:
        two_parts = [part[304:] for part in one_parts]
        one_parts = [part[0:304] for part in one_parts]
    else:
        two_flat = jnp.concatenate([two_keep, got[144 : 144 + CHUNK]])
        two_flat = {
            0: lambda: two_flat,
            1: lambda: after(two_flat, *one_parts[1:]),
            2: lambda: after(two_flat, one_others),
            3: lambda: after(two_flat, a1, b1),
            4: lambda: after(two_flat, a1, b1, one_others),
        }[OPT["w2_after"]]()
        two_parts = spread_z([two_flat] * 4)
    pre_one, masked, weight_one, stat_one, gains = call(
        first_conv_kernel,
        [
            shape_of((PIXELS, LANES), F32),
            shape_of((PIXELS, C1)),
            shape_of((TAPS, MB, 32, C1)),
            shape_of((8, LANES), F32),
            shape_of((8, LANES), F32),
        ],
        [VM] + [ANY] * 6 + [VM] * 5,
        [VM] * 5,
        [pltpu.SemaphoreType.DMA((8 * MB,))],
    )(
        after(facts, *two_parts[1:]) if OPT["w2_before"] == 2 else facts, *inputs, *one_parts, one_others
    )
    stat_one_other = swap(stat_one, "core")

    ha0, hb0 = call(
        hidden_kernel, [shape_of((HALF, LANES))] * 2, [VM] * 5, [VM] * 2
    )(
        after(facts, *two_parts[1:]) if OPT["w2_before"] == 1 else facts, pre_one, stat_one, stat_one_other, gains
    )
    hidden_parts = spread_plane(ha0, hb0)

    two_all = jnp.concatenate(two_parts)
    if OPT["core_w2_after"] == 1:
        two_all = after(two_all, ha0)
    if OPT["core_w2_after"] == 2:
        two_all = after(two_all, hidden_parts[1], hidden_parts[5])
    two_all_other = swap(two_all, "core")
    two_all = pin("kw2_after", two_all, hidden_parts[1], hidden_parts[5])
    weight_two = call(
        second_weight_kernel,
        shape_of((TAPS, MB, 32, C2)),
        [ANY, ANY],
        VM,
        [pltpu.VMEM((MB, 4, CHUNK, LANES), BF), pltpu.SemaphoreType.DMA((16,))],
    )(two_all, two_all_other)

    pre_two, stat_two = call(
        second_conv_kernel,
        [shape_of((PIXELS, LANES), F32), shape_of((8, LANES), F32)],
        [VM] + [ANY] * 8 + [VM],
        [VM] * 2,
        [pltpu.VMEM((PIXELS, C2), BF), pltpu.SemaphoreType.DMA((8,))],
    )(facts, *hidden_parts, weight_two)
    stat_two_other = swap(stat_two, "core")
    slope_two, sum_two, pooled_own = call(
        pool_kernel,
        [shape_of((PIXELS, LANES), F32), shape_of((8, LANES), F32), shape_of((16, LANES))],
        [VM] * 7,
        [VM] * 3,
    )(facts, pre_two, stat_two, stat_two_other, gains, cot_own, got)
    sum_two_other = swap(sum_two, "core")
    if OPT["rs"] == "far":
        columns_two, a_far, b_far = call(
            grad_columns_kernel,
            [shape_of((PIXELS, TAPS * LANES))] + [shape_of((HALF, LANES))] * 2,
            [VM] * 9,
            [VM] * 3,
        )(facts, slope_two, pre_two, stat_two, stat_two_other, sum_two, sum_two_other, gains, weight_two)
        a_got, b_got = swap(a_far, "x"), swap(b_far, "y")
        a_own, a_mid, a_near, b_own, b_mid, b_near = call(
            hidden_grad_kernel,
            [shape_of((HALF, LANES), F32)] * 2
            + [shape_of((HALF + 16, LANES))]
            + [shape_of((HALF, LANES), F32)] * 2
            + [shape_of((HALF, LANES))],
            [VM] * 3,
            [VM] * 6,
            [pltpu.VMEM((ROWS, C2), F32)],
        )(columns_two, weight_two, pooled_own)
        a_near, b_near = swap(a_near, "x"), swap(b_near, "y")
        a_pool = a_near[HALF:]
    else:
        columns_two, a_own, a_mid, a_send, b_own, b_mid, b_send = call(
            both_grad_kernel,
            [shape_of((PIXELS, TAPS * LANES))]
            + [shape_of((HALF, LANES), F32)] * 2
            + [shape_of((2 * HALF + 16, LANES))]
            + [shape_of((HALF, LANES), F32)] * 2
            + [shape_of((2 * HALF, LANES))],
            [VM] * 10,
            [VM] * 7,
            [pltpu.VMEM((ROWS, C2), F32)],
        )(
            facts, slope_two, pre_two, stat_two, stat_two_other, sum_two, sum_two_other, gains,
            weight_two, pooled_own,
        )
        a_got = a_near = swap(a_send, "x")
        b_got = b_near = swap(b_send, "y")
        a_pool = a_got[2 * HALF :]
    two_part, two_part_send = call(
        second_weight_grad_kernel,
        [shape_of((MB, 2, CHUNK, LANES), F32)] * 2,
        [ANY] * 8 + [VM],
        [VM] * 2,
        [
            pltpu.VMEM((PIXELS, C2), BF),
            pltpu.VMEM((LANES, C2), F32),
            pltpu.SemaphoreType.DMA((8,)),
        ],
    )(*hidden_parts, columns_two)
    a_next, b_next = call(pass_on_kernel, [shape_of((HALF, LANES))] * 2, [VM] * 4, [VM] * 2)(
        a_mid,
        pin("pass_after_near", pin("pass_after_g2", a_got, two_part), a_near, b_near),
        b_mid,
        b_got,
    )
    a_next = jnp.concatenate([a_next, pooled_own, a_pool])
    a_last, b_last = swap(a_next, "y"), swap(b_next, "x")
    two_own, t1, t2, t3 = call(
        second_core_kernel,
        [shape_of((2, CHUNK, LANES), F32)] + [shape_of((2, CHUNK, LANES))] * 3,
        [VM] * 2,
        [VM] * 4,
    )(two_part, swap(pin("core_g2_after", two_part_send, a_next), "core"))
    slope_one, sum_one = call(
        first_slope_kernel,
        [shape_of((PIXELS, LANES), F32), shape_of((8, LANES), F32)],
        [VM] * 11,
        [VM] * 2,
    )(pin("k5_after", facts, t1), a_own, a_near, a_last, b_own, b_near, b_last, pre_one, stat_one, stat_one_other, gains)
    sum_one_other = swap(sum_one, "core")

    input_part, one_part, one_part_send = call(
        first_grads_kernel,
        [shape_of((4, ROWS, C1))] + [shape_of((MB, CHUNK, LANES), F32)] * 2,
        [VM] * 10,
        [VM] * 3,
        [pltpu.VMEM((PIXELS, TAPS * LANES), BF), pltpu.VMEM((PIXELS, C1), BF)],
    )(
        facts, slope_one, pre_one, stat_one, stat_one_other, sum_one, sum_one_other, gains, weight_one,
        masked,
    )
    two_keep_sum, two_send_sum, square_two = call(
        second_sum_kernel,
        [shape_of((CHUNK, LANES), F32)] * 2 + [shape_of((8, LANES), F32)],
        [VM] * 4,
        [VM] * 3,
    )(*spread_z([two_own, t1, t2, t3]))
    two_got_sum = swap(two_send_sum, "y") if not OPT['y2_after'] else None

    one_own, n0, n1, n2, n3 = call(
        first_core_kernel,
        [shape_of((CHUNK, LANES), F32)] + [shape_of((CHUNK + 32, LANES))] * MB,
        [VM] * 9,
        [VM] * 5,
        [pltpu.VMEM((16, LANES), F32)],
    )(
        pin("core1_after_g2", one_part, square_two),
        swap(pin("core_g1_after_g2", one_part_send, square_two), "core"),
        sum_one, sum_one_other, sum_two, sum_two_other,
        pooled_own, a_pool, a_last,
    )
    g1, g2, g3 = spread_z([n0, n1, n2, n3])[1:]
    input_part = pin("a2a_after_core1", input_part, n1)
    input_got = lax.all_to_all(input_part, ("x", "y"), 0, 0, tiled=True)
    f0, f1, f2, f3 = call(
        input_sum_kernel, [shape_of((CL_MB, 64, C1))] * MB, [VM] * 2, [VM] * 4
    )(facts, input_got)
    if OPT["y2_after"]:
        two_got_sum = swap(after(two_send_sum, n1), "y")
    if not OPT["f_after_sum"]:
        f1, f2, f3 = spread_z([f0, f1, f2, f3])[1:]
    told, one_keep_sum, one_send_sum, norm_sum = call(
        first_sum_kernel,
        [
            shape_of((32 * 8, LANES), F32),
            shape_of((144, LANES), F32),
            shape_of((152, LANES), F32),
            shape_of((8, LANES), F32),
        ],
        [VM] * 6,
        [VM] * 4,
    )(
        pin("sum_after_y", pin("sum_after_f", one_own, f0), two_got_sum), n0, g1, g2, g3, square_two
    )
    if OPT["f_after_sum"]:
        f1, f2, f3 = spread_z([f0, after(f1, told), after(f2, told), after(f3, told)])[1:]
    told = lax.all_to_all(told, AXES, 0, 0, tiled=True)
    grad_norm = jnp.sqrt(jnp.sum(pin("told_after_f", told, f1, f2, f3)))
    factor = jnp.minimum(1.0, CLIP_NORM / (grad_norm + 1e-06))
    one_got_sum = swap(one_send_sum, "y")
    grad_one_shard, norm_shard = call(
        shard_kernel,
        [shape_of((TAPS, 64, 64), F32), shape_of((4, 64), F32)],
        [VM] * 3,
        [VM] * 2,
    )(one_keep_sum, one_got_sum, norm_sum)
    y = lax.axis_index("y")
    cut = (TAPS, 32, LANES)
    keep, got = two_keep_sum.reshape(cut), two_got_sum.reshape(cut)
    grad_two_shard = jnp.where(
        y == 0, jnp.concatenate([keep, got], axis=1), jnp.concatenate([got, keep], axis=1)
    )
    grad_two_shard = jnp.swapaxes(grad_two_shard, 1, 2)

    first_update = adam_step(
        kernel_one, kernel_one_mean, kernel_one_square, grad_one_shard, factor, (9 * C1) ** (-0.5), WEIGHT_DECAY
    )
    second_update = adam_step(
        kernel_two, kernel_two_mean, kernel_two_square, grad_two_shard, factor, (9 * C2) ** (-0.5), WEIGHT_DECAY
    )
    norm_update = adam_step(norm_params, norm_mean, norm_square, norm_shard, factor, GAIN_RATE, 0.0)

    input_grad, pooled = call(
        finish_kernel,
        [shape_of((MB * CL_MB, 64, C1)), shape_of((MB * CL_MB, C2), F32)],
        [SM] + [VM] * 8,
        [VM] * 2,
        [pltpu.VMEM((2, MB * CL_MB, C2), F32)],
    )(clip_order, f0, f1, f2, f3, n0, g1, g2, g3)
    input_grad = input_grad.reshape(clip_input.shape)
    return (pooled, input_grad, grad_norm) + first_update + second_update + norm_update


def solution(mesh):
    if mesh.shape["tm"] == 2 * MB and mesh.shape["batch"] == 4:
        grid = Mesh(mesh.devices.reshape(MB, 2, 2, 2), AXES)
        tm, batch, chosen = ("z", "x"), ("y", "core"), fast_body
    else:
        grid, tm, batch, chosen = mesh, "tm", "batch", general_body
    kernels = (P(None, batch, tm),) * 3
    norms = (P(None, tm),) * 3
    in_specs = (P(batch, tm, None, None), P(), P(), P(batch, None)) + 2 * kernels + norms
    out_specs = (P(batch, None), P(batch, tm, None, None), P())
    out_specs = out_specs + (P(None, batch, tm),) * 10 + (P(None, tm),) * 5
    return jax.shard_map(chosen, mesh=grid, in_specs=in_specs, out_specs=out_specs, check_vma=False)
```

```python
import functools

import jax
import jax.numpy as jnp
from jax import lax
from jax.experimental import pallas as pl
from jax.experimental.pallas import tpu as pltpu
from jax.sharding import Mesh, PartitionSpec as P

OPT = {'flop': 0, 'zorder': [2, 3, 1], 'merge_w': False, 'w1_after_in': False, 'core_w1': 1, 'core_w1_after': 0, 'fwd_after_core_w1': False, 'w2_after': 1, 'w2_before': 1, 'core_w2_after': 1, 'kw2_after': False, 'rs': 'two', 'pass_after_g2': True, 'pass_after_near': False, 'k5_after': True, 'core1_after_g2': False, 'core_g1_after_g2': True, 'a2a_after_core1': False, 'sum_after_f': False, 'f_after_sum': False, 'told_after_f': False, 'prep_after_take': True, 'finish_last': True, 'split_first': True, 'split_conv': True, 'ki_after_kg': False, 'load': False, 'a2a_after_g2': False, 'core_g2': 0, 'adam_limit': 62}
C1 = 256
C2 = 512
MEL = 8
FR_DEV = 8
CL_MB = 2
MB = 4
STEP = 10


BETA_ONE = 0.9
BETA_TWO = 0.999
ADAM_EPS = 1e-08
NORM_EPS = 1e-05
WEIGHT_DECAY = 0.01
CLIP_NORM = 0.5
GAIN_RATE = 1.0


def extended(block, sides, width):
    for axis, dim in sides:
        count = lax.axis_size(axis)
        forward = [(i, i + 1) for i in range(count - 1)]
        backward = [(target, source) for source, target in forward]
        low = lax.ppermute(
            lax.slice_in_dim(block, block.shape[dim] - width, None, axis=dim), axis, forward
        )
        high = lax.ppermute(lax.slice_in_dim(block, 0, width, axis=dim), axis, backward)
        block = jnp.concatenate([low, block, high], axis=dim)
    return block


def silu_slope(shaped):
    sigmoid_value = jax.nn.sigmoid(shaped)
    return sigmoid_value * (1.0 + shaped * (1.0 - sigmoid_value))


def pad_mel(field_data):
    return jnp.pad(field_data, ((0, 0), (0, 0), (1, 1), (0, 0)))


def frame_rim(field_data):
    return pad_mel(extended(field_data, (("tm", 1),), 1))


def grad_rim(field_data):
    return pad_mel(extended(field_data, (("tm", 1),), 1))


def patches(padded, frame_count, mel_count):
    pieces = [
        padded[:, step_time : step_time + frame_count, step_mel : step_mel + mel_count, :]
        for step_time in range(3)
        for step_mel in range(3)
    ]
    columns = jnp.concatenate(pieces, axis=-1)
    return columns.reshape(-1, columns.shape[-1])


def norm_forward(pre_norm, frame_mask, pixels, gain_row, shift_row):
    masked = pre_norm * frame_mask
    total_sum, square_sum = lax.psum(
        (jnp.sum(masked, axis=(0, 1, 2)), jnp.sum(masked * pre_norm, axis=(0, 1, 2))),
        ("tm", "batch"),
    )
    channel_mean = total_sum / pixels
    variance = square_sum / pixels - channel_mean * channel_mean
    inv_scale = lax.rsqrt(variance + NORM_EPS)
    normed = (pre_norm - channel_mean) * inv_scale
    return (normed, inv_scale, gain_row * normed + shift_row)


def norm_backward(outer_grad, frame_mask, shaped, normed, inv_scale, gain_row, pixels):
    slope_grad = outer_grad * frame_mask * silu_slope(shaped)
    shift_grad, gain_grad = lax.psum(
        (jnp.sum(slope_grad, axis=(0, 1, 2)), jnp.sum(slope_grad * normed, axis=(0, 1, 2))),
        ("tm", "batch"),
    )
    pre_grad = (
        frame_mask
        * inv_scale
        * gain_row
        * (slope_grad - shift_grad / pixels - normed * gain_grad / pixels)
    )
    return (pre_grad.astype(jnp.bfloat16), gain_grad, shift_grad)


def adam_step(weight, moment, square, summed, factor, step_rate, decay_rate):
    clipped = summed * factor
    moment_new = BETA_ONE * moment + (1.0 - BETA_ONE) * clipped
    square_new = BETA_TWO * square + (1.0 - BETA_TWO) * clipped * clipped
    corrected = moment_new / (1.0 - BETA_ONE**STEP)
    scaled = jnp.sqrt(square_new / (1.0 - BETA_TWO**STEP)) + ADAM_EPS
    weight_new = weight - step_rate * (corrected / scaled + decay_rate * weight)
    return (clipped, moment_new, square_new, weight_new, weight_new.astype(jnp.bfloat16))


def contract_rows(columns, grads):
    return lax.dot_general(
        columns, grads, (((0,), (0,)), ((), ())), preferred_element_type=jnp.float32
    )


def general_body(
    clip_input,
    frame_counts,
    clip_order,
    cotangent,
    kernel_one,
    kernel_one_mean,
    kernel_one_square,
    kernel_two,
    kernel_two_mean,
    kernel_two_square,
    norm_params,
    norm_mean,
    norm_square,
):
    batch_count = lax.axis_size("batch")
    tm_count = lax.axis_size("tm")
    tm_index = lax.axis_index("tm")
    batch_index = lax.axis_index("batch")
    half_frames = FR_DEV // 2
    counts_table = jnp.take_along_axis(frame_counts.reshape(batch_count, -1), clip_order, axis=1)
    valid_pixels = (
        MEL * jnp.sum(counts_table.reshape(batch_count, MB, CL_MB), axis=(0, 2))
    ).astype(jnp.float32)
    local_order = lax.dynamic_index_in_dim(clip_order, batch_index, 0, keepdims=False)
    local_counts = lax.dynamic_index_in_dim(counts_table, batch_index, 0, keepdims=False)
    frame_place = tm_index * FR_DEV + jnp.arange(FR_DEV, dtype=jnp.int32)
    pooled_place = 2 * (tm_index * half_frames + jnp.arange(half_frames, dtype=jnp.int32)) + 1
    low_one = kernel_one.astype(jnp.bfloat16)
    low_two = kernel_two.astype(jnp.bfloat16)
    low_gains = norm_params.astype(jnp.bfloat16)
    shape_out = (CL_MB, FR_DEV, MEL, C2)
    pooled = jnp.zeros((MB * CL_MB, C2), jnp.float32)
    input_grad = jnp.zeros(clip_input.shape, jnp.bfloat16)
    sum_one = jnp.zeros((9 * C1, C2), jnp.float32)
    sum_two = jnp.zeros((9 * C2, C2), jnp.float32)
    norm_sum = jnp.zeros((4, C2), jnp.float32)
    for micro_step in range(MB):
        tm_parts = (
            lax.all_gather(low_one, "tm", axis=2, tiled=True),
            lax.all_gather(low_two, "tm", axis=2, tiled=True),
            lax.all_gather(low_gains, "tm", axis=1, tiled=True),
        )
        full_one, full_two = (
            lax.all_gather(tm_parts[0], "batch", axis=1, tiled=True),
            lax.all_gather(tm_parts[1], "batch", axis=1, tiled=True),
        )
        weights = (full_one, full_two, tm_parts[2])
        gain_table = weights[2].astype(jnp.float32)
        flat_one = weights[0].reshape(9 * C1, C2)
        flat_two = weights[1].reshape(9 * C2, C2)
        slot_ids = local_order[micro_step * CL_MB : (micro_step + 1) * CL_MB]
        clip_counts = local_counts[micro_step * CL_MB : (micro_step + 1) * CL_MB]
        frame_mask = (frame_place[None, :] < clip_counts[:, None]).astype(jnp.float32)[
            :, :, None, None
        ]
        pool_mask = (pooled_place[None, :] < clip_counts[:, None]).astype(jnp.float32)[:, :, None]
        halves = (clip_counts // 2).astype(jnp.float32)[:, None]
        pixels = valid_pixels[micro_step]
        masked_input = jnp.take(clip_input, slot_ids, axis=0) * frame_mask.astype(jnp.bfloat16)
        input_columns = patches(frame_rim(masked_input), FR_DEV, MEL)
        pre_one = jnp.dot(input_columns, flat_one, preferred_element_type=jnp.float32).reshape(
            shape_out
        )
        normed_one, scale_one, shaped_one = norm_forward(
            pre_one, frame_mask, pixels, gain_table[0], gain_table[1]
        )
        hidden = (jax.nn.silu(shaped_one) * frame_mask).astype(jnp.bfloat16)
        hidden_columns = patches(frame_rim(hidden), FR_DEV, MEL)
        pre_two = jnp.dot(hidden_columns, flat_two, preferred_element_type=jnp.float32).reshape(
            shape_out
        )
        normed_two, scale_two, shaped_two = norm_forward(
            pre_two, frame_mask, pixels, gain_table[2], gain_table[3]
        )
        activation = jax.nn.silu(shaped_two) * frame_mask
        summary = jnp.mean(activation.reshape(CL_MB, half_frames, 2, MEL, C2), axis=(2, 3))
        exp_summary = jnp.exp(summary)
        mean_part, exp_part = lax.psum(
            (jnp.sum(summary * pool_mask, axis=1), jnp.sum(exp_summary * pool_mask, axis=1)), "tm"
        )
        pooled = pooled.at[slot_ids].set(mean_part / halves + jnp.log(exp_part / halves))
        cot_rows = jnp.take(cotangent, slot_ids, axis=0)[:, None, :]
        summary_grad = pool_mask * (
            cot_rows / halves[:, :, None] + cot_rows * exp_summary / exp_part[:, None, :]
        )
        activation_grad = jnp.broadcast_to(
            (summary_grad / (2 * MEL))[:, :, None, None, :], (CL_MB, half_frames, 2, MEL, C2)
        ).reshape(shape_out)
        grad_two, gain_two_grad, shift_two_grad = norm_backward(
            activation_grad, frame_mask, shaped_two, normed_two, scale_two, gain_table[2], pixels
        )
        sum_two = sum_two + contract_rows(hidden_columns, grad_two.reshape(-1, C2))
        flip_two = weights[1][::-1].transpose(0, 2, 1).reshape(9 * C2, C2)
        hidden_grad = jnp.dot(
            patches(grad_rim(grad_two), FR_DEV, MEL), flip_two, preferred_element_type=jnp.float32
        ).reshape(shape_out)
        grad_one, gain_one_grad, shift_one_grad = norm_backward(
            hidden_grad, frame_mask, shaped_one, normed_one, scale_one, gain_table[0], pixels
        )
        sum_one = sum_one + contract_rows(input_columns, grad_one.reshape(-1, C2))
        flip_one = weights[0][::-1].transpose(0, 2, 1).reshape(9 * C2, C1)
        rows_grad = jnp.dot(
            patches(grad_rim(grad_one), FR_DEV, MEL), flip_one, preferred_element_type=jnp.float32
        ).reshape(CL_MB, FR_DEV, MEL, C1)
        input_grad = input_grad.at[slot_ids].set((rows_grad * frame_mask).astype(jnp.bfloat16))
        norm_sum = norm_sum + jnp.stack(
            [gain_one_grad, shift_one_grad, gain_two_grad, shift_two_grad]
        )
    batch_parts = (
        lax.psum_scatter(sum_one.reshape(9, C1, C2), "batch", scatter_dimension=1, tiled=True),
        lax.psum_scatter(sum_two.reshape(9, C2, C2), "batch", scatter_dimension=1, tiled=True),
    )
    grad_one_shard, grad_two_shard = (
        lax.psum_scatter(batch_parts[0], "tm", scatter_dimension=2, tiled=True),
        lax.psum_scatter(batch_parts[1], "tm", scatter_dimension=2, tiled=True),
    )
    shard_width = C2 // tm_count
    norm_shard = lax.dynamic_slice_in_dim(norm_sum, tm_index * shard_width, shard_width, 1)
    norm_term = jnp.where(batch_index == 0, jnp.sum(norm_shard * norm_shard), 0.0)
    own_squares = (
        jnp.sum(grad_one_shard * grad_one_shard)
        + jnp.sum(grad_two_shard * grad_two_shard)
        + norm_term
    )
    grad_norm = jnp.sqrt(lax.psum(own_squares, ("tm", "batch")))
    factor = jnp.minimum(1.0, CLIP_NORM / (grad_norm + 1e-06))
    first_update = adam_step(
        kernel_one,
        kernel_one_mean,
        kernel_one_square,
        grad_one_shard,
        factor,
        (9 * C1) ** (-0.5),
        WEIGHT_DECAY,
    )
    second_update = adam_step(
        kernel_two,
        kernel_two_mean,
        kernel_two_square,
        grad_two_shard,
        factor,
        (9 * C2) ** (-0.5),
        WEIGHT_DECAY,
    )
    norm_update = adam_step(norm_params, norm_mean, norm_square, norm_shard, factor, GAIN_RATE, 0.0)
    return (pooled, input_grad, grad_norm) + first_update + second_update + norm_update


AXES = ("z", "x", "y", "core")
BF = jnp.bfloat16
F32 = jnp.float32
ROWS = 512
CLIPS_CORE = 4
PIXELS = ROWS * CLIPS_CORE
HALF = PIXELS // 2
LANES = 128
TAPS = 9
CHUNK = TAPS * 32
ANY = pl.BlockSpec(memory_space=pl.ANY)
VM = pl.BlockSpec(memory_space=pltpu.VMEM)
SM = pl.BlockSpec(memory_space=pltpu.SMEM)
HB = pl.BlockSpec(memory_space=pltpu.HBM)
VMEM_LIMIT = 16 * 1024 * 1024


def shape_of(shape, dtype=BF):
    return jax.ShapeDtypeStruct(shape, dtype)


def call(kernel, out, in_specs, out_specs, scratch=(), limit=VMEM_LIMIT):
    cost = COSTS[kernel] * OPT.get(kernel.__name__, 1)
    return pl.pallas_call(
        kernel,
        out_shape=out,
        in_specs=in_specs,
        out_specs=out_specs,
        scratch_shapes=list(scratch),
        compiler_params=pltpu.CompilerParams(vmem_limit_bytes=limit),
        cost_estimate=pl.CostEstimate(
            flops=int(cost * FLOP_SCALE), bytes_accessed=int(cost * BYTE_SCALE), transcendentals=0
        ),
    )


def swap(value, axis, step=1):
    size = lax.axis_size(axis)
    return lax.ppermute(value, axis, [(i, i ^ step) for i in range(size)])


def start_copies(copies, sems, base=0):
    started = []
    for at, (source, target) in enumerate(copies):
        copy = pltpu.make_async_copy(source, target, sems.at[base + at])
        copy.start()
        started.append(copy)
    return started


def wait_all(copies):
    for copy in copies:
        copy.wait()


def place(*axes):
    found = tuple(lax.axis_index(axis) for axis in axes)
    return found if len(found) > 1 else found[0]


def after(value, *others):
    return lax.optimization_barrier((value,) + others)[0]


def pin(name, value, *others):
    return after(value, *others) if OPT[name] else value


def steps_of():
    return OPT["zorder"]


def order_entry(order, row, column):
    row_of = lax.broadcasted_iota(jnp.int32, order.shape, 0)
    column_of = lax.broadcasted_iota(jnp.int32, order.shape, 1)
    chosen = jnp.where((row_of == row) & (column_of == column), order, 0).astype(F32)
    return jnp.sum(jnp.sum(chosen, axis=1, keepdims=True), axis=0, keepdims=True)


def write_facts(order_ref, counts_ref, facts_ref):
    z, y, core = place("z", "y", "core")
    order, counts = order_ref[...], counts_ref[...]
    column_of = lax.broadcasted_iota(jnp.int32, counts.shape, 1)
    row_of = lax.broadcasted_iota(jnp.int32, (16, LANES), 0)
    facts = jnp.zeros((16, LANES), F32)
    total = jnp.zeros((1, 1), F32)
    for row in range(4):
        for j in range(CL_MB):
            clip = order_entry(order, row, z * CL_MB + j).astype(jnp.int32) + row * 8
            count = jnp.sum(
                jnp.where(column_of == clip, counts, 0).astype(F32), axis=1, keepdims=True
            )
            total = total + count
            target = jnp.where(row % 2 == core, row // 2 * CL_MB + j, -1)
            facts = jnp.where(row_of == target, count, facts)
    facts = jnp.where(row_of == 4, MEL * total, facts)
    for slot in range(MB * CL_MB):
        facts = jnp.where(row_of == 8 + slot, order_entry(order, y * 2 + core, slot), facts)
    facts_ref[...] = facts.astype(jnp.int32)


def count_row(facts_ref, clip):
    return facts_ref[clip : clip + 1, :]


def pixel_row(facts_ref):
    return facts_ref[4:5, :].astype(F32)


def time_shift(rows, step):
    zero = jnp.zeros((MEL, rows.shape[1]), rows.dtype)
    if step == 1:
        return jnp.concatenate([rows[MEL:], zero], axis=0)
    if step == -1:
        return jnp.concatenate([zero, rows[:-MEL]], axis=0)
    return rows


def mel_shift(rows, step):
    if step == 0:
        return rows
    cube = rows.reshape(rows.shape[0] // MEL, MEL, rows.shape[1])
    turned = pltpu.roll(cube, (-step) % MEL, 1)
    bin_at = lax.broadcasted_iota(jnp.int32, cube.shape, 1) + step
    keep = (bin_at >= 0) & (bin_at < MEL)
    return jnp.where(keep, turned, 0.0).reshape(rows.shape)


def valid_rows(facts_ref, clip):
    frame = lax.broadcasted_iota(jnp.int32, (ROWS, LANES), 0) // MEL
    return (frame < count_row(facts_ref, clip)).astype(F32)


def dot_nt(left, right):
    return lax.dot_general(left, right, (((1,), (1,)), ((), ())), preferred_element_type=F32)


def dot_nn(left, right):
    return lax.dot_general(left, right, (((1,), (0,)), ((), ())), preferred_element_type=F32)


def dot_tn(left, right):
    return lax.dot_general(left, right, (((0,), (0,)), ((), ())), preferred_element_type=F32)


def lanes_of(tap):
    return slice(tap * LANES, (tap + 1) * LANES)


def gather_taps(product):
    total = None
    for mel in range(3):
        column = None
        for time in range(3):
            term = time_shift(product[:, lanes_of(3 * time + mel)], time - 1)
            column = term if column is None else column + term
        column = mel_shift(column, mel - 1)
        total = column if total is None else total + column
    return total


def scatter_taps(grad, target, base):
    for mel in range(3):
        moved = mel_shift(grad, 1 - mel)
        for time in range(3):
            target[base : base + ROWS, lanes_of(3 * time + mel)] = time_shift(moved, 1 - time).astype(
                BF
            )


def channel_sums(first, second):
    return (jnp.sum(first, axis=0, keepdims=True), jnp.sum(second, axis=0, keepdims=True))


def pair_sums(own_ref, other_ref):
    return (own_ref[0:1, :] + other_ref[0:1, :], own_ref[1:2, :] + other_ref[1:2, :])


def norm_rows(own_ref, other_ref, pixels):
    total, squares = pair_sums(own_ref, other_ref)
    mean = total / pixels
    return mean, lax.rsqrt(squares / pixels - mean * mean + NORM_EPS)


def put_pair(ref, first, second):
    ref[...] = jnp.zeros(ref.shape, F32)
    ref[0:1, :] = first
    ref[1:2, :] = second


def exchange_matrix(rows, columns, source_of):
    row = lax.broadcasted_iota(jnp.int32, (rows, columns), 0)
    column = lax.broadcasted_iota(jnp.int32, (rows, columns), 1)
    return (row == source_of(column)).astype(BF)


def block_exchange(column):
    return ((column // 32) % 4) * 128 + (column // 128) * 32 + column % 32


def lane_index(rows):
    return lax.broadcasted_iota(jnp.int32, (rows, LANES), 1)


def take_kernel(order_ref, clip_ref, p0, p1, p2, p3):
    z, y, core = place("z", "y", "core")
    order = order_ref[...]
    for step, piece in enumerate((p0, p1, p2, p3)):
        plane = jnp.bitwise_xor(z, step)
        for j in range(CL_MB):
            clip = order_entry(order, y * 2 + core, plane * CL_MB + j)[0, 0].astype(jnp.int32)
            piece[j] = clip_ref[clip]


def prepare_kernel(
    order_ref, counts_ref, one_in, two_in, norm_in, cot_in, one_keep,
    two_keep, send_ref, gain_ref, cot_own, facts_ref, one_ref, two_ref, norm_ref, cot_ref, sems
):
    z, x, y, core = place(*AXES)
    group = y * 2 + core
    loads = start_copies(
        [(one_in, one_ref), (two_in, two_ref), (norm_in, norm_ref), (cot_in, cot_ref)], sems
    )
    write_facts(order_ref, counts_ref, facts_ref)
    wait_all(loads)
    for tap in range(TAPS):
        turned = jnp.swapaxes(one_ref[tap], 0, 1)
        rows = [turned[at * 16 : (at + 1) * 16] for at in range(4)]
        low = jnp.concatenate([rows[0], rows[1]], axis=1).astype(BF)
        high = jnp.concatenate([rows[2], rows[3]], axis=1).astype(BF)
        span = slice(tap * 16, (tap + 1) * 16)
        one_keep[span, :] = jnp.where(y == 0, low, high)
        send_ref[span, :] = jnp.where(y == 0, high, low)
        low, high = two_ref[tap, 0:32, :].astype(BF), two_ref[tap, 32:64, :].astype(BF)
        span = slice(tap * 32, (tap + 1) * 32)
        two_keep[span, :] = jnp.where(y == 0, low, high)
        span = slice(144 + tap * 32, 144 + (tap + 1) * 32)
        send_ref[span, :] = jnp.where(y == 0, high, low)
    wide = jnp.concatenate([norm_ref[...], norm_ref[...]], axis=1)
    wide = jnp.concatenate([wide, jnp.zeros((4, LANES), F32)], axis=0)
    turned = pltpu.roll(wide, (z * 32 - y * 32) % LANES, 1)
    gain_rows = jnp.where(lane_index(8) // 32 == z, turned, 0.0)
    gain_ref[...] = jnp.concatenate([gain_rows, jnp.zeros((8, LANES), F32)], axis=0).astype(BF)

    def cot_rows(y_of):
        rows = []
        for j in range(CL_MB):
            clip = order_entry(order_ref[...], group, z * CL_MB + j)[0, 0].astype(jnp.int32)
            row = cot_ref[pl.ds(clip, 1), :]
            picked = jnp.zeros((1, LANES), F32)
            for block in range(MB):
                moved = pltpu.roll(
                    jnp.broadcast_to(row[:, lanes_of(block)], (8, LANES)),
                    (block * 32 - x * 64 - y_of * 32) % LANES,
                    1,
                )[0:1]
                picked = jnp.where(lane_index(1) // 32 == block, moved, picked)
            rows.append(picked)
        return rows

    own, send = cot_rows(y), cot_rows(1 - y)
    cot_own[...] = jnp.concatenate(own + [jnp.zeros((6, LANES), F32)], axis=0)
    high = [row.astype(BF).astype(F32) for row in send]
    rest = [row - top for row, top in zip(send, high)]
    middle = [row.astype(BF).astype(F32) for row in rest]
    low = [row - top for row, top in zip(rest, middle)]
    packed = jnp.concatenate(high + middle + low + [jnp.zeros((10, LANES), F32)], axis=0)
    send_ref[144 + CHUNK : 160 + CHUNK, :] = packed.astype(BF)


def first_weight_kernel(o0, o1, o2, o3, others, weight_ref, gain_ref):
    z, y, core = place("z", "y", "core")
    gains = jnp.zeros((8, LANES), F32)
    for half in range(2):

        def source_of(column, half=half):
            from_core = jnp.bitwise_xor((column // 64) % 2, core)
            from_y = jnp.bitwise_xor(column // 128, y)
            return from_core * 256 + from_y * 128 + half * 64 + column % 64

        spread = exchange_matrix(512, C1, source_of)
        for step, own in enumerate((o0, o1, o2, o3)):
            z_of = jnp.bitwise_xor(z, step)
            other = others[step * 304 : step * 304 + 288]
            four = jnp.concatenate([own[0:144], own[144:288], other[0:144], other[144:288]], axis=1)
            both = dot_nn(four, spread).astype(BF)
            for tap in range(TAPS):
                weight_ref[tap, z_of, half * 16 : half * 16 + 16] = both[tap * 16 : (tap + 1) * 16]
            if half == 0:
                gains = gains + own[CHUNK : CHUNK + 16].astype(F32)[0:8]
    gain_ref[...] = gains


def first_conv_kernel(
    facts_ref, a0, a1, a23, b0, b1, b23, weight_ref, pre_ref, x_ref, stat_ref, sems
):
    z, x, y, core = place(*AXES)
    copies = []
    for j, pieces in (
        (0, ((a0, 0, x, y), (a1, 0, 1 - x, y), (a23, 0, x, 1 - y), (a23, MB, 1 - x, 1 - y))),
        (1, ((b0, 0, x, y), (b1, 0, x, 1 - y), (b23, 0, 1 - x, y), (b23, MB, 1 - x, 1 - y))),
    ):
        for source, base, x_of, y_of in pieces:
            for step in range(MB):
                frames = (jnp.bitwise_xor(z, step) * 2 + x_of) * 64
                row = pl.multiple_of((y_of * CL_MB + j) * ROWS + frames, 64)
                copies.append((source.at[base + step], x_ref.at[pl.ds(row, 64), :]))
    started = start_copies(copies, sems)
    wait_all(started)
    weight = weight_ref[...].reshape(TAPS * LANES, C1)
    first = jnp.zeros((1, LANES), F32)
    second = jnp.zeros((1, LANES), F32)
    for clip in range(CLIPS_CORE):
        span = slice(clip * ROWS, (clip + 1) * ROWS)
        mask = valid_rows(facts_ref, clip)
        masked = x_ref[span, :] * jnp.concatenate([mask, mask], axis=1).astype(BF)
        x_ref[span, :] = masked
        pre = gather_taps(dot_nt(masked, weight))
        pre_ref[span, :] = pre
        kept = pre * mask
        plus = channel_sums(kept, kept * pre)
        first, second = first + plus[0], second + plus[1]
    put_pair(stat_ref, first, second)


def hidden_kernel(facts_ref, pre_ref, own_ref, other_ref, gain_ref, a_ref, b_ref):
    mean, scale = norm_rows(own_ref, other_ref, pixel_row(facts_ref))
    for clip in range(CLIPS_CORE):
        pre = pre_ref[clip * ROWS : (clip + 1) * ROWS, :]
        shaped = gain_ref[0:1, :] * ((pre - mean) * scale) + gain_ref[1:2, :]
        value = shaped * jax.nn.sigmoid(shaped) * valid_rows(facts_ref, clip)
        target = a_ref if clip < 2 else b_ref
        target[(clip % 2) * ROWS : (clip % 2 + 1) * ROWS, :] = value.astype(BF)


def second_weight_kernel(own_ref, other_ref, weight_ref):
    z, y, core = place("z", "y", "core")
    spread = exchange_matrix(C2, C2, block_exchange)
    for step in range(MB):
        z_of = jnp.bitwise_xor(z, step)
        spans = [slice((step * 2 + turn) * CHUNK, (step * 2 + turn + 1) * CHUNK) for turn in range(2)]
        parts = []
        for y_of in range(2):
            own = jnp.where(y == y_of, own_ref[spans[0]], own_ref[spans[1]])
            other = jnp.where(y == y_of, other_ref[spans[0]], other_ref[spans[1]])
            parts += [jnp.where(core == 0, own, other), jnp.where(core == 0, other, own)]
        both = dot_nn(jnp.concatenate(parts, axis=1), spread).astype(BF)
        for tap in range(TAPS):
            weight_ref[tap, z_of] = both[tap * 32 : (tap + 1) * 32]


def hidden_copies(parts, target):
    x, y = place("x", "y")
    chips = ((x, y), (1 - x, y), (x, 1 - y), (1 - x, 1 - y), (x, y), (x, 1 - y), (1 - x, y), (1 - x, 1 - y))
    copies = []
    for at, (source, (x_of, y_of)) in enumerate(zip(parts, chips)):
        lane = pl.multiple_of((x_of * 2 + y_of) * LANES, LANES)
        copies.append((source, target.at[pl.ds((at // 4) * HALF, HALF), pl.ds(lane, LANES)]))
    return copies


def second_conv_kernel(facts_ref, *rest):
    parts, (weight_ref, pre_ref, stat_ref, hidden, sems) = rest[:8], rest[8:]
    started = start_copies(hidden_copies(parts, hidden), sems)
    weight = weight_ref[...].reshape(TAPS * LANES, C2)
    wait_all(started)
    first = jnp.zeros((1, LANES), F32)
    second = jnp.zeros((1, LANES), F32)
    for clip in range(CLIPS_CORE):
        span = slice(clip * ROWS, (clip + 1) * ROWS)
        pre = gather_taps(dot_nt(hidden[span, :], weight))
        pre_ref[span, :] = pre
        kept = pre * valid_rows(facts_ref, clip)
        plus = channel_sums(kept, kept * pre)
        first, second = first + plus[0], second + plus[1]
    put_pair(stat_ref, first, second)


def near_conv_kernel(a0, a1, a2, b0, b1, b2, weight_ref, pre_ref):
    x, y = place("x", "y")

    def lane(x_of, y_of):
        return pl.ds(pl.multiple_of((x_of * 2 + y_of) * LANES, LANES), LANES)

    weight = jnp.concatenate(
        [
            weight_ref[:, :, :, lane(*chip)].reshape(TAPS * LANES, LANES)
            for chip in ((x, y), (1 - x, y), (x, 1 - y))
        ],
        axis=1,
    )
    for clip in range(CLIPS_CORE):
        parts = (a0, a1, a2) if clip < 2 else (b0, b2, b1)
        rows = slice((clip % 2) * ROWS, (clip % 2 + 1) * ROWS)
        three = jnp.concatenate([part[rows, :] for part in parts], axis=1)
        pre_ref[clip * ROWS : (clip + 1) * ROWS, :] = gather_taps(dot_nt(three, weight))


def far_conv_kernel(facts_ref, a3, b3, weight_ref, near_ref, pre_ref, stat_ref):
    x, y = place("x", "y")
    lane = pl.multiple_of(((1 - x) * 2 + 1 - y) * LANES, LANES)
    weight = weight_ref[:, :, :, pl.ds(lane, LANES)].reshape(TAPS * LANES, LANES)
    first = jnp.zeros((1, LANES), F32)
    second = jnp.zeros((1, LANES), F32)
    for clip in range(CLIPS_CORE):
        span = slice(clip * ROWS, (clip + 1) * ROWS)
        part = a3 if clip < 2 else b3
        rows = slice((clip % 2) * ROWS, (clip % 2 + 1) * ROWS)
        pre = near_ref[span, :] + gather_taps(dot_nt(part[rows, :], weight))
        pre_ref[span, :] = pre
        kept = pre * valid_rows(facts_ref, clip)
        plus = channel_sums(kept, kept * pre)
        first, second = first + plus[0], second + plus[1]
    put_pair(stat_ref, first, second)


def pool_kernel(
    facts_ref, pre_ref, own_ref, other_ref, gain_ref, cot_own, cot_got,
    slope_ref, sum_ref, pooled_ref
):
    y = place("y")
    mean, scale = norm_rows(own_ref, other_ref, pixel_row(facts_ref))
    first = jnp.zeros((1, LANES), F32)
    second = jnp.zeros((1, LANES), F32)
    slots = ROWS // (2 * MEL)
    got = cot_got[144 + CHUNK : 160 + CHUNK, :].astype(F32)
    pooled = []
    for clip in range(CLIPS_CORE):
        span = slice(clip * ROWS, (clip + 1) * ROWS)
        count = count_row(facts_ref, clip)
        j = clip % CL_MB
        told = got[j : j + 1] + got[2 + j : 3 + j] + got[4 + j : 5 + j]
        cot = jnp.where(y == clip // CL_MB, cot_own[j : j + 1, :], told)
        mask = valid_rows(facts_ref, clip)
        normed = (pre_ref[span, :] - mean) * scale
        shaped = gain_ref[2:3, :] * normed + gain_ref[3:4, :]
        gate = jax.nn.sigmoid(shaped)
        active = (shaped * gate * mask).reshape(slots, 2 * MEL, LANES)
        summary = jnp.sum(active, axis=1) / (2 * MEL)
        slot = lax.broadcasted_iota(jnp.int32, (slots, LANES), 0)
        keep = (2 * slot + 1 < count).astype(F32)
        raised = jnp.exp(summary)
        exp_total = jnp.sum(raised * keep, axis=0, keepdims=True)
        halves = (count // 2).astype(F32)
        pooled.append(
            jnp.sum(summary * keep, axis=0, keepdims=True) / halves + jnp.log(exp_total / halves)
        )
        summary_grad = keep * (cot / halves + cot * raised / exp_total) / (2 * MEL)
        spread = jnp.broadcast_to(summary_grad[:, None, :], (slots, 2 * MEL, LANES))
        slope = spread.reshape(ROWS, LANES) * mask * (gate * (1.0 + shaped * (1.0 - gate)))
        slope_ref[span, :] = slope
        plus = channel_sums(slope, slope * normed)
        first, second = first + plus[0], second + plus[1]
    put_pair(sum_ref, first, second)
    high = [row.astype(BF).astype(F32) for row in pooled]
    low = [row - top for row, top in zip(pooled, high)]
    rows = jnp.concatenate(high + low + [jnp.zeros((8, LANES), F32)], axis=0)
    pooled_ref[...] = rows.astype(BF)


def pre_grad(slope, pre, mask, mean, scale, gain, sums, pixels):
    normed = (pre - mean) * scale
    return mask * (scale * gain) * (slope - sums[0] / pixels - normed * (sums[1] / pixels))


def grad_columns_kernel(
    facts_ref, slope_ref, pre_ref, own_ref, other_ref, sum_own, sum_other, gain_ref, weight_ref,
    columns, a_far, b_far
):
    x, y = place("x", "y")
    pixels = pixel_row(facts_ref)
    mean, scale = norm_rows(own_ref, other_ref, pixels)
    sums = pair_sums(sum_own, sum_other)
    lane = pl.multiple_of(((1 - x) * 2 + 1 - y) * LANES, LANES)
    weight = weight_ref[:, :, :, pl.ds(lane, LANES)].reshape(TAPS * LANES, LANES)
    for clip in range(CLIPS_CORE):
        span = slice(clip * ROWS, (clip + 1) * ROWS)
        mask = valid_rows(facts_ref, clip)
        grad = pre_grad(
            slope_ref[span, :], pre_ref[span, :], mask, mean, scale, gain_ref[2:3, :], sums, pixels
        )
        scatter_taps(grad, columns, clip * ROWS)
        rows = slice((clip % 2) * ROWS, (clip % 2 + 1) * ROWS)
        target = a_far if clip < 2 else b_far
        target[rows, :] = dot_nn(columns[span, :], weight).astype(BF)


def hidden_grad_kernel(
    columns, weight_ref, pooled_ref, a_own, a_mid, a_near, b_own, b_mid, b_near, partial
):
    x, y = place("x", "y")
    weight = weight_ref[...].reshape(TAPS * LANES, C2)
    a_near[HALF : HALF + 16, :] = pooled_ref[...]

    def lane(x_of, y_of):
        return pl.ds(pl.multiple_of((x_of * 2 + y_of) * LANES, LANES), LANES)

    for clip in range(CLIPS_CORE):
        span = slice(clip * ROWS, (clip + 1) * ROWS)
        partial[...] = dot_nn(columns[span, :], weight)
        rows = slice((clip % 2) * ROWS, (clip % 2 + 1) * ROWS)
        if clip < 2:
            a_own[rows, :] = partial[:, lane(x, y)]
            a_mid[rows, :] = partial[:, lane(x, 1 - y)]
            a_near[rows, :] = partial[:, lane(1 - x, y)].astype(BF)
        else:
            b_own[rows, :] = partial[:, lane(x, y)]
            b_mid[rows, :] = partial[:, lane(1 - x, y)]
            b_near[rows, :] = partial[:, lane(x, 1 - y)].astype(BF)


def both_grad_kernel(
    facts_ref, slope_ref, pre_ref, own_ref, other_ref, sum_own, sum_other, gain_ref, weight_ref,
    pooled_ref, columns, a_own, a_mid, a_send, b_own, b_mid, b_send, partial
):
    x, y = place("x", "y")
    pixels = pixel_row(facts_ref)
    mean, scale = norm_rows(own_ref, other_ref, pixels)
    sums = pair_sums(sum_own, sum_other)
    weight = weight_ref[...].reshape(TAPS * LANES, C2)
    a_send[2 * HALF : 2 * HALF + 16, :] = pooled_ref[...]

    def lane(x_of, y_of):
        return pl.ds(pl.multiple_of((x_of * 2 + y_of) * LANES, LANES), LANES)

    for clip in range(CLIPS_CORE):
        span = slice(clip * ROWS, (clip + 1) * ROWS)
        mask = valid_rows(facts_ref, clip)
        grad = pre_grad(
            slope_ref[span, :], pre_ref[span, :], mask, mean, scale, gain_ref[2:3, :], sums, pixels
        )
        scatter_taps(grad, columns, clip * ROWS)
        partial[...] = dot_nn(columns[span, :], weight)
        rows = slice((clip % 2) * ROWS, (clip % 2 + 1) * ROWS)
        near_rows = slice(HALF + (clip % 2) * ROWS, HALF + (clip % 2 + 1) * ROWS)
        far = partial[:, lane(1 - x, 1 - y)].astype(BF)
        if clip < 2:
            a_own[rows, :] = partial[:, lane(x, y)]
            a_mid[rows, :] = partial[:, lane(x, 1 - y)]
            a_send[rows, :] = far
            a_send[near_rows, :] = partial[:, lane(1 - x, y)].astype(BF)
        else:
            b_own[rows, :] = partial[:, lane(x, y)]
            b_mid[rows, :] = partial[:, lane(1 - x, y)]
            b_send[rows, :] = far
            b_send[near_rows, :] = partial[:, lane(x, 1 - y)].astype(BF)


def pass_on_kernel(a_mid, a_got, b_mid, b_got, a_next, b_next):
    a_next[...] = (a_mid[...] + a_got[0:HALF].astype(F32)).astype(BF)
    b_next[...] = (b_mid[...] + b_got[0:HALF].astype(F32)).astype(BF)


def second_weight_grad_kernel(*rest):
    parts, columns, keeps, sends = rest[:8], rest[8], rest[9:12], rest[12:15]
    hidden, natural, sems = rest[15:]
    core = place("core")
    started = start_copies(hidden_copies(parts, hidden), sems)
    spread = exchange_matrix(C2, C2, block_exchange)
    wait_all(started)
    for clip in range(CLIPS_CORE):
        span = slice(clip * ROWS, (clip + 1) * ROWS)
        hidden[span, :] = dot_nn(hidden[span, :], spread).astype(BF)
    for tap in range(TAPS):
        natural[...] = dot_tn(columns[:, lanes_of(tap)], hidden[...])
        keep_ref, send_ref = keeps[tap // 3], sends[tap // 3]
        target = slice(tap % 3 * 32, (tap % 3 + 1) * 32)
        for y_of in range(2):
            keep = natural[:, pl.ds(pl.multiple_of((y_of * 2 + core) * LANES, LANES), LANES)]
            send = natural[:, pl.ds(pl.multiple_of((y_of * 2 + 1 - core) * LANES, LANES), LANES)]
            for z_of in range(MB):
                rows = slice(z_of * 32, (z_of + 1) * 32)
                keep_ref[z_of, y_of, target] = keep[rows]
                send_ref[z_of, y_of, target] = send[rows]


def second_core_kernel(k0, k1, k2, g0, g1, g2, own_ref, n1, n2, n3):
    z = place("z")
    for third, (keep_ref, got_ref) in enumerate(((k0, g0), (k1, g1), (k2, g2))):
        rows = slice(third * 96, (third + 1) * 96)
        own_ref[:, rows] = keep_ref[z] + got_ref[z]
        for step, target in ((1, n1), (2, n2), (3, n3)):
            at = jnp.bitwise_xor(z, step)
            target[:, rows] = (keep_ref[at] + got_ref[at]).astype(BF)


def second_sum_kernel(own_ref, g1, g2, g3, keep_ref, send_ref, square_ref):
    y = place("y")
    total = own_ref[...] + g1[...].astype(F32) + g2[...].astype(F32) + g3[...].astype(F32)
    keep_ref[...] = jnp.where(y == 0, total[0], total[1])
    send_ref[...] = jnp.where(y == 0, total[1], total[0])
    square_ref[...] = jnp.sum(total * total, axis=(0, 1), keepdims=False)[None, :] * jnp.ones((8, 1), F32)


def first_slope_kernel(
    facts_ref, a_own, a_near, a_last, b_own, b_near, b_last, pre_ref, own_ref, other_ref,
    gain_ref, slope_ref, sum_ref
):
    mean, scale = norm_rows(own_ref, other_ref, pixel_row(facts_ref))
    first = jnp.zeros((1, LANES), F32)
    second = jnp.zeros((1, LANES), F32)
    for clip in range(CLIPS_CORE):
        span = slice(clip * ROWS, (clip + 1) * ROWS)
        rows = slice((clip % 2) * ROWS, (clip % 2 + 1) * ROWS)
        own, near, last = (a_own, a_near, a_last) if clip < 2 else (b_own, b_near, b_last)
        base = near.shape[0] // HALF * HALF - HALF
        near_rows = slice(base + (clip % 2) * ROWS, base + (clip % 2 + 1) * ROWS)
        outer = own[rows, :] + near[near_rows, :].astype(F32) + last[rows, :].astype(F32)
        normed = (pre_ref[span, :] - mean) * scale
        shaped = gain_ref[0:1, :] * normed + gain_ref[1:2, :]
        gate = jax.nn.sigmoid(shaped)
        slope = outer * valid_rows(facts_ref, clip) * (gate * (1.0 + shaped * (1.0 - gate)))
        slope_ref[span, :] = slope
        plus = channel_sums(slope, slope * normed)
        first, second = first + plus[0], second + plus[1]
    put_pair(sum_ref, first, second)


def first_grads_kernel(
    facts_ref, slope_ref, pre_ref, own_ref, other_ref, sum_own, sum_other, gain_ref, weight_ref, x_ref,
    part_ref, keep_ref, send_ref, columns, turned
):
    core = place("core")
    pixels = pixel_row(facts_ref)
    mean, scale = norm_rows(own_ref, other_ref, pixels)
    sums = pair_sums(sum_own, sum_other)
    weight = weight_ref[...].reshape(TAPS * LANES, C1)

    def source_of(column):
        core_of = jnp.where(column < 128, core, 1 - core)
        return ((column // 64) % 2) * 128 + core_of * 64 + column % 64

    spread = exchange_matrix(C1, C1, source_of)
    for clip in range(CLIPS_CORE):
        span = slice(clip * ROWS, (clip + 1) * ROWS)
        mask = valid_rows(facts_ref, clip)
        grad = pre_grad(
            slope_ref[span, :], pre_ref[span, :], mask, mean, scale, gain_ref[0:1, :], sums, pixels
        )
        scatter_taps(grad, columns, clip * ROWS)
        partial = dot_nn(columns[span, :], weight).astype(BF)
        turned[span, :] = dot_nn(x_ref[span, :], spread).astype(BF)
        for z_of in range(MB):
            for x_of in range(2):
                target = slice(((clip % 2) * MB + z_of) * 64, ((clip % 2) * MB + z_of + 1) * 64)
                rows = slice((z_of * 2 + x_of) * 64, (z_of * 2 + x_of + 1) * 64)
                part_ref[x_of * 2 + clip // 2, target, :] = partial[rows]
    for tap in range(TAPS):
        both = dot_tn(columns[:, lanes_of(tap)], turned[...])
        for z_of in range(MB):
            rows = slice(z_of * 32, (z_of + 1) * 32)
            target = slice(tap * 32, (tap + 1) * 32)
            keep_ref[z_of, target] = both[rows, 0:LANES]
            send_ref[z_of, target] = both[rows, LANES : 2 * LANES]


def first_weight_grad_kernel(
    facts_ref, slope_ref, pre_ref, own_ref, other_ref, sum_own, sum_other, gain_ref, x_ref,
    columns, keep_ref, send_ref, turned
):
    core = place("core")
    pixels = pixel_row(facts_ref)
    mean, scale = norm_rows(own_ref, other_ref, pixels)
    sums = pair_sums(sum_own, sum_other)

    def source_of(column):
        core_of = jnp.where(column < 128, core, 1 - core)
        return ((column // 64) % 2) * 128 + core_of * 64 + column % 64

    spread = exchange_matrix(C1, C1, source_of)
    for clip in range(CLIPS_CORE):
        span = slice(clip * ROWS, (clip + 1) * ROWS)
        mask = valid_rows(facts_ref, clip)
        grad = pre_grad(
            slope_ref[span, :], pre_ref[span, :], mask, mean, scale, gain_ref[0:1, :], sums, pixels
        )
        scatter_taps(grad, columns, clip * ROWS)
        turned[span, :] = dot_nn(x_ref[span, :], spread).astype(BF)
    for tap in range(TAPS):
        both = dot_tn(columns[:, lanes_of(tap)], turned[...])
        for z_of in range(MB):
            rows = slice(z_of * 32, (z_of + 1) * 32)
            target = slice(tap * 32, (tap + 1) * 32)
            keep_ref[z_of, target] = both[rows, 0:LANES]
            send_ref[z_of, target] = both[rows, LANES : 2 * LANES]


def input_grad_kernel(columns, weight_ref, part_ref):
    weight = weight_ref[...].reshape(TAPS * LANES, C1)
    for clip in range(CLIPS_CORE):
        partial = dot_nn(columns[clip * ROWS : (clip + 1) * ROWS, :], weight).astype(BF)
        for z_of in range(MB):
            for x_of in range(2):
                target = slice(((clip % 2) * MB + z_of) * 64, ((clip % 2) * MB + z_of + 1) * 64)
                rows = slice((z_of * 2 + x_of) * 64, (z_of * 2 + x_of + 1) * 64)
                part_ref[x_of * 2 + clip // 2, target, :] = partial[rows]


def first_core_kernel(
    keep_ref, got_ref, one_own, one_other, two_own, two_other, pooled_own, pooled_near, pooled_last,
    own_ref, n0, n1, n2, n3, scratch
):
    z, x, y = place("z", "x", "y")
    own_ref[...] = keep_ref[z] + got_ref[z]
    one, two = pair_sums(one_own, one_other), pair_sums(two_own, two_other)
    sums = jnp.concatenate([one[1], one[0], two[1], two[0]], axis=0)
    high = sums.astype(BF).astype(F32)
    norm_tile = jnp.concatenate([high, sums - high, jnp.zeros((8, LANES), F32)], axis=0).astype(BF)
    last = pooled_last[HALF : HALF + 32, :].astype(F32)
    near = pooled_near[...].astype(F32)
    own = pooled_own[...].astype(F32)
    for rows, x_of, y_of in (
        (own, x, y),
        (near, 1 - x, y),
        (last[0:16], x, 1 - y),
        (last[16:32], 1 - x, 1 - y),
    ):
        for part in range(2):
            for j in range(CL_MB):
                row = jnp.where(
                    y == 0, rows[part * 4 + j : part * 4 + j + 1], rows[part * 4 + 2 + j : part * 4 + 3 + j]
                )
                scratch[pl.ds((x_of * 2 + y_of) * 4 + part * 2 + j, 1), :] = row
    pooled_tile = scratch[...].astype(BF)
    for step, target in ((0, n0), (1, n1), (2, n2), (3, n3)):
        at = jnp.bitwise_xor(z, step)
        target[0:CHUNK, :] = (keep_ref[at] + got_ref[at]).astype(BF)
        target[CHUNK : CHUNK + 16, :] = norm_tile
        target[CHUNK + 16 : CHUNK + 32, :] = pooled_tile


def first_sum_kernel(own_ref, n0, g1, g2, g3, square_two, two_send, told_ref, keep_ref, send_ref, norm_ref):
    z, y, core = place("z", "y", "core")
    total = own_ref[...]
    norm = n0[CHUNK : CHUNK + 16, :].astype(F32)
    for got in (g1, g2, g3):
        total = total + got[0:CHUNK, :].astype(F32)
        norm = norm + got[CHUNK : CHUNK + 16, :].astype(F32)
    norm = norm[0:4] + norm[4:8]
    mine = (lane_index(4) // 32 == z) & (core == 0)
    squares = jnp.sum(total * total, axis=0, keepdims=True) + jnp.sum(
        jnp.where(mine, norm * norm, 0.0), axis=0, keepdims=True
    )
    first_rows = lax.broadcasted_iota(jnp.int32, told_ref.shape, 0) % 8 == 0
    told_ref[...] = jnp.where(first_rows, squares + square_two[0:1, :], 0.0)
    turned = pltpu.roll(total, 64, 1)
    low = jnp.where(y == 0, total, turned)
    high = jnp.where(y == 0, turned, total)
    left = lane_index(144) < 64
    keep_ref[...] = jnp.where(left, low[0:144], pltpu.roll(low[144:288], 64, 1))
    send_ref[0:144, :] = jnp.where(left, high[0:144], pltpu.roll(high[144:288], 64, 1))
    rows = jnp.concatenate([norm, jnp.zeros((4, LANES), F32)], axis=0)
    send_ref[144:152, :] = rows
    send_ref[152 : 152 + CHUNK, :] = two_send[...]
    norm_ref[...] = rows


def load_kernel(*refs):
    half = (len(refs) - 1) // 2
    wait_all(start_copies(list(zip(refs[:half], refs[half : 2 * half])), refs[-1]))


def adam_write(refs, outs, gradient, factor, step_rate, decay_rate, at):
    weight, moment, square = (ref[at] for ref in refs)
    clipped = gradient * factor
    moment_new = BETA_ONE * moment + (1.0 - BETA_ONE) * clipped
    square_new = BETA_TWO * square + (1.0 - BETA_TWO) * clipped * clipped
    corrected = moment_new * (1.0 / (1.0 - BETA_ONE**STEP))
    scaled = jnp.sqrt(square_new * (1.0 / (1.0 - BETA_TWO**STEP))) + ADAM_EPS
    weight_new = weight - step_rate * (corrected / scaled + decay_rate * weight)
    for out, value in zip(outs, (clipped, moment_new, square_new, weight_new, weight_new.astype(BF))):
        out[at] = value


def adam_kernel(told_ref, keep_ref, got_ref, norm_ref, two_keep, *refs):
    z, y = place("z", "y")
    one, two, norm, outs = refs[0:3], refs[3:6], refs[6:9], refs[9:]
    norm_out, one_out, two_out, small_out = outs[0], outs[1:6], outs[6:11], outs[11:16]
    told = jnp.sum(told_ref[...], axis=0, keepdims=True)
    length = jnp.sqrt(jnp.sum(told, axis=1, keepdims=True))
    norm_out[...] = length
    factor = jnp.minimum(1.0, CLIP_NORM / (length + 1e-06))
    keep, got = keep_ref[...], got_ref[0:144, :]
    first, second = jnp.where(y == 0, keep, got), jnp.where(y == 0, got, keep)
    spans = [jnp.concatenate([half[:, 0:64], half[:, 64:128]], axis=0) for half in (first, second)]
    for tap in range(TAPS):
        rows = slice(tap * 32, (tap + 1) * 32)
        gradient = jnp.swapaxes(jnp.concatenate([span[rows] for span in spans], axis=0), 0, 1)
        adam_write(one, one_out, gradient, factor, (9 * C1) ** (-0.5), WEIGHT_DECAY, tap)
        keep, got = two_keep[rows, :], got_ref[152 + tap * 32 : 152 + (tap + 1) * 32, :]
        gradient = jnp.concatenate(
            [jnp.where(y == 0, keep, got), jnp.where(y == 0, got, keep)], axis=0
        )
        adam_write(two, two_out, gradient, factor, (9 * C2) ** (-0.5), WEIGHT_DECAY, tap)
    keep, got = norm_ref[...], got_ref[144:152, :]
    first, second = jnp.where(y == 0, keep, got), jnp.where(y == 0, got, keep)
    low = pltpu.roll(first, (0 - z * 32) % LANES, 1)
    high = pltpu.roll(second, (32 - z * 32) % LANES, 1)
    gradient = jnp.where(lane_index(8) < 32, low, high)[0:4, 0:64]
    adam_write(norm, small_out, gradient, factor, GAIN_RATE, 0.0, slice(None))


def input_sum_kernel(facts_ref, got_ref, f0, f1, f2, f3):
    z, x, y = place("z", "x", "y")
    for j in range(CL_MB):
        count = jnp.where(y == 0, count_row(facts_ref, j), count_row(facts_ref, CL_MB + j))
        count = jnp.concatenate([count, count], axis=1)
        for step, target in enumerate((f0, f1, f2, f3)):
            at = jnp.bitwise_xor(z, step)
            rows = pl.ds(pl.multiple_of((j * MB + at) * 64, 64), 64)
            total = got_ref[0, rows, :].astype(F32)
            for chip in range(1, 4):
                total = total + got_ref[chip, rows, :].astype(F32)
            frame = (at * 2 + x) * 8 + lax.broadcasted_iota(jnp.int32, (64, C1), 0) // MEL
            target[j] = jnp.where(frame < count, total, 0.0).astype(BF)


def finish_kernel(facts_ref, f0, g1, g2, g3, n0, n1, n2, n3, grad_ref, pooled_ref, scratch):
    z = place("z")
    for step, (piece, told) in enumerate(((f0, n0), (g1, n1), (g2, n2), (g3, n3))):
        at = jnp.bitwise_xor(z, step)
        rows = told[CHUNK + 16 : CHUNK + 32, :].astype(F32)
        for j in range(CL_MB):
            clip = facts_ref[pl.ds(8 + at * CL_MB + j, 1), :][0, 0]
            grad_ref[clip] = piece[j]
            for part in range(2):
                chips = [rows[chip * 4 + part * 2 + j : chip * 4 + part * 2 + j + 1] for chip in range(4)]
                scratch[part, pl.ds(clip, 1), :] = jnp.concatenate(chips, axis=1)
    spread = exchange_matrix(C2, C2, block_exchange)
    pooled_ref[...] = dot_nn(scratch[0].astype(BF), spread) + dot_nn(scratch[1].astype(BF), spread)


FLOP_SCALE = OPT['flop']
BYTE_SCALE = 0
COSTS = {
    take_kernel: 1,
    prepare_kernel: 2,
    first_weight_kernel: 1,
    first_conv_kernel: 4,
    hidden_kernel: 0.4,
    second_weight_kernel: 2.8,
    second_conv_kernel: 3.5,
    near_conv_kernel: 3,
    far_conv_kernel: 2,
    pool_kernel: 1.1,
    grad_columns_kernel: 1.7,
    hidden_grad_kernel: 3.4,
    both_grad_kernel: 4,
    second_weight_grad_kernel: 5,
    pass_on_kernel: 0.2,
    second_core_kernel: 0.2,
    second_sum_kernel: 0.2,
    first_slope_kernel: 0.8,
    first_grads_kernel: 4,
    first_weight_grad_kernel: 2,
    input_grad_kernel: 1.5,
    first_core_kernel: 0.2,
    first_sum_kernel: 0.8,
    adam_kernel: 2,
    load_kernel: 1,
    input_sum_kernel: 0.3,
    finish_kernel: 1.5,
}


def spread_plane(a0, b0):
    a1, b1 = swap(a0, "x"), swap(b0, "y")
    a2, b2 = swap(a0, "y"), swap(b0, "x")
    a3, b3 = swap(a1, "y"), swap(b1, "x")
    return (a0, a1, a2, a3, b0, b1, b2, b3)


def fast_body(
    clip_input,
    frame_counts,
    clip_order,
    cotangent,
    kernel_one,
    kernel_one_mean,
    kernel_one_square,
    kernel_two,
    kernel_two_mean,
    kernel_two_square,
    norm_params,
    norm_mean,
    norm_square,
):
    one_view, two_view = kernel_one, jnp.swapaxes(kernel_two, 1, 2)
    p0, p1, p2, p3 = call(
        take_kernel, [shape_of((CL_MB, 64, C1))] * MB, [VM] * 2, [VM] * MB, limit=62 * 1024 * 1024
    )(clip_order, clip_input.reshape(MB * CL_MB, 64, C1))
    one_keep, two_keep, send, gain_rows, cot_own, facts = call(
        prepare_kernel,
        [shape_of((144, LANES)), shape_of((CHUNK, LANES)), shape_of((160 + CHUNK, LANES))]
        + [shape_of((16, LANES)), shape_of((8, LANES), F32), shape_of((16, LANES), jnp.int32)],
        [VM, VM] + [HB] * 4,
        [VM] * 6,
        [
            pltpu.VMEM(one_view.shape, F32),
            pltpu.VMEM(two_view.shape, F32),
            pltpu.VMEM(norm_params.shape, F32),
            pltpu.VMEM(cotangent.shape, F32),
            pltpu.SemaphoreType.DMA((4,)),
        ],
        limit=62 * 1024 * 1024,
    )(
        pin("prep_after_take", clip_order, p0), frame_counts.reshape(1, 32), one_view, two_view, norm_params, cotangent
    )

    def spread_z(values):
        got = {step: swap(values[step], "z", step) for step in steps_of()}
        return [values[0]] + [got[step] for step in (1, 2, 3)]

    arrived = spread_z([p0, p1, p2, p3])
    got = swap(send, "y")
    a0 = jnp.stack([piece[0] for piece in arrived])
    b0 = jnp.stack([piece[1] for piece in arrived])
    one_flat = pin("w1_after_in", jnp.concatenate([one_keep, got[0:144], gain_rows]), a0, b0)
    a1, b1 = swap(a0, "x"), swap(b0, "y")
    if OPT["merge_w"]:
        flat = jnp.concatenate([one_flat, two_keep, got[144 : 144 + CHUNK]])
        one_parts = spread_z([flat] * 4)
    else:
        one_parts = spread_z([one_flat] * 4)
    a01, b01 = jnp.concatenate([a0, a1]), jnp.concatenate([b0, b1])
    if OPT["core_w1_after"] < 2:
        deps = (a1, b1) if OPT["core_w1_after"] else ()
        if OPT["core_w1"] == 4:
            one_others = jnp.concatenate([swap(after(part[0:304], *deps), "core") for part in one_parts])
        else:
            one_others = swap(after(jnp.concatenate([part[0:304] for part in one_parts]), *deps), "core")
        a01, b01 = pin("fwd_after_core_w1", a01, one_others), pin("fwd_after_core_w1", b01, one_others)
        a23, b23 = swap(a01, "y"), swap(b01, "x")
    else:
        a23, b23 = swap(a01, "y"), swap(b01, "x")
        deps = (a23, b23)
        if OPT["core_w1"] == 4:
            one_others = jnp.concatenate([swap(after(part[0:304], *deps), "core") for part in one_parts])
        else:
            one_others = swap(after(jnp.concatenate([part[0:304] for part in one_parts]), *deps), "core")
    inputs = (a0, a1, a23, b0, b1, b23)
    if OPT["merge_w"]:
        two_parts = [part[304:] for part in one_parts]
        one_parts = [part[0:304] for part in one_parts]
    else:
        two_flat = jnp.concatenate([two_keep, got[144 : 144 + CHUNK]])
        two_flat = {
            0: lambda: two_flat,
            1: lambda: after(two_flat, *one_parts[1:]),
            2: lambda: after(two_flat, one_others),
            3: lambda: after(two_flat, a1, b1),
            4: lambda: after(two_flat, a1, b1, one_others),
        }[OPT["w2_after"]]()
        two_parts = spread_z([two_flat] * 4)
    weight_one, gains = call(
        first_weight_kernel,
        [shape_of((TAPS, MB, 32, C1)), shape_of((8, LANES), F32)],
        [VM] * 5,
        [VM] * 2,
    )(*one_parts, one_others)
    pre_one, masked, stat_one = call(
        first_conv_kernel,
        [shape_of((PIXELS, LANES), F32), shape_of((PIXELS, C1)), shape_of((8, LANES), F32)],
        [VM] + [ANY] * 6 + [VM],
        [VM] * 3,
        [pltpu.SemaphoreType.DMA((8 * MB,))],
    )(
        after(facts, *two_parts[1:]) if OPT["w2_before"] == 2 else facts, *inputs, weight_one
    )
    stat_one_other = swap(stat_one, "core")

    ha0, hb0 = call(
        hidden_kernel, [shape_of((HALF, LANES))] * 2, [VM] * 5, [VM] * 2
    )(
        after(facts, *two_parts[1:]) if OPT["w2_before"] == 1 else facts, pre_one, stat_one, stat_one_other, gains
    )
    hidden_parts = spread_plane(ha0, hb0)

    two_all = jnp.concatenate(two_parts)
    if OPT["core_w2_after"] == 1:
        two_all = after(two_all, ha0)
    if OPT["core_w2_after"] == 2:
        two_all = after(two_all, hidden_parts[1], hidden_parts[5])
    two_all_other = swap(two_all, "core")
    two_all = pin("kw2_after", two_all, hidden_parts[1], hidden_parts[5])
    weight_two = call(
        second_weight_kernel, shape_of((TAPS, MB, 32, C2)), [VM, VM], VM
    )(two_all, two_all_other)

    if OPT["split_conv"]:
        ha = hidden_parts
        near_two = call(near_conv_kernel, shape_of((PIXELS, LANES), F32), [VM] * 7, VM)(
            ha[0], ha[1], ha[2], ha[4], ha[5], ha[6], weight_two
        )
        pre_two, stat_two = call(
            far_conv_kernel,
            [shape_of((PIXELS, LANES), F32), shape_of((8, LANES), F32)],
            [VM] * 5,
            [VM] * 2,
        )(facts, ha[3], ha[7], weight_two, near_two)
    else:
        pre_two, stat_two = call(
            second_conv_kernel,
            [shape_of((PIXELS, LANES), F32), shape_of((8, LANES), F32)],
            [VM] + [ANY] * 8 + [VM],
            [VM] * 2,
            [pltpu.VMEM((PIXELS, C2), BF), pltpu.SemaphoreType.DMA((8,))],
        )(facts, *hidden_parts, weight_two)
    stat_two_other = swap(stat_two, "core")
    slope_two, sum_two, pooled_own = call(
        pool_kernel,
        [shape_of((PIXELS, LANES), F32), shape_of((8, LANES), F32), shape_of((16, LANES))],
        [VM] * 7,
        [VM] * 3,
    )(facts, pre_two, stat_two, stat_two_other, gains, cot_own, got)
    sum_two_other = swap(sum_two, "core")
    if OPT["rs"] == "far":
        columns_two, a_far, b_far = call(
            grad_columns_kernel,
            [shape_of((PIXELS, TAPS * LANES))] + [shape_of((HALF, LANES))] * 2,
            [VM] * 9,
            [VM] * 3,
        )(facts, slope_two, pre_two, stat_two, stat_two_other, sum_two, sum_two_other, gains, weight_two)
        a_got, b_got = swap(a_far, "x"), swap(b_far, "y")
        a_own, a_mid, a_near, b_own, b_mid, b_near = call(
            hidden_grad_kernel,
            [shape_of((HALF, LANES), F32)] * 2
            + [shape_of((HALF + 16, LANES))]
            + [shape_of((HALF, LANES), F32)] * 2
            + [shape_of((HALF, LANES))],
            [VM] * 3,
            [VM] * 6,
            [pltpu.VMEM((ROWS, C2), F32)],
        )(columns_two, weight_two, pooled_own)
        a_near, b_near = swap(a_near, "x"), swap(b_near, "y")
        a_pool = a_near[HALF:]
    else:
        columns_two, a_own, a_mid, a_send, b_own, b_mid, b_send = call(
            both_grad_kernel,
            [shape_of((PIXELS, TAPS * LANES))]
            + [shape_of((HALF, LANES), F32)] * 2
            + [shape_of((2 * HALF + 16, LANES))]
            + [shape_of((HALF, LANES), F32)] * 2
            + [shape_of((2 * HALF, LANES))],
            [VM] * 10,
            [VM] * 7,
            [pltpu.VMEM((ROWS, C2), F32)],
        )(
            facts, slope_two, pre_two, stat_two, stat_two_other, sum_two, sum_two_other, gains,
            weight_two, pooled_own,
        )
        a_got = a_near = swap(a_send, "x")
        b_got = b_near = swap(b_send, "y")
        a_pool = a_got[2 * HALF :]
    thirds = call(
        second_weight_grad_kernel,
        [shape_of((MB, 2, 96, LANES), F32)] * 6,
        [ANY] * 8 + [VM],
        [VM] * 6,
        [
            pltpu.VMEM((PIXELS, C2), BF),
            pltpu.VMEM((LANES, C2), F32),
            pltpu.SemaphoreType.DMA((8,)),
        ],
    )(*hidden_parts, columns_two)

    def sum_cores(*deps):
        sends = [after(part, *deps) if deps else part for part in thirds[3:6]]
        return call(
            second_core_kernel,
            [shape_of((2, CHUNK, LANES), F32)] + [shape_of((2, CHUNK, LANES))] * 3,
            [VM] * 6,
            [VM] * 4,
        )(*thirds[0:3], *[swap(part, "core") for part in sends])

    if OPT["core_g2"] == 0:
        two_own, t1, t2, t3 = sum_cores()
        a_got = after(a_got, t1)
    else:
        a_got = pin("pass_after_g2", a_got, thirds[0])
    a_next, b_next = call(pass_on_kernel, [shape_of((HALF, LANES))] * 2, [VM] * 4, [VM] * 2)(
        a_mid,
        pin("pass_after_near", a_got, a_near, b_near),
        b_mid,
        b_got,
    )
    a_next = jnp.concatenate([a_next, pooled_own, a_pool])
    a_last, b_last = swap(a_next, "y"), swap(b_next, "x")
    if OPT["core_g2"] == 1:
        two_own, t1, t2, t3 = sum_cores(a_next)
    slope_one, sum_one = call(
        first_slope_kernel,
        [shape_of((PIXELS, LANES), F32), shape_of((8, LANES), F32)],
        [VM] * 11,
        [VM] * 2,
    )(pin("k5_after", facts, t1), a_own, a_near, a_last, b_own, b_near, b_last, pre_one, stat_one, stat_one_other, gains)
    sum_one_other = swap(sum_one, "core")

    if OPT["split_first"]:
        columns_one, one_part, one_part_send = call(
            first_weight_grad_kernel,
            [shape_of((PIXELS, TAPS * LANES))] + [shape_of((MB, CHUNK, LANES), F32)] * 2,
            [VM] * 9,
            [VM] * 3,
            [pltpu.VMEM((PIXELS, C1), BF)],
        )(facts, slope_one, pre_one, stat_one, stat_one_other, sum_one, sum_one_other, gains, masked)
        input_part = call(input_grad_kernel, shape_of((4, ROWS, C1)), [VM] * 2, VM)(
            pin("ki_after_kg", columns_one, one_part), weight_one
        )
    else:
        input_part, one_part, one_part_send = call(
            first_grads_kernel,
            [shape_of((4, ROWS, C1))] + [shape_of((MB, CHUNK, LANES), F32)] * 2,
            [VM] * 10,
            [VM] * 3,
            [pltpu.VMEM((PIXELS, TAPS * LANES), BF), pltpu.VMEM((PIXELS, C1), BF)],
        )(
            facts, slope_one, pre_one, stat_one, stat_one_other, sum_one, sum_one_other, gains, weight_one,
            masked,
        )

    two_keep_sum, two_send_sum, square_two = call(
        second_sum_kernel,
        [shape_of((CHUNK, LANES), F32)] * 2 + [shape_of((8, LANES), F32)],
        [VM] * 4,
        [VM] * 3,
    )(*spread_z([two_own, t1, t2, t3]))

    one_own, n0, n1, n2, n3 = call(
        first_core_kernel,
        [shape_of((CHUNK, LANES), F32)] + [shape_of((CHUNK + 32, LANES))] * MB,
        [VM] * 9,
        [VM] * 5,
        [pltpu.VMEM((16, LANES), F32)],
    )(
        pin("core1_after_g2", one_part, square_two),
        swap(pin("core_g1_after_g2", one_part_send, square_two), "core"),
        sum_one, sum_one_other, sum_two, sum_two_other,
        pooled_own, a_pool, a_last,
    )
    g1, g2, g3 = spread_z([n0, n1, n2, n3])[1:]
    input_part = pin("a2a_after_g2", pin("a2a_after_core1", input_part, n1), square_two)
    input_got = lax.all_to_all(input_part, ("x", "y"), 0, 0, tiled=True)
    f0, f1, f2, f3 = call(
        input_sum_kernel, [shape_of((CL_MB, 64, C1))] * MB, [VM] * 2, [VM] * 4
    )(facts, input_got)
    if not OPT["f_after_sum"]:
        f1, f2, f3 = spread_z([f0, f1, f2, f3])[1:]
    told, one_keep_sum, one_send_sum, norm_sum = call(
        first_sum_kernel,
        [
            shape_of((32 * 8, LANES), F32),
            shape_of((144, LANES), F32),
            shape_of((152 + CHUNK, LANES), F32),
            shape_of((8, LANES), F32),
        ],
        [VM] * 7,
        [VM] * 4,
    )(
        pin("sum_after_f", one_own, f0), n0, g1, g2, g3, square_two, two_send_sum
    )
    if OPT["f_after_sum"]:
        f1, f2, f3 = spread_z([f0, after(f1, told), after(f2, told), after(f3, told)])[1:]
    told = lax.all_to_all(told, AXES, 0, 0, tiled=True)
    one_got_sum = swap(one_send_sum, "y")
    one_shapes = [shape_of(one_view.shape, F32)] * 4 + [shape_of(one_view.shape)]
    two_shapes = [shape_of(two_view.shape, F32)] * 4 + [shape_of(two_view.shape)]
    norm_shapes = [shape_of(norm_params.shape, F32)] * 4 + [shape_of(norm_params.shape)]
    state = (
        kernel_one,
        kernel_one_mean,
        kernel_one_square,
        two_view,
        jnp.swapaxes(kernel_two_mean, 1, 2),
        jnp.swapaxes(kernel_two_square, 1, 2),
        norm_params,
        norm_mean,
        norm_square,
    )
    if OPT["load"]:
        state = (after(state[0], hidden_parts[1], hidden_parts[5]),) + state[1:]
        state = call(
            load_kernel,
            [shape_of(part.shape, F32) for part in state],
            [HB] * 9,
            [VM] * 9,
            [pltpu.SemaphoreType.DMA((9,))],
        )(*state)
    updates = call(
        adam_kernel,
        [shape_of((1, 1), F32)] + one_shapes + two_shapes + norm_shapes,
        [VM] * 14,
        [VM] * 16,
        limit=OPT['adam_limit'] * 1024 * 1024,
    )(
        pin("told_after_f", told, f1, f2, f3),
        one_keep_sum,
        one_got_sum,
        norm_sum,
        two_keep_sum,
        *state,
    )
    grad_norm = updates[0].reshape(())
    first_update, norm_update = tuple(updates[1:6]), tuple(updates[11:16])
    second_update = tuple(jnp.swapaxes(part, 1, 2) for part in updates[6:11])
    input_grad, pooled = call(
        finish_kernel,
        [shape_of((MB * CL_MB, 64, C1)), shape_of((MB * CL_MB, C2), F32)],
        [VM] * 9,
        [VM] * 2,
        [pltpu.VMEM((2, MB * CL_MB, C2), F32)],
    )(facts, pin("finish_last", f0, updates[0]), f1, f2, f3, n0, g1, g2, g3)
    input_grad = input_grad.reshape(clip_input.shape)
    return (pooled, input_grad, grad_norm) + first_update + second_update + norm_update


def solution(mesh):
    if mesh.shape["tm"] == 2 * MB and mesh.shape["batch"] == 4:
        grid = Mesh(mesh.devices.reshape(MB, 2, 2, 2), AXES)
        tm, batch, chosen = ("z", "x"), ("y", "core"), fast_body
    else:
        grid, tm, batch, chosen = mesh, "tm", "batch", general_body
    kernels = (P(None, batch, tm),) * 3
    norms = (P(None, tm),) * 3
    in_specs = (P(batch, tm, None, None), P(), P(), P(batch, None)) + 2 * kernels + norms
    out_specs = (P(batch, None), P(batch, tm, None, None), P())
    out_specs = out_specs + (P(None, batch, tm),) * 10 + (P(None, tm),) * 5
    return jax.shard_map(chosen, mesh=grid, in_specs=in_specs, out_specs=out_specs, check_vma=False)
```

```python
import functools

import jax
import jax.numpy as jnp
from jax import lax
from jax.experimental import pallas as pl
from jax.experimental.pallas import tpu as pltpu
from jax.sharding import Mesh, PartitionSpec as P

OPT = {'flop': 0, 'zorder': [2, 3, 1], 'merge_w': False, 'w1_after_in': False, 'core_w1': 4, 'core_w1_after': 0, 'fwd_after_core_w1': False, 'w2_after': 1, 'w2_before': 1, 'core_w2_after': 1, 'kw2_after': False, 'rs': 'two', 'pass_after_g2': True, 'pass_after_near': False, 'k5_after': True, 'core1_after_g2': False, 'core_g1_after_g2': True, 'a2a_after_core1': False, 'sum_after_f': False, 'f_after_sum': False, 'told_after_f': False, 'prep_after_take': True, 'finish_last': True, 'split_first': True, 'split_conv': True, 'ki_after_kg': False, 'load': False, 'a2a_after_g2': False, 'core_g2': 0, 'adam_limit': 62, 'pad_p': 32, 'pad_s': 48, 'y2_after': True, 'sum_after_y2': False, 'pooled_after': True, 'zin_after_prep': False, 'pad_in': 16, 'y2_after_y1': True, 'take_limit': 16, 'prep_limit': 62}
C1 = 256
C2 = 512
MEL = 8
FR_DEV = 8
CL_MB = 2
MB = 4
STEP = 10


BETA_ONE = 0.9
BETA_TWO = 0.999
ADAM_EPS = 1e-08
NORM_EPS = 1e-05
WEIGHT_DECAY = 0.01
CLIP_NORM = 0.5
GAIN_RATE = 1.0


def extended(block, sides, width):
    for axis, dim in sides:
        count = lax.axis_size(axis)
        forward = [(i, i + 1) for i in range(count - 1)]
        backward = [(target, source) for source, target in forward]
        low = lax.ppermute(
            lax.slice_in_dim(block, block.shape[dim] - width, None, axis=dim), axis, forward
        )
        high = lax.ppermute(lax.slice_in_dim(block, 0, width, axis=dim), axis, backward)
        block = jnp.concatenate([low, block, high], axis=dim)
    return block


def silu_slope(shaped):
    sigmoid_value = jax.nn.sigmoid(shaped)
    return sigmoid_value * (1.0 + shaped * (1.0 - sigmoid_value))


def pad_mel(field_data):
    return jnp.pad(field_data, ((0, 0), (0, 0), (1, 1), (0, 0)))


def frame_rim(field_data):
    return pad_mel(extended(field_data, (("tm", 1),), 1))


def grad_rim(field_data):
    return pad_mel(extended(field_data, (("tm", 1),), 1))


def patches(padded, frame_count, mel_count):
    pieces = [
        padded[:, step_time : step_time + frame_count, step_mel : step_mel + mel_count, :]
        for step_time in range(3)
        for step_mel in range(3)
    ]
    columns = jnp.concatenate(pieces, axis=-1)
    return columns.reshape(-1, columns.shape[-1])


def norm_forward(pre_norm, frame_mask, pixels, gain_row, shift_row):
    masked = pre_norm * frame_mask
    total_sum, square_sum = lax.psum(
        (jnp.sum(masked, axis=(0, 1, 2)), jnp.sum(masked * pre_norm, axis=(0, 1, 2))),
        ("tm", "batch"),
    )
    channel_mean = total_sum / pixels
    variance = square_sum / pixels - channel_mean * channel_mean
    inv_scale = lax.rsqrt(variance + NORM_EPS)
    normed = (pre_norm - channel_mean) * inv_scale
    return (normed, inv_scale, gain_row * normed + shift_row)


def norm_backward(outer_grad, frame_mask, shaped, normed, inv_scale, gain_row, pixels):
    slope_grad = outer_grad * frame_mask * silu_slope(shaped)
    shift_grad, gain_grad = lax.psum(
        (jnp.sum(slope_grad, axis=(0, 1, 2)), jnp.sum(slope_grad * normed, axis=(0, 1, 2))),
        ("tm", "batch"),
    )
    pre_grad = (
        frame_mask
        * inv_scale
        * gain_row
        * (slope_grad - shift_grad / pixels - normed * gain_grad / pixels)
    )
    return (pre_grad.astype(jnp.bfloat16), gain_grad, shift_grad)


def adam_step(weight, moment, square, summed, factor, step_rate, decay_rate):
    clipped = summed * factor
    moment_new = BETA_ONE * moment + (1.0 - BETA_ONE) * clipped
    square_new = BETA_TWO * square + (1.0 - BETA_TWO) * clipped * clipped
    corrected = moment_new / (1.0 - BETA_ONE**STEP)
    scaled = jnp.sqrt(square_new / (1.0 - BETA_TWO**STEP)) + ADAM_EPS
    weight_new = weight - step_rate * (corrected / scaled + decay_rate * weight)
    return (clipped, moment_new, square_new, weight_new, weight_new.astype(jnp.bfloat16))


def contract_rows(columns, grads):
    return lax.dot_general(
        columns, grads, (((0,), (0,)), ((), ())), preferred_element_type=jnp.float32
    )


def general_body(
    clip_input,
    frame_counts,
    clip_order,
    cotangent,
    kernel_one,
    kernel_one_mean,
    kernel_one_square,
    kernel_two,
    kernel_two_mean,
    kernel_two_square,
    norm_params,
    norm_mean,
    norm_square,
):
    batch_count = lax.axis_size("batch")
    tm_count = lax.axis_size("tm")
    tm_index = lax.axis_index("tm")
    batch_index = lax.axis_index("batch")
    half_frames = FR_DEV // 2
    counts_table = jnp.take_along_axis(frame_counts.reshape(batch_count, -1), clip_order, axis=1)
    valid_pixels = (
        MEL * jnp.sum(counts_table.reshape(batch_count, MB, CL_MB), axis=(0, 2))
    ).astype(jnp.float32)
    local_order = lax.dynamic_index_in_dim(clip_order, batch_index, 0, keepdims=False)
    local_counts = lax.dynamic_index_in_dim(counts_table, batch_index, 0, keepdims=False)
    frame_place = tm_index * FR_DEV + jnp.arange(FR_DEV, dtype=jnp.int32)
    pooled_place = 2 * (tm_index * half_frames + jnp.arange(half_frames, dtype=jnp.int32)) + 1
    low_one = kernel_one.astype(jnp.bfloat16)
    low_two = kernel_two.astype(jnp.bfloat16)
    low_gains = norm_params.astype(jnp.bfloat16)
    shape_out = (CL_MB, FR_DEV, MEL, C2)
    pooled = jnp.zeros((MB * CL_MB, C2), jnp.float32)
    input_grad = jnp.zeros(clip_input.shape, jnp.bfloat16)
    sum_one = jnp.zeros((9 * C1, C2), jnp.float32)
    sum_two = jnp.zeros((9 * C2, C2), jnp.float32)
    norm_sum = jnp.zeros((4, C2), jnp.float32)
    for micro_step in range(MB):
        tm_parts = (
            lax.all_gather(low_one, "tm", axis=2, tiled=True),
            lax.all_gather(low_two, "tm", axis=2, tiled=True),
            lax.all_gather(low_gains, "tm", axis=1, tiled=True),
        )
        full_one, full_two = (
            lax.all_gather(tm_parts[0], "batch", axis=1, tiled=True),
            lax.all_gather(tm_parts[1], "batch", axis=1, tiled=True),
        )
        weights = (full_one, full_two, tm_parts[2])
        gain_table = weights[2].astype(jnp.float32)
        flat_one = weights[0].reshape(9 * C1, C2)
        flat_two = weights[1].reshape(9 * C2, C2)
        slot_ids = local_order[micro_step * CL_MB : (micro_step + 1) * CL_MB]
        clip_counts = local_counts[micro_step * CL_MB : (micro_step + 1) * CL_MB]
        frame_mask = (frame_place[None, :] < clip_counts[:, None]).astype(jnp.float32)[
            :, :, None, None
        ]
        pool_mask = (pooled_place[None, :] < clip_counts[:, None]).astype(jnp.float32)[:, :, None]
        halves = (clip_counts // 2).astype(jnp.float32)[:, None]
        pixels = valid_pixels[micro_step]
        masked_input = jnp.take(clip_input, slot_ids, axis=0) * frame_mask.astype(jnp.bfloat16)
        input_columns = patches(frame_rim(masked_input), FR_DEV, MEL)
        pre_one = jnp.dot(input_columns, flat_one, preferred_element_type=jnp.float32).reshape(
            shape_out
        )
        normed_one, scale_one, shaped_one = norm_forward(
            pre_one, frame_mask, pixels, gain_table[0], gain_table[1]
        )
        hidden = (jax.nn.silu(shaped_one) * frame_mask).astype(jnp.bfloat16)
        hidden_columns = patches(frame_rim(hidden), FR_DEV, MEL)
        pre_two = jnp.dot(hidden_columns, flat_two, preferred_element_type=jnp.float32).reshape(
            shape_out
        )
        normed_two, scale_two, shaped_two = norm_forward(
            pre_two, frame_mask, pixels, gain_table[2], gain_table[3]
        )
        activation = jax.nn.silu(shaped_two) * frame_mask
        summary = jnp.mean(activation.reshape(CL_MB, half_frames, 2, MEL, C2), axis=(2, 3))
        exp_summary = jnp.exp(summary)
        mean_part, exp_part = lax.psum(
            (jnp.sum(summary * pool_mask, axis=1), jnp.sum(exp_summary * pool_mask, axis=1)), "tm"
        )
        pooled = pooled.at[slot_ids].set(mean_part / halves + jnp.log(exp_part / halves))
        cot_rows = jnp.take(cotangent, slot_ids, axis=0)[:, None, :]
        summary_grad = pool_mask * (
            cot_rows / halves[:, :, None] + cot_rows * exp_summary / exp_part[:, None, :]
        )
        activation_grad = jnp.broadcast_to(
            (summary_grad / (2 * MEL))[:, :, None, None, :], (CL_MB, half_frames, 2, MEL, C2)
        ).reshape(shape_out)
        grad_two, gain_two_grad, shift_two_grad = norm_backward(
            activation_grad, frame_mask, shaped_two, normed_two, scale_two, gain_table[2], pixels
        )
        sum_two = sum_two + contract_rows(hidden_columns, grad_two.reshape(-1, C2))
        flip_two = weights[1][::-1].transpose(0, 2, 1).reshape(9 * C2, C2)
        hidden_grad = jnp.dot(
            patches(grad_rim(grad_two), FR_DEV, MEL), flip_two, preferred_element_type=jnp.float32
        ).reshape(shape_out)
        grad_one, gain_one_grad, shift_one_grad = norm_backward(
            hidden_grad, frame_mask, shaped_one, normed_one, scale_one, gain_table[0], pixels
        )
        sum_one = sum_one + contract_rows(input_columns, grad_one.reshape(-1, C2))
        flip_one = weights[0][::-1].transpose(0, 2, 1).reshape(9 * C2, C1)
        rows_grad = jnp.dot(
            patches(grad_rim(grad_one), FR_DEV, MEL), flip_one, preferred_element_type=jnp.float32
        ).reshape(CL_MB, FR_DEV, MEL, C1)
        input_grad = input_grad.at[slot_ids].set((rows_grad * frame_mask).astype(jnp.bfloat16))
        norm_sum = norm_sum + jnp.stack(
            [gain_one_grad, shift_one_grad, gain_two_grad, shift_two_grad]
        )
    batch_parts = (
        lax.psum_scatter(sum_one.reshape(9, C1, C2), "batch", scatter_dimension=1, tiled=True),
        lax.psum_scatter(sum_two.reshape(9, C2, C2), "batch", scatter_dimension=1, tiled=True),
    )
    grad_one_shard, grad_two_shard = (
        lax.psum_scatter(batch_parts[0], "tm", scatter_dimension=2, tiled=True),
        lax.psum_scatter(batch_parts[1], "tm", scatter_dimension=2, tiled=True),
    )
    shard_width = C2 // tm_count
    norm_shard = lax.dynamic_slice_in_dim(norm_sum, tm_index * shard_width, shard_width, 1)
    norm_term = jnp.where(batch_index == 0, jnp.sum(norm_shard * norm_shard), 0.0)
    own_squares = (
        jnp.sum(grad_one_shard * grad_one_shard)
        + jnp.sum(grad_two_shard * grad_two_shard)
        + norm_term
    )
    grad_norm = jnp.sqrt(lax.psum(own_squares, ("tm", "batch")))
    factor = jnp.minimum(1.0, CLIP_NORM / (grad_norm + 1e-06))
    first_update = adam_step(
        kernel_one,
        kernel_one_mean,
        kernel_one_square,
        grad_one_shard,
        factor,
        (9 * C1) ** (-0.5),
        WEIGHT_DECAY,
    )
    second_update = adam_step(
        kernel_two,
        kernel_two_mean,
        kernel_two_square,
        grad_two_shard,
        factor,
        (9 * C2) ** (-0.5),
        WEIGHT_DECAY,
    )
    norm_update = adam_step(norm_params, norm_mean, norm_square, norm_shard, factor, GAIN_RATE, 0.0)
    return (pooled, input_grad, grad_norm) + first_update + second_update + norm_update


AXES = ("z", "x", "y", "core")
BF = jnp.bfloat16
F32 = jnp.float32
ROWS = 512
CLIPS_CORE = 4
PIXELS = ROWS * CLIPS_CORE
HALF = PIXELS // 2
LANES = 128
TAPS = 9
CHUNK = TAPS * 32
ANY = pl.BlockSpec(memory_space=pl.ANY)
VM = pl.BlockSpec(memory_space=pltpu.VMEM)
SM = pl.BlockSpec(memory_space=pltpu.SMEM)
HB = pl.BlockSpec(memory_space=pltpu.HBM)
VMEM_LIMIT = 16 * 1024 * 1024


def shape_of(shape, dtype=BF):
    return jax.ShapeDtypeStruct(shape, dtype)


def call(kernel, out, in_specs, out_specs, scratch=(), limit=VMEM_LIMIT):
    return pl.pallas_call(
        kernel,
        out_shape=out,
        in_specs=in_specs,
        out_specs=out_specs,
        scratch_shapes=list(scratch),
        compiler_params=pltpu.CompilerParams(vmem_limit_bytes=limit),
        cost_estimate=pl.CostEstimate(flops=0, bytes_accessed=0, transcendentals=0),
    )


def join_kernel(*refs):
    base = 0
    for ref in refs[:-1]:
        refs[-1][base : base + ref.shape[0]] = ref[...]
        base += ref.shape[0]


def join(*parts):
    rows = sum(part.shape[0] for part in parts)
    out = shape_of((rows,) + parts[0].shape[1:], parts[0].dtype)
    return call(join_kernel, out, [VM] * len(parts), VM)(*parts)


def swap(value, axis, step=1):
    size = lax.axis_size(axis)
    return lax.ppermute(value, axis, [(i, i ^ step) for i in range(size)])


def start_copies(copies, sems, base=0):
    started = []
    for at, (source, target) in enumerate(copies):
        copy = pltpu.make_async_copy(source, target, sems.at[base + at])
        copy.start()
        started.append(copy)
    return started


def wait_all(copies):
    for copy in copies:
        copy.wait()


def place(*axes):
    found = tuple(lax.axis_index(axis) for axis in axes)
    return found if len(found) > 1 else found[0]


def after(value, *others):
    return lax.optimization_barrier((value,) + others)[0]


def pin(name, value, *others):
    return after(value, *others) if OPT[name] else value


def steps_of():
    return OPT["zorder"]


def order_entry(order, row, column):
    row_of = lax.broadcasted_iota(jnp.int32, order.shape, 0)
    column_of = lax.broadcasted_iota(jnp.int32, order.shape, 1)
    chosen = jnp.where((row_of == row) & (column_of == column), order, 0).astype(F32)
    return jnp.sum(jnp.sum(chosen, axis=1, keepdims=True), axis=0, keepdims=True)


def write_facts(order_ref, counts_ref, facts_ref):
    z, y, core = place("z", "y", "core")
    order, counts = order_ref[...], counts_ref[...]
    column_of = lax.broadcasted_iota(jnp.int32, counts.shape, 1)
    row_of = lax.broadcasted_iota(jnp.int32, (16, LANES), 0)
    facts = jnp.zeros((16, LANES), F32)
    total = jnp.zeros((1, 1), F32)
    for row in range(4):
        for j in range(CL_MB):
            clip = order_entry(order, row, z * CL_MB + j).astype(jnp.int32) + row * 8
            count = jnp.sum(
                jnp.where(column_of == clip, counts, 0).astype(F32), axis=1, keepdims=True
            )
            total = total + count
            target = jnp.where(row % 2 == core, row // 2 * CL_MB + j, -1)
            facts = jnp.where(row_of == target, count, facts)
    facts = jnp.where(row_of == 4, MEL * total, facts)
    for slot in range(MB * CL_MB):
        facts = jnp.where(row_of == 8 + slot, order_entry(order, y * 2 + core, slot), facts)
    facts_ref[...] = facts.astype(jnp.int32)


def count_row(facts_ref, clip):
    return facts_ref[clip : clip + 1, :]


def pixel_row(facts_ref):
    return facts_ref[4:5, :].astype(F32)


def time_shift(rows, step):
    zero = jnp.zeros((MEL, rows.shape[1]), rows.dtype)
    if step == 1:
        return jnp.concatenate([rows[MEL:], zero], axis=0)
    if step == -1:
        return jnp.concatenate([zero, rows[:-MEL]], axis=0)
    return rows


def mel_shift(rows, step):
    if step == 0:
        return rows
    cube = rows.reshape(rows.shape[0] // MEL, MEL, rows.shape[1])
    turned = pltpu.roll(cube, (-step) % MEL, 1)
    bin_at = lax.broadcasted_iota(jnp.int32, cube.shape, 1) + step
    keep = (bin_at >= 0) & (bin_at < MEL)
    return jnp.where(keep, turned, 0.0).reshape(rows.shape)


def valid_rows(facts_ref, clip):
    frame = lax.broadcasted_iota(jnp.int32, (ROWS, LANES), 0) // MEL
    return (frame < count_row(facts_ref, clip)).astype(F32)


def dot_nt(left, right):
    return lax.dot_general(left, right, (((1,), (1,)), ((), ())), preferred_element_type=F32)


def dot_nn(left, right):
    return lax.dot_general(left, right, (((1,), (0,)), ((), ())), preferred_element_type=F32)


def dot_tn(left, right):
    return lax.dot_general(left, right, (((0,), (0,)), ((), ())), preferred_element_type=F32)


def lanes_of(tap):
    return slice(tap * LANES, (tap + 1) * LANES)


def gather_taps(product):
    total = None
    for mel in range(3):
        column = None
        for time in range(3):
            term = time_shift(product[:, lanes_of(3 * time + mel)], time - 1)
            column = term if column is None else column + term
        column = mel_shift(column, mel - 1)
        total = column if total is None else total + column
    return total


def scatter_taps(grad, target, base):
    for mel in range(3):
        moved = mel_shift(grad, 1 - mel)
        for time in range(3):
            target[base : base + ROWS, lanes_of(3 * time + mel)] = time_shift(moved, 1 - time).astype(
                BF
            )


def channel_sums(first, second):
    return (jnp.sum(first, axis=0, keepdims=True), jnp.sum(second, axis=0, keepdims=True))


def pair_sums(own_ref, other_ref):
    return (own_ref[0:1, :] + other_ref[0:1, :], own_ref[1:2, :] + other_ref[1:2, :])


def norm_rows(own_ref, other_ref, pixels):
    total, squares = pair_sums(own_ref, other_ref)
    mean = total / pixels
    return mean, lax.rsqrt(squares / pixels - mean * mean + NORM_EPS)


def put_pair(ref, first, second):
    ref[...] = jnp.zeros(ref.shape, F32)
    ref[0:1, :] = first
    ref[1:2, :] = second


def exchange_matrix(rows, columns, source_of):
    row = lax.broadcasted_iota(jnp.int32, (rows, columns), 0)
    column = lax.broadcasted_iota(jnp.int32, (rows, columns), 1)
    return (row == source_of(column)).astype(BF)


def block_exchange(column):
    return ((column // 32) % 4) * 128 + (column // 128) * 32 + column % 32


def lane_index(rows):
    return lax.broadcasted_iota(jnp.int32, (rows, LANES), 1)


def take_kernel(order_ref, clip_ref, p0, p1, p2, p3):
    z, y, core = place("z", "y", "core")
    order = order_ref[...]
    for step, piece in enumerate((p0, p1, p2, p3)):
        plane = jnp.bitwise_xor(z, step)
        for j in range(CL_MB):
            clip = order_entry(order, y * 2 + core, plane * CL_MB + j)[0, 0].astype(jnp.int32)
            piece[j * 64 : (j + 1) * 64, :] = clip_ref[clip]
        piece[CL_MB * 64 :, :] = jnp.zeros((piece.shape[0] - CL_MB * 64, C1), BF)


def prepare_kernel(
    order_ref, counts_ref, one_in, two_in, norm_in, cot_in, one_keep,
    two_keep, send_ref, gain_ref, cot_own, facts_ref, one_ref, two_ref, norm_ref, cot_ref, sems
):
    z, x, y, core = place(*AXES)
    group = y * 2 + core
    loads = start_copies(
        [(one_in, one_ref), (two_in, two_ref), (norm_in, norm_ref), (cot_in, cot_ref)], sems
    )
    write_facts(order_ref, counts_ref, facts_ref)
    wait_all(loads)
    for tap in range(TAPS):
        turned = jnp.swapaxes(one_ref[tap], 0, 1)
        rows = [turned[at * 16 : (at + 1) * 16] for at in range(4)]
        low = jnp.concatenate([rows[0], rows[1]], axis=1).astype(BF)
        high = jnp.concatenate([rows[2], rows[3]], axis=1).astype(BF)
        span = slice(tap * 16, (tap + 1) * 16)
        one_keep[span, :] = jnp.where(y == 0, low, high)
        send_ref[span, :] = jnp.where(y == 0, high, low)
        low, high = two_ref[tap, 0:32, :].astype(BF), two_ref[tap, 32:64, :].astype(BF)
        span = slice(tap * 32, (tap + 1) * 32)
        two_keep[span, :] = jnp.where(y == 0, low, high)
        span = slice(144 + tap * 32, 144 + (tap + 1) * 32)
        send_ref[span, :] = jnp.where(y == 0, high, low)
    wide = jnp.concatenate([norm_ref[...], norm_ref[...]], axis=1)
    wide = jnp.concatenate([wide, jnp.zeros((4, LANES), F32)], axis=0)
    turned = pltpu.roll(wide, (z * 32 - y * 32) % LANES, 1)
    gain_rows = jnp.where(lane_index(8) // 32 == z, turned, 0.0)
    gain_ref[...] = jnp.concatenate([gain_rows, jnp.zeros((8, LANES), F32)], axis=0).astype(BF)

    def cot_rows(y_of):
        rows = []
        for j in range(CL_MB):
            clip = order_entry(order_ref[...], group, z * CL_MB + j)[0, 0].astype(jnp.int32)
            row = cot_ref[pl.ds(clip, 1), :]
            picked = jnp.zeros((1, LANES), F32)
            for block in range(MB):
                moved = pltpu.roll(
                    jnp.broadcast_to(row[:, lanes_of(block)], (8, LANES)),
                    (block * 32 - x * 64 - y_of * 32) % LANES,
                    1,
                )[0:1]
                picked = jnp.where(lane_index(1) // 32 == block, moved, picked)
            rows.append(picked)
        return rows

    own, send = cot_rows(y), cot_rows(1 - y)
    cot_own[...] = jnp.concatenate(own + [jnp.zeros((6, LANES), F32)], axis=0)
    high = [row.astype(BF).astype(F32) for row in send]
    rest = [row - top for row, top in zip(send, high)]
    middle = [row.astype(BF).astype(F32) for row in rest]
    low = [row - top for row, top in zip(rest, middle)]
    packed = jnp.concatenate(high + middle + low + [jnp.zeros((10, LANES), F32)], axis=0)
    send_ref[144 + CHUNK : 160 + CHUNK, :] = packed.astype(BF)


def first_weight_kernel(o0, o1, o2, o3, others, facts_in, weight_ref, gain_ref, facts_ref):
    facts_ref[...] = facts_in[...]
    z, y, core = place("z", "y", "core")
    gains = jnp.zeros((8, LANES), F32)
    for half in range(2):

        def source_of(column, half=half):
            from_core = jnp.bitwise_xor((column // 64) % 2, core)
            from_y = jnp.bitwise_xor(column // 128, y)
            return from_core * 256 + from_y * 128 + half * 64 + column % 64

        spread = exchange_matrix(512, C1, source_of)
        for step, own in enumerate((o0, o1, o2, o3)):
            z_of = jnp.bitwise_xor(z, step)
            other = others[step * 304 : step * 304 + 288]
            four = jnp.concatenate([own[0:144], own[144:288], other[0:144], other[144:288]], axis=1)
            both = dot_nn(four, spread).astype(BF)
            for tap in range(TAPS):
                weight_ref[tap, z_of, half * 16 : half * 16 + 16] = both[tap * 16 : (tap + 1) * 16]
            if half == 0:
                gains = gains + own[CHUNK : CHUNK + 16].astype(F32)[0:8]
    gain_ref[...] = gains


def first_conv_kernel(
    facts_ref, a0, a1, a23, b0, b1, b23, weight_ref, pre_ref, x_ref, stat_ref
):
    z, x, y = place("z", "x", "y")
    frame = lax.broadcasted_iota(jnp.int32, (64, LANES), 0) // MEL
    for j, pieces in (
        (0, ((a0, 0, x, y), (a1, 0, 1 - x, y), (a23, 0, x, 1 - y), (a23, MB, 1 - x, 1 - y))),
        (1, ((b0, 0, x, y), (b1, 0, x, 1 - y), (b23, 0, 1 - x, y), (b23, MB, 1 - x, 1 - y))),
    ):
        for source, base, x_of, y_of in pieces:
            count = facts_ref[pl.ds(y_of * CL_MB + j, 1), :]
            for step in range(MB):
                frames = (jnp.bitwise_xor(z, step) * 2 + x_of) * 8
                mask = (frame + frames < count).astype(F32).astype(BF)
                row = pl.multiple_of((y_of * CL_MB + j) * ROWS + frames * MEL, 64)
                x_ref[pl.ds(row, 64), :] = source[base + step] * jnp.concatenate([mask, mask], axis=1)
    weight = weight_ref[...].reshape(TAPS * LANES, C1)
    first = jnp.zeros((1, LANES), F32)
    second = jnp.zeros((1, LANES), F32)
    for clip in range(CLIPS_CORE):
        span = slice(clip * ROWS, (clip + 1) * ROWS)
        pre = gather_taps(dot_nt(x_ref[span, :], weight))
        pre_ref[span, :] = pre
        kept = pre * valid_rows(facts_ref, clip)
        plus = channel_sums(kept, kept * pre)
        first, second = first + plus[0], second + plus[1]
    put_pair(stat_ref, first, second)


def stack_kernel(p0, p1, p2, p3, a_ref, b_ref):
    for step, piece in enumerate((p0, p1, p2, p3)):
        a_ref[step] = piece[0:64]
        b_ref[step] = piece[64:128]


def hidden_kernel(facts_ref, pre_ref, own_ref, other_ref, gain_ref, *outs):
    mean, scale = norm_rows(own_ref, other_ref, pixel_row(facts_ref))
    for clip in range(CLIPS_CORE):
        pre = pre_ref[clip * ROWS : (clip + 1) * ROWS, :]
        shaped = gain_ref[0:1, :] * ((pre - mean) * scale) + gain_ref[1:2, :]
        value = shaped * jax.nn.sigmoid(shaped) * valid_rows(facts_ref, clip)
        for target in outs[clip // 2 * 2 : clip // 2 * 2 + 2]:
            target[(clip % 2) * ROWS : (clip % 2 + 1) * ROWS, :] = value.astype(BF)
    for target in outs:
        target[HALF:, :] = jnp.zeros((target.shape[0] - HALF, LANES), BF)


def second_weight_kernel(o0, o1, o2, o3, s0, s1, s2, s3, weight_ref):
    z, y, core = place("z", "y", "core")
    spread = exchange_matrix(C2, C2, block_exchange)
    spans = [slice(0, CHUNK), slice(CHUNK, 2 * CHUNK)]
    for step, (own_ref, other_ref) in enumerate(((o0, s0), (o1, s1), (o2, s2), (o3, s3))):
        z_of = jnp.bitwise_xor(z, step)
        parts = []
        for y_of in range(2):
            own = jnp.where(y == y_of, own_ref[spans[0]], own_ref[spans[1]])
            other = jnp.where(y == y_of, other_ref[spans[0]], other_ref[spans[1]])
            parts += [jnp.where(core == 0, own, other), jnp.where(core == 0, other, own)]
        both = dot_nn(jnp.concatenate(parts, axis=1), spread).astype(BF)
        for tap in range(TAPS):
            weight_ref[tap, z_of] = both[tap * 32 : (tap + 1) * 32]


def hidden_copies(parts, target):
    x, y = place("x", "y")
    chips = ((x, y), (1 - x, y), (x, 1 - y), (1 - x, 1 - y), (x, y), (x, 1 - y), (1 - x, y), (1 - x, 1 - y))
    copies = []
    for at, (source, (x_of, y_of)) in enumerate(zip(parts, chips)):
        lane = pl.multiple_of((x_of * 2 + y_of) * LANES, LANES)
        copies.append(
            (source.at[pl.ds(0, HALF)], target.at[pl.ds((at // 4) * HALF, HALF), pl.ds(lane, LANES)])
        )
    return copies


def second_conv_kernel(facts_ref, *rest):
    parts, (weight_ref, pre_ref, stat_ref, hidden, sems) = rest[:8], rest[8:]
    started = start_copies(hidden_copies(parts, hidden), sems)
    weight = weight_ref[...].reshape(TAPS * LANES, C2)
    wait_all(started)
    first = jnp.zeros((1, LANES), F32)
    second = jnp.zeros((1, LANES), F32)
    for clip in range(CLIPS_CORE):
        span = slice(clip * ROWS, (clip + 1) * ROWS)
        pre = gather_taps(dot_nt(hidden[span, :], weight))
        pre_ref[span, :] = pre
        kept = pre * valid_rows(facts_ref, clip)
        plus = channel_sums(kept, kept * pre)
        first, second = first + plus[0], second + plus[1]
    put_pair(stat_ref, first, second)


def near_conv_kernel(a0, a1, a2, b0, b1, b2, weight_ref, pre_ref):
    x, y = place("x", "y")

    def lane(x_of, y_of):
        return pl.ds(pl.multiple_of((x_of * 2 + y_of) * LANES, LANES), LANES)

    weight = jnp.concatenate(
        [
            weight_ref[:, :, :, lane(*chip)].reshape(TAPS * LANES, LANES)
            for chip in ((x, y), (1 - x, y), (x, 1 - y))
        ],
        axis=1,
    )
    for clip in range(CLIPS_CORE):
        parts = (a0, a1, a2) if clip < 2 else (b0, b2, b1)
        rows = slice((clip % 2) * ROWS, (clip % 2 + 1) * ROWS)
        three = jnp.concatenate([part[rows, :] for part in parts], axis=1)
        pre_ref[clip * ROWS : (clip + 1) * ROWS, :] = gather_taps(dot_nt(three, weight))


def far_conv_kernel(facts_ref, a3, b3, weight_ref, near_ref, pre_ref, stat_ref):
    x, y = place("x", "y")
    lane = pl.multiple_of(((1 - x) * 2 + 1 - y) * LANES, LANES)
    weight = weight_ref[:, :, :, pl.ds(lane, LANES)].reshape(TAPS * LANES, LANES)
    first = jnp.zeros((1, LANES), F32)
    second = jnp.zeros((1, LANES), F32)
    for clip in range(CLIPS_CORE):
        span = slice(clip * ROWS, (clip + 1) * ROWS)
        part = a3 if clip < 2 else b3
        rows = slice((clip % 2) * ROWS, (clip % 2 + 1) * ROWS)
        pre = near_ref[span, :] + gather_taps(dot_nt(part[rows, :], weight))
        pre_ref[span, :] = pre
        kept = pre * valid_rows(facts_ref, clip)
        plus = channel_sums(kept, kept * pre)
        first, second = first + plus[0], second + plus[1]
    put_pair(stat_ref, first, second)


def pool_kernel(
    facts_ref, pre_ref, own_ref, other_ref, gain_ref, cot_own, cot_got,
    slope_ref, sum_ref, pooled_ref
):
    y = place("y")
    mean, scale = norm_rows(own_ref, other_ref, pixel_row(facts_ref))
    first = jnp.zeros((1, LANES), F32)
    second = jnp.zeros((1, LANES), F32)
    slots = ROWS // (2 * MEL)
    got = cot_got[144 + CHUNK : 160 + CHUNK, :].astype(F32)
    pooled = []
    for clip in range(CLIPS_CORE):
        span = slice(clip * ROWS, (clip + 1) * ROWS)
        count = count_row(facts_ref, clip)
        j = clip % CL_MB
        told = got[j : j + 1] + got[2 + j : 3 + j] + got[4 + j : 5 + j]
        cot = jnp.where(y == clip // CL_MB, cot_own[j : j + 1, :], told)
        mask = valid_rows(facts_ref, clip)
        normed = (pre_ref[span, :] - mean) * scale
        shaped = gain_ref[2:3, :] * normed + gain_ref[3:4, :]
        gate = jax.nn.sigmoid(shaped)
        active = (shaped * gate * mask).reshape(slots, 2 * MEL, LANES)
        summary = jnp.sum(active, axis=1) / (2 * MEL)
        slot = lax.broadcasted_iota(jnp.int32, (slots, LANES), 0)
        keep = (2 * slot + 1 < count).astype(F32)
        raised = jnp.exp(summary)
        exp_total = jnp.sum(raised * keep, axis=0, keepdims=True)
        halves = (count // 2).astype(F32)
        pooled.append(
            jnp.sum(summary * keep, axis=0, keepdims=True) / halves + jnp.log(exp_total / halves)
        )
        summary_grad = keep * (cot / halves + cot * raised / exp_total) / (2 * MEL)
        spread = jnp.broadcast_to(summary_grad[:, None, :], (slots, 2 * MEL, LANES))
        slope = spread.reshape(ROWS, LANES) * mask * (gate * (1.0 + shaped * (1.0 - gate)))
        slope_ref[span, :] = slope
        plus = channel_sums(slope, slope * normed)
        first, second = first + plus[0], second + plus[1]
    put_pair(sum_ref, first, second)
    high = [row.astype(BF).astype(F32) for row in pooled]
    low = [row - top for row, top in zip(pooled, high)]
    rows = jnp.concatenate(high + low + [jnp.zeros((8, LANES), F32)], axis=0)
    pooled_ref[...] = rows.astype(BF)


def pre_grad(slope, pre, mask, mean, scale, gain, sums, pixels):
    normed = (pre - mean) * scale
    return mask * (scale * gain) * (slope - sums[0] / pixels - normed * (sums[1] / pixels))


def grad_columns_kernel(
    facts_ref, slope_ref, pre_ref, own_ref, other_ref, sum_own, sum_other, gain_ref, weight_ref,
    columns, a_far, b_far
):
    x, y = place("x", "y")
    pixels = pixel_row(facts_ref)
    mean, scale = norm_rows(own_ref, other_ref, pixels)
    sums = pair_sums(sum_own, sum_other)
    lane = pl.multiple_of(((1 - x) * 2 + 1 - y) * LANES, LANES)
    weight = weight_ref[:, :, :, pl.ds(lane, LANES)].reshape(TAPS * LANES, LANES)
    for clip in range(CLIPS_CORE):
        span = slice(clip * ROWS, (clip + 1) * ROWS)
        mask = valid_rows(facts_ref, clip)
        grad = pre_grad(
            slope_ref[span, :], pre_ref[span, :], mask, mean, scale, gain_ref[2:3, :], sums, pixels
        )
        scatter_taps(grad, columns, clip * ROWS)
        rows = slice((clip % 2) * ROWS, (clip % 2 + 1) * ROWS)
        target = a_far if clip < 2 else b_far
        target[rows, :] = dot_nn(columns[span, :], weight).astype(BF)


def hidden_grad_kernel(
    columns, weight_ref, pooled_ref, a_own, a_mid, a_near, b_own, b_mid, b_near, partial
):
    x, y = place("x", "y")
    weight = weight_ref[...].reshape(TAPS * LANES, C2)
    a_near[HALF : HALF + 16, :] = pooled_ref[...]

    def lane(x_of, y_of):
        return pl.ds(pl.multiple_of((x_of * 2 + y_of) * LANES, LANES), LANES)

    for clip in range(CLIPS_CORE):
        span = slice(clip * ROWS, (clip + 1) * ROWS)
        partial[...] = dot_nn(columns[span, :], weight)
        rows = slice((clip % 2) * ROWS, (clip % 2 + 1) * ROWS)
        if clip < 2:
            a_own[rows, :] = partial[:, lane(x, y)]
            a_mid[rows, :] = partial[:, lane(x, 1 - y)]
            a_near[rows, :] = partial[:, lane(1 - x, y)].astype(BF)
        else:
            b_own[rows, :] = partial[:, lane(x, y)]
            b_mid[rows, :] = partial[:, lane(1 - x, y)]
            b_near[rows, :] = partial[:, lane(x, 1 - y)].astype(BF)


def both_grad_kernel(
    facts_ref, slope_ref, pre_ref, own_ref, other_ref, sum_own, sum_other, gain_ref, weight_ref,
    pooled_ref, columns, a_own, a_mid, a_send, b_own, b_mid, b_send, weight
):
    x, y = place("x", "y")
    pixels = pixel_row(facts_ref)
    mean, scale = norm_rows(own_ref, other_ref, pixels)
    sums = pair_sums(sum_own, sum_other)
    a_send[2 * HALF : 2 * HALF + 16, :] = pooled_ref[...]

    for at, (x_of, y_of) in enumerate(((x, y), (x, 1 - y), (1 - x, y), (1 - x, 1 - y))):
        lane = pl.multiple_of((x_of * 2 + y_of) * LANES, LANES)
        weight[:, lanes_of(at)] = weight_ref[:, :, :, pl.ds(lane, LANES)].reshape(TAPS * LANES, LANES)
    for clip in range(CLIPS_CORE):
        span = slice(clip * ROWS, (clip + 1) * ROWS)
        mask = valid_rows(facts_ref, clip)
        grad = pre_grad(
            slope_ref[span, :], pre_ref[span, :], mask, mean, scale, gain_ref[2:3, :], sums, pixels
        )
        scatter_taps(grad, columns, clip * ROWS)
        partial = dot_nn(columns[span, :], weight[...])
        rows = slice((clip % 2) * ROWS, (clip % 2 + 1) * ROWS)
        near_rows = slice(HALF + (clip % 2) * ROWS, HALF + (clip % 2 + 1) * ROWS)
        far = partial[:, lanes_of(3)].astype(BF)
        if clip < 2:
            a_own[rows, :] = partial[:, lanes_of(0)]
            a_mid[rows, :] = partial[:, lanes_of(1)]
            a_send[rows, :] = far
            a_send[near_rows, :] = partial[:, lanes_of(2)].astype(BF)
        else:
            b_own[rows, :] = partial[:, lanes_of(0)]
            b_mid[rows, :] = partial[:, lanes_of(2)]
            b_send[rows, :] = far
            b_send[near_rows, :] = partial[:, lanes_of(1)].astype(BF)


def pass_on_kernel(a_mid, a_got, b_mid, b_got, pooled_ref, a_next, b_next):
    a_next[HALF : HALF + 16, :] = pooled_ref[...]
    a_next[HALF + 16 : HALF + 32, :] = a_got[2 * HALF : 2 * HALF + 16]
    a_next[0:HALF, :] = (a_mid[...] + a_got[0:HALF].astype(F32)).astype(BF)
    b_next[...] = (b_mid[...] + b_got[0:HALF].astype(F32)).astype(BF)


def second_weight_grad_kernel(*rest):
    parts, columns, keeps, sends = rest[:8], rest[8], rest[9:12], rest[12:15]
    hidden, natural, sems = rest[15:]
    core = place("core")
    started = start_copies(hidden_copies(parts, hidden), sems)
    spread = exchange_matrix(C2, C2, block_exchange)
    wait_all(started)
    for clip in range(CLIPS_CORE):
        span = slice(clip * ROWS, (clip + 1) * ROWS)
        hidden[span, :] = dot_nn(hidden[span, :], spread).astype(BF)
    for tap in range(TAPS):
        natural[...] = dot_tn(columns[:, lanes_of(tap)], hidden[...])
        keep_ref, send_ref = keeps[tap // 3], sends[tap // 3]
        target = slice(tap % 3 * 32, (tap % 3 + 1) * 32)
        for y_of in range(2):
            keep = natural[:, pl.ds(pl.multiple_of((y_of * 2 + core) * LANES, LANES), LANES)]
            send = natural[:, pl.ds(pl.multiple_of((y_of * 2 + 1 - core) * LANES, LANES), LANES)]
            for z_of in range(MB):
                rows = slice(z_of * 32, (z_of + 1) * 32)
                keep_ref[z_of, y_of, target] = keep[rows]
                send_ref[z_of, y_of, target] = send[rows]


def second_core_kernel(k0, k1, k2, g0, g1, g2, own_ref, n1, n2, n3):
    z = place("z")
    for third, (keep_ref, got_ref) in enumerate(((k0, g0), (k1, g1), (k2, g2))):
        rows = slice(third * 96, (third + 1) * 96)
        own_ref[:, rows] = keep_ref[z] + got_ref[z]
        for step, target in ((1, n1), (2, n2), (3, n3)):
            at = jnp.bitwise_xor(z, step)
            target[:, rows] = (keep_ref[at] + got_ref[at]).astype(BF)


def second_sum_kernel(own_ref, g1, g2, g3, keep_ref, send_ref, square_ref):
    y = place("y")
    total = own_ref[...] + g1[...].astype(F32) + g2[...].astype(F32) + g3[...].astype(F32)
    keep_ref[...] = jnp.where(y == 0, total[0], total[1])
    send_ref[...] = jnp.where(y == 0, total[1], total[0]).astype(BF)
    square_ref[...] = jnp.sum(total * total, axis=(0, 1), keepdims=False)[None, :] * jnp.ones((8, 1), F32)


def first_slope_kernel(
    facts_ref, a_own, a_near, a_last, b_own, b_near, b_last, pre_ref, own_ref, other_ref,
    gain_ref, slope_ref, sum_ref
):
    mean, scale = norm_rows(own_ref, other_ref, pixel_row(facts_ref))
    first = jnp.zeros((1, LANES), F32)
    second = jnp.zeros((1, LANES), F32)
    for clip in range(CLIPS_CORE):
        span = slice(clip * ROWS, (clip + 1) * ROWS)
        rows = slice((clip % 2) * ROWS, (clip % 2 + 1) * ROWS)
        own, near, last = (a_own, a_near, a_last) if clip < 2 else (b_own, b_near, b_last)
        base = near.shape[0] // HALF * HALF - HALF
        near_rows = slice(base + (clip % 2) * ROWS, base + (clip % 2 + 1) * ROWS)
        outer = own[rows, :] + near[near_rows, :].astype(F32) + last[rows, :].astype(F32)
        normed = (pre_ref[span, :] - mean) * scale
        shaped = gain_ref[0:1, :] * normed + gain_ref[1:2, :]
        gate = jax.nn.sigmoid(shaped)
        slope = outer * valid_rows(facts_ref, clip) * (gate * (1.0 + shaped * (1.0 - gate)))
        slope_ref[span, :] = slope
        plus = channel_sums(slope, slope * normed)
        first, second = first + plus[0], second + plus[1]
    put_pair(sum_ref, first, second)


def first_grads_kernel(
    facts_ref, slope_ref, pre_ref, own_ref, other_ref, sum_own, sum_other, gain_ref, weight_ref, x_ref,
    part_ref, keep_ref, send_ref, columns, turned
):
    core = place("core")
    pixels = pixel_row(facts_ref)
    mean, scale = norm_rows(own_ref, other_ref, pixels)
    sums = pair_sums(sum_own, sum_other)
    weight = weight_ref[...].reshape(TAPS * LANES, C1)

    def source_of(column):
        core_of = jnp.where(column < 128, core, 1 - core)
        return ((column // 64) % 2) * 128 + core_of * 64 + column % 64

    spread = exchange_matrix(C1, C1, source_of)
    for clip in range(CLIPS_CORE):
        span = slice(clip * ROWS, (clip + 1) * ROWS)
        mask = valid_rows(facts_ref, clip)
        grad = pre_grad(
            slope_ref[span, :], pre_ref[span, :], mask, mean, scale, gain_ref[0:1, :], sums, pixels
        )
        scatter_taps(grad, columns, clip * ROWS)
        partial = dot_nn(columns[span, :], weight).astype(BF)
        turned[span, :] = dot_nn(x_ref[span, :], spread).astype(BF)
        for z_of in range(MB):
            for x_of in range(2):
                target = slice(((clip % 2) * MB + z_of) * 64, ((clip % 2) * MB + z_of + 1) * 64)
                rows = slice((z_of * 2 + x_of) * 64, (z_of * 2 + x_of + 1) * 64)
                part_ref[x_of * 2 + clip // 2, target, :] = partial[rows]
    for tap in range(TAPS):
        both = dot_tn(columns[:, lanes_of(tap)], turned[...])
        for z_of in range(MB):
            rows = slice(z_of * 32, (z_of + 1) * 32)
            target = slice(tap * 32, (tap + 1) * 32)
            keep_ref[z_of, target] = both[rows, 0:LANES]
            send_ref[z_of, target] = both[rows, LANES : 2 * LANES]


def first_weight_grad_kernel(
    facts_ref, slope_ref, pre_ref, own_ref, other_ref, sum_own, sum_other, gain_ref, x_ref,
    columns, keep_ref, send_ref, turned
):
    core = place("core")
    pixels = pixel_row(facts_ref)
    mean, scale = norm_rows(own_ref, other_ref, pixels)
    sums = pair_sums(sum_own, sum_other)

    def source_of(column):
        core_of = jnp.where(column < 128, core, 1 - core)
        return ((column // 64) % 2) * 128 + core_of * 64 + column % 64

    spread = exchange_matrix(C1, C1, source_of)
    for clip in range(CLIPS_CORE):
        span = slice(clip * ROWS, (clip + 1) * ROWS)
        mask = valid_rows(facts_ref, clip)
        grad = pre_grad(
            slope_ref[span, :], pre_ref[span, :], mask, mean, scale, gain_ref[0:1, :], sums, pixels
        )
        scatter_taps(grad, columns, clip * ROWS)
        turned[span, :] = dot_nn(x_ref[span, :], spread).astype(BF)
    for tap in range(TAPS):
        both = dot_tn(columns[:, lanes_of(tap)], turned[...])
        for z_of in range(MB):
            rows = slice(z_of * 32, (z_of + 1) * 32)
            target = slice(tap * 32, (tap + 1) * 32)
            keep_ref[z_of, target] = both[rows, 0:LANES]
            send_ref[z_of, target] = both[rows, LANES : 2 * LANES]


def input_grad_kernel(columns, weight_ref, part_ref):
    weight = weight_ref[...].reshape(TAPS * LANES, C1)
    for clip in range(CLIPS_CORE):
        partial = dot_nn(columns[clip * ROWS : (clip + 1) * ROWS, :], weight).astype(BF)
        for z_of in range(MB):
            for x_of in range(2):
                target = slice(((clip % 2) * MB + z_of) * 64, ((clip % 2) * MB + z_of + 1) * 64)
                rows = slice((z_of * 2 + x_of) * 64, (z_of * 2 + x_of + 1) * 64)
                part_ref[x_of * 2 + clip // 2, target, :] = partial[rows]


def first_core_kernel(
    keep_ref, got_ref, one_own, one_other, two_own, two_other, pooled_own, pooled_near, pooled_last,
    own_ref, n0, n1, n2, n3, scratch
):
    z, x, y = place("z", "x", "y")
    own_ref[...] = keep_ref[z] + got_ref[z]
    one, two = pair_sums(one_own, one_other), pair_sums(two_own, two_other)
    sums = jnp.concatenate([one[1], one[0], two[1], two[0]], axis=0)
    high = sums.astype(BF).astype(F32)
    norm_tile = jnp.concatenate([high, sums - high, jnp.zeros((8, LANES), F32)], axis=0).astype(BF)
    last = pooled_last[HALF : HALF + 32, :].astype(F32)
    near = pooled_near[...].astype(F32)
    own = pooled_own[...].astype(F32)
    for rows, x_of, y_of in (
        (own, x, y),
        (near, 1 - x, y),
        (last[0:16], x, 1 - y),
        (last[16:32], 1 - x, 1 - y),
    ):
        for part in range(2):
            for j in range(CL_MB):
                row = jnp.where(
                    y == 0, rows[part * 4 + j : part * 4 + j + 1], rows[part * 4 + 2 + j : part * 4 + 3 + j]
                )
                scratch[pl.ds((x_of * 2 + y_of) * 4 + part * 2 + j, 1), :] = row
    pooled_tile = scratch[...].astype(BF)
    for step, target in ((0, n0), (1, n1), (2, n2), (3, n3)):
        at = jnp.bitwise_xor(z, step)
        target[0:CHUNK, :] = (keep_ref[at] + got_ref[at]).astype(BF)
        target[CHUNK : CHUNK + 16, :] = norm_tile
        target[CHUNK + 16 : CHUNK + 32, :] = pooled_tile


def first_sum_kernel(own_ref, n0, g1, g2, g3, square_two, told_ref, keep_ref, send_ref, norm_ref):
    z, y, core = place("z", "y", "core")
    total = own_ref[...]
    norm = n0[CHUNK : CHUNK + 16, :].astype(F32)
    for got in (g1, g2, g3):
        total = total + got[0:CHUNK, :].astype(F32)
        norm = norm + got[CHUNK : CHUNK + 16, :].astype(F32)
    norm = norm[0:4] + norm[4:8]
    mine = (lane_index(4) // 32 == z) & (core == 0)
    squares = jnp.sum(total * total, axis=0, keepdims=True) + jnp.sum(
        jnp.where(mine, norm * norm, 0.0), axis=0, keepdims=True
    )
    first_rows = lax.broadcasted_iota(jnp.int32, told_ref.shape, 0) % 8 == 0
    told_ref[...] = jnp.where(first_rows, squares + square_two[0:1, :], 0.0)
    turned = pltpu.roll(total, 64, 1)
    low = jnp.where(y == 0, total, turned)
    high = jnp.where(y == 0, turned, total)
    left = lane_index(144) < 64
    keep_ref[...] = jnp.where(left, low[0:144], pltpu.roll(low[144:288], 64, 1))
    send_ref[0:144, :] = jnp.where(left, high[0:144], pltpu.roll(high[144:288], 64, 1))
    rows = jnp.concatenate([norm, jnp.zeros((4, LANES), F32)], axis=0)
    send_ref[144:152, :] = rows
    norm_ref[...] = rows


def load_kernel(*refs):
    half = (len(refs) - 1) // 2
    wait_all(start_copies(list(zip(refs[:half], refs[half : 2 * half])), refs[-1]))


def adam_write(refs, outs, gradient, factor, step_rate, decay_rate, at):
    weight, moment, square = (ref[at] for ref in refs)
    clipped = gradient * factor
    moment_new = BETA_ONE * moment + (1.0 - BETA_ONE) * clipped
    square_new = BETA_TWO * square + (1.0 - BETA_TWO) * clipped * clipped
    corrected = moment_new * (1.0 / (1.0 - BETA_ONE**STEP))
    scaled = jnp.sqrt(square_new * (1.0 / (1.0 - BETA_TWO**STEP))) + ADAM_EPS
    weight_new = weight - step_rate * (corrected / scaled + decay_rate * weight)
    for out, value in zip(outs, (clipped, moment_new, square_new, weight_new, weight_new.astype(BF))):
        out[at] = value


def adam_kernel(told_ref, keep_ref, got_ref, norm_ref, two_keep, two_got, *refs):
    z, y = place("z", "y")
    one, two, norm, outs = refs[0:3], refs[3:6], refs[6:9], refs[9:]
    norm_out, one_out, two_out, small_out = outs[0], outs[1:6], outs[6:11], outs[11:16]
    told = jnp.sum(told_ref[...], axis=0, keepdims=True)
    length = jnp.sqrt(jnp.sum(told, axis=1, keepdims=True))
    norm_out[...] = length
    factor = jnp.minimum(1.0, CLIP_NORM / (length + 1e-06))
    keep, got = keep_ref[...], got_ref[0:144, :]
    first, second = jnp.where(y == 0, keep, got), jnp.where(y == 0, got, keep)
    spans = [jnp.concatenate([half[:, 0:64], half[:, 64:128]], axis=0) for half in (first, second)]
    for tap in range(TAPS):
        rows = slice(tap * 32, (tap + 1) * 32)
        gradient = jnp.swapaxes(jnp.concatenate([span[rows] for span in spans], axis=0), 0, 1)
        adam_write(one, one_out, gradient, factor, (9 * C1) ** (-0.5), WEIGHT_DECAY, tap)
        keep, got = two_keep[rows, :], two_got[rows, :].astype(F32)
        gradient = jnp.concatenate(
            [jnp.where(y == 0, keep, got), jnp.where(y == 0, got, keep)], axis=0
        )
        adam_write(two, two_out, gradient, factor, (9 * C2) ** (-0.5), WEIGHT_DECAY, tap)
    keep, got = norm_ref[...], got_ref[144:152, :]
    first, second = jnp.where(y == 0, keep, got), jnp.where(y == 0, got, keep)
    low = pltpu.roll(first, (0 - z * 32) % LANES, 1)
    high = pltpu.roll(second, (32 - z * 32) % LANES, 1)
    gradient = jnp.where(lane_index(8) < 32, low, high)[0:4, 0:64]
    adam_write(norm, small_out, gradient, factor, GAIN_RATE, 0.0, slice(None))


def input_sum_kernel(facts_ref, got_ref, f0, f1, f2, f3):
    z, x, y = place("z", "x", "y")
    for j in range(CL_MB):
        count = jnp.where(y == 0, count_row(facts_ref, j), count_row(facts_ref, CL_MB + j))
        count = jnp.concatenate([count, count], axis=1)
        for step, target in enumerate((f0, f1, f2, f3)):
            at = jnp.bitwise_xor(z, step)
            rows = pl.ds(pl.multiple_of((j * MB + at) * 64, 64), 64)
            total = got_ref[0, rows, :].astype(F32)
            for chip in range(1, 4):
                total = total + got_ref[chip, rows, :].astype(F32)
            frame = (at * 2 + x) * 8 + lax.broadcasted_iota(jnp.int32, (64, C1), 0) // MEL
            target[j] = jnp.where(frame < count, total, 0.0).astype(BF)


def finish_kernel(facts_ref, f0, g1, g2, g3, grad_ref):
    z = place("z")
    for step, piece in enumerate((f0, g1, g2, g3)):
        at = jnp.bitwise_xor(z, step)
        for j in range(CL_MB):
            clip = facts_ref[pl.ds(8 + at * CL_MB + j, 1), :][0, 0]
            grad_ref[clip] = piece[j]


def pooled_kernel(facts_ref, n0, n1, n2, n3, pooled_ref, scratch):
    z = place("z")
    for step, told in enumerate((n0, n1, n2, n3)):
        at = jnp.bitwise_xor(z, step)
        rows = told[CHUNK + 16 : CHUNK + 32, :].astype(F32)
        for j in range(CL_MB):
            clip = facts_ref[pl.ds(8 + at * CL_MB + j, 1), :][0, 0]
            for part in range(2):
                chips = [rows[chip * 4 + part * 2 + j : chip * 4 + part * 2 + j + 1] for chip in range(4)]
                scratch[part, pl.ds(clip, 1), :] = jnp.concatenate(chips, axis=1)
    spread = exchange_matrix(C2, C2, block_exchange)
    pooled_ref[...] = dot_nn(scratch[0].astype(BF), spread) + dot_nn(scratch[1].astype(BF), spread)


def spread_plane(a0, b0):
    a1, b1 = swap(a0, "x"), swap(b0, "y")
    a2, b2 = swap(a0, "y"), swap(b0, "x")
    a3, b3 = swap(a1, "y"), swap(b1, "x")
    return (a0, a1, a2, a3, b0, b1, b2, b3)


def fast_body(
    clip_input,
    frame_counts,
    clip_order,
    cotangent,
    kernel_one,
    kernel_one_mean,
    kernel_one_square,
    kernel_two,
    kernel_two_mean,
    kernel_two_square,
    norm_params,
    norm_mean,
    norm_square,
):
    one_view, two_view = kernel_one, jnp.swapaxes(kernel_two, 1, 2)
    p0, p1, p2, p3 = call(
        take_kernel, [shape_of((CL_MB * 64 + OPT['pad_in'], C1))] * MB, [VM] * 2, [VM] * MB, limit=OPT['take_limit'] * 1024 * 1024
    )(clip_order, clip_input.reshape(MB * CL_MB, 64, C1))
    one_keep, two_keep, send, gain_rows, cot_own, facts = call(
        prepare_kernel,
        [shape_of((144, LANES)), shape_of((CHUNK, LANES)), shape_of((160 + CHUNK, LANES))]
        + [shape_of((16, LANES)), shape_of((8, LANES), F32), shape_of((16, LANES), jnp.int32)],
        [VM, VM] + [HB] * 4,
        [VM] * 6,
        [
            pltpu.VMEM(one_view.shape, F32),
            pltpu.VMEM(two_view.shape, F32),
            pltpu.VMEM(norm_params.shape, F32),
            pltpu.VMEM(cotangent.shape, F32),
            pltpu.SemaphoreType.DMA((4,)),
        ],
        limit=OPT['prep_limit'] * 1024 * 1024,
    )(
        pin("prep_after_take", clip_order, p0), frame_counts.reshape(1, 32), one_view, two_view, norm_params, cotangent
    )

    def spread_z(values):
        got = {step: swap(values[step], "z", step) for step in steps_of()}
        return [values[0]] + [got[step] for step in (1, 2, 3)]

    p1, p2, p3 = (pin("zin_after_prep", part, send) for part in (p1, p2, p3))
    arrived = spread_z([p0, p1, p2, p3])
    got = swap(send, "y")
    a0, b0 = call(stack_kernel, [shape_of((MB, 64, C1))] * 2, [VM] * 4, [VM] * 2)(*arrived)
    one_flat = pin("w1_after_in", join(one_keep, got[0:144], gain_rows), a0, b0)
    a1, b1 = swap(a0, "x"), swap(b0, "y")
    one_parts = spread_z([one_flat] * 4)
    a01, b01 = join(a0, a1), join(b0, b1)
    deps = (a1, b1) if OPT["core_w1_after"] == 1 else ()
    if OPT["core_w1"] == 2:
        halves = [join(*one_parts[0:2]), join(*one_parts[2:4])]
        one_others = join(*[swap(after(part, *deps), "core") for part in halves])
    elif OPT["core_w1"] == 4:
        one_others = join(*[swap(after(part, *deps), "core") for part in one_parts])
    else:
        one_others = swap(after(join(*one_parts), *deps), "core")
    a23, b23 = swap(a01, "y"), swap(b01, "x")
    inputs = (a0, a1, a23, b0, b1, b23)
    two_flat = join(two_keep, got[144 : 144 + CHUNK])
    two_flat = {
        0: lambda: two_flat,
        1: lambda: after(two_flat, *one_parts[1:]),
        2: lambda: after(two_flat, one_others),
        3: lambda: after(two_flat, a1, b1),
        4: lambda: after(two_flat, a1, b1, one_others),
    }[OPT["w2_after"]]()
    two_parts = spread_z([two_flat] * 4)
    weight_one, gains, facts = call(
        first_weight_kernel,
        [shape_of((TAPS, MB, 32, C1)), shape_of((8, LANES), F32), shape_of((16, LANES), jnp.int32)],
        [VM] * 6,
        [VM] * 3,
    )(*one_parts, one_others, facts)
    pre_one, masked, stat_one = call(
        first_conv_kernel,
        [shape_of((PIXELS, LANES), F32), shape_of((PIXELS, C1)), shape_of((8, LANES), F32)],
        [VM] * 8,
        [VM] * 3,
    )(
        after(facts, *two_parts[1:]) if OPT["w2_before"] == 2 else facts, *inputs, weight_one
    )
    stat_one_other = swap(stat_one, "core")

    ha_on, ha0, hb_on, hb0 = call(
        hidden_kernel,
        [shape_of((HALF + pad, LANES)) for pad in (OPT['pad_p'], OPT['pad_s'])] * 2,
        [VM] * 5,
        [VM] * 4,
    )(
        after(facts, *two_parts[1:]) if OPT["w2_before"] == 1 else facts, pre_one, stat_one, stat_one_other, gains
    )
    ha1, hb1 = swap(ha_on, "x"), swap(hb_on, "y")
    ha2, hb2 = swap(ha0, "y"), swap(hb0, "x")
    ha3, hb3 = swap(ha1, "y"), swap(hb1, "x")
    hidden_parts = (ha0, ha1, ha2, ha3, hb0, hb1, hb2, hb3)

    deps = {0: (), 1: (ha0,), 2: (ha1, hb1)}[OPT["core_w2_after"]]
    two_others = [swap(after(part, *deps), "core") for part in two_parts]
    weight_two = call(second_weight_kernel, shape_of((TAPS, MB, 32, C2)), [VM] * 8, VM)(
        *two_parts, *two_others
    )

    if OPT["split_conv"]:
        ha = hidden_parts
        near_two = call(near_conv_kernel, shape_of((PIXELS, LANES), F32), [VM] * 7, VM)(
            ha[0], ha[1], ha[2], ha[4], ha[5], ha[6], weight_two
        )
        pre_two, stat_two = call(
            far_conv_kernel,
            [shape_of((PIXELS, LANES), F32), shape_of((8, LANES), F32)],
            [VM] * 5,
            [VM] * 2,
        )(facts, ha[3], ha[7], weight_two, near_two)
    else:
        pre_two, stat_two = call(
            second_conv_kernel,
            [shape_of((PIXELS, LANES), F32), shape_of((8, LANES), F32)],
            [VM] + [ANY] * 8 + [VM],
            [VM] * 2,
            [pltpu.VMEM((PIXELS, C2), BF), pltpu.SemaphoreType.DMA((8,))],
        )(facts, *hidden_parts, weight_two)
    stat_two_other = swap(stat_two, "core")
    slope_two, sum_two, pooled_own = call(
        pool_kernel,
        [shape_of((PIXELS, LANES), F32), shape_of((8, LANES), F32), shape_of((16, LANES))],
        [VM] * 7,
        [VM] * 3,
    )(facts, pre_two, stat_two, stat_two_other, gains, cot_own, got)
    sum_two_other = swap(sum_two, "core")
    if OPT["rs"] == "far":
        columns_two, a_far, b_far = call(
            grad_columns_kernel,
            [shape_of((PIXELS, TAPS * LANES))] + [shape_of((HALF, LANES))] * 2,
            [VM] * 9,
            [VM] * 3,
        )(facts, slope_two, pre_two, stat_two, stat_two_other, sum_two, sum_two_other, gains, weight_two)
        a_got, b_got = swap(a_far, "x"), swap(b_far, "y")
        a_own, a_mid, a_near, b_own, b_mid, b_near = call(
            hidden_grad_kernel,
            [shape_of((HALF, LANES), F32)] * 2
            + [shape_of((HALF + 16, LANES))]
            + [shape_of((HALF, LANES), F32)] * 2
            + [shape_of((HALF, LANES))],
            [VM] * 3,
            [VM] * 6,
            [pltpu.VMEM((ROWS, C2), F32)],
        )(columns_two, weight_two, pooled_own)
        a_near, b_near = swap(a_near, "x"), swap(b_near, "y")
        a_pool = a_near[HALF:]
    else:
        columns_two, a_own, a_mid, a_send, b_own, b_mid, b_send = call(
            both_grad_kernel,
            [shape_of((PIXELS, TAPS * LANES))]
            + [shape_of((HALF, LANES), F32)] * 2
            + [shape_of((2 * HALF + 16, LANES))]
            + [shape_of((HALF, LANES), F32)] * 2
            + [shape_of((2 * HALF, LANES))],
            [VM] * 10,
            [VM] * 7,
            [pltpu.VMEM((TAPS * LANES, C2), BF)],
        )(
            facts, slope_two, pre_two, stat_two, stat_two_other, sum_two, sum_two_other, gains,
            weight_two, pooled_own,
        )
        a_got = a_near = swap(a_send, "x")
        b_got = b_near = swap(b_send, "y")
        a_pool = a_got[2 * HALF :]
    thirds = call(
        second_weight_grad_kernel,
        [shape_of((MB, 2, 96, LANES), F32)] * 6,
        [ANY] * 8 + [VM],
        [VM] * 6,
        [
            pltpu.VMEM((PIXELS, C2), BF),
            pltpu.VMEM((LANES, C2), F32),
            pltpu.SemaphoreType.DMA((8,)),
        ],
    )(*hidden_parts, columns_two)

    def sum_cores(*deps):
        sends = [after(part, *deps) if deps else part for part in thirds[3:6]]
        return call(
            second_core_kernel,
            [shape_of((2, CHUNK, LANES), F32)] + [shape_of((2, CHUNK, LANES))] * 3,
            [VM] * 6,
            [VM] * 4,
        )(*thirds[0:3], *[swap(part, "core") for part in sends])

    if OPT["core_g2"] == 0:
        two_own, t1, t2, t3 = sum_cores()
        a_got = after(a_got, t1)
    else:
        a_got = pin("pass_after_g2", a_got, thirds[0])
    a_next, b_next = call(
        pass_on_kernel, [shape_of((HALF + 32, LANES)), shape_of((HALF, LANES))], [VM] * 5, [VM] * 2
    )(a_mid, a_got, b_mid, b_got, pooled_own)
    a_last, b_last = swap(a_next, "y"), swap(b_next, "x")
    if OPT["core_g2"] == 1:
        two_own, t1, t2, t3 = sum_cores(a_next)
    slope_one, sum_one = call(
        first_slope_kernel,
        [shape_of((PIXELS, LANES), F32), shape_of((8, LANES), F32)],
        [VM] * 11,
        [VM] * 2,
    )(pin("k5_after", facts, t1), a_own, a_near, a_last, b_own, b_near, b_last, pre_one, stat_one, stat_one_other, gains)
    sum_one_other = swap(sum_one, "core")

    if OPT["split_first"]:
        columns_one, one_part, one_part_send = call(
            first_weight_grad_kernel,
            [shape_of((PIXELS, TAPS * LANES))] + [shape_of((MB, CHUNK, LANES), F32)] * 2,
            [VM] * 9,
            [VM] * 3,
            [pltpu.VMEM((PIXELS, C1), BF)],
        )(facts, slope_one, pre_one, stat_one, stat_one_other, sum_one, sum_one_other, gains, masked)
        input_part = call(input_grad_kernel, shape_of((4, ROWS, C1)), [VM] * 2, VM)(
            pin("ki_after_kg", columns_one, one_part), weight_one
        )
    else:
        input_part, one_part, one_part_send = call(
            first_grads_kernel,
            [shape_of((4, ROWS, C1))] + [shape_of((MB, CHUNK, LANES), F32)] * 2,
            [VM] * 10,
            [VM] * 3,
            [pltpu.VMEM((PIXELS, TAPS * LANES), BF), pltpu.VMEM((PIXELS, C1), BF)],
        )(
            facts, slope_one, pre_one, stat_one, stat_one_other, sum_one, sum_one_other, gains, weight_one,
            masked,
        )

    two_keep_sum, two_send_sum, square_two = call(
        second_sum_kernel,
        [shape_of((CHUNK, LANES), F32), shape_of((CHUNK, LANES)), shape_of((8, LANES), F32)],
        [VM] * 4,
        [VM] * 3,
    )(*spread_z([two_own, t1, t2, t3]))

    one_own, n0, n1, n2, n3 = call(
        first_core_kernel,
        [shape_of((CHUNK, LANES), F32)] + [shape_of((CHUNK + 32, LANES))] * MB,
        [VM] * 9,
        [VM] * 5,
        [pltpu.VMEM((16, LANES), F32)],
    )(
        pin("core1_after_g2", one_part, square_two),
        swap(pin("core_g1_after_g2", one_part_send, square_two), "core"),
        sum_one, sum_one_other, sum_two, sum_two_other,
        pooled_own, a_pool, a_last,
    )
    g1, g2, g3 = spread_z([n0, n1, n2, n3])[1:]
    input_part = pin("a2a_after_g2", pin("a2a_after_core1", input_part, n1), square_two)
    input_got = lax.all_to_all(input_part, ("x", "y"), 0, 0, tiled=True)
    f0, f1, f2, f3 = call(
        input_sum_kernel, [shape_of((CL_MB, 64, C1))] * MB, [VM] * 2, [VM] * 4
    )(facts, input_got)
    two_got_sum = swap(pin("y2_after", two_send_sum, n1), "y")
    if not OPT["f_after_sum"]:
        f1, f2, f3 = spread_z([f0, f1, f2, f3])[1:]
    told, one_keep_sum, one_send_sum, norm_sum = call(
        first_sum_kernel,
        [
            shape_of((32 * 8, LANES), F32),
            shape_of((144, LANES), F32),
            shape_of((152, LANES), F32),
            shape_of((8, LANES), F32),
        ],
        [VM] * 6,
        [VM] * 4,
    )(
        pin("sum_after_y2", pin("sum_after_f", one_own, f0), two_got_sum), n0, g1, g2, g3, square_two
    )
    if OPT["f_after_sum"]:
        f1, f2, f3 = spread_z([f0, after(f1, told), after(f2, told), after(f3, told)])[1:]
    told_sent = told
    told = lax.all_to_all(told, AXES, 0, 0, tiled=True)
    one_got_sum = swap(one_send_sum, "y")
    one_shapes = [shape_of(one_view.shape, F32)] * 4 + [shape_of(one_view.shape)]
    two_shapes = [shape_of(two_view.shape, F32)] * 4 + [shape_of(two_view.shape)]
    norm_shapes = [shape_of(norm_params.shape, F32)] * 4 + [shape_of(norm_params.shape)]
    state = (
        kernel_one,
        kernel_one_mean,
        kernel_one_square,
        two_view,
        jnp.swapaxes(kernel_two_mean, 1, 2),
        jnp.swapaxes(kernel_two_square, 1, 2),
        norm_params,
        norm_mean,
        norm_square,
    )
    if OPT["load"]:
        state = (after(state[0], hidden_parts[1], hidden_parts[5]),) + state[1:]
        state = call(
            load_kernel,
            [shape_of(part.shape, F32) for part in state],
            [HB] * 9,
            [VM] * 9,
            [pltpu.SemaphoreType.DMA((9,))],
        )(*state)
    updates = call(
        adam_kernel,
        [shape_of((1, 1), F32)] + one_shapes + two_shapes + norm_shapes,
        [VM] * 15,
        [VM] * 16,
        limit=OPT['adam_limit'] * 1024 * 1024,
    )(
        pin("told_after_f", told, f1, f2, f3),
        one_keep_sum,
        one_got_sum,
        norm_sum,
        two_keep_sum,
        two_got_sum,
        *state,
    )
    grad_norm = updates[0].reshape(())
    first_update, norm_update = tuple(updates[1:6]), tuple(updates[11:16])
    second_update = tuple(jnp.swapaxes(part, 1, 2) for part in updates[6:11])
    pooled = call(
        pooled_kernel,
        shape_of((MB * CL_MB, C2), F32),
        [VM] * 5,
        VM,
        [pltpu.VMEM((2, MB * CL_MB, C2), F32)],
    )(facts, pin("pooled_after", n0, told_sent), g1, g2, g3)
    input_grad = call(finish_kernel, shape_of((MB * CL_MB, 64, C1)), [VM] * 5, VM)(
        facts, pin("finish_last", f0, updates[0]), f1, f2, f3
    )
    input_grad = input_grad.reshape(clip_input.shape)
    return (pooled, input_grad, grad_norm) + first_update + second_update + norm_update


def solution(mesh):
    if mesh.shape["tm"] == 2 * MB and mesh.shape["batch"] == 4:
        grid = Mesh(mesh.devices.reshape(MB, 2, 2, 2), AXES)
        tm, batch, chosen = ("z", "x"), ("y", "core"), fast_body
    else:
        grid, tm, batch, chosen = mesh, "tm", "batch", general_body
    kernels = (P(None, batch, tm),) * 3
    norms = (P(None, tm),) * 3
    in_specs = (P(batch, tm, None, None), P(), P(), P(batch, None)) + 2 * kernels + norms
    out_specs = (P(batch, None), P(batch, tm, None, None), P())
    out_specs = out_specs + (P(None, batch, tm),) * 10 + (P(None, tm),) * 5
    return jax.shard_map(chosen, mesh=grid, in_specs=in_specs, out_specs=out_specs, check_vma=False)
```

```python
import jax
import jax.numpy as jnp
from jax import lax
from jax.experimental import pallas as pl
from jax.experimental.pallas import tpu as pltpu
from jax.sharding import Mesh, PartitionSpec as P

C1 = 256
C2 = 512
MEL = 8
FR_DEV = 8
CL_MB = 2
MB = 4
STEP = 10


BETA_ONE = 0.9
BETA_TWO = 0.999
ADAM_EPS = 1e-08
NORM_EPS = 1e-05
WEIGHT_DECAY = 0.01
CLIP_NORM = 0.5
GAIN_RATE = 1.0


def extended(block, sides, width):
    for axis, dim in sides:
        count = lax.axis_size(axis)
        forward = [(i, i + 1) for i in range(count - 1)]
        backward = [(target, source) for source, target in forward]
        low = lax.ppermute(
            lax.slice_in_dim(block, block.shape[dim] - width, None, axis=dim), axis, forward
        )
        high = lax.ppermute(lax.slice_in_dim(block, 0, width, axis=dim), axis, backward)
        block = jnp.concatenate([low, block, high], axis=dim)
    return block


def silu_slope(shaped):
    sigmoid_value = jax.nn.sigmoid(shaped)
    return sigmoid_value * (1.0 + shaped * (1.0 - sigmoid_value))


def pad_mel(field_data):
    return jnp.pad(field_data, ((0, 0), (0, 0), (1, 1), (0, 0)))


def frame_rim(field_data):
    return pad_mel(extended(field_data, (("tm", 1),), 1))


def grad_rim(field_data):
    return pad_mel(extended(field_data, (("tm", 1),), 1))


def patches(padded, frame_count, mel_count):
    pieces = [
        padded[:, step_time : step_time + frame_count, step_mel : step_mel + mel_count, :]
        for step_time in range(3)
        for step_mel in range(3)
    ]
    columns = jnp.concatenate(pieces, axis=-1)
    return columns.reshape(-1, columns.shape[-1])


def norm_forward(pre_norm, frame_mask, pixels, gain_row, shift_row):
    masked = pre_norm * frame_mask
    total_sum, square_sum = lax.psum(
        (jnp.sum(masked, axis=(0, 1, 2)), jnp.sum(masked * pre_norm, axis=(0, 1, 2))),
        ("tm", "batch"),
    )
    channel_mean = total_sum / pixels
    variance = square_sum / pixels - channel_mean * channel_mean
    inv_scale = lax.rsqrt(variance + NORM_EPS)
    normed = (pre_norm - channel_mean) * inv_scale
    return (normed, inv_scale, gain_row * normed + shift_row)


def norm_backward(outer_grad, frame_mask, shaped, normed, inv_scale, gain_row, pixels):
    slope_grad = outer_grad * frame_mask * silu_slope(shaped)
    shift_grad, gain_grad = lax.psum(
        (jnp.sum(slope_grad, axis=(0, 1, 2)), jnp.sum(slope_grad * normed, axis=(0, 1, 2))),
        ("tm", "batch"),
    )
    pre_grad = (
        frame_mask
        * inv_scale
        * gain_row
        * (slope_grad - shift_grad / pixels - normed * gain_grad / pixels)
    )
    return (pre_grad.astype(jnp.bfloat16), gain_grad, shift_grad)


def adam_step(weight, moment, square, summed, factor, step_rate, decay_rate):
    clipped = summed * factor
    moment_new = BETA_ONE * moment + (1.0 - BETA_ONE) * clipped
    square_new = BETA_TWO * square + (1.0 - BETA_TWO) * clipped * clipped
    corrected = moment_new / (1.0 - BETA_ONE**STEP)
    scaled = jnp.sqrt(square_new / (1.0 - BETA_TWO**STEP)) + ADAM_EPS
    weight_new = weight - step_rate * (corrected / scaled + decay_rate * weight)
    return (clipped, moment_new, square_new, weight_new, weight_new.astype(jnp.bfloat16))


def contract_rows(columns, grads):
    return lax.dot_general(
        columns, grads, (((0,), (0,)), ((), ())), preferred_element_type=jnp.float32
    )


def general_body(
    clip_input,
    frame_counts,
    clip_order,
    cotangent,
    kernel_one,
    kernel_one_mean,
    kernel_one_square,
    kernel_two,
    kernel_two_mean,
    kernel_two_square,
    norm_params,
    norm_mean,
    norm_square,
):
    batch_count = lax.axis_size("batch")
    tm_count = lax.axis_size("tm")
    tm_index = lax.axis_index("tm")
    batch_index = lax.axis_index("batch")
    half_frames = FR_DEV // 2
    counts_table = jnp.take_along_axis(frame_counts.reshape(batch_count, -1), clip_order, axis=1)
    valid_pixels = (
        MEL * jnp.sum(counts_table.reshape(batch_count, MB, CL_MB), axis=(0, 2))
    ).astype(jnp.float32)
    local_order = lax.dynamic_index_in_dim(clip_order, batch_index, 0, keepdims=False)
    local_counts = lax.dynamic_index_in_dim(counts_table, batch_index, 0, keepdims=False)
    frame_place = tm_index * FR_DEV + jnp.arange(FR_DEV, dtype=jnp.int32)
    pooled_place = 2 * (tm_index * half_frames + jnp.arange(half_frames, dtype=jnp.int32)) + 1
    low_one = kernel_one.astype(jnp.bfloat16)
    low_two = kernel_two.astype(jnp.bfloat16)
    low_gains = norm_params.astype(jnp.bfloat16)
    shape_out = (CL_MB, FR_DEV, MEL, C2)
    pooled = jnp.zeros((MB * CL_MB, C2), jnp.float32)
    input_grad = jnp.zeros(clip_input.shape, jnp.bfloat16)
    sum_one = jnp.zeros((9 * C1, C2), jnp.float32)
    sum_two = jnp.zeros((9 * C2, C2), jnp.float32)
    norm_sum = jnp.zeros((4, C2), jnp.float32)
    for micro_step in range(MB):
        tm_parts = (
            lax.all_gather(low_one, "tm", axis=2, tiled=True),
            lax.all_gather(low_two, "tm", axis=2, tiled=True),
            lax.all_gather(low_gains, "tm", axis=1, tiled=True),
        )
        full_one, full_two = (
            lax.all_gather(tm_parts[0], "batch", axis=1, tiled=True),
            lax.all_gather(tm_parts[1], "batch", axis=1, tiled=True),
        )
        weights = (full_one, full_two, tm_parts[2])
        gain_table = weights[2].astype(jnp.float32)
        flat_one = weights[0].reshape(9 * C1, C2)
        flat_two = weights[1].reshape(9 * C2, C2)
        slot_ids = local_order[micro_step * CL_MB : (micro_step + 1) * CL_MB]
        clip_counts = local_counts[micro_step * CL_MB : (micro_step + 1) * CL_MB]
        frame_mask = (frame_place[None, :] < clip_counts[:, None]).astype(jnp.float32)[
            :, :, None, None
        ]
        pool_mask = (pooled_place[None, :] < clip_counts[:, None]).astype(jnp.float32)[:, :, None]
        halves = (clip_counts // 2).astype(jnp.float32)[:, None]
        pixels = valid_pixels[micro_step]
        masked_input = jnp.take(clip_input, slot_ids, axis=0) * frame_mask.astype(jnp.bfloat16)
        input_columns = patches(frame_rim(masked_input), FR_DEV, MEL)
        pre_one = jnp.dot(input_columns, flat_one, preferred_element_type=jnp.float32).reshape(
            shape_out
        )
        normed_one, scale_one, shaped_one = norm_forward(
            pre_one, frame_mask, pixels, gain_table[0], gain_table[1]
        )
        hidden = (jax.nn.silu(shaped_one) * frame_mask).astype(jnp.bfloat16)
        hidden_columns = patches(frame_rim(hidden), FR_DEV, MEL)
        pre_two = jnp.dot(hidden_columns, flat_two, preferred_element_type=jnp.float32).reshape(
            shape_out
        )
        normed_two, scale_two, shaped_two = norm_forward(
            pre_two, frame_mask, pixels, gain_table[2], gain_table[3]
        )
        activation = jax.nn.silu(shaped_two) * frame_mask
        summary = jnp.mean(activation.reshape(CL_MB, half_frames, 2, MEL, C2), axis=(2, 3))
        exp_summary = jnp.exp(summary)
        mean_part, exp_part = lax.psum(
            (jnp.sum(summary * pool_mask, axis=1), jnp.sum(exp_summary * pool_mask, axis=1)), "tm"
        )
        pooled = pooled.at[slot_ids].set(mean_part / halves + jnp.log(exp_part / halves))
        cot_rows = jnp.take(cotangent, slot_ids, axis=0)[:, None, :]
        summary_grad = pool_mask * (
            cot_rows / halves[:, :, None] + cot_rows * exp_summary / exp_part[:, None, :]
        )
        activation_grad = jnp.broadcast_to(
            (summary_grad / (2 * MEL))[:, :, None, None, :], (CL_MB, half_frames, 2, MEL, C2)
        ).reshape(shape_out)
        grad_two, gain_two_grad, shift_two_grad = norm_backward(
            activation_grad, frame_mask, shaped_two, normed_two, scale_two, gain_table[2], pixels
        )
        sum_two = sum_two + contract_rows(hidden_columns, grad_two.reshape(-1, C2))
        flip_two = weights[1][::-1].transpose(0, 2, 1).reshape(9 * C2, C2)
        hidden_grad = jnp.dot(
            patches(grad_rim(grad_two), FR_DEV, MEL), flip_two, preferred_element_type=jnp.float32
        ).reshape(shape_out)
        grad_one, gain_one_grad, shift_one_grad = norm_backward(
            hidden_grad, frame_mask, shaped_one, normed_one, scale_one, gain_table[0], pixels
        )
        sum_one = sum_one + contract_rows(input_columns, grad_one.reshape(-1, C2))
        flip_one = weights[0][::-1].transpose(0, 2, 1).reshape(9 * C2, C1)
        rows_grad = jnp.dot(
            patches(grad_rim(grad_one), FR_DEV, MEL), flip_one, preferred_element_type=jnp.float32
        ).reshape(CL_MB, FR_DEV, MEL, C1)
        input_grad = input_grad.at[slot_ids].set((rows_grad * frame_mask).astype(jnp.bfloat16))
        norm_sum = norm_sum + jnp.stack(
            [gain_one_grad, shift_one_grad, gain_two_grad, shift_two_grad]
        )
    batch_parts = (
        lax.psum_scatter(sum_one.reshape(9, C1, C2), "batch", scatter_dimension=1, tiled=True),
        lax.psum_scatter(sum_two.reshape(9, C2, C2), "batch", scatter_dimension=1, tiled=True),
    )
    grad_one_shard, grad_two_shard = (
        lax.psum_scatter(batch_parts[0], "tm", scatter_dimension=2, tiled=True),
        lax.psum_scatter(batch_parts[1], "tm", scatter_dimension=2, tiled=True),
    )
    shard_width = C2 // tm_count
    norm_shard = lax.dynamic_slice_in_dim(norm_sum, tm_index * shard_width, shard_width, 1)
    norm_term = jnp.where(batch_index == 0, jnp.sum(norm_shard * norm_shard), 0.0)
    own_squares = (
        jnp.sum(grad_one_shard * grad_one_shard)
        + jnp.sum(grad_two_shard * grad_two_shard)
        + norm_term
    )
    grad_norm = jnp.sqrt(lax.psum(own_squares, ("tm", "batch")))
    factor = jnp.minimum(1.0, CLIP_NORM / (grad_norm + 1e-06))
    first_update = adam_step(
        kernel_one,
        kernel_one_mean,
        kernel_one_square,
        grad_one_shard,
        factor,
        (9 * C1) ** (-0.5),
        WEIGHT_DECAY,
    )
    second_update = adam_step(
        kernel_two,
        kernel_two_mean,
        kernel_two_square,
        grad_two_shard,
        factor,
        (9 * C2) ** (-0.5),
        WEIGHT_DECAY,
    )
    norm_update = adam_step(norm_params, norm_mean, norm_square, norm_shard, factor, GAIN_RATE, 0.0)
    return (pooled, input_grad, grad_norm) + first_update + second_update + norm_update


AXES = ('z', 'x', 'y', 'core')
BF = jnp.bfloat16
F32 = jnp.float32
ROWS = 512
CLIPS_CORE = 4
PIXELS = ROWS * CLIPS_CORE
HALF = PIXELS // 2
LANES = 128
TAPS = 9
CHUNK = TAPS * 32
ANY = pl.BlockSpec(memory_space=pl.ANY)
VM = pl.BlockSpec(memory_space=pltpu.VMEM)
HB = pl.BlockSpec(memory_space=pltpu.HBM)
VMEM_LIMIT = 16 * 1024 * 1024


def shape_of(shape, dtype=BF):
    return jax.ShapeDtypeStruct(shape, dtype)


def call(kernel, out, in_specs, out_specs, scratch=(), limit=VMEM_LIMIT):
    return pl.pallas_call(kernel, out_shape=out, in_specs=in_specs, out_specs=out_specs, scratch_shapes=list(scratch), compiler_params=pltpu.CompilerParams(vmem_limit_bytes=limit), cost_estimate=pl.CostEstimate(flops=0, bytes_accessed=0, transcendentals=0))


def join_kernel(*refs):
    base = 0
    for ref in refs[:-1]:
        refs[-1][base:base + ref.shape[0]] = ref[...]
        base += ref.shape[0]


def join(*parts):
    rows = sum((part.shape[0] for part in parts))
    out = shape_of((rows,) + parts[0].shape[1:], parts[0].dtype)
    return call(join_kernel, out, [VM] * len(parts), VM)(*parts)


def swap(value, axis, step=1):
    size = lax.axis_size(axis)
    return lax.ppermute(value, axis, [(i, i ^ step) for i in range(size)])


def start_copies(copies, sems, base=0):
    started = []
    for at, (source, target) in enumerate(copies):
        copy = pltpu.make_async_copy(source, target, sems.at[base + at])
        copy.start()
        started.append(copy)
    return started


def wait_all(copies):
    for copy in copies:
        copy.wait()


def place(*axes):
    found = tuple((lax.axis_index(axis) for axis in axes))
    return found if len(found) > 1 else found[0]


def after(value, *others):
    return lax.optimization_barrier((value,) + others)[0]


def steps_of():
    return [2, 3, 1]


def order_entry(order, row, column):
    row_of = lax.broadcasted_iota(jnp.int32, order.shape, 0)
    column_of = lax.broadcasted_iota(jnp.int32, order.shape, 1)
    chosen = jnp.where((row_of == row) & (column_of == column), order, 0).astype(F32)
    return jnp.sum(jnp.sum(chosen, axis=1, keepdims=True), axis=0, keepdims=True)


def write_facts(order_ref, counts_ref, facts_ref):
    z, y, core = place('z', 'y', 'core')
    order, counts = (order_ref[...], counts_ref[...])
    column_of = lax.broadcasted_iota(jnp.int32, counts.shape, 1)
    row_of = lax.broadcasted_iota(jnp.int32, (16, LANES), 0)
    facts = jnp.zeros((16, LANES), F32)
    total = jnp.zeros((1, 1), F32)
    for row in range(4):
        for j in range(CL_MB):
            clip = order_entry(order, row, z * CL_MB + j).astype(jnp.int32) + row * 8
            count = jnp.sum(jnp.where(column_of == clip, counts, 0).astype(F32), axis=1, keepdims=True)
            total = total + count
            target = jnp.where(row % 2 == core, row // 2 * CL_MB + j, -1)
            facts = jnp.where(row_of == target, count, facts)
    facts = jnp.where(row_of == 4, MEL * total, facts)
    for slot in range(MB * CL_MB):
        facts = jnp.where(row_of == 8 + slot, order_entry(order, y * 2 + core, slot), facts)
    facts_ref[...] = facts.astype(jnp.int32)


def count_row(facts_ref, clip):
    return facts_ref[clip:clip + 1, :]


def pixel_row(facts_ref):
    return facts_ref[4:5, :].astype(F32)


def time_shift(rows, step):
    zero = jnp.zeros((MEL, rows.shape[1]), rows.dtype)
    if step == 1:
        return jnp.concatenate([rows[MEL:], zero], axis=0)
    if step == -1:
        return jnp.concatenate([zero, rows[:-MEL]], axis=0)
    return rows


def mel_shift(rows, step):
    if step == 0:
        return rows
    cube = rows.reshape(rows.shape[0] // MEL, MEL, rows.shape[1])
    turned = pltpu.roll(cube, -step % MEL, 1)
    bin_at = lax.broadcasted_iota(jnp.int32, cube.shape, 1) + step
    keep = (bin_at >= 0) & (bin_at < MEL)
    return jnp.where(keep, turned, 0.0).reshape(rows.shape)


def valid_rows(facts_ref, clip):
    frame = lax.broadcasted_iota(jnp.int32, (ROWS, LANES), 0) // MEL
    return (frame < count_row(facts_ref, clip)).astype(F32)


def dot_nt(left, right):
    return lax.dot_general(left, right, (((1,), (1,)), ((), ())), preferred_element_type=F32)


def dot_nn(left, right):
    return lax.dot_general(left, right, (((1,), (0,)), ((), ())), preferred_element_type=F32)


def dot_tn(left, right):
    return lax.dot_general(left, right, (((0,), (0,)), ((), ())), preferred_element_type=F32)


def lanes_of(tap):
    return slice(tap * LANES, (tap + 1) * LANES)


def gather_taps(product):
    total = None
    for mel in range(3):
        column = None
        for time in range(3):
            term = time_shift(product[:, lanes_of(3 * time + mel)], time - 1)
            column = term if column is None else column + term
        column = mel_shift(column, mel - 1)
        total = column if total is None else total + column
    return total


def scatter_taps(grad, target, base):
    for mel in range(3):
        moved = mel_shift(grad, 1 - mel)
        for time in range(3):
            target[base:base + ROWS, lanes_of(3 * time + mel)] = time_shift(moved, 1 - time).astype(BF)


def channel_sums(first, second):
    return (jnp.sum(first, axis=0, keepdims=True), jnp.sum(second, axis=0, keepdims=True))


def pair_sums(own_ref, other_ref):
    return (own_ref[0:1, :] + other_ref[0:1, :], own_ref[1:2, :] + other_ref[1:2, :])


def norm_rows(own_ref, other_ref, pixels):
    total, squares = pair_sums(own_ref, other_ref)
    mean = total / pixels
    return (mean, lax.rsqrt(squares / pixels - mean * mean + NORM_EPS))


def put_pair(ref, first, second):
    ref[...] = jnp.zeros(ref.shape, F32)
    ref[0:1, :] = first
    ref[1:2, :] = second


def exchange_matrix(rows, columns, source_of):
    row = lax.broadcasted_iota(jnp.int32, (rows, columns), 0)
    column = lax.broadcasted_iota(jnp.int32, (rows, columns), 1)
    return (row == source_of(column)).astype(BF)


def block_exchange(column):
    return column // 32 % 4 * 128 + column // 128 * 32 + column % 32


def lane_index(rows):
    return lax.broadcasted_iota(jnp.int32, (rows, LANES), 1)


def take_kernel(order_ref, clip_ref, p0, p1, p2, p3):
    z, y, core = place('z', 'y', 'core')
    order = order_ref[...]
    for step, piece in enumerate((p0, p1, p2, p3)):
        plane = jnp.bitwise_xor(z, step)
        for j in range(CL_MB):
            clip = order_entry(order, y * 2 + core, plane * CL_MB + j)[0, 0].astype(jnp.int32)
            piece[j * 64:(j + 1) * 64, :] = clip_ref[clip]
        piece[CL_MB * 64:, :] = jnp.zeros((piece.shape[0] - CL_MB * 64, C1), BF)


def prepare_kernel(order_ref, counts_ref, one_in, two_in, norm_in, cot_in, one_keep, two_keep, send_ref, gain_ref, cot_own, facts_ref, one_ref, two_ref, norm_ref, cot_ref, sems):
    z, x, y, core = place(*AXES)
    group = y * 2 + core
    loads = start_copies([(one_in, one_ref), (two_in, two_ref), (norm_in, norm_ref), (cot_in, cot_ref)], sems)
    write_facts(order_ref, counts_ref, facts_ref)
    wait_all(loads)
    for tap in range(TAPS):
        turned = jnp.swapaxes(one_ref[tap], 0, 1)
        rows = [turned[at * 16:(at + 1) * 16] for at in range(4)]
        low = jnp.concatenate([rows[0], rows[1]], axis=1).astype(BF)
        high = jnp.concatenate([rows[2], rows[3]], axis=1).astype(BF)
        span = slice(tap * 16, (tap + 1) * 16)
        one_keep[span, :] = jnp.where(y == 0, low, high)
        send_ref[span, :] = jnp.where(y == 0, high, low)
        low, high = (two_ref[tap, 0:32, :].astype(BF), two_ref[tap, 32:64, :].astype(BF))
        span = slice(tap * 32, (tap + 1) * 32)
        two_keep[span, :] = jnp.where(y == 0, low, high)
        span = slice(144 + tap * 32, 144 + (tap + 1) * 32)
        send_ref[span, :] = jnp.where(y == 0, high, low)
    wide = jnp.concatenate([norm_ref[...], norm_ref[...]], axis=1)
    wide = jnp.concatenate([wide, jnp.zeros((4, LANES), F32)], axis=0)
    turned = pltpu.roll(wide, (z * 32 - y * 32) % LANES, 1)
    gain_rows = jnp.where(lane_index(8) // 32 == z, turned, 0.0)
    gain_ref[...] = jnp.concatenate([gain_rows, jnp.zeros((8, LANES), F32)], axis=0).astype(BF)

    def cot_rows(y_of):
        rows = []
        for j in range(CL_MB):
            clip = order_entry(order_ref[...], group, z * CL_MB + j)[0, 0].astype(jnp.int32)
            row = cot_ref[pl.ds(clip, 1), :]
            picked = jnp.zeros((1, LANES), F32)
            for block in range(MB):
                moved = pltpu.roll(jnp.broadcast_to(row[:, lanes_of(block)], (8, LANES)), (block * 32 - x * 64 - y_of * 32) % LANES, 1)[0:1]
                picked = jnp.where(lane_index(1) // 32 == block, moved, picked)
            rows.append(picked)
        return rows
    own, send = (cot_rows(y), cot_rows(1 - y))
    cot_own[...] = jnp.concatenate(own + [jnp.zeros((6, LANES), F32)], axis=0)
    high = [row.astype(BF).astype(F32) for row in send]
    rest = [row - top for row, top in zip(send, high)]
    middle = [row.astype(BF).astype(F32) for row in rest]
    low = [row - top for row, top in zip(rest, middle)]
    packed = jnp.concatenate(high + middle + low + [jnp.zeros((10, LANES), F32)], axis=0)
    send_ref[144 + CHUNK:160 + CHUNK, :] = packed.astype(BF)


def first_weight_kernel(o0, o1, o2, o3, others, facts_in, weight_ref, gain_ref, facts_ref):
    facts_ref[...] = facts_in[...]
    z, y, core = place('z', 'y', 'core')
    gains = jnp.zeros((8, LANES), F32)
    for half in range(2):

        def source_of(column, half=half):
            from_core = jnp.bitwise_xor(column // 64 % 2, core)
            from_y = jnp.bitwise_xor(column // 128, y)
            return from_core * 256 + from_y * 128 + half * 64 + column % 64
        spread = exchange_matrix(512, C1, source_of)
        for step, own in enumerate((o0, o1, o2, o3)):
            z_of = jnp.bitwise_xor(z, step)
            other = others[step * 304:step * 304 + 288]
            four = jnp.concatenate([own[0:144], own[144:288], other[0:144], other[144:288]], axis=1)
            both = dot_nn(four, spread).astype(BF)
            for tap in range(TAPS):
                weight_ref[tap, z_of, half * 16:half * 16 + 16] = both[tap * 16:(tap + 1) * 16]
            if half == 0:
                gains = gains + own[CHUNK:CHUNK + 16].astype(F32)[0:8]
    gain_ref[...] = gains


def first_conv_kernel(facts_ref, a0, a1, a23, b0, b1, b23, weight_ref, pre_ref, x_ref, stat_ref):
    z, x, y = place('z', 'x', 'y')
    frame = lax.broadcasted_iota(jnp.int32, (64, LANES), 0) // MEL
    for j, pieces in ((0, ((a0, 0, x, y), (a1, 0, 1 - x, y), (a23, 0, x, 1 - y), (a23, MB, 1 - x, 1 - y))), (1, ((b0, 0, x, y), (b1, 0, x, 1 - y), (b23, 0, 1 - x, y), (b23, MB, 1 - x, 1 - y)))):
        for source, base, x_of, y_of in pieces:
            count = facts_ref[pl.ds(y_of * CL_MB + j, 1), :]
            for step in range(MB):
                frames = (jnp.bitwise_xor(z, step) * 2 + x_of) * 8
                mask = (frame + frames < count).astype(F32).astype(BF)
                row = pl.multiple_of((y_of * CL_MB + j) * ROWS + frames * MEL, 64)
                x_ref[pl.ds(row, 64), :] = source[base + step] * jnp.concatenate([mask, mask], axis=1)
    weight = weight_ref[...].reshape(TAPS * LANES, C1)
    first = jnp.zeros((1, LANES), F32)
    second = jnp.zeros((1, LANES), F32)
    for clip in range(CLIPS_CORE):
        span = slice(clip * ROWS, (clip + 1) * ROWS)
        pre = gather_taps(dot_nt(x_ref[span, :], weight))
        pre_ref[span, :] = pre
        kept = pre * valid_rows(facts_ref, clip)
        plus = channel_sums(kept, kept * pre)
        first, second = (first + plus[0], second + plus[1])
    put_pair(stat_ref, first, second)


def stack_kernel(p0, p1, p2, p3, a_ref, b_ref):
    for step, piece in enumerate((p0, p1, p2, p3)):
        a_ref[step] = piece[0:64]
        b_ref[step] = piece[64:128]


def hidden_kernel(facts_ref, pre_ref, own_ref, other_ref, gain_ref, *outs):
    mean, scale = norm_rows(own_ref, other_ref, pixel_row(facts_ref))
    for clip in range(CLIPS_CORE):
        pre = pre_ref[clip * ROWS:(clip + 1) * ROWS, :]
        shaped = gain_ref[0:1, :] * ((pre - mean) * scale) + gain_ref[1:2, :]
        value = shaped * jax.nn.sigmoid(shaped) * valid_rows(facts_ref, clip)
        for target in outs[clip // 2 * 2:clip // 2 * 2 + 2]:
            target[clip % 2 * ROWS:(clip % 2 + 1) * ROWS, :] = value.astype(BF)
    for target in outs:
        target[HALF:, :] = jnp.zeros((target.shape[0] - HALF, LANES), BF)


def second_weight_kernel(o0, o1, o2, o3, s0, s1, s2, s3, weight_ref):
    z, y, core = place('z', 'y', 'core')
    spread = exchange_matrix(C2, C2, block_exchange)
    spans = [slice(0, CHUNK), slice(CHUNK, 2 * CHUNK)]
    for step, (own_ref, other_ref) in enumerate(((o0, s0), (o1, s1), (o2, s2), (o3, s3))):
        z_of = jnp.bitwise_xor(z, step)
        parts = []
        for y_of in range(2):
            own = jnp.where(y == y_of, own_ref[spans[0]], own_ref[spans[1]])
            other = jnp.where(y == y_of, other_ref[spans[0]], other_ref[spans[1]])
            parts += [jnp.where(core == 0, own, other), jnp.where(core == 0, other, own)]
        both = dot_nn(jnp.concatenate(parts, axis=1), spread).astype(BF)
        for tap in range(TAPS):
            weight_ref[tap, z_of] = both[tap * 32:(tap + 1) * 32]


def hidden_copies(parts, target):
    x, y = place('x', 'y')
    chips = ((x, y), (1 - x, y), (x, 1 - y), (1 - x, 1 - y), (x, y), (x, 1 - y), (1 - x, y), (1 - x, 1 - y))
    copies = []
    for at, (source, (x_of, y_of)) in enumerate(zip(parts, chips)):
        lane = pl.multiple_of((x_of * 2 + y_of) * LANES, LANES)
        copies.append((source.at[pl.ds(0, HALF)], target.at[pl.ds(at // 4 * HALF, HALF), pl.ds(lane, LANES)]))
    return copies


def near_conv_kernel(a0, a1, a2, b0, b1, b2, weight_ref, pre_ref):
    x, y = place('x', 'y')

    def lane(x_of, y_of):
        return pl.ds(pl.multiple_of((x_of * 2 + y_of) * LANES, LANES), LANES)
    weight = jnp.concatenate([weight_ref[:, :, :, lane(*chip)].reshape(TAPS * LANES, LANES) for chip in ((x, y), (1 - x, y), (x, 1 - y))], axis=1)
    for clip in range(CLIPS_CORE):
        parts = (a0, a1, a2) if clip < 2 else (b0, b2, b1)
        rows = slice(clip % 2 * ROWS, (clip % 2 + 1) * ROWS)
        three = jnp.concatenate([part[rows, :] for part in parts], axis=1)
        pre_ref[clip * ROWS:(clip + 1) * ROWS, :] = gather_taps(dot_nt(three, weight))


def far_conv_kernel(facts_ref, a3, b3, weight_ref, near_ref, pre_ref, stat_ref):
    x, y = place('x', 'y')
    lane = pl.multiple_of(((1 - x) * 2 + 1 - y) * LANES, LANES)
    weight = weight_ref[:, :, :, pl.ds(lane, LANES)].reshape(TAPS * LANES, LANES)
    first = jnp.zeros((1, LANES), F32)
    second = jnp.zeros((1, LANES), F32)
    for clip in range(CLIPS_CORE):
        span = slice(clip * ROWS, (clip + 1) * ROWS)
        part = a3 if clip < 2 else b3
        rows = slice(clip % 2 * ROWS, (clip % 2 + 1) * ROWS)
        pre = near_ref[span, :] + gather_taps(dot_nt(part[rows, :], weight))
        pre_ref[span, :] = pre
        kept = pre * valid_rows(facts_ref, clip)
        plus = channel_sums(kept, kept * pre)
        first, second = (first + plus[0], second + plus[1])
    put_pair(stat_ref, first, second)


def pool_kernel(facts_ref, pre_ref, own_ref, other_ref, gain_ref, cot_own, cot_got, slope_ref, sum_ref, pooled_ref):
    y = place('y')
    mean, scale = norm_rows(own_ref, other_ref, pixel_row(facts_ref))
    first = jnp.zeros((1, LANES), F32)
    second = jnp.zeros((1, LANES), F32)
    slots = ROWS // (2 * MEL)
    got = cot_got[144 + CHUNK:160 + CHUNK, :].astype(F32)
    pooled = []
    for clip in range(CLIPS_CORE):
        span = slice(clip * ROWS, (clip + 1) * ROWS)
        count = count_row(facts_ref, clip)
        j = clip % CL_MB
        told = got[j:j + 1] + got[2 + j:3 + j] + got[4 + j:5 + j]
        cot = jnp.where(y == clip // CL_MB, cot_own[j:j + 1, :], told)
        mask = valid_rows(facts_ref, clip)
        normed = (pre_ref[span, :] - mean) * scale
        shaped = gain_ref[2:3, :] * normed + gain_ref[3:4, :]
        gate = jax.nn.sigmoid(shaped)
        active = (shaped * gate * mask).reshape(slots, 2 * MEL, LANES)
        summary = jnp.sum(active, axis=1) / (2 * MEL)
        slot = lax.broadcasted_iota(jnp.int32, (slots, LANES), 0)
        keep = (2 * slot + 1 < count).astype(F32)
        raised = jnp.exp(summary)
        exp_total = jnp.sum(raised * keep, axis=0, keepdims=True)
        halves = (count // 2).astype(F32)
        pooled.append(jnp.sum(summary * keep, axis=0, keepdims=True) / halves + jnp.log(exp_total / halves))
        summary_grad = keep * (cot / halves + cot * raised / exp_total) / (2 * MEL)
        spread = jnp.broadcast_to(summary_grad[:, None, :], (slots, 2 * MEL, LANES))
        slope = spread.reshape(ROWS, LANES) * mask * (gate * (1.0 + shaped * (1.0 - gate)))
        slope_ref[span, :] = slope
        plus = channel_sums(slope, slope * normed)
        first, second = (first + plus[0], second + plus[1])
    put_pair(sum_ref, first, second)
    high = [row.astype(BF).astype(F32) for row in pooled]
    low = [row - top for row, top in zip(pooled, high)]
    rows = jnp.concatenate(high + low + [jnp.zeros((8, LANES), F32)], axis=0)
    pooled_ref[...] = rows.astype(BF)


def pre_grad(slope, pre, mask, mean, scale, gain, sums, pixels):
    normed = (pre - mean) * scale
    return mask * (scale * gain) * (slope - sums[0] / pixels - normed * (sums[1] / pixels))


def both_grad_kernel(facts_ref, slope_ref, pre_ref, own_ref, other_ref, sum_own, sum_other, gain_ref, weight_ref, pooled_ref, columns, a_own, a_mid, a_send, b_own, b_mid, b_send, weight):
    x, y = place('x', 'y')
    pixels = pixel_row(facts_ref)
    mean, scale = norm_rows(own_ref, other_ref, pixels)
    sums = pair_sums(sum_own, sum_other)
    a_send[2 * HALF:2 * HALF + 16, :] = pooled_ref[...]
    for at, (x_of, y_of) in enumerate(((x, y), (x, 1 - y), (1 - x, y), (1 - x, 1 - y))):
        lane = pl.multiple_of((x_of * 2 + y_of) * LANES, LANES)
        weight[:, lanes_of(at)] = weight_ref[:, :, :, pl.ds(lane, LANES)].reshape(TAPS * LANES, LANES)
    for clip in range(CLIPS_CORE):
        span = slice(clip * ROWS, (clip + 1) * ROWS)
        mask = valid_rows(facts_ref, clip)
        grad = pre_grad(slope_ref[span, :], pre_ref[span, :], mask, mean, scale, gain_ref[2:3, :], sums, pixels)
        scatter_taps(grad, columns, clip * ROWS)
        partial = dot_nn(columns[span, :], weight[...])
        rows = slice(clip % 2 * ROWS, (clip % 2 + 1) * ROWS)
        near_rows = slice(HALF + clip % 2 * ROWS, HALF + (clip % 2 + 1) * ROWS)
        far = partial[:, lanes_of(3)].astype(BF)
        if clip < 2:
            a_own[rows, :] = partial[:, lanes_of(0)]
            a_mid[rows, :] = partial[:, lanes_of(1)]
            a_send[rows, :] = far
            a_send[near_rows, :] = partial[:, lanes_of(2)].astype(BF)
        else:
            b_own[rows, :] = partial[:, lanes_of(0)]
            b_mid[rows, :] = partial[:, lanes_of(2)]
            b_send[rows, :] = far
            b_send[near_rows, :] = partial[:, lanes_of(1)].astype(BF)


def pass_on_kernel(a_mid, a_got, b_mid, b_got, pooled_ref, a_next, b_next):
    a_next[HALF:HALF + 16, :] = pooled_ref[...]
    a_next[HALF + 16:HALF + 32, :] = a_got[2 * HALF:2 * HALF + 16]
    a_next[0:HALF, :] = (a_mid[...] + a_got[0:HALF].astype(F32)).astype(BF)
    b_next[...] = (b_mid[...] + b_got[0:HALF].astype(F32)).astype(BF)


def second_weight_grad_kernel(*rest):
    parts, columns, keeps, sends = (rest[:8], rest[8], rest[9:12], rest[12:15])
    hidden, natural, sems = rest[15:]
    core = place('core')
    started = start_copies(hidden_copies(parts, hidden), sems)
    spread = exchange_matrix(C2, C2, block_exchange)
    wait_all(started)
    for clip in range(CLIPS_CORE):
        span = slice(clip * ROWS, (clip + 1) * ROWS)
        hidden[span, :] = dot_nn(hidden[span, :], spread).astype(BF)
    for tap in range(TAPS):
        natural[...] = dot_tn(columns[:, lanes_of(tap)], hidden[...])
        keep_ref, send_ref = (keeps[tap // 3], sends[tap // 3])
        target = slice(tap % 3 * 32, (tap % 3 + 1) * 32)
        for y_of in range(2):
            keep = natural[:, pl.ds(pl.multiple_of((y_of * 2 + core) * LANES, LANES), LANES)]
            send = natural[:, pl.ds(pl.multiple_of((y_of * 2 + 1 - core) * LANES, LANES), LANES)]
            for z_of in range(MB):
                rows = slice(z_of * 32, (z_of + 1) * 32)
                keep_ref[z_of, y_of, target] = keep[rows]
                send_ref[z_of, y_of, target] = send[rows]


def second_core_kernel(k0, k1, k2, g0, g1, g2, own_ref, n1, n2, n3):
    z = place('z')
    for third, (keep_ref, got_ref) in enumerate(((k0, g0), (k1, g1), (k2, g2))):
        rows = slice(third * 96, (third + 1) * 96)
        own_ref[:, rows] = keep_ref[z] + got_ref[z]
        for step, target in ((1, n1), (2, n2), (3, n3)):
            at = jnp.bitwise_xor(z, step)
            target[:, rows] = (keep_ref[at] + got_ref[at]).astype(BF)


def second_sum_kernel(own_ref, g1, g2, g3, keep_ref, send_ref, square_ref):
    y = place('y')
    total = own_ref[...] + g1[...].astype(F32) + g2[...].astype(F32) + g3[...].astype(F32)
    keep_ref[...] = jnp.where(y == 0, total[0], total[1])
    send_ref[...] = jnp.where(y == 0, total[1], total[0]).astype(BF)
    square_ref[...] = jnp.sum(total * total, axis=(0, 1), keepdims=False)[None, :] * jnp.ones((8, 1), F32)


def first_slope_kernel(facts_ref, a_own, a_near, a_last, b_own, b_near, b_last, pre_ref, own_ref, other_ref, gain_ref, slope_ref, sum_ref):
    mean, scale = norm_rows(own_ref, other_ref, pixel_row(facts_ref))
    first = jnp.zeros((1, LANES), F32)
    second = jnp.zeros((1, LANES), F32)
    for clip in range(CLIPS_CORE):
        span = slice(clip * ROWS, (clip + 1) * ROWS)
        rows = slice(clip % 2 * ROWS, (clip % 2 + 1) * ROWS)
        own, near, last = (a_own, a_near, a_last) if clip < 2 else (b_own, b_near, b_last)
        base = near.shape[0] // HALF * HALF - HALF
        near_rows = slice(base + clip % 2 * ROWS, base + (clip % 2 + 1) * ROWS)
        outer = own[rows, :] + near[near_rows, :].astype(F32) + last[rows, :].astype(F32)
        normed = (pre_ref[span, :] - mean) * scale
        shaped = gain_ref[0:1, :] * normed + gain_ref[1:2, :]
        gate = jax.nn.sigmoid(shaped)
        slope = outer * valid_rows(facts_ref, clip) * (gate * (1.0 + shaped * (1.0 - gate)))
        slope_ref[span, :] = slope
        plus = channel_sums(slope, slope * normed)
        first, second = (first + plus[0], second + plus[1])
    put_pair(sum_ref, first, second)


def first_weight_grad_kernel(facts_ref, slope_ref, pre_ref, own_ref, other_ref, sum_own, sum_other, gain_ref, x_ref, columns, keep_ref, send_ref, turned):
    core = place('core')
    pixels = pixel_row(facts_ref)
    mean, scale = norm_rows(own_ref, other_ref, pixels)
    sums = pair_sums(sum_own, sum_other)

    def source_of(column):
        core_of = jnp.where(column < 128, core, 1 - core)
        return column // 64 % 2 * 128 + core_of * 64 + column % 64
    spread = exchange_matrix(C1, C1, source_of)
    for clip in range(CLIPS_CORE):
        span = slice(clip * ROWS, (clip + 1) * ROWS)
        mask = valid_rows(facts_ref, clip)
        grad = pre_grad(slope_ref[span, :], pre_ref[span, :], mask, mean, scale, gain_ref[0:1, :], sums, pixels)
        scatter_taps(grad, columns, clip * ROWS)
        turned[span, :] = dot_nn(x_ref[span, :], spread).astype(BF)
    for tap in range(TAPS):
        both = dot_tn(columns[:, lanes_of(tap)], turned[...])
        for z_of in range(MB):
            rows = slice(z_of * 32, (z_of + 1) * 32)
            target = slice(tap * 32, (tap + 1) * 32)
            keep_ref[z_of, target] = both[rows, 0:LANES]
            send_ref[z_of, target] = both[rows, LANES:2 * LANES]


def input_grad_kernel(columns, weight_ref, part_ref):
    weight = weight_ref[...].reshape(TAPS * LANES, C1)
    for clip in range(CLIPS_CORE):
        partial = dot_nn(columns[clip * ROWS:(clip + 1) * ROWS, :], weight).astype(BF)
        for z_of in range(MB):
            for x_of in range(2):
                target = slice((clip % 2 * MB + z_of) * 64, (clip % 2 * MB + z_of + 1) * 64)
                rows = slice((z_of * 2 + x_of) * 64, (z_of * 2 + x_of + 1) * 64)
                part_ref[x_of * 2 + clip // 2, target, :] = partial[rows]


def first_core_kernel(keep_ref, got_ref, one_own, one_other, two_own, two_other, pooled_own, pooled_near, pooled_last, own_ref, n0, n1, n2, n3, scratch):
    z, x, y = place('z', 'x', 'y')
    own_ref[...] = keep_ref[z] + got_ref[z]
    one, two = (pair_sums(one_own, one_other), pair_sums(two_own, two_other))
    sums = jnp.concatenate([one[1], one[0], two[1], two[0]], axis=0)
    high = sums.astype(BF).astype(F32)
    norm_tile = jnp.concatenate([high, sums - high, jnp.zeros((8, LANES), F32)], axis=0).astype(BF)
    last = pooled_last[HALF:HALF + 32, :].astype(F32)
    near = pooled_near[...].astype(F32)
    own = pooled_own[...].astype(F32)
    for rows, x_of, y_of in ((own, x, y), (near, 1 - x, y), (last[0:16], x, 1 - y), (last[16:32], 1 - x, 1 - y)):
        for part in range(2):
            for j in range(CL_MB):
                row = jnp.where(y == 0, rows[part * 4 + j:part * 4 + j + 1], rows[part * 4 + 2 + j:part * 4 + 3 + j])
                scratch[pl.ds((x_of * 2 + y_of) * 4 + part * 2 + j, 1), :] = row
    pooled_tile = scratch[...].astype(BF)
    for step, target in ((0, n0), (1, n1), (2, n2), (3, n3)):
        at = jnp.bitwise_xor(z, step)
        target[0:CHUNK, :] = (keep_ref[at] + got_ref[at]).astype(BF)
        target[CHUNK:CHUNK + 16, :] = norm_tile
        target[CHUNK + 16:CHUNK + 32, :] = pooled_tile


def first_sum_kernel(own_ref, n0, g1, g2, g3, square_two, told_ref, keep_ref, send_ref, norm_ref):
    z, y, core = place('z', 'y', 'core')
    total = own_ref[...]
    norm = n0[CHUNK:CHUNK + 16, :].astype(F32)
    for got in (g1, g2, g3):
        total = total + got[0:CHUNK, :].astype(F32)
        norm = norm + got[CHUNK:CHUNK + 16, :].astype(F32)
    norm = norm[0:4] + norm[4:8]
    mine = (lane_index(4) // 32 == z) & (core == 0)
    squares = jnp.sum(total * total, axis=0, keepdims=True) + jnp.sum(jnp.where(mine, norm * norm, 0.0), axis=0, keepdims=True)
    first_rows = lax.broadcasted_iota(jnp.int32, told_ref.shape, 0) % 8 == 0
    told_ref[...] = jnp.where(first_rows, squares + square_two[0:1, :], 0.0)
    turned = pltpu.roll(total, 64, 1)
    low = jnp.where(y == 0, total, turned)
    high = jnp.where(y == 0, turned, total)
    left = lane_index(144) < 64
    keep_ref[...] = jnp.where(left, low[0:144], pltpu.roll(low[144:288], 64, 1))
    send_ref[0:144, :] = jnp.where(left, high[0:144], pltpu.roll(high[144:288], 64, 1))
    rows = jnp.concatenate([norm, jnp.zeros((4, LANES), F32)], axis=0)
    send_ref[144:152, :] = rows
    norm_ref[...] = rows


def adam_write(refs, outs, gradient, factor, step_rate, decay_rate, at):
    weight, moment, square = (ref[at] for ref in refs)
    clipped = gradient * factor
    moment_new = BETA_ONE * moment + (1.0 - BETA_ONE) * clipped
    square_new = BETA_TWO * square + (1.0 - BETA_TWO) * clipped * clipped
    corrected = moment_new * (1.0 / (1.0 - BETA_ONE ** STEP))
    scaled = jnp.sqrt(square_new * (1.0 / (1.0 - BETA_TWO ** STEP))) + ADAM_EPS
    weight_new = weight - step_rate * (corrected / scaled + decay_rate * weight)
    for out, value in zip(outs, (clipped, moment_new, square_new, weight_new, weight_new.astype(BF))):
        out[at] = value


def adam_kernel(told_ref, keep_ref, got_ref, norm_ref, two_keep, two_got, *refs):
    z, y = place('z', 'y')
    one, two, norm, outs = (refs[0:3], refs[3:6], refs[6:9], refs[9:])
    norm_out, one_out, two_out, small_out = (outs[0], outs[1:6], outs[6:11], outs[11:16])
    told = jnp.sum(told_ref[...], axis=0, keepdims=True)
    length = jnp.sqrt(jnp.sum(told, axis=1, keepdims=True))
    norm_out[...] = length
    factor = jnp.minimum(1.0, CLIP_NORM / (length + 1e-06))
    keep, got = (keep_ref[...], got_ref[0:144, :])
    first, second = (jnp.where(y == 0, keep, got), jnp.where(y == 0, got, keep))
    spans = [jnp.concatenate([half[:, 0:64], half[:, 64:128]], axis=0) for half in (first, second)]
    for tap in range(TAPS):
        rows = slice(tap * 32, (tap + 1) * 32)
        gradient = jnp.swapaxes(jnp.concatenate([span[rows] for span in spans], axis=0), 0, 1)
        adam_write(one, one_out, gradient, factor, (9 * C1) ** (-0.5), WEIGHT_DECAY, tap)
        keep, got = (two_keep[rows, :], two_got[rows, :].astype(F32))
        gradient = jnp.concatenate([jnp.where(y == 0, keep, got), jnp.where(y == 0, got, keep)], axis=0)
        adam_write(two, two_out, gradient, factor, (9 * C2) ** (-0.5), WEIGHT_DECAY, tap)
    keep, got = (norm_ref[...], got_ref[144:152, :])
    first, second = (jnp.where(y == 0, keep, got), jnp.where(y == 0, got, keep))
    low = pltpu.roll(first, (0 - z * 32) % LANES, 1)
    high = pltpu.roll(second, (32 - z * 32) % LANES, 1)
    gradient = jnp.where(lane_index(8) < 32, low, high)[0:4, 0:64]
    adam_write(norm, small_out, gradient, factor, GAIN_RATE, 0.0, slice(None))


def input_sum_kernel(facts_ref, got_ref, f0, f1, f2, f3):
    z, x, y = place('z', 'x', 'y')
    for j in range(CL_MB):
        count = jnp.where(y == 0, count_row(facts_ref, j), count_row(facts_ref, CL_MB + j))
        count = jnp.concatenate([count, count], axis=1)
        for step, target in enumerate((f0, f1, f2, f3)):
            at = jnp.bitwise_xor(z, step)
            rows = pl.ds(pl.multiple_of((j * MB + at) * 64, 64), 64)
            total = got_ref[0, rows, :].astype(F32)
            for chip in range(1, 4):
                total = total + got_ref[chip, rows, :].astype(F32)
            frame = (at * 2 + x) * 8 + lax.broadcasted_iota(jnp.int32, (64, C1), 0) // MEL
            target[j] = jnp.where(frame < count, total, 0.0).astype(BF)


def finish_kernel(facts_ref, f0, g1, g2, g3, grad_ref):
    z = place('z')
    for step, piece in enumerate((f0, g1, g2, g3)):
        at = jnp.bitwise_xor(z, step)
        for j in range(CL_MB):
            clip = facts_ref[pl.ds(8 + at * CL_MB + j, 1), :][0, 0]
            grad_ref[clip] = piece[j]


def pooled_kernel(facts_ref, n0, n1, n2, n3, pooled_ref, scratch):
    z = place('z')
    for step, told in enumerate((n0, n1, n2, n3)):
        at = jnp.bitwise_xor(z, step)
        rows = told[CHUNK + 16:CHUNK + 32, :].astype(F32)
        for j in range(CL_MB):
            clip = facts_ref[pl.ds(8 + at * CL_MB + j, 1), :][0, 0]
            for part in range(2):
                chips = [rows[chip * 4 + part * 2 + j:chip * 4 + part * 2 + j + 1] for chip in range(4)]
                scratch[part, pl.ds(clip, 1), :] = jnp.concatenate(chips, axis=1)
    spread = exchange_matrix(C2, C2, block_exchange)
    pooled_ref[...] = dot_nn(scratch[0].astype(BF), spread) + dot_nn(scratch[1].astype(BF), spread)


def fast_body(clip_input, frame_counts, clip_order, cotangent, kernel_one, kernel_one_mean, kernel_one_square, kernel_two, kernel_two_mean, kernel_two_square, norm_params, norm_mean, norm_square):
    one_view, two_view = (kernel_one, jnp.swapaxes(kernel_two, 1, 2))
    p0, p1, p2, p3 = call(take_kernel, [shape_of((CL_MB * 64 + 16, C1))] * MB, [VM] * 2, [VM] * MB, limit=16 * 1024 * 1024)(clip_order, clip_input.reshape(MB * CL_MB, 64, C1))
    one_keep, two_keep, send, gain_rows, cot_own, facts = call(prepare_kernel, [shape_of((144, LANES)), shape_of((CHUNK, LANES)), shape_of((160 + CHUNK, LANES))] + [shape_of((16, LANES)), shape_of((8, LANES), F32), shape_of((16, LANES), jnp.int32)], [VM, VM] + [HB] * 4, [VM] * 6, [pltpu.VMEM(one_view.shape, F32), pltpu.VMEM(two_view.shape, F32), pltpu.VMEM(norm_params.shape, F32), pltpu.VMEM(cotangent.shape, F32), pltpu.SemaphoreType.DMA((4,))], limit=16 * 1024 * 1024)(after(clip_order, p0), frame_counts.reshape(1, 32), one_view, two_view, norm_params, cotangent)

    def spread_z(values):
        got = {step: swap(values[step], 'z', step) for step in steps_of()}
        return [values[0]] + [got[step] for step in (1, 2, 3)]
    p1, p2, p3 = (part for part in (p1, p2, p3))
    arrived = spread_z([p0, p1, p2, p3])
    got = swap(send, 'y')
    a0, b0 = call(stack_kernel, [shape_of((MB, 64, C1))] * 2, [VM] * 4, [VM] * 2)(*arrived)
    one_flat = join(one_keep, got[0:144], gain_rows)
    a1, b1 = (swap(a0, 'x'), swap(b0, 'y'))
    one_parts = spread_z([one_flat] * 4)
    a01, b01 = (join(a0, a1), join(b0, b1))
    deps = ()
    one_others = join(*[swap(after(part, *deps), 'core') for part in one_parts])
    a23, b23 = (swap(a01, 'y'), swap(b01, 'x'))
    inputs = (a0, a1, a23, b0, b1, b23)
    two_flat = join(two_keep, got[144:144 + CHUNK])
    two_flat = after(two_flat, *one_parts[1:])
    two_parts = spread_z([two_flat] * 4)
    weight_one, gains, facts = call(first_weight_kernel, [shape_of((TAPS, MB, 32, C1)), shape_of((8, LANES), F32), shape_of((16, LANES), jnp.int32)], [VM] * 6, [VM] * 3)(*one_parts, one_others, facts)
    pre_one, masked, stat_one = call(first_conv_kernel, [shape_of((PIXELS, LANES), F32), shape_of((PIXELS, C1)), shape_of((8, LANES), F32)], [VM] * 8, [VM] * 3)(facts, *inputs, weight_one)
    stat_one_other = swap(stat_one, 'core')
    ha_on, ha0, hb_on, hb0 = call(hidden_kernel, [shape_of((HALF + pad, LANES)) for pad in (32, 48)] * 2, [VM] * 5, [VM] * 4)(after(facts, *two_parts[1:]), pre_one, stat_one, stat_one_other, gains)
    ha1, hb1 = (swap(ha_on, 'x'), swap(hb_on, 'y'))
    ha2, hb2 = (swap(ha0, 'y'), swap(hb0, 'x'))
    ha3, hb3 = (swap(ha1, 'y'), swap(hb1, 'x'))
    hidden_parts = (ha0, ha1, ha2, ha3, hb0, hb1, hb2, hb3)
    deps = (ha0,)
    two_others = [swap(after(part, *deps), 'core') for part in two_parts]
    weight_two = call(second_weight_kernel, shape_of((TAPS, MB, 32, C2)), [VM] * 8, VM)(*two_parts, *two_others)
    ha = hidden_parts
    near_two = call(near_conv_kernel, shape_of((PIXELS, LANES), F32), [VM] * 7, VM)(ha[0], ha[1], ha[2], ha[4], ha[5], ha[6], weight_two)
    pre_two, stat_two = call(far_conv_kernel, [shape_of((PIXELS, LANES), F32), shape_of((8, LANES), F32)], [VM] * 5, [VM] * 2)(facts, ha[3], ha[7], weight_two, near_two)
    stat_two_other = swap(stat_two, 'core')
    slope_two, sum_two, pooled_own = call(pool_kernel, [shape_of((PIXELS, LANES), F32), shape_of((8, LANES), F32), shape_of((16, LANES))], [VM] * 7, [VM] * 3)(facts, pre_two, stat_two, stat_two_other, gains, cot_own, got)
    sum_two_other = swap(sum_two, 'core')
    columns_two, a_own, a_mid, a_send, b_own, b_mid, b_send = call(both_grad_kernel, [shape_of((PIXELS, TAPS * LANES))] + [shape_of((HALF, LANES), F32)] * 2 + [shape_of((2 * HALF + 16, LANES))] + [shape_of((HALF, LANES), F32)] * 2 + [shape_of((2 * HALF, LANES))], [VM] * 10, [VM] * 7, [pltpu.VMEM((TAPS * LANES, C2), BF)])(facts, slope_two, pre_two, stat_two, stat_two_other, sum_two, sum_two_other, gains, weight_two, pooled_own)
    a_got = a_near = swap(a_send, 'x')
    b_got = b_near = swap(b_send, 'y')
    a_pool = a_got[2 * HALF:]
    thirds = call(second_weight_grad_kernel, [shape_of((MB, 2, 96, LANES), F32)] * 6, [ANY] * 8 + [VM], [VM] * 6, [pltpu.VMEM((PIXELS, C2), BF), pltpu.VMEM((LANES, C2), F32), pltpu.SemaphoreType.DMA((8,))])(*hidden_parts, columns_two)

    def sum_cores(*deps):
        sends = [after(part, *deps) if deps else part for part in thirds[3:6]]
        return call(second_core_kernel, [shape_of((2, CHUNK, LANES), F32)] + [shape_of((2, CHUNK, LANES))] * 3, [VM] * 6, [VM] * 4)(*thirds[0:3], *[swap(part, 'core') for part in sends])
    two_own, t1, t2, t3 = sum_cores()
    a_got = after(a_got, t1)
    a_next, b_next = call(pass_on_kernel, [shape_of((HALF + 32, LANES)), shape_of((HALF, LANES))], [VM] * 5, [VM] * 2)(a_mid, a_got, b_mid, b_got, pooled_own)
    a_last, b_last = (swap(a_next, 'y'), swap(b_next, 'x'))
    slope_one, sum_one = call(first_slope_kernel, [shape_of((PIXELS, LANES), F32), shape_of((8, LANES), F32)], [VM] * 11, [VM] * 2)(after(facts, t1), a_own, a_near, a_last, b_own, b_near, b_last, pre_one, stat_one, stat_one_other, gains)
    sum_one_other = swap(sum_one, 'core')
    columns_one, one_part, one_part_send = call(first_weight_grad_kernel, [shape_of((PIXELS, TAPS * LANES))] + [shape_of((MB, CHUNK, LANES), F32)] * 2, [VM] * 9, [VM] * 3, [pltpu.VMEM((PIXELS, C1), BF)])(facts, slope_one, pre_one, stat_one, stat_one_other, sum_one, sum_one_other, gains, masked)
    input_part = call(input_grad_kernel, shape_of((4, ROWS, C1)), [VM] * 2, VM)(columns_one, weight_one)
    two_keep_sum, two_send_sum, square_two = call(second_sum_kernel, [shape_of((CHUNK, LANES), F32), shape_of((CHUNK, LANES)), shape_of((8, LANES), F32)], [VM] * 4, [VM] * 3)(*spread_z([two_own, t1, t2, t3]))
    one_own, n0, n1, n2, n3 = call(first_core_kernel, [shape_of((CHUNK, LANES), F32)] + [shape_of((CHUNK + 32, LANES))] * MB, [VM] * 9, [VM] * 5, [pltpu.VMEM((16, LANES), F32)])(one_part, swap(after(one_part_send, square_two), 'core'), sum_one, sum_one_other, sum_two, sum_two_other, pooled_own, a_pool, a_last)
    g1, g2, g3 = spread_z([n0, n1, n2, n3])[1:]
    input_got = lax.all_to_all(input_part, ('x', 'y'), 0, 0, tiled=True)
    f0, f1, f2, f3 = call(input_sum_kernel, [shape_of((CL_MB, 64, C1))] * MB, [VM] * 2, [VM] * 4)(facts, input_got)
    two_got_sum = swap(after(two_send_sum, n1), 'y')
    f1, f2, f3 = spread_z([f0, f1, f2, f3])[1:]
    told, one_keep_sum, one_send_sum, norm_sum = call(first_sum_kernel, [shape_of((32 * 8, LANES), F32), shape_of((144, LANES), F32), shape_of((152, LANES), F32), shape_of((8, LANES), F32)], [VM] * 6, [VM] * 4)(one_own, n0, g1, g2, g3, square_two)
    told_sent = told
    told = lax.all_to_all(told, AXES, 0, 0, tiled=True)
    one_got_sum = swap(one_send_sum, 'y')
    one_shapes = [shape_of(one_view.shape, F32)] * 4 + [shape_of(one_view.shape)]
    two_shapes = [shape_of(two_view.shape, F32)] * 4 + [shape_of(two_view.shape)]
    norm_shapes = [shape_of(norm_params.shape, F32)] * 4 + [shape_of(norm_params.shape)]
    state = (kernel_one, kernel_one_mean, kernel_one_square, two_view, jnp.swapaxes(kernel_two_mean, 1, 2), jnp.swapaxes(kernel_two_square, 1, 2), norm_params, norm_mean, norm_square)
    updates = call(adam_kernel, [shape_of((1, 1), F32)] + one_shapes + two_shapes + norm_shapes, [VM] * 15, [VM] * 16, limit=62 * 1024 * 1024)(told, one_keep_sum, one_got_sum, norm_sum, two_keep_sum, two_got_sum, *state)
    grad_norm = updates[0].reshape(())
    first_update, norm_update = (tuple(updates[1:6]), tuple(updates[11:16]))
    second_update = tuple((jnp.swapaxes(part, 1, 2) for part in updates[6:11]))
    pooled = call(pooled_kernel, shape_of((MB * CL_MB, C2), F32), [VM] * 5, VM, [pltpu.VMEM((2, MB * CL_MB, C2), F32)])(facts, n0, g1, g2, g3)
    input_grad = call(finish_kernel, shape_of((MB * CL_MB, 64, C1)), [VM] * 5, VM)(facts, after(f0, updates[0]), f1, f2, f3)
    input_grad = input_grad.reshape(clip_input.shape)
    return (pooled, input_grad, grad_norm) + first_update + second_update + norm_update


def solution(mesh):
    if mesh.shape['tm'] == 2 * MB and mesh.shape['batch'] == 4:
        grid = Mesh(mesh.devices.reshape(MB, 2, 2, 2), AXES)
        tm, batch, chosen = (('z', 'x'), ('y', 'core'), fast_body)
    else:
        grid, tm, batch, chosen = (mesh, 'tm', 'batch', general_body)
    kernels = (P(None, batch, tm),) * 3
    norms = (P(None, tm),) * 3
    in_specs = (P(batch, tm, None, None), P(), P(), P(batch, None)) + 2 * kernels + norms
    out_specs = (P(batch, None), P(batch, tm, None, None), P())
    out_specs = out_specs + (P(None, batch, tm),) * 10 + (P(None, tm),) * 5
    return jax.shard_map(chosen, mesh=grid, in_specs=in_specs, out_specs=out_specs, check_vma=False)
```

```python
import jax
import jax.numpy as jnp
from jax import lax
from jax.experimental import pallas as pl
from jax.experimental.pallas import tpu as pltpu
from jax.sharding import Mesh, PartitionSpec as P

C1 = 256
C2 = 512
MEL = 8
FR_DEV = 8
CL_MB = 2
MB = 4
STEP = 10


BETA_ONE = 0.9
BETA_TWO = 0.999
ADAM_EPS = 1e-08
NORM_EPS = 1e-05
WEIGHT_DECAY = 0.01
CLIP_NORM = 0.5
GAIN_RATE = 1.0


def extended(block, sides, width):
    for axis, dim in sides:
        count = lax.axis_size(axis)
        forward = [(i, i + 1) for i in range(count - 1)]
        backward = [(target, source) for source, target in forward]
        low = lax.ppermute(
            lax.slice_in_dim(block, block.shape[dim] - width, None, axis=dim), axis, forward
        )
        high = lax.ppermute(lax.slice_in_dim(block, 0, width, axis=dim), axis, backward)
        block = jnp.concatenate([low, block, high], axis=dim)
    return block


def silu_slope(shaped):
    sigmoid_value = jax.nn.sigmoid(shaped)
    return sigmoid_value * (1.0 + shaped * (1.0 - sigmoid_value))


def pad_mel(field_data):
    return jnp.pad(field_data, ((0, 0), (0, 0), (1, 1), (0, 0)))


def frame_rim(field_data):
    return pad_mel(extended(field_data, (("tm", 1),), 1))


def grad_rim(field_data):
    return pad_mel(extended(field_data, (("tm", 1),), 1))


def patches(padded, frame_count, mel_count):
    pieces = [
        padded[:, step_time : step_time + frame_count, step_mel : step_mel + mel_count, :]
        for step_time in range(3)
        for step_mel in range(3)
    ]
    columns = jnp.concatenate(pieces, axis=-1)
    return columns.reshape(-1, columns.shape[-1])


def norm_forward(pre_norm, frame_mask, pixels, gain_row, shift_row):
    masked = pre_norm * frame_mask
    total_sum, square_sum = lax.psum(
        (jnp.sum(masked, axis=(0, 1, 2)), jnp.sum(masked * pre_norm, axis=(0, 1, 2))),
        ("tm", "batch"),
    )
    channel_mean = total_sum / pixels
    variance = square_sum / pixels - channel_mean * channel_mean
    inv_scale = lax.rsqrt(variance + NORM_EPS)
    normed = (pre_norm - channel_mean) * inv_scale
    return (normed, inv_scale, gain_row * normed + shift_row)


def norm_backward(outer_grad, frame_mask, shaped, normed, inv_scale, gain_row, pixels):
    slope_grad = outer_grad * frame_mask * silu_slope(shaped)
    shift_grad, gain_grad = lax.psum(
        (jnp.sum(slope_grad, axis=(0, 1, 2)), jnp.sum(slope_grad * normed, axis=(0, 1, 2))),
        ("tm", "batch"),
    )
    pre_grad = (
        frame_mask
        * inv_scale
        * gain_row
        * (slope_grad - shift_grad / pixels - normed * gain_grad / pixels)
    )
    return (pre_grad.astype(jnp.bfloat16), gain_grad, shift_grad)


def adam_step(weight, moment, square, summed, factor, step_rate, decay_rate):
    clipped = summed * factor
    moment_new = BETA_ONE * moment + (1.0 - BETA_ONE) * clipped
    square_new = BETA_TWO * square + (1.0 - BETA_TWO) * clipped * clipped
    corrected = moment_new / (1.0 - BETA_ONE**STEP)
    scaled = jnp.sqrt(square_new / (1.0 - BETA_TWO**STEP)) + ADAM_EPS
    weight_new = weight - step_rate * (corrected / scaled + decay_rate * weight)
    return (clipped, moment_new, square_new, weight_new, weight_new.astype(jnp.bfloat16))


def contract_rows(columns, grads):
    return lax.dot_general(
        columns, grads, (((0,), (0,)), ((), ())), preferred_element_type=jnp.float32
    )


def general_body(
    clip_input,
    frame_counts,
    clip_order,
    cotangent,
    kernel_one,
    kernel_one_mean,
    kernel_one_square,
    kernel_two,
    kernel_two_mean,
    kernel_two_square,
    norm_params,
    norm_mean,
    norm_square,
):
    batch_count = lax.axis_size("batch")
    tm_count = lax.axis_size("tm")
    tm_index = lax.axis_index("tm")
    batch_index = lax.axis_index("batch")
    half_frames = FR_DEV // 2
    counts_table = jnp.take_along_axis(frame_counts.reshape(batch_count, -1), clip_order, axis=1)
    valid_pixels = (
        MEL * jnp.sum(counts_table.reshape(batch_count, MB, CL_MB), axis=(0, 2))
    ).astype(jnp.float32)
    local_order = lax.dynamic_index_in_dim(clip_order, batch_index, 0, keepdims=False)
    local_counts = lax.dynamic_index_in_dim(counts_table, batch_index, 0, keepdims=False)
    frame_place = tm_index * FR_DEV + jnp.arange(FR_DEV, dtype=jnp.int32)
    pooled_place = 2 * (tm_index * half_frames + jnp.arange(half_frames, dtype=jnp.int32)) + 1
    low_one = kernel_one.astype(jnp.bfloat16)
    low_two = kernel_two.astype(jnp.bfloat16)
    low_gains = norm_params.astype(jnp.bfloat16)
    shape_out = (CL_MB, FR_DEV, MEL, C2)
    pooled = jnp.zeros((MB * CL_MB, C2), jnp.float32)
    input_grad = jnp.zeros(clip_input.shape, jnp.bfloat16)
    sum_one = jnp.zeros((9 * C1, C2), jnp.float32)
    sum_two = jnp.zeros((9 * C2, C2), jnp.float32)
    norm_sum = jnp.zeros((4, C2), jnp.float32)
    for micro_step in range(MB):
        tm_parts = (
            lax.all_gather(low_one, "tm", axis=2, tiled=True),
            lax.all_gather(low_two, "tm", axis=2, tiled=True),
            lax.all_gather(low_gains, "tm", axis=1, tiled=True),
        )
        full_one, full_two = (
            lax.all_gather(tm_parts[0], "batch", axis=1, tiled=True),
            lax.all_gather(tm_parts[1], "batch", axis=1, tiled=True),
        )
        weights = (full_one, full_two, tm_parts[2])
        gain_table = weights[2].astype(jnp.float32)
        flat_one = weights[0].reshape(9 * C1, C2)
        flat_two = weights[1].reshape(9 * C2, C2)
        slot_ids = local_order[micro_step * CL_MB : (micro_step + 1) * CL_MB]
        clip_counts = local_counts[micro_step * CL_MB : (micro_step + 1) * CL_MB]
        frame_mask = (frame_place[None, :] < clip_counts[:, None]).astype(jnp.float32)[
            :, :, None, None
        ]
        pool_mask = (pooled_place[None, :] < clip_counts[:, None]).astype(jnp.float32)[:, :, None]
        halves = (clip_counts // 2).astype(jnp.float32)[:, None]
        pixels = valid_pixels[micro_step]
        masked_input = jnp.take(clip_input, slot_ids, axis=0) * frame_mask.astype(jnp.bfloat16)
        input_columns = patches(frame_rim(masked_input), FR_DEV, MEL)
        pre_one = jnp.dot(input_columns, flat_one, preferred_element_type=jnp.float32).reshape(
            shape_out
        )
        normed_one, scale_one, shaped_one = norm_forward(
            pre_one, frame_mask, pixels, gain_table[0], gain_table[1]
        )
        hidden = (jax.nn.silu(shaped_one) * frame_mask).astype(jnp.bfloat16)
        hidden_columns = patches(frame_rim(hidden), FR_DEV, MEL)
        pre_two = jnp.dot(hidden_columns, flat_two, preferred_element_type=jnp.float32).reshape(
            shape_out
        )
        normed_two, scale_two, shaped_two = norm_forward(
            pre_two, frame_mask, pixels, gain_table[2], gain_table[3]
        )
        activation = jax.nn.silu(shaped_two) * frame_mask
        summary = jnp.mean(activation.reshape(CL_MB, half_frames, 2, MEL, C2), axis=(2, 3))
        exp_summary = jnp.exp(summary)
        mean_part, exp_part = lax.psum(
            (jnp.sum(summary * pool_mask, axis=1), jnp.sum(exp_summary * pool_mask, axis=1)), "tm"
        )
        pooled = pooled.at[slot_ids].set(mean_part / halves + jnp.log(exp_part / halves))
        cot_rows = jnp.take(cotangent, slot_ids, axis=0)[:, None, :]
        summary_grad = pool_mask * (
            cot_rows / halves[:, :, None] + cot_rows * exp_summary / exp_part[:, None, :]
        )
        activation_grad = jnp.broadcast_to(
            (summary_grad / (2 * MEL))[:, :, None, None, :], (CL_MB, half_frames, 2, MEL, C2)
        ).reshape(shape_out)
        grad_two, gain_two_grad, shift_two_grad = norm_backward(
            activation_grad, frame_mask, shaped_two, normed_two, scale_two, gain_table[2], pixels
        )
        sum_two = sum_two + contract_rows(hidden_columns, grad_two.reshape(-1, C2))
        flip_two = weights[1][::-1].transpose(0, 2, 1).reshape(9 * C2, C2)
        hidden_grad = jnp.dot(
            patches(grad_rim(grad_two), FR_DEV, MEL), flip_two, preferred_element_type=jnp.float32
        ).reshape(shape_out)
        grad_one, gain_one_grad, shift_one_grad = norm_backward(
            hidden_grad, frame_mask, shaped_one, normed_one, scale_one, gain_table[0], pixels
        )
        sum_one = sum_one + contract_rows(input_columns, grad_one.reshape(-1, C2))
        flip_one = weights[0][::-1].transpose(0, 2, 1).reshape(9 * C2, C1)
        rows_grad = jnp.dot(
            patches(grad_rim(grad_one), FR_DEV, MEL), flip_one, preferred_element_type=jnp.float32
        ).reshape(CL_MB, FR_DEV, MEL, C1)
        input_grad = input_grad.at[slot_ids].set((rows_grad * frame_mask).astype(jnp.bfloat16))
        norm_sum = norm_sum + jnp.stack(
            [gain_one_grad, shift_one_grad, gain_two_grad, shift_two_grad]
        )
    batch_parts = (
        lax.psum_scatter(sum_one.reshape(9, C1, C2), "batch", scatter_dimension=1, tiled=True),
        lax.psum_scatter(sum_two.reshape(9, C2, C2), "batch", scatter_dimension=1, tiled=True),
    )
    grad_one_shard, grad_two_shard = (
        lax.psum_scatter(batch_parts[0], "tm", scatter_dimension=2, tiled=True),
        lax.psum_scatter(batch_parts[1], "tm", scatter_dimension=2, tiled=True),
    )
    shard_width = C2 // tm_count
    norm_shard = lax.dynamic_slice_in_dim(norm_sum, tm_index * shard_width, shard_width, 1)
    norm_term = jnp.where(batch_index == 0, jnp.sum(norm_shard * norm_shard), 0.0)
    own_squares = (
        jnp.sum(grad_one_shard * grad_one_shard)
        + jnp.sum(grad_two_shard * grad_two_shard)
        + norm_term
    )
    grad_norm = jnp.sqrt(lax.psum(own_squares, ("tm", "batch")))
    factor = jnp.minimum(1.0, CLIP_NORM / (grad_norm + 1e-06))
    first_update = adam_step(
        kernel_one,
        kernel_one_mean,
        kernel_one_square,
        grad_one_shard,
        factor,
        (9 * C1) ** (-0.5),
        WEIGHT_DECAY,
    )
    second_update = adam_step(
        kernel_two,
        kernel_two_mean,
        kernel_two_square,
        grad_two_shard,
        factor,
        (9 * C2) ** (-0.5),
        WEIGHT_DECAY,
    )
    norm_update = adam_step(norm_params, norm_mean, norm_square, norm_shard, factor, GAIN_RATE, 0.0)
    return (pooled, input_grad, grad_norm) + first_update + second_update + norm_update


AXES = ('z', 'x', 'y', 'core')
BF = jnp.bfloat16
F32 = jnp.float32
ROWS = 512
CLIPS_CORE = 4
PIXELS = ROWS * CLIPS_CORE
HALF = PIXELS // 2
LANES = 128
TAPS = 9
CHUNK = TAPS * 32
ANY = pl.BlockSpec(memory_space=pl.ANY)
VM = pl.BlockSpec(memory_space=pltpu.VMEM)
HB = pl.BlockSpec(memory_space=pltpu.HBM)
VMEM_LIMIT = 16 * 1024 * 1024


def shape_of(shape, dtype=BF):
    return jax.ShapeDtypeStruct(shape, dtype)


def call(kernel, out, in_specs, out_specs, scratch=(), limit=VMEM_LIMIT):
    return pl.pallas_call(kernel, out_shape=out, in_specs=in_specs, out_specs=out_specs, scratch_shapes=list(scratch), compiler_params=pltpu.CompilerParams(vmem_limit_bytes=limit), cost_estimate=pl.CostEstimate(flops=0, bytes_accessed=0, transcendentals=0))


def join_kernel(*refs):
    base = 0
    for ref in refs[:-1]:
        refs[-1][base:base + ref.shape[0]] = ref[...]
        base += ref.shape[0]


def join(*parts):
    rows = sum((part.shape[0] for part in parts))
    out = shape_of((rows,) + parts[0].shape[1:], parts[0].dtype)
    return call(join_kernel, out, [VM] * len(parts), VM)(*parts)


def swap(value, axis, step=1):
    size = lax.axis_size(axis)
    return lax.ppermute(value, axis, [(i, i ^ step) for i in range(size)])


def start_copies(copies, sems, base=0):
    started = []
    for at, (source, target) in enumerate(copies):
        copy = pltpu.make_async_copy(source, target, sems.at[base + at])
        copy.start()
        started.append(copy)
    return started


def wait_all(copies):
    for copy in copies:
        copy.wait()


def place(*axes):
    found = tuple((lax.axis_index(axis) for axis in axes))
    return found if len(found) > 1 else found[0]


def after(value, *others):
    return lax.optimization_barrier((value,) + others)[0]


def steps_of():
    return [2, 3, 1]


def order_entry(order, row, column):
    row_of = lax.broadcasted_iota(jnp.int32, order.shape, 0)
    column_of = lax.broadcasted_iota(jnp.int32, order.shape, 1)
    chosen = jnp.where((row_of == row) & (column_of == column), order, 0).astype(F32)
    return jnp.sum(jnp.sum(chosen, axis=1, keepdims=True), axis=0, keepdims=True)


def write_facts(order_ref, counts_ref, facts_ref):
    z, y, core = place('z', 'y', 'core')
    order, counts = (order_ref[...], counts_ref[...])
    column_of = lax.broadcasted_iota(jnp.int32, counts.shape, 1)
    row_of = lax.broadcasted_iota(jnp.int32, (16, LANES), 0)
    facts = jnp.zeros((16, LANES), F32)
    total = jnp.zeros((1, 1), F32)
    for row in range(4):
        for j in range(CL_MB):
            clip = order_entry(order, row, z * CL_MB + j).astype(jnp.int32) + row * 8
            count = jnp.sum(jnp.where(column_of == clip, counts, 0).astype(F32), axis=1, keepdims=True)
            total = total + count
            target = jnp.where(row % 2 == core, row // 2 * CL_MB + j, -1)
            facts = jnp.where(row_of == target, count, facts)
    facts = jnp.where(row_of == 4, MEL * total, facts)
    for slot in range(MB * CL_MB):
        facts = jnp.where(row_of == 8 + slot, order_entry(order, y * 2 + core, slot), facts)
    facts_ref[...] = facts.astype(jnp.int32)


def count_row(facts_ref, clip):
    return facts_ref[clip:clip + 1, :]


def pixel_row(facts_ref):
    return facts_ref[4:5, :].astype(F32)


def time_shift(rows, step):
    zero = jnp.zeros((MEL, rows.shape[1]), rows.dtype)
    if step == 1:
        return jnp.concatenate([rows[MEL:], zero], axis=0)
    if step == -1:
        return jnp.concatenate([zero, rows[:-MEL]], axis=0)
    return rows


def mel_shift(rows, step):
    if step == 0:
        return rows
    cube = rows.reshape(rows.shape[0] // MEL, MEL, rows.shape[1])
    turned = pltpu.roll(cube, -step % MEL, 1)
    bin_at = lax.broadcasted_iota(jnp.int32, cube.shape, 1) + step
    keep = (bin_at >= 0) & (bin_at < MEL)
    return jnp.where(keep, turned, 0.0).reshape(rows.shape)


def valid_rows(facts_ref, clip):
    frame = lax.broadcasted_iota(jnp.int32, (ROWS, LANES), 0) // MEL
    return (frame < count_row(facts_ref, clip)).astype(F32)


def dot_nt(left, right):
    return lax.dot_general(left, right, (((1,), (1,)), ((), ())), preferred_element_type=F32)


def dot_nn(left, right):
    return lax.dot_general(left, right, (((1,), (0,)), ((), ())), preferred_element_type=F32)


def dot_tn(left, right):
    return lax.dot_general(left, right, (((0,), (0,)), ((), ())), preferred_element_type=F32)


def lanes_of(tap):
    return slice(tap * LANES, (tap + 1) * LANES)


def gather_taps(product):
    total = None
    for mel in range(3):
        column = None
        for time in range(3):
            term = time_shift(product[:, lanes_of(3 * time + mel)], time - 1)
            column = term if column is None else column + term
        column = mel_shift(column, mel - 1)
        total = column if total is None else total + column
    return total


def scatter_taps(grad, target, base):
    for mel in range(3):
        moved = mel_shift(grad, 1 - mel)
        for time in range(3):
            target[base:base + ROWS, lanes_of(3 * time + mel)] = time_shift(moved, 1 - time).astype(BF)


def channel_sums(first, second):
    return (jnp.sum(first, axis=0, keepdims=True), jnp.sum(second, axis=0, keepdims=True))


def pair_sums(own_ref, other_ref):
    return (own_ref[0:1, :] + other_ref[0:1, :], own_ref[1:2, :] + other_ref[1:2, :])


def norm_rows(own_ref, other_ref, pixels):
    total, squares = pair_sums(own_ref, other_ref)
    mean = total / pixels
    return (mean, lax.rsqrt(squares / pixels - mean * mean + NORM_EPS))


def put_pair(ref, first, second):
    ref[...] = jnp.zeros(ref.shape, F32)
    ref[0:1, :] = first
    ref[1:2, :] = second


def exchange_matrix(rows, columns, source_of):
    row = lax.broadcasted_iota(jnp.int32, (rows, columns), 0)
    column = lax.broadcasted_iota(jnp.int32, (rows, columns), 1)
    return (row == source_of(column)).astype(BF)


def block_exchange(column):
    return column // 32 % 4 * 128 + column // 128 * 32 + column % 32


def lane_index(rows):
    return lax.broadcasted_iota(jnp.int32, (rows, LANES), 1)


def take_kernel(order_ref, clip_ref, p0, p1, p2, p3):
    z, y, core = place('z', 'y', 'core')
    order = order_ref[...]
    for step, piece in enumerate((p0, p1, p2, p3)):
        plane = jnp.bitwise_xor(z, step)
        for j in range(CL_MB):
            clip = order_entry(order, y * 2 + core, plane * CL_MB + j)[0, 0].astype(jnp.int32)
            piece[j * 64:(j + 1) * 64, :] = clip_ref[clip]
        piece[CL_MB * 64:, :] = jnp.zeros((piece.shape[0] - CL_MB * 64, C1), BF)


def prepare_kernel(order_ref, counts_ref, one_in, two_in, norm_in, cot_in, one_keep, two_keep, send_ref, gain_ref, cot_own, facts_ref, one_ref, two_ref, norm_ref, cot_ref, sems):
    z, x, y, core = place(*AXES)
    group = y * 2 + core
    loads = start_copies([(one_in, one_ref), (two_in, two_ref), (norm_in, norm_ref), (cot_in, cot_ref)], sems)
    write_facts(order_ref, counts_ref, facts_ref)
    wait_all(loads)
    for tap in range(TAPS):
        turned = jnp.swapaxes(one_ref[tap], 0, 1)
        rows = [turned[at * 16:(at + 1) * 16] for at in range(4)]
        low = jnp.concatenate([rows[0], rows[1]], axis=1).astype(BF)
        high = jnp.concatenate([rows[2], rows[3]], axis=1).astype(BF)
        span = slice(tap * 16, (tap + 1) * 16)
        one_keep[span, :] = jnp.where(y == 0, low, high)
        send_ref[span, :] = jnp.where(y == 0, high, low)
        low, high = (two_ref[tap, 0:32, :].astype(BF), two_ref[tap, 32:64, :].astype(BF))
        span = slice(tap * 32, (tap + 1) * 32)
        two_keep[span, :] = jnp.where(y == 0, low, high)
        span = slice(144 + tap * 32, 144 + (tap + 1) * 32)
        send_ref[span, :] = jnp.where(y == 0, high, low)
    wide = jnp.concatenate([norm_ref[...], norm_ref[...]], axis=1)
    wide = jnp.concatenate([wide, jnp.zeros((4, LANES), F32)], axis=0)
    turned = pltpu.roll(wide, (z * 32 - y * 32) % LANES, 1)
    gain_rows = jnp.where(lane_index(8) // 32 == z, turned, 0.0)
    gain_ref[...] = jnp.concatenate([gain_rows, jnp.zeros((8, LANES), F32)], axis=0).astype(BF)

    def cot_rows(y_of):
        rows = []
        for j in range(CL_MB):
            clip = order_entry(order_ref[...], group, z * CL_MB + j)[0, 0].astype(jnp.int32)
            row = cot_ref[pl.ds(clip, 1), :]
            picked = jnp.zeros((1, LANES), F32)
            for block in range(MB):
                moved = pltpu.roll(jnp.broadcast_to(row[:, lanes_of(block)], (8, LANES)), (block * 32 - x * 64 - y_of * 32) % LANES, 1)[0:1]
                picked = jnp.where(lane_index(1) // 32 == block, moved, picked)
            rows.append(picked)
        return rows
    own, send = (cot_rows(y), cot_rows(1 - y))
    cot_own[...] = jnp.concatenate(own + [jnp.zeros((6, LANES), F32)], axis=0)
    high = [row.astype(BF).astype(F32) for row in send]
    rest = [row - top for row, top in zip(send, high)]
    middle = [row.astype(BF).astype(F32) for row in rest]
    low = [row - top for row, top in zip(rest, middle)]
    packed = jnp.concatenate(high + middle + low + [jnp.zeros((10, LANES), F32)], axis=0)
    send_ref[144 + CHUNK:160 + CHUNK, :] = packed.astype(BF)


def first_weight_kernel(o0, o1, o2, o3, others, facts_in, weight_ref, gain_ref, facts_ref):
    facts_ref[...] = facts_in[...]
    z, y, core = place('z', 'y', 'core')
    gains = jnp.zeros((8, LANES), F32)
    for half in range(2):

        def source_of(column, half=half):
            from_core = jnp.bitwise_xor(column // 64 % 2, core)
            from_y = jnp.bitwise_xor(column // 128, y)
            return from_core * 256 + from_y * 128 + half * 64 + column % 64
        spread = exchange_matrix(512, C1, source_of)
        for step, own in enumerate((o0, o1, o2, o3)):
            z_of = jnp.bitwise_xor(z, step)
            other = others[step * 304:step * 304 + 288]
            four = jnp.concatenate([own[0:144], own[144:288], other[0:144], other[144:288]], axis=1)
            both = dot_nn(four, spread).astype(BF)
            for tap in range(TAPS):
                weight_ref[tap, z_of, half * 16:half * 16 + 16] = both[tap * 16:(tap + 1) * 16]
            if half == 0:
                gains = gains + own[CHUNK:CHUNK + 16].astype(F32)[0:8]
    gain_ref[...] = gains


def first_conv_kernel(facts_ref, a0, a1, a23, b0, b1, b23, weight_ref, pre_ref, x_ref, stat_ref):
    z, x, y = place('z', 'x', 'y')
    frame = lax.broadcasted_iota(jnp.int32, (64, LANES), 0) // MEL
    for j, pieces in ((0, ((a0, 0, x, y), (a1, 0, 1 - x, y), (a23, 0, x, 1 - y), (a23, MB, 1 - x, 1 - y))), (1, ((b0, 0, x, y), (b1, 0, x, 1 - y), (b23, 0, 1 - x, y), (b23, MB, 1 - x, 1 - y)))):
        for source, base, x_of, y_of in pieces:
            count = facts_ref[pl.ds(y_of * CL_MB + j, 1), :]
            for step in range(MB):
                frames = (jnp.bitwise_xor(z, step) * 2 + x_of) * 8
                mask = (frame + frames < count).astype(F32).astype(BF)
                row = pl.multiple_of((y_of * CL_MB + j) * ROWS + frames * MEL, 64)
                x_ref[pl.ds(row, 64), :] = source[base + step] * jnp.concatenate([mask, mask], axis=1)
    weight = weight_ref[...].reshape(TAPS * LANES, C1)
    first = jnp.zeros((1, LANES), F32)
    second = jnp.zeros((1, LANES), F32)
    for clip in range(CLIPS_CORE):
        span = slice(clip * ROWS, (clip + 1) * ROWS)
        pre = gather_taps(dot_nt(x_ref[span, :], weight))
        pre_ref[span, :] = pre
        kept = pre * valid_rows(facts_ref, clip)
        plus = channel_sums(kept, kept * pre)
        first, second = (first + plus[0], second + plus[1])
    put_pair(stat_ref, first, second)


def stack_kernel(p0, p1, p2, p3, a_ref, b_ref):
    for step, piece in enumerate((p0, p1, p2, p3)):
        a_ref[step] = piece[0:64]
        b_ref[step] = piece[64:128]


def hidden_kernel(facts_ref, pre_ref, own_ref, other_ref, gain_ref, *outs):
    mean, scale = norm_rows(own_ref, other_ref, pixel_row(facts_ref))
    for clip in range(CLIPS_CORE):
        pre = pre_ref[clip * ROWS:(clip + 1) * ROWS, :]
        shaped = gain_ref[0:1, :] * ((pre - mean) * scale) + gain_ref[1:2, :]
        value = shaped * jax.nn.sigmoid(shaped) * valid_rows(facts_ref, clip)
        for target in outs[clip // 2 * 2:clip // 2 * 2 + 2]:
            target[clip % 2 * ROWS:(clip % 2 + 1) * ROWS, :] = value.astype(BF)
    for target in outs:
        target[HALF:, :] = jnp.zeros((target.shape[0] - HALF, LANES), BF)


def second_weight_kernel(o0, o1, o2, o3, s0, s1, s2, s3, weight_ref):
    z, y, core = place('z', 'y', 'core')
    spread = exchange_matrix(C2, C2, block_exchange)
    spans = [slice(0, CHUNK), slice(CHUNK, 2 * CHUNK)]
    for step, (own_ref, other_ref) in enumerate(((o0, s0), (o1, s1), (o2, s2), (o3, s3))):
        z_of = jnp.bitwise_xor(z, step)
        parts = []
        for y_of in range(2):
            own = jnp.where(y == y_of, own_ref[spans[0]], own_ref[spans[1]])
            other = jnp.where(y == y_of, other_ref[spans[0]], other_ref[spans[1]])
            parts += [jnp.where(core == 0, own, other), jnp.where(core == 0, other, own)]
        both = dot_nn(jnp.concatenate(parts, axis=1), spread).astype(BF)
        for tap in range(TAPS):
            weight_ref[tap, z_of] = both[tap * 32:(tap + 1) * 32]


def hidden_copies(parts, target):
    x, y = place('x', 'y')
    chips = ((x, y), (1 - x, y), (x, 1 - y), (1 - x, 1 - y), (x, y), (x, 1 - y), (1 - x, y), (1 - x, 1 - y))
    copies = []
    for at, (source, (x_of, y_of)) in enumerate(zip(parts, chips)):
        lane = pl.multiple_of((x_of * 2 + y_of) * LANES, LANES)
        copies.append((source.at[pl.ds(0, HALF)], target.at[pl.ds(at // 4 * HALF, HALF), pl.ds(lane, LANES)]))
    return copies


def near_conv_kernel(a0, a1, a2, b0, b1, b2, weight_ref, pre_ref):
    x, y = place('x', 'y')

    def lane(x_of, y_of):
        return pl.ds(pl.multiple_of((x_of * 2 + y_of) * LANES, LANES), LANES)
    weight = jnp.concatenate([weight_ref[:, :, :, lane(*chip)].reshape(TAPS * LANES, LANES) for chip in ((x, y), (1 - x, y), (x, 1 - y))], axis=1)
    for clip in range(CLIPS_CORE):
        parts = (a0, a1, a2) if clip < 2 else (b0, b2, b1)
        rows = slice(clip % 2 * ROWS, (clip % 2 + 1) * ROWS)
        three = jnp.concatenate([part[rows, :] for part in parts], axis=1)
        pre_ref[clip * ROWS:(clip + 1) * ROWS, :] = gather_taps(dot_nt(three, weight))


def far_conv_kernel(facts_ref, a3, b3, weight_ref, near_ref, pre_ref, stat_ref):
    x, y = place('x', 'y')
    lane = pl.multiple_of(((1 - x) * 2 + 1 - y) * LANES, LANES)
    weight = weight_ref[:, :, :, pl.ds(lane, LANES)].reshape(TAPS * LANES, LANES)
    first = jnp.zeros((1, LANES), F32)
    second = jnp.zeros((1, LANES), F32)
    for clip in range(CLIPS_CORE):
        span = slice(clip * ROWS, (clip + 1) * ROWS)
        part = a3 if clip < 2 else b3
        rows = slice(clip % 2 * ROWS, (clip % 2 + 1) * ROWS)
        pre = near_ref[span, :] + gather_taps(dot_nt(part[rows, :], weight))
        pre_ref[span, :] = pre
        kept = pre * valid_rows(facts_ref, clip)
        plus = channel_sums(kept, kept * pre)
        first, second = (first + plus[0], second + plus[1])
    put_pair(stat_ref, first, second)


def pool_kernel(facts_ref, pre_ref, own_ref, other_ref, gain_ref, cot_own, cot_got, slope_ref, sum_ref, pooled_ref):
    y = place('y')
    mean, scale = norm_rows(own_ref, other_ref, pixel_row(facts_ref))
    first = jnp.zeros((1, LANES), F32)
    second = jnp.zeros((1, LANES), F32)
    slots = ROWS // (2 * MEL)
    got = cot_got[144 + CHUNK:160 + CHUNK, :].astype(F32)
    pooled = []
    for clip in range(CLIPS_CORE):
        span = slice(clip * ROWS, (clip + 1) * ROWS)
        count = count_row(facts_ref, clip)
        j = clip % CL_MB
        told = got[j:j + 1] + got[2 + j:3 + j] + got[4 + j:5 + j]
        cot = jnp.where(y == clip // CL_MB, cot_own[j:j + 1, :], told)
        mask = valid_rows(facts_ref, clip)
        normed = (pre_ref[span, :] - mean) * scale
        shaped = gain_ref[2:3, :] * normed + gain_ref[3:4, :]
        gate = jax.nn.sigmoid(shaped)
        active = (shaped * gate * mask).reshape(slots, 2 * MEL, LANES)
        summary = jnp.sum(active, axis=1) / (2 * MEL)
        slot = lax.broadcasted_iota(jnp.int32, (slots, LANES), 0)
        keep = (2 * slot + 1 < count).astype(F32)
        raised = jnp.exp(summary)
        exp_total = jnp.sum(raised * keep, axis=0, keepdims=True)
        halves = (count // 2).astype(F32)
        pooled.append(jnp.sum(summary * keep, axis=0, keepdims=True) / halves + jnp.log(exp_total / halves))
        summary_grad = keep * (cot / halves + cot * raised / exp_total) / (2 * MEL)
        spread = jnp.broadcast_to(summary_grad[:, None, :], (slots, 2 * MEL, LANES))
        slope = spread.reshape(ROWS, LANES) * mask * (gate * (1.0 + shaped * (1.0 - gate)))
        slope_ref[span, :] = slope
        plus = channel_sums(slope, slope * normed)
        first, second = (first + plus[0], second + plus[1])
    put_pair(sum_ref, first, second)
    high = [row.astype(BF).astype(F32) for row in pooled]
    low = [row - top for row, top in zip(pooled, high)]
    rows = jnp.concatenate(high + low + [jnp.zeros((8, LANES), F32)], axis=0)
    pooled_ref[...] = rows.astype(BF)


def pre_grad(slope, pre, mask, mean, scale, gain, sums, pixels):
    normed = (pre - mean) * scale
    return mask * (scale * gain) * (slope - sums[0] / pixels - normed * (sums[1] / pixels))


def both_grad_kernel(facts_ref, slope_ref, pre_ref, own_ref, other_ref, sum_own, sum_other, gain_ref, weight_ref, pooled_ref, columns, a_own, a_mid, a_send, b_own, b_mid, b_send, weight):
    x, y = place('x', 'y')
    pixels = pixel_row(facts_ref)
    mean, scale = norm_rows(own_ref, other_ref, pixels)
    sums = pair_sums(sum_own, sum_other)
    a_send[2 * HALF:2 * HALF + 16, :] = pooled_ref[...]
    for at, (x_of, y_of) in enumerate(((x, y), (x, 1 - y), (1 - x, y), (1 - x, 1 - y))):
        lane = pl.multiple_of((x_of * 2 + y_of) * LANES, LANES)
        weight[:, lanes_of(at)] = weight_ref[:, :, :, pl.ds(lane, LANES)].reshape(TAPS * LANES, LANES)
    for clip in range(CLIPS_CORE):
        span = slice(clip * ROWS, (clip + 1) * ROWS)
        mask = valid_rows(facts_ref, clip)
        grad = pre_grad(slope_ref[span, :], pre_ref[span, :], mask, mean, scale, gain_ref[2:3, :], sums, pixels)
        scatter_taps(grad, columns, clip * ROWS)
        partial = dot_nn(columns[span, :], weight[...])
        rows = slice(clip % 2 * ROWS, (clip % 2 + 1) * ROWS)
        near_rows = slice(HALF + clip % 2 * ROWS, HALF + (clip % 2 + 1) * ROWS)
        far = partial[:, lanes_of(3)].astype(BF)
        if clip < 2:
            a_own[rows, :] = partial[:, lanes_of(0)]
            a_mid[rows, :] = partial[:, lanes_of(1)]
            a_send[rows, :] = far
            a_send[near_rows, :] = partial[:, lanes_of(2)].astype(BF)
        else:
            b_own[rows, :] = partial[:, lanes_of(0)]
            b_mid[rows, :] = partial[:, lanes_of(2)]
            b_send[rows, :] = far
            b_send[near_rows, :] = partial[:, lanes_of(1)].astype(BF)


def pass_on_kernel(a_mid, a_got, b_mid, b_got, pooled_ref, a_next, b_next):
    a_next[HALF:HALF + 16, :] = pooled_ref[...]
    a_next[HALF + 16:HALF + 32, :] = a_got[2 * HALF:2 * HALF + 16]
    a_next[0:HALF, :] = (a_mid[...] + a_got[0:HALF].astype(F32)).astype(BF)
    b_next[...] = (b_mid[...] + b_got[0:HALF].astype(F32)).astype(BF)


def second_weight_grad_kernel(*rest):
    parts, columns, keeps, sends = (rest[:8], rest[8], rest[9:12], rest[12:15])
    hidden, natural, sems = rest[15:]
    core = place('core')
    started = start_copies(hidden_copies(parts, hidden), sems)
    spread = exchange_matrix(C2, C2, block_exchange)
    wait_all(started)
    for clip in range(CLIPS_CORE):
        span = slice(clip * ROWS, (clip + 1) * ROWS)
        hidden[span, :] = dot_nn(hidden[span, :], spread).astype(BF)
    for tap in range(TAPS):
        natural[...] = dot_tn(columns[:, lanes_of(tap)], hidden[...])
        keep_ref, send_ref = (keeps[tap // 3], sends[tap // 3])
        target = slice(tap % 3 * 32, (tap % 3 + 1) * 32)
        for y_of in range(2):
            keep = natural[:, pl.ds(pl.multiple_of((y_of * 2 + core) * LANES, LANES), LANES)]
            send = natural[:, pl.ds(pl.multiple_of((y_of * 2 + 1 - core) * LANES, LANES), LANES)]
            for z_of in range(MB):
                rows = slice(z_of * 32, (z_of + 1) * 32)
                keep_ref[z_of, y_of, target] = keep[rows]
                send_ref[z_of, y_of, target] = send[rows]


def second_core_kernel(k0, k1, k2, g0, g1, g2, own_ref, n1, n2, n3):
    z = place('z')
    for third, (keep_ref, got_ref) in enumerate(((k0, g0), (k1, g1), (k2, g2))):
        rows = slice(third * 96, (third + 1) * 96)
        own_ref[:, rows] = keep_ref[z] + got_ref[z]
        for step, target in ((1, n1), (2, n2), (3, n3)):
            at = jnp.bitwise_xor(z, step)
            target[:, rows] = (keep_ref[at] + got_ref[at]).astype(BF)


def second_sum_kernel(own_ref, g1, g2, g3, keep_ref, send_ref, square_ref):
    y = place('y')
    total = own_ref[...] + g1[...].astype(F32) + g2[...].astype(F32) + g3[...].astype(F32)
    keep_ref[...] = jnp.where(y == 0, total[0], total[1])
    send_ref[...] = jnp.where(y == 0, total[1], total[0]).astype(BF)
    square_ref[...] = jnp.sum(total * total, axis=(0, 1), keepdims=False)[None, :] * jnp.ones((8, 1), F32)


def first_slope_kernel(facts_ref, a_own, a_near, a_last, b_own, b_near, b_last, pre_ref, own_ref, other_ref, gain_ref, slope_ref, sum_ref):
    mean, scale = norm_rows(own_ref, other_ref, pixel_row(facts_ref))
    first = jnp.zeros((1, LANES), F32)
    second = jnp.zeros((1, LANES), F32)
    for clip in range(CLIPS_CORE):
        span = slice(clip * ROWS, (clip + 1) * ROWS)
        rows = slice(clip % 2 * ROWS, (clip % 2 + 1) * ROWS)
        own, near, last = (a_own, a_near, a_last) if clip < 2 else (b_own, b_near, b_last)
        base = near.shape[0] // HALF * HALF - HALF
        near_rows = slice(base + clip % 2 * ROWS, base + (clip % 2 + 1) * ROWS)
        outer = own[rows, :] + near[near_rows, :].astype(F32) + last[rows, :].astype(F32)
        normed = (pre_ref[span, :] - mean) * scale
        shaped = gain_ref[0:1, :] * normed + gain_ref[1:2, :]
        gate = jax.nn.sigmoid(shaped)
        slope = outer * valid_rows(facts_ref, clip) * (gate * (1.0 + shaped * (1.0 - gate)))
        slope_ref[span, :] = slope
        plus = channel_sums(slope, slope * normed)
        first, second = (first + plus[0], second + plus[1])
    put_pair(sum_ref, first, second)


def turn_kernel(x_ref, turned):
    core = place('core')

    def source_of(column):
        core_of = jnp.where(column < 128, core, 1 - core)
        return column // 64 % 2 * 128 + core_of * 64 + column % 64
    spread = exchange_matrix(C1, C1, source_of)
    for clip in range(CLIPS_CORE):
        span = slice(clip * ROWS, (clip + 1) * ROWS)
        turned[span, :] = dot_nn(x_ref[span, :], spread).astype(BF)


def first_weight_grad_kernel(facts_ref, slope_ref, pre_ref, own_ref, other_ref, sum_own, sum_other, gain_ref, turned, columns, keep_ref, send_ref):
    pixels = pixel_row(facts_ref)
    mean, scale = norm_rows(own_ref, other_ref, pixels)
    sums = pair_sums(sum_own, sum_other)

    for clip in range(CLIPS_CORE):
        span = slice(clip * ROWS, (clip + 1) * ROWS)
        mask = valid_rows(facts_ref, clip)
        grad = pre_grad(slope_ref[span, :], pre_ref[span, :], mask, mean, scale, gain_ref[0:1, :], sums, pixels)
        scatter_taps(grad, columns, clip * ROWS)
    for tap in range(TAPS):
        both = dot_tn(columns[:, lanes_of(tap)], turned[...])
        for z_of in range(MB):
            rows = slice(z_of * 32, (z_of + 1) * 32)
            target = slice(tap * 32, (tap + 1) * 32)
            keep_ref[z_of, target] = both[rows, 0:LANES]
            send_ref[z_of, target] = both[rows, LANES:2 * LANES]


def input_grad_kernel(columns, weight_ref, part_ref):
    weight = weight_ref[...].reshape(TAPS * LANES, C1)
    for clip in range(CLIPS_CORE):
        partial = dot_nn(columns[clip * ROWS:(clip + 1) * ROWS, :], weight).astype(BF)
        for z_of in range(MB):
            for x_of in range(2):
                target = slice((clip % 2 * MB + z_of) * 64, (clip % 2 * MB + z_of + 1) * 64)
                rows = slice((z_of * 2 + x_of) * 64, (z_of * 2 + x_of + 1) * 64)
                part_ref[x_of * 2 + clip // 2, target, :] = partial[rows]


def first_core_kernel(keep_ref, got_ref, one_own, one_other, two_own, two_other, pooled_own, pooled_near, pooled_last, own_ref, n0, n1, n2, n3, scratch):
    z, x, y = place('z', 'x', 'y')
    own_ref[...] = keep_ref[z] + got_ref[z]
    one, two = (pair_sums(one_own, one_other), pair_sums(two_own, two_other))
    sums = jnp.concatenate([one[1], one[0], two[1], two[0]], axis=0)
    high = sums.astype(BF).astype(F32)
    norm_tile = jnp.concatenate([high, sums - high, jnp.zeros((8, LANES), F32)], axis=0).astype(BF)
    last = pooled_last[HALF:HALF + 32, :].astype(F32)
    near = pooled_near[...].astype(F32)
    own = pooled_own[...].astype(F32)
    for rows, x_of, y_of in ((own, x, y), (near, 1 - x, y), (last[0:16], x, 1 - y), (last[16:32], 1 - x, 1 - y)):
        for part in range(2):
            for j in range(CL_MB):
                row = jnp.where(y == 0, rows[part * 4 + j:part * 4 + j + 1], rows[part * 4 + 2 + j:part * 4 + 3 + j])
                scratch[pl.ds((x_of * 2 + y_of) * 4 + part * 2 + j, 1), :] = row
    pooled_tile = scratch[...].astype(BF)
    for step, target in ((0, n0), (1, n1), (2, n2), (3, n3)):
        at = jnp.bitwise_xor(z, step)
        target[0:CHUNK, :] = (keep_ref[at] + got_ref[at]).astype(BF)
        target[CHUNK:CHUNK + 16, :] = norm_tile
        target[CHUNK + 16:CHUNK + 32, :] = pooled_tile


def first_sum_kernel(own_ref, n0, g1, g2, g3, square_two, told_ref, keep_ref, send_ref, norm_ref):
    z, y, core = place('z', 'y', 'core')
    total = own_ref[...]
    norm = n0[CHUNK:CHUNK + 16, :].astype(F32)
    for got in (g1, g2, g3):
        total = total + got[0:CHUNK, :].astype(F32)
        norm = norm + got[CHUNK:CHUNK + 16, :].astype(F32)
    norm = norm[0:4] + norm[4:8]
    mine = (lane_index(4) // 32 == z) & (core == 0)
    squares = jnp.sum(total * total, axis=0, keepdims=True) + jnp.sum(jnp.where(mine, norm * norm, 0.0), axis=0, keepdims=True)
    first_rows = lax.broadcasted_iota(jnp.int32, told_ref.shape, 0) % 8 == 0
    told_ref[...] = jnp.where(first_rows, squares + square_two[0:1, :], 0.0)
    turned = pltpu.roll(total, 64, 1)
    low = jnp.where(y == 0, total, turned)
    high = jnp.where(y == 0, turned, total)
    left = lane_index(144) < 64
    keep_ref[...] = jnp.where(left, low[0:144], pltpu.roll(low[144:288], 64, 1))
    send_ref[0:144, :] = jnp.where(left, high[0:144], pltpu.roll(high[144:288], 64, 1))
    rows = jnp.concatenate([norm, jnp.zeros((4, LANES), F32)], axis=0)
    send_ref[144:152, :] = rows
    norm_ref[...] = rows


def adam_write(refs, outs, gradient, factor, step_rate, decay_rate, at):
    weight, moment, square = (ref[at] for ref in refs)
    clipped = gradient * factor
    moment_new = BETA_ONE * moment + (1.0 - BETA_ONE) * clipped
    square_new = BETA_TWO * square + (1.0 - BETA_TWO) * clipped * clipped
    corrected = moment_new * (1.0 / (1.0 - BETA_ONE ** STEP))
    scaled = jnp.sqrt(square_new * (1.0 / (1.0 - BETA_TWO ** STEP))) + ADAM_EPS
    weight_new = weight - step_rate * (corrected / scaled + decay_rate * weight)
    for out, value in zip(outs, (clipped, moment_new, square_new, weight_new, weight_new.astype(BF))):
        out[at] = value


def adam_kernel(told_ref, keep_ref, got_ref, norm_ref, two_keep, two_got, *refs):
    z, y = place('z', 'y')
    one, two, norm, outs = (refs[0:3], refs[3:6], refs[6:9], refs[9:])
    norm_out, one_out, two_out, small_out = (outs[0], outs[1:6], outs[6:11], outs[11:16])
    told = jnp.sum(told_ref[...], axis=0, keepdims=True)
    length = jnp.sqrt(jnp.sum(told, axis=1, keepdims=True))
    norm_out[...] = length
    factor = jnp.minimum(1.0, CLIP_NORM / (length + 1e-06))
    keep, got = (keep_ref[...], got_ref[0:144, :])
    first, second = (jnp.where(y == 0, keep, got), jnp.where(y == 0, got, keep))
    spans = [jnp.concatenate([half[:, 0:64], half[:, 64:128]], axis=0) for half in (first, second)]
    for tap in range(TAPS):
        rows = slice(tap * 32, (tap + 1) * 32)
        gradient = jnp.swapaxes(jnp.concatenate([span[rows] for span in spans], axis=0), 0, 1)
        adam_write(one, one_out, gradient, factor, (9 * C1) ** (-0.5), WEIGHT_DECAY, tap)
        keep, got = (two_keep[rows, :], two_got[rows, :].astype(F32))
        gradient = jnp.concatenate([jnp.where(y == 0, keep, got), jnp.where(y == 0, got, keep)], axis=0)
        adam_write(two, two_out, gradient, factor, (9 * C2) ** (-0.5), WEIGHT_DECAY, tap)
    keep, got = (norm_ref[...], got_ref[144:152, :])
    first, second = (jnp.where(y == 0, keep, got), jnp.where(y == 0, got, keep))
    low = pltpu.roll(first, (0 - z * 32) % LANES, 1)
    high = pltpu.roll(second, (32 - z * 32) % LANES, 1)
    gradient = jnp.where(lane_index(8) < 32, low, high)[0:4, 0:64]
    adam_write(norm, small_out, gradient, factor, GAIN_RATE, 0.0, slice(None))


def input_sum_kernel(facts_ref, got_ref, f0, f1, f2, f3):
    z, x, y = place('z', 'x', 'y')
    for j in range(CL_MB):
        count = jnp.where(y == 0, count_row(facts_ref, j), count_row(facts_ref, CL_MB + j))
        count = jnp.concatenate([count, count], axis=1)
        for step, target in enumerate((f0, f1, f2, f3)):
            at = jnp.bitwise_xor(z, step)
            rows = pl.ds(pl.multiple_of((j * MB + at) * 64, 64), 64)
            total = got_ref[0, rows, :].astype(F32)
            for chip in range(1, 4):
                total = total + got_ref[chip, rows, :].astype(F32)
            frame = (at * 2 + x) * 8 + lax.broadcasted_iota(jnp.int32, (64, C1), 0) // MEL
            target[j] = jnp.where(frame < count, total, 0.0).astype(BF)


def finish_kernel(facts_ref, f0, g1, g2, g3, grad_ref):
    z = place('z')
    for step, piece in enumerate((f0, g1, g2, g3)):
        at = jnp.bitwise_xor(z, step)
        for j in range(CL_MB):
            clip = facts_ref[pl.ds(8 + at * CL_MB + j, 1), :][0, 0]
            grad_ref[clip] = piece[j]


def pooled_kernel(facts_ref, n0, n1, n2, n3, pooled_ref, scratch):
    z = place('z')
    for step, told in enumerate((n0, n1, n2, n3)):
        at = jnp.bitwise_xor(z, step)
        rows = told[CHUNK + 16:CHUNK + 32, :].astype(F32)
        for j in range(CL_MB):
            clip = facts_ref[pl.ds(8 + at * CL_MB + j, 1), :][0, 0]
            for part in range(2):
                chips = [rows[chip * 4 + part * 2 + j:chip * 4 + part * 2 + j + 1] for chip in range(4)]
                scratch[part, pl.ds(clip, 1), :] = jnp.concatenate(chips, axis=1)
    spread = exchange_matrix(C2, C2, block_exchange)
    pooled_ref[...] = dot_nn(scratch[0].astype(BF), spread) + dot_nn(scratch[1].astype(BF), spread)


def fast_body(clip_input, frame_counts, clip_order, cotangent, kernel_one, kernel_one_mean, kernel_one_square, kernel_two, kernel_two_mean, kernel_two_square, norm_params, norm_mean, norm_square):
    one_view, two_view = (kernel_one, jnp.swapaxes(kernel_two, 1, 2))
    p0, p1, p2, p3 = call(take_kernel, [shape_of((CL_MB * 64 + 16, C1))] * MB, [VM] * 2, [VM] * MB, limit=16 * 1024 * 1024)(clip_order, clip_input.reshape(MB * CL_MB, 64, C1))
    one_keep, two_keep, send, gain_rows, cot_own, facts = call(prepare_kernel, [shape_of((144, LANES)), shape_of((CHUNK, LANES)), shape_of((160 + CHUNK, LANES))] + [shape_of((16, LANES)), shape_of((8, LANES), F32), shape_of((16, LANES), jnp.int32)], [VM, VM] + [HB] * 4, [VM] * 6, [pltpu.VMEM(one_view.shape, F32), pltpu.VMEM(two_view.shape, F32), pltpu.VMEM(norm_params.shape, F32), pltpu.VMEM(cotangent.shape, F32), pltpu.SemaphoreType.DMA((4,))], limit=16 * 1024 * 1024)(after(clip_order, p0), frame_counts.reshape(1, 32), one_view, two_view, norm_params, cotangent)

    def spread_z(values):
        got = {step: swap(values[step], 'z', step) for step in steps_of()}
        return [values[0]] + [got[step] for step in (1, 2, 3)]
    p1, p2, p3 = (part for part in (p1, p2, p3))
    arrived = spread_z([p0, p1, p2, p3])
    got = swap(send, 'y')
    a0, b0 = call(stack_kernel, [shape_of((MB, 64, C1))] * 2, [VM] * 4, [VM] * 2)(*arrived)
    one_flat = join(one_keep, got[0:144], gain_rows)
    a1, b1 = (swap(a0, 'x'), swap(b0, 'y'))
    one_parts = spread_z([one_flat] * 4)
    a01, b01 = (join(a0, a1), join(b0, b1))
    deps = ()
    one_others = join(*[swap(after(part, *deps), 'core') for part in one_parts])
    a23, b23 = (swap(a01, 'y'), swap(b01, 'x'))
    inputs = (a0, a1, a23, b0, b1, b23)
    two_flat = join(two_keep, got[144:144 + CHUNK])
    two_flat = after(two_flat, *one_parts[1:])
    two_parts = spread_z([two_flat] * 4)
    weight_one, gains, facts = call(first_weight_kernel, [shape_of((TAPS, MB, 32, C1)), shape_of((8, LANES), F32), shape_of((16, LANES), jnp.int32)], [VM] * 6, [VM] * 3)(*one_parts, one_others, facts)
    pre_one, masked, stat_one = call(first_conv_kernel, [shape_of((PIXELS, LANES), F32), shape_of((PIXELS, C1)), shape_of((8, LANES), F32)], [VM] * 8, [VM] * 3)(facts, *inputs, weight_one)
    stat_one_other = swap(stat_one, 'core')
    ha_on, ha0, hb_on, hb0 = call(hidden_kernel, [shape_of((HALF + pad, LANES)) for pad in (32, 48)] * 2, [VM] * 5, [VM] * 4)(after(facts, *two_parts[1:]), pre_one, stat_one, stat_one_other, gains)
    ha1, hb1 = (swap(ha_on, 'x'), swap(hb_on, 'y'))
    ha2, hb2 = (swap(ha0, 'y'), swap(hb0, 'x'))
    ha3, hb3 = (swap(ha1, 'y'), swap(hb1, 'x'))
    hidden_parts = (ha0, ha1, ha2, ha3, hb0, hb1, hb2, hb3)
    deps = (ha0,)
    two_others = [swap(after(part, *deps), 'core') for part in two_parts]
    weight_two = call(second_weight_kernel, shape_of((TAPS, MB, 32, C2)), [VM] * 8, VM)(*two_parts, *two_others)
    ha = hidden_parts
    turned = call(turn_kernel, shape_of((PIXELS, C1)), [VM], VM)(masked)
    near_two = call(near_conv_kernel, shape_of((PIXELS, LANES), F32), [VM] * 7, VM)(ha[0], ha[1], ha[2], ha[4], ha[5], ha[6], after(weight_two, turned))
    pre_two, stat_two = call(far_conv_kernel, [shape_of((PIXELS, LANES), F32), shape_of((8, LANES), F32)], [VM] * 5, [VM] * 2)(facts, ha[3], ha[7], weight_two, near_two)
    stat_two_other = swap(stat_two, 'core')
    slope_two, sum_two, pooled_own = call(pool_kernel, [shape_of((PIXELS, LANES), F32), shape_of((8, LANES), F32), shape_of((16, LANES))], [VM] * 7, [VM] * 3)(facts, pre_two, stat_two, stat_two_other, gains, cot_own, got)
    sum_two_other = swap(sum_two, 'core')
    columns_two, a_own, a_mid, a_send, b_own, b_mid, b_send = call(both_grad_kernel, [shape_of((PIXELS, TAPS * LANES))] + [shape_of((HALF, LANES), F32)] * 2 + [shape_of((2 * HALF + 16, LANES))] + [shape_of((HALF, LANES), F32)] * 2 + [shape_of((2 * HALF, LANES))], [VM] * 10, [VM] * 7, [pltpu.VMEM((TAPS * LANES, C2), BF)])(facts, slope_two, pre_two, stat_two, stat_two_other, sum_two, sum_two_other, gains, weight_two, pooled_own)
    a_got = a_near = swap(a_send, 'x')
    b_got = b_near = swap(b_send, 'y')
    a_pool = a_got[2 * HALF:]
    thirds = call(second_weight_grad_kernel, [shape_of((MB, 2, 96, LANES), F32)] * 6, [ANY] * 8 + [VM], [VM] * 6, [pltpu.VMEM((PIXELS, C2), BF), pltpu.VMEM((LANES, C2), F32), pltpu.SemaphoreType.DMA((8,))])(*hidden_parts, columns_two)

    def sum_cores(*deps):
        sends = [after(part, *deps) if deps else part for part in thirds[3:6]]
        return call(second_core_kernel, [shape_of((2, CHUNK, LANES), F32)] + [shape_of((2, CHUNK, LANES))] * 3, [VM] * 6, [VM] * 4)(*thirds[0:3], *[swap(part, 'core') for part in sends])
    two_own, t1, t2, t3 = sum_cores()
    a_got = after(a_got, t1)
    a_next, b_next = call(pass_on_kernel, [shape_of((HALF + 32, LANES)), shape_of((HALF, LANES))], [VM] * 5, [VM] * 2)(a_mid, a_got, b_mid, b_got, pooled_own)
    a_last, b_last = (swap(a_next, 'y'), swap(b_next, 'x'))
    slope_one, sum_one = call(first_slope_kernel, [shape_of((PIXELS, LANES), F32), shape_of((8, LANES), F32)], [VM] * 11, [VM] * 2)(after(facts, t1), a_own, a_near, a_last, b_own, b_near, b_last, pre_one, stat_one, stat_one_other, gains)
    sum_one_other = swap(sum_one, 'core')
    columns_one, one_part, one_part_send = call(first_weight_grad_kernel, [shape_of((PIXELS, TAPS * LANES))] + [shape_of((MB, CHUNK, LANES), F32)] * 2, [VM] * 9, [VM] * 3)(facts, slope_one, pre_one, stat_one, stat_one_other, sum_one, sum_one_other, gains, turned)
    input_part = call(input_grad_kernel, shape_of((4, ROWS, C1)), [VM] * 2, VM)(columns_one, weight_one)
    two_keep_sum, two_send_sum, square_two = call(second_sum_kernel, [shape_of((CHUNK, LANES), F32), shape_of((CHUNK, LANES)), shape_of((8, LANES), F32)], [VM] * 4, [VM] * 3)(*spread_z([two_own, t1, t2, t3]))
    one_own, n0, n1, n2, n3 = call(first_core_kernel, [shape_of((CHUNK, LANES), F32)] + [shape_of((CHUNK + 32, LANES))] * MB, [VM] * 9, [VM] * 5, [pltpu.VMEM((16, LANES), F32)])(one_part, swap(after(one_part_send, square_two), 'core'), sum_one, sum_one_other, sum_two, sum_two_other, pooled_own, a_pool, a_last)
    g1, g2, g3 = spread_z([n0, n1, n2, n3])[1:]
    input_got = lax.all_to_all(input_part, ('x', 'y'), 0, 0, tiled=True)
    f0, f1, f2, f3 = call(input_sum_kernel, [shape_of((CL_MB, 64, C1))] * MB, [VM] * 2, [VM] * 4)(facts, input_got)
    two_got_sum = swap(after(two_send_sum, n1), 'y')
    f1, f2, f3 = spread_z([f0, f1, f2, f3])[1:]
    told, one_keep_sum, one_send_sum, norm_sum = call(first_sum_kernel, [shape_of((32 * 8, LANES), F32), shape_of((144, LANES), F32), shape_of((152, LANES), F32), shape_of((8, LANES), F32)], [VM] * 6, [VM] * 4)(one_own, n0, g1, g2, g3, square_two)
    told_sent = told
    told = lax.all_to_all(told, AXES, 0, 0, tiled=True)
    one_got_sum = swap(one_send_sum, 'y')
    one_shapes = [shape_of(one_view.shape, F32)] * 4 + [shape_of(one_view.shape)]
    two_shapes = [shape_of(two_view.shape, F32)] * 4 + [shape_of(two_view.shape)]
    norm_shapes = [shape_of(norm_params.shape, F32)] * 4 + [shape_of(norm_params.shape)]
    state = (kernel_one, kernel_one_mean, kernel_one_square, two_view, jnp.swapaxes(kernel_two_mean, 1, 2), jnp.swapaxes(kernel_two_square, 1, 2), norm_params, norm_mean, norm_square)
    updates = call(adam_kernel, [shape_of((1, 1), F32)] + one_shapes + two_shapes + norm_shapes, [VM] * 15, [VM] * 16, limit=62 * 1024 * 1024)(told, one_keep_sum, one_got_sum, norm_sum, two_keep_sum, two_got_sum, *state)
    grad_norm = updates[0].reshape(())
    first_update, norm_update = (tuple(updates[1:6]), tuple(updates[11:16]))
    second_update = tuple((jnp.swapaxes(part, 1, 2) for part in updates[6:11]))
    pooled = call(pooled_kernel, shape_of((MB * CL_MB, C2), F32), [VM] * 5, VM, [pltpu.VMEM((2, MB * CL_MB, C2), F32)])(facts, n0, g1, g2, g3)
    input_grad = call(finish_kernel, shape_of((MB * CL_MB, 64, C1)), [VM] * 5, VM)(facts, after(f0, updates[0]), f1, f2, f3)
    input_grad = input_grad.reshape(clip_input.shape)
    return (pooled, input_grad, grad_norm) + first_update + second_update + norm_update


def solution(mesh):
    if mesh.shape['tm'] == 2 * MB and mesh.shape['batch'] == 4:
        grid = Mesh(mesh.devices.reshape(MB, 2, 2, 2), AXES)
        tm, batch, chosen = (('z', 'x'), ('y', 'core'), fast_body)
    else:
        grid, tm, batch, chosen = (mesh, 'tm', 'batch', general_body)
    kernels = (P(None, batch, tm),) * 3
    norms = (P(None, tm),) * 3
    in_specs = (P(batch, tm, None, None), P(), P(), P(batch, None)) + 2 * kernels + norms
    out_specs = (P(batch, None), P(batch, tm, None, None), P())
    out_specs = out_specs + (P(None, batch, tm),) * 10 + (P(None, tm),) * 5
    return jax.shard_map(chosen, mesh=grid, in_specs=in_specs, out_specs=out_specs, check_vma=False)
```
